32 devices in a mesh: seq: 4 (over y, core), dp: 8 (over z, x).
Axes of the slice: x: 2, y: 2, z: 4, core: 2. Of those that a mesh axis runs over, the one named last changes fastest.
Arguments:
- tokens: bfloat16 [8, 2048, 768], P('dp', 'seq'), may hold values from -6 to 6
- item_lengths: int32 [8, 4], P('dp'), may hold values from 1 to 2045, as said below
- w_query: bfloat16 [768, 768], replicated, may hold values from -0.21875 to 0.21875
- w_key: bfloat16 [768, 768], replicated, may hold values from -0.21875 to 0.21875
- w_value: bfloat16 [768, 768], replicated, may hold values from -0.21875 to 0.21875
- w_out: bfloat16 [768, 768], replicated, may hold values from -2.5 to 2.5
- w_in: bfloat16 [768, 3072], replicated, may hold values from -0.21875 to 0.21875
- w_back: bfloat16 [3072, 768], replicated, may hold values from -0.109375 to 0.109375
- norm1_gain: float32 [768], replicated, may hold values from 0.5 to 1.5
- norm1_bias: float32 [768], replicated, may hold values from -1 to 1
- norm2_gain: float32 [768], replicated, may hold values from 0.5 to 1.5
- norm2_bias: float32 [768], replicated, may hold values from -1 to 1
- pool_weight: float32 [768, 5], replicated, may hold values from 0.1 to 0.5
- out_grad: bfloat16 [8, 2048, 768], P('dp', 'seq'), may hold values from -6 to 6
Outputs:
- mixed: bfloat16 [8, 2048, 768], P('dp', 'seq')
- tokens_grad: bfloat16 [8, 2048, 768], P('dp', 'seq')
- grad_w_query: float32 [768, 768], P(('seq', 'dp'))
- grad_w_key: float32 [768, 768], P(('seq', 'dp'))
- grad_w_value: float32 [768, 768], P(('seq', 'dp'))
- grad_w_out: float32 [768, 768], P(('seq', 'dp'))
- grad_w_in: float32 [768, 3072], P(('seq', 'dp'))
- grad_w_back: float32 [3072, 768], P(('seq', 'dp'))
- grad_norm1_gain: float32 [768], P(('seq', 'dp'))
- grad_norm1_bias: float32 [768], P(('seq', 'dp'))
- grad_norm2_gain: float32 [768], P(('seq', 'dp'))
- grad_norm2_bias: float32 [768], P(('seq', 'dp'))
- grad_pool_weight: float32 [768, 5], P(('seq', 'dp'))
The draws below stay inside these ranges and needn't reach their ends.
Inputs may be any that keep to these rules, and one draw needn't show every extreme that they name: `item_lengths`: in each row the lengths sum to 2048 or less; one item, at a slot drawn per row, starts within the row's first 512 tokens and ends within its last 512.
All inputs are finite; a program needn't handle non-finite values.
Results may differ from the reference program's by a relative error of at most 0.014.
Values may be sent and summed in bfloat16 or wider, within the bound.
A program may use at most 192 MiB of HBM per device.

```python
import jax
import jax.numpy as jnp
from jax import lax

D = 768
H = 12
DH = 64
FF = 3072
ROW_LEN = 2048
HALF = 64
PWIN = 512
ITEMS = 4
TOK_SEQ = 512
ROWS = 8


def draw_item_lengths(key, part):
    key = jax.random.fold_in(key, 11)
    short_key, place_key, pad_key = jax.random.split(key, 3)
    shorts = jax.random.randint(short_key, (ROWS, ITEMS), 1, TOK_SEQ // 4 + 1)
    chosen = jax.random.randint(place_key, (ROWS, 1), 0, ITEMS)
    padding = jax.random.randint(pad_key, (ROWS, 1), 0, TOK_SEQ // 4)
    first_row = jnp.arange(ROWS)[:, None] == 0
    shorts = jnp.where(first_row, 1, shorts)
    padding = jnp.where(first_row, 0, padding)
    is_long = jnp.arange(ITEMS)[None, :] == chosen
    others = jnp.sum(jnp.where(is_long, 0, shorts), axis=1, keepdims=True)
    return jnp.where(is_long, ROW_LEN - others - padding, shorts).astype(jnp.int32)


def shard_levels(key, shape, pieces, low, top_value):
    factor_of = 1.0
    for position, shards_of in pieces:
        draws = jax.random.uniform(jax.random.fold_in(jax.random.fold_in(key, 6), position), (shards_of,), jnp.float32, low / len(pieces), top_value / len(pieces))
        factor_of = factor_of * jnp.repeat(jnp.exp(draws), shape[position] // shards_of).reshape((-1,) + (1,) * (len(shape) - 1 - position))
    return factor_of


def scatter_about(stream_key, extent, deviation, bound, cuts=(), held_as=jnp.bfloat16):
    factor_of = shard_levels(stream_key, extent, cuts, -0.22, 0.18) if cuts else 1.0
    result = jax.random.normal(stream_key, extent, jnp.float32) * deviation * factor_of
    return jnp.minimum(jnp.maximum(result, -bound), bound).astype(held_as)


def setup_inputs(seed: int = 0) -> dict:
    key_list = jax.random.split(jax.random.key(seed), 15)
    tokens = scatter_about(key_list[0], (ROWS, ROW_LEN, D), 1.0, 6.0, ((0, 8), (1, 4)))
    item_lengths = draw_item_lengths(jax.random.fold_in(key_list[14], 71), 0)
    w_query = scatter_about(key_list[2], (D, D), D ** -0.5, 0.21875)
    w_key = scatter_about(key_list[3], (D, D), D ** -0.5, 0.21875)
    w_value = scatter_about(key_list[4], (D, D), D ** -0.5, 0.21875)
    w_out = scatter_about(key_list[5], (D, D), (D // 128) ** -0.5, 2.5)
    w_in = scatter_about(key_list[6], (D, FF), D ** -0.5, 0.21875)
    w_back = scatter_about(key_list[7], (FF, D), FF ** -0.5, 0.109375)
    norm1_gain = jnp.clip(1.0 + 0.1 * jax.random.normal(key_list[8], (D,), jnp.float32), 0.5, 1.5)
    norm1_bias = scatter_about(key_list[9], (D,), 0.2, 1.0, (), jnp.float32)
    norm2_gain = jnp.clip(1.0 + 0.1 * jax.random.normal(key_list[10], (D,), jnp.float32), 0.5, 1.5)
    norm2_bias = scatter_about(key_list[11], (D,), 0.2, 1.0, (), jnp.float32)
    pool_weight = jnp.clip(jax.random.uniform(key_list[12], (D, 5), jnp.float32, 0.1, 0.5), 0.1, 0.5)
    out_grad = scatter_about(key_list[13], (ROWS, ROW_LEN, D), 1.0, 6.0, ((0, 8), (1, 4)))
    return {"tokens": tokens, "item_lengths": item_lengths, "w_query": w_query, "w_key": w_key, "w_value": w_value, "w_out": w_out, "w_in": w_in, "w_back": w_back, "norm1_gain": norm1_gain, "norm1_bias": norm1_bias, "norm2_gain": norm2_gain, "norm2_bias": norm2_bias, "pool_weight": pool_weight, "out_grad": out_grad}


@jax.custom_vjp
def low(v):
    return lax.optimization_barrier(v.astype(jnp.bfloat16)).astype(jnp.float32)

@jax.custom_vjp
def low_back(v):
    return v

def low_keep(v):
    return (low(v), None)

def low_pass(kept, grad):
    return (grad,)

def back_keep(v):
    return (v, None)

def back_low(kept, grad):
    return (low(grad),)
low.defvjp(low_keep, low_pass)
low_back.defvjp(back_keep, back_low)
highest = lax.Precision.HIGHEST

def rounded(value):
    return low_back(low(value))

def matmul(left, right):
    return jnp.dot(left, right, precision=highest)

def layer_norm(values, gain, offset):
    center = lax.optimization_barrier(jnp.mean(values, axis=-1, keepdims=True))
    shifted = values - center
    spread = lax.optimization_barrier(jnp.mean(shifted * shifted, axis=-1, keepdims=True))
    return shifted * lax.rsqrt(spread + 1e-05) * gain + offset

def segment_ids(lengths_row):
    places = jnp.arange(ROW_LEN, dtype=jnp.int32)
    bounds = jnp.cumsum(lengths_row).astype(jnp.int32)
    return lax.optimization_barrier(jnp.sum((places[:, None] >= bounds[None, :]).astype(jnp.int32), axis=1)).astype(jnp.int32)

def pool_conv(values, segments, weight):
    padded = jnp.pad(values, ((2, 2), (0, 0)))
    segment_pad = jnp.pad(segments, (2, 2), constant_values=-2)
    centers = segments[::4]
    total = jnp.zeros((ROW_LEN // 4, values.shape[1]), jnp.float32)
    for tap_index in range(5):
        taken = padded[tap_index:tap_index + ROW_LEN:4]
        keep = (segment_pad[tap_index:tap_index + ROW_LEN:4] == centers).astype(jnp.float32)
        total = total + taken * keep[:, None] * weight[:, tap_index]
    return total

def row_forward(parameters, row_input, segments):
    w_query, w_key, w_value, w_out, w_in, w_back, gain_one, offset_one, gain_two, offset_two, pool_weight = parameters
    queries = rounded(matmul(row_input, w_query))
    keys_row = rounded(matmul(row_input, w_key))
    values_row = rounded(matmul(row_input, w_value))
    pool_count = ROW_LEN // 4
    pooled_keys = low(pool_conv(keys_row, segments, pool_weight)).reshape(pool_count, H, DH)
    pooled_values = low(pool_conv(values_row, segments, pool_weight)).reshape(pool_count, H, DH)
    block_len = min(512, ROW_LEN)
    span = block_len + 2 * HALF
    keys_pad = jnp.pad(keys_row, ((HALF, HALF), (0, 0)))
    values_pad = jnp.pad(values_row, ((HALF, HALF), (0, 0)))
    segment_pad = jnp.pad(segments, (HALF, HALF), constant_values=-2)
    pool_place = 4 * jnp.arange(pool_count, dtype=jnp.int32)
    pool_segments = segments[::4]

    def attend_block(start):
        query_part = lax.dynamic_slice_in_dim(queries, start, block_len, 0).reshape(block_len, H, DH)
        query_segments = lax.dynamic_slice_in_dim(segments, start, block_len, 0)
        key_part = lax.dynamic_slice_in_dim(keys_pad, start, span, 0).reshape(span, H, DH)
        value_part = lax.dynamic_slice_in_dim(values_pad, start, span, 0).reshape(span, H, DH)
        key_segments = lax.dynamic_slice_in_dim(segment_pad, start, span, 0)
        query_place = start + jnp.arange(block_len, dtype=jnp.int32)
        key_place = start - HALF + jnp.arange(span, dtype=jnp.int32)
        near_mask = (jnp.abs(query_place[:, None] - key_place[None, :]) <= HALF) & (query_segments[:, None] == key_segments[None, :])
        pool_mask = (jnp.abs(query_place[:, None] - pool_place[None, :]) <= 2 * PWIN) & (query_segments[:, None] == pool_segments[None, :])
        near_scores = low_back(jnp.einsum('the,khe->htk', query_part, key_part, precision=highest) * 0.125)
        near_scores = jnp.where(near_mask[None], near_scores, -1e+30)
        pool_scores = low_back(jnp.einsum('the,khe->htk', query_part, pooled_keys, precision=highest) * 0.125)
        pool_scores = jnp.where(pool_mask[None], pool_scores, -1e+30)
        scores = jnp.concatenate([near_scores, pool_scores], axis=2)
        top = lax.optimization_barrier(jnp.max(scores, axis=2, keepdims=True))
        weights_exp = jnp.exp(scores - top)
        probs = low(weights_exp / lax.optimization_barrier(jnp.sum(weights_exp, axis=2, keepdims=True)))
        mixed_part = jnp.einsum('htk,khe->the', probs[:, :, :span], value_part, precision=highest)
        mixed_part = mixed_part + jnp.einsum('htk,khe->the', probs[:, :, span:], pooled_values, precision=highest)
        return mixed_part.reshape(block_len, H * DH)
    starts = block_len * jnp.arange(ROW_LEN // block_len, dtype=jnp.int32)
    attention = lax.map(jax.checkpoint(attend_block), starts).reshape(ROW_LEN, H * DH)
    attended = rounded(attention)
    branch = low_back(matmul(attended, w_out))
    first = layer_norm(row_input + branch, gain_one, offset_one)
    inner = low_back(matmul(low(first), w_in))
    activated = low(jax.nn.gelu(inner, approximate=False))
    feed = low_back(matmul(activated, w_back))
    return layer_norm(first + feed, gain_two, offset_two)

def reference(tokens, item_lengths, w_query, w_key, w_value, w_out, w_in, w_back, norm1_gain, norm1_bias, norm2_gain, norm2_bias, pool_weight, out_grad):
    parameters = (w_query.astype(jnp.float32), w_key.astype(jnp.float32), w_value.astype(jnp.float32), w_out.astype(jnp.float32), w_in.astype(jnp.float32), w_back.astype(jnp.float32), norm1_gain, norm1_bias, norm2_gain, norm2_bias, pool_weight)

    def each_row(totals, items):
        row_input, row_grad, row_lengths = items
        segments = segment_ids(row_lengths)

        def forward(weights_in, values_in):
            return row_forward(weights_in, values_in, segments)
        output, backward = jax.vjp(forward, parameters, row_input)
        param_grads, input_grad = backward(row_grad)
        totals = jax.tree.map(jnp.add, totals, param_grads)
        return (totals, (output.astype(jnp.bfloat16), input_grad.astype(jnp.bfloat16)))
    zeroed = jax.tree.map(jnp.zeros_like, parameters)
    totals, (outputs, input_grads) = lax.scan(each_row, zeroed, (tokens.astype(jnp.float32), out_grad.astype(jnp.float32), item_lengths))
    return (outputs, input_grads, totals[0], totals[1], totals[2], totals[3], totals[4], totals[5], totals[6], totals[7], totals[8], totals[9], totals[10])
```

```python
from functools import partial

import jax
import jax.numpy as jnp
from jax import lax
from jax.sharding import PartitionSpec as P

H = 12
DH = 64
HALF = 64
PWIN = 512


def with_halo(cells, sides, width):
    for axis, dim in sides:
        count = lax.axis_size(axis)
        ends = count - 1
        head = lax.slice_in_dim(cells, 0, width, axis=dim)
        tail = lax.slice_in_dim(cells, cells.shape[dim] - width, cells.shape[dim], axis=dim)
        cells = jnp.concatenate(
            [
                lax.ppermute(tail, axis, [(i, (i + 1) % count) for i in range(ends)]),
                cells,
                lax.ppermute(head, axis, [((i + 1) % count, i) for i in range(ends)]),
            ],
            axis=dim,
        )
    return cells


def shifted_2(shard, axis, by):
    size = lax.axis_size(axis)
    pairs = [(i, i + by) for i in range(size) if 0 <= i + by < size]
    return lax.ppermute(shard, axis, pairs)


def swap_stage(parts, dim, axis, count, stride):
    size = lax.axis_size(axis)
    me = lax.axis_index(axis)
    mine = (me // stride) % count
    total = lax.dynamic_index_in_dim(parts, mine, dim, keepdims=False)
    for hop in range(1, count):
        pairs = []
        for device in range(size):
            place = (device // stride) % count
            pairs.append((device, device + ((place + hop) % count - place) * stride))
        block = lax.dynamic_index_in_dim(parts, (mine + hop) % count, dim, keepdims=False)
        total = total + lax.ppermute(block.astype(jnp.bfloat16), axis, pairs).astype(jnp.float32)
    return total


def scatter_sum(grad, seq_first):
    seq, dp = lax.axis_size("seq"), lax.axis_size("dp")
    rows = grad.shape[0] // (seq * dp)
    parts = grad.reshape(seq // 2, 2, dp // 2, 2, rows, grad.shape[1])
    parts = swap_stage(parts, 1, "seq", 2, 1)
    if seq_first:
        parts = swap_stage(parts, 0, "seq", seq // 2, 2)
        parts = swap_stage(parts, 1, "dp", 2, 1)
    else:
        parts = swap_stage(parts, 2, "dp", 2, 1)
        parts = swap_stage(parts, 0, "seq", seq // 2, 2)
    return swap_stage(parts, 0, "dp", dp // 2, 2)


def layer_norm(values, gain, offset):
    center = jnp.mean(values, axis=-1, keepdims=True)
    shifted = values - center
    spread = jnp.mean(shifted * shifted, axis=-1, keepdims=True)
    return shifted * lax.rsqrt(spread + 1e-05) * gain + offset


def score_pair(query_group, pair_group, pool_group, near_mask, pool_mask):
    group_size = query_group.shape[0]
    span = pair_group.shape[2]
    pool_count = pool_group.shape[2]
    key_heads = pair_group[:, 0].reshape(group_size, span, H, DH)
    pool_heads = pool_group[:, 0].reshape(group_size, pool_count, H, DH)
    near_scores = (
        jnp.einsum("gthe,gkhe->ghtk", query_group, key_heads, preferred_element_type=jnp.float32)
        * 0.125
    )
    pool_scores = (
        jnp.einsum("gthe,gkhe->ghtk", query_group, pool_heads, preferred_element_type=jnp.float32)
        * 0.125
    )
    near_scores = jnp.where(near_mask[:, None], near_scores, -1e30)
    pool_scores = jnp.where(pool_mask[:, None], pool_scores, -1e30)
    value_heads = pair_group[:, 1].reshape(group_size, span, H, DH)
    pool_values = pool_group[:, 1].reshape(group_size, pool_count, H, DH)
    return (near_scores, pool_scores, key_heads, pool_heads, value_heads, pool_values)


def attend_forward(items):
    query_group, pair_group, pool_group, near_mask, pool_mask = items
    near_scores, pool_scores, key_heads, pool_heads, value_heads, pool_values = score_pair(
        query_group, pair_group, pool_group, near_mask, pool_mask
    )
    top = jnp.maximum(jnp.max(near_scores, axis=3), jnp.max(pool_scores, axis=3))
    near_exp = jnp.exp(near_scores - top[..., None])
    pool_exp = jnp.exp(pool_scores - top[..., None])
    total = jnp.sum(near_exp, axis=3) + jnp.sum(pool_exp, axis=3)
    near_probs = (near_exp / total[..., None]).astype(jnp.bfloat16)
    pool_probs = (pool_exp / total[..., None]).astype(jnp.bfloat16)
    mixed = jnp.einsum(
        "ghtk,gkhe->gthe", near_probs, value_heads, preferred_element_type=jnp.float32
    )
    mixed = mixed + jnp.einsum(
        "ghtk,gkhe->gthe", pool_probs, pool_values, preferred_element_type=jnp.float32
    )
    return (mixed.reshape(mixed.shape[0], mixed.shape[1], H * DH), top + jnp.log(total))


def attend_backward(items):
    query_group, pair_group, pool_group, near_mask, pool_mask, log_total, grad_group = items
    near_scores, pool_scores, key_heads, pool_heads, value_heads, pool_values = score_pair(
        query_group, pair_group, pool_group, near_mask, pool_mask
    )
    group_size, tok_count = (query_group.shape[0], query_group.shape[1])
    span, pool_count = (key_heads.shape[1], pool_heads.shape[1])
    near_probs = jnp.exp(near_scores - log_total[..., None])
    pool_probs = jnp.exp(pool_scores - log_total[..., None])
    near_low = near_probs.astype(jnp.bfloat16)
    pool_low = pool_probs.astype(jnp.bfloat16)
    grad_heads = grad_group.reshape(group_size, tok_count, H, DH)
    near_dprob = jnp.einsum(
        "gthe,gkhe->ghtk", grad_heads, value_heads, preferred_element_type=jnp.float32
    )
    pool_dprob = jnp.einsum(
        "gthe,gkhe->ghtk", grad_heads, pool_values, preferred_element_type=jnp.float32
    )
    inner_sum = jnp.sum(near_probs * near_dprob, axis=3) + jnp.sum(pool_probs * pool_dprob, axis=3)
    near_dscore = (near_probs * (near_dprob - inner_sum[..., None])).astype(jnp.bfloat16)
    pool_dscore = (pool_probs * (pool_dprob - inner_sum[..., None])).astype(jnp.bfloat16)
    grad_query = jnp.einsum(
        "ghtk,gkhe->gthe", near_dscore, key_heads, preferred_element_type=jnp.float32
    )
    grad_query = (
        grad_query
        + jnp.einsum("ghtk,gkhe->gthe", pool_dscore, pool_heads, preferred_element_type=jnp.float32)
    ) * 0.125
    near_key_grad = (
        jnp.einsum("ghtk,gthe->gkhe", near_dscore, query_group, preferred_element_type=jnp.float32)
        * 0.125
    )
    near_value_grad = jnp.einsum(
        "ghtk,gthe->gkhe", near_low, grad_heads, preferred_element_type=jnp.float32
    )
    pool_key_grad = (
        jnp.einsum("ghtk,gthe->gkhe", pool_dscore, query_group, preferred_element_type=jnp.float32)
        * 0.125
    )
    pool_value_grad = jnp.einsum(
        "ghtk,gthe->gkhe", pool_low, grad_heads, preferred_element_type=jnp.float32
    )
    width_all = H * DH
    near_grads = jnp.stack(
        [
            near_key_grad.reshape(group_size, span, width_all),
            near_value_grad.reshape(group_size, span, width_all),
        ],
        axis=1,
    )
    pool_grads = jnp.stack(
        [
            pool_key_grad.reshape(group_size, pool_count, width_all),
            pool_value_grad.reshape(group_size, pool_count, width_all),
        ],
        axis=1,
    )
    return (grad_query.reshape(group_size, tok_count, width_all), near_grads, pool_grads)


def per_device(
    tokens,
    item_lengths,
    w_query,
    w_key,
    w_value,
    w_out,
    w_in,
    w_back,
    norm1_gain,
    norm1_bias,
    norm2_gain,
    norm2_bias,
    pool_weight,
    out_grad,
):
    row_count, tok_count, model_width = tokens.shape
    row_len = tok_count * lax.axis_size("seq")
    row_start = lax.axis_index("seq") * tok_count
    span = tok_count + 2 * HALF
    pool_all = row_len // 4
    places = jnp.arange(row_len, dtype=jnp.int32)
    bounds = jnp.cumsum(item_lengths, axis=1)
    segment_all = jnp.sum((places[None, :, None] >= bounds[:, None, :]).astype(jnp.int32), axis=2)
    segment_pad = jnp.pad(segment_all, ((0, 0), (HALF, HALF)), constant_values=-2)
    key_segments = lax.dynamic_slice_in_dim(segment_pad, row_start, span, 1)
    query_segments = key_segments[:, HALF : HALF + tok_count]
    pool_segments = segment_all[:, ::4]
    query_place = row_start + jnp.arange(tok_count, dtype=jnp.int32)
    key_place = row_start - HALF + jnp.arange(span, dtype=jnp.int32)
    pool_place = 4 * jnp.arange(pool_all, dtype=jnp.int32)
    near_mask = (jnp.abs(query_place[:, None] - key_place[None, :]) <= HALF)[None] & (
        query_segments[:, :, None] == key_segments[:, None, :]
    )
    pool_mask = (jnp.abs(query_place[:, None] - pool_place[None, :]) <= 2 * PWIN)[None] & (
        query_segments[:, :, None] == pool_segments[:, None, :]
    )
    tap_masks = []
    for tap_index in range(5):
        begin = HALF + tap_index - 2
        tap_masks.append(
            (key_segments[:, begin : begin + tok_count : 4] == query_segments[:, ::4]).astype(
                jnp.float32
            )
        )
    flat_tokens = tokens.reshape(row_count * tok_count, model_width)
    queries = jnp.dot(flat_tokens, w_query, preferred_element_type=jnp.float32).astype(jnp.bfloat16)
    keys_low = jnp.dot(flat_tokens, w_key, preferred_element_type=jnp.float32).astype(jnp.bfloat16)
    values_low = jnp.dot(flat_tokens, w_value, preferred_element_type=jnp.float32).astype(
        jnp.bfloat16
    )
    key_value = jnp.stack(
        [
            keys_low.reshape(row_count, tok_count, model_width),
            values_low.reshape(row_count, tok_count, model_width),
        ],
        axis=1,
    )
    pair_halo = with_halo(key_value, (("seq", 2),), HALF)
    pooled_sum = jnp.zeros((row_count, 2, tok_count // 4, model_width), jnp.float32)
    for tap_index in range(5):
        begin = HALF + tap_index - 2
        taken = pair_halo[:, :, begin : begin + tok_count : 4].astype(jnp.float32)
        pooled_sum = (
            pooled_sum + taken * tap_masks[tap_index][:, None, :, None] * pool_weight[:, tap_index]
        )
    pooled_low = pooled_sum.astype(jnp.bfloat16)
    pooled_rows = lax.all_gather(pooled_low, "seq", axis=2, tiled=True)
    group_size = min(row_count, max(1, 512 // tok_count))
    group_count = row_count // group_size

    def grouped(array):
        return array.reshape((group_count, group_size) + array.shape[1:])

    query_heads = queries.reshape(row_count, tok_count, H, DH)
    shared = (
        grouped(query_heads),
        grouped(pair_halo),
        grouped(pooled_rows),
        grouped(near_mask),
        grouped(pool_mask),
    )
    attention, log_total = lax.map(attend_forward, shared)
    attended = attention.reshape(row_count * tok_count, model_width).astype(jnp.bfloat16)
    branch = jnp.dot(attended, w_out, preferred_element_type=jnp.float32)
    first, first_back = jax.vjp(
        layer_norm, flat_tokens.astype(jnp.float32) + branch, norm1_gain, norm1_bias
    )
    first_low = first.astype(jnp.bfloat16)
    inner = jnp.dot(first_low, w_in, preferred_element_type=jnp.float32)
    activated, gelu_back = jax.vjp(partial(jax.nn.gelu, approximate=False), inner)
    activated_low = activated.astype(jnp.bfloat16)
    feed = jnp.dot(activated_low, w_back, preferred_element_type=jnp.float32)
    output, second_back = jax.vjp(layer_norm, first + feed, norm2_gain, norm2_bias)
    mixed = output.astype(jnp.bfloat16).reshape(row_count, tok_count, model_width)
    upstream = out_grad.reshape(row_count * tok_count, model_width).astype(jnp.float32)
    z_grad, grad_gain_two, grad_bias_two = second_back(upstream)
    feed_grad = z_grad.astype(jnp.bfloat16)
    grad_back_weight = jnp.einsum(
        "nf,nd->fd", activated_low, feed_grad, preferred_element_type=jnp.float32
    )
    activated_grad = jnp.einsum("nd,fd->nf", feed_grad, w_back, preferred_element_type=jnp.float32)
    (inner_grad,) = gelu_back(activated_grad)
    inner_low = inner_grad.astype(jnp.bfloat16)
    grad_in_weight = jnp.einsum(
        "nd,nf->df", first_low, inner_low, preferred_element_type=jnp.float32
    )
    first_grad = z_grad + jnp.einsum(
        "nf,df->nd", inner_low, w_in, preferred_element_type=jnp.float32
    )
    sum_grad, grad_gain_one, grad_bias_one = first_back(first_grad)
    branch_grad = sum_grad.astype(jnp.bfloat16)
    grad_out_weight = jnp.einsum(
        "nd,ne->de", attended, branch_grad, preferred_element_type=jnp.float32
    )
    attended_grad = jnp.einsum(
        "ne,de->nd", branch_grad, w_out, preferred_element_type=jnp.float32
    ).astype(jnp.bfloat16)
    query_grad, near_grads, pool_grads = lax.map(
        attend_backward,
        shared + (log_total, grouped(attended_grad.reshape(row_count, tok_count, model_width))),
    )
    pool_grads = pool_grads.reshape(row_count, 2, pool_all, model_width)
    pooled_grad = lax.psum_scatter(
        pool_grads.astype(jnp.bfloat16), "seq", scatter_dimension=2, tiled=True
    ).astype(jnp.float32)
    halo_grad = near_grads.reshape(row_count, 2, span, model_width)
    tap_columns = []
    for tap_index in range(5):
        begin = HALF + tap_index - 2
        weighted = pooled_grad * tap_masks[tap_index][:, None, :, None]
        taken = pair_halo[:, :, begin : begin + tok_count : 4].astype(jnp.float32)
        tap_columns.append(jnp.sum(weighted * taken, axis=(0, 1, 2)))
        halo_grad = halo_grad.at[:, :, begin : begin + tok_count : 4].add(
            weighted * pool_weight[:, tap_index]
        )
    grad_pool = jnp.stack(tap_columns, axis=1)
    from_above = shifted_2(halo_grad[:, :, :HALF].astype(jnp.bfloat16), "seq", -1).astype(
        jnp.float32
    )
    from_below = shifted_2(
        halo_grad[:, :, HALF + tok_count :].astype(jnp.bfloat16), "seq", 1
    ).astype(jnp.float32)
    own_grad = halo_grad[:, :, HALF : HALF + tok_count]
    own_grad = own_grad.at[:, :, :HALF].add(from_below)
    own_grad = own_grad.at[:, :, tok_count - HALF :].add(from_above)
    key_grad = own_grad[:, 0].reshape(row_count * tok_count, model_width).astype(jnp.bfloat16)
    value_grad = own_grad[:, 1].reshape(row_count * tok_count, model_width).astype(jnp.bfloat16)
    query_low = query_grad.reshape(row_count * tok_count, model_width).astype(jnp.bfloat16)
    grad_query_weight = jnp.einsum(
        "nd,ne->de", flat_tokens, query_low, preferred_element_type=jnp.float32
    )
    grad_key_weight = jnp.einsum(
        "nd,ne->de", flat_tokens, key_grad, preferred_element_type=jnp.float32
    )
    grad_value_weight = jnp.einsum(
        "nd,ne->de", flat_tokens, value_grad, preferred_element_type=jnp.float32
    )
    input_grad = sum_grad + jnp.einsum(
        "ne,de->nd", query_low, w_query, preferred_element_type=jnp.float32
    )
    input_grad = input_grad + jnp.einsum(
        "ne,de->nd", key_grad, w_key, preferred_element_type=jnp.float32
    )
    input_grad = input_grad + jnp.einsum(
        "ne,de->nd", value_grad, w_value, preferred_element_type=jnp.float32
    )
    tokens_grad = input_grad.astype(jnp.bfloat16).reshape(row_count, tok_count, model_width)
    small = jnp.concatenate(
        [
            jnp.stack([grad_gain_one, grad_bias_one, grad_gain_two, grad_bias_two], axis=1),
            grad_pool,
            jnp.zeros((model_width, 128 - 9), jnp.float32),
        ],
        axis=1,
    )
    sum_in = scatter_sum(grad_in_weight, True)
    sum_back = scatter_sum(grad_back_weight, False)
    sum_out = scatter_sum(jnp.concatenate([grad_out_weight, small], axis=1), True)
    sum_value = scatter_sum(grad_value_weight, False)
    sum_query = scatter_sum(grad_query_weight, False)
    sum_key = scatter_sum(grad_key_weight, True)
    vectors = sum_out[:, model_width:]
    summed = (
        sum_query,
        sum_key,
        sum_value,
        sum_out[:, :model_width],
        sum_in,
        sum_back,
        vectors[:, 0],
        vectors[:, 1],
        vectors[:, 2],
        vectors[:, 3],
        vectors[:, 4:9],
    )
    return (
        mixed,
        tokens_grad,
        summed[0],
        summed[1],
        summed[2],
        summed[3],
        summed[4],
        summed[5],
        summed[6],
        summed[7],
        summed[8],
        summed[9],
        summed[10],
    )


def solution(mesh):
    return jax.shard_map(
        per_device,
        mesh=mesh,
        in_specs=(
            P("dp", "seq", None),
            P("dp", None),
            P(),
            P(),
            P(),
            P(),
            P(),
            P(),
            P(),
            P(),
            P(),
            P(),
            P(),
            P("dp", "seq", None),
        ),
        out_specs=(
            P("dp", "seq", None),
            P("dp", "seq", None),
            P(("seq", "dp"), None),
            P(("seq", "dp"), None),
            P(("seq", "dp"), None),
            P(("seq", "dp"), None),
            P(("seq", "dp"), None),
            P(("seq", "dp"), None),
            P(("seq", "dp")),
            P(("seq", "dp")),
            P(("seq", "dp")),
            P(("seq", "dp")),
            P(("seq", "dp"), None),
        ),
        check_vma=False,
    )
```

```python
from functools import partial

import jax
import jax.numpy as jnp
from jax import lax
from jax.experimental import pallas as pl
from jax.experimental.pallas import tpu as pltpu
from jax.sharding import PartitionSpec as P

D = 768
FF = 3072
H = 12
PAIRS = H // 2
HALF = 64
PWIN = 512
QB = 128
EXTRA = 16
LANES = 128
BF16 = jnp.bfloat16
F32 = jnp.float32
MB = 1 << 20


def nn(left, right):
    return jnp.dot(left, right, preferred_element_type=F32)


def nt(left, right, precision=None):
    return lax.dot_general(
        left, right, (((1,), (1,)), ((), ())), preferred_element_type=F32, precision=precision
    )


def iota(shape, dim):
    return lax.broadcasted_iota(jnp.int32, shape, dim)


def segment_of(info, place, row_len):
    item = jnp.zeros_like(place)
    for m in range(4):
        item = item + (place >= info[m]).astype(jnp.int32)
    return jnp.where((place >= 0) & (place < row_len), item, -2)


def head_half(block, head):
    lane = iota(block.shape, 1)
    return jnp.where((lane < 64) == (head == 0), block, jnp.zeros_like(block))


def tap_mask(info, tap, shift, count, row_len):
    center = info[4] + 4 * (iota((count, 1), 0) + shift)
    same = segment_of(info, center + tap - 2, row_len) == segment_of(info, center, row_len)
    return (same & (center < row_len)).astype(F32)


def project_kernel(info, tok, left, right, wq, wk, wv, taps, q_out, k_out, v_out, pool_out, tt_out, x, cells, *, row_len):
    count = tok.shape[0]
    x[0:HALF] = left[...]
    x[HALF : HALF + count] = tok[...]
    x[HALF + count :] = right[...]
    k_low = nn(x[...], wk[...]).astype(BF16)
    k_out[...] = k_low
    v_low = nn(x[...], wv[...]).astype(BF16)
    v_out[...] = v_low
    masks = [tap_mask(info, tap, 0, count // 4, row_len) for tap in range(5)]
    for which, low in ((0, k_low), (1, v_low)):
        wide = low.astype(F32)
        for c in range(D // LANES):
            lanes = slice(c * LANES, (c + 1) * LANES)
            cells[c] = wide[:, lanes]
            total = jnp.zeros((count // 4, LANES), F32)
            for tap in range(5):
                taken = cells.at[c][pl.ds(HALF + tap - 2, count // 4, stride=4), :]
                total = total + taken * masks[tap] * taps[tap : tap + 1, lanes]
            pool_out[which, :, lanes] = total.astype(BF16)
    q_out[...] = (nn(tok[...], wq[...]).astype(BF16).astype(F32) * 0.125).astype(BF16)
    tt_out[...] = tok[...].T


def near_forward_kernel(info, q, k, v, e_out, o_out, st_out, bias, *, row_len):
    count, span = q.shape[0], k.shape[0]
    blocks = count // QB

    @pl.when(pl.program_id(0) == 0)
    def _():
        for b in range(blocks):
            query_place = info[4] + b * QB + iota((1, QB), 1)
            key_place = info[4] - HALF + b * QB + iota((2 * QB, 1), 0)
            same = segment_of(info, key_place, row_len) == segment_of(info, query_place, row_len)
            near = jnp.abs(key_place - query_place) <= HALF
            bias[b] = jnp.where(same & near, 0.0, -1e30)

    vt = v[...].T
    ones = jnp.ones((16, span), BF16)
    st_out[...] = jnp.zeros_like(st_out)
    for head in range(2):
        qh = head_half(q[...], head)
        va = jnp.concatenate([vt[head * 64 : head * 64 + 64], ones], axis=0)
        for b in range(blocks):
            cols = slice(b * QB, (b + 1) * QB)
            keys = slice(b * QB, (b + 2) * QB)
            s = nt(k[keys, :], qh[cols]) + bias[b]
            top = jnp.max(s, axis=0, keepdims=True)
            e = jnp.exp(s - top).astype(BF16)
            e_out[head, b] = e
            oa = nn(va[:, keys], e)
            o_out[head * 64 : head * 64 + 64, cols] = oa[:64]
            st_out[0, head : head + 1, cols] = top
            st_out[0, 2 + head : 3 + head, cols] = oa[64:65]


def pool_forward_kernel(info, q, o_near, st, *rest, row_len, pieces):
    kv = rest[:pieces]
    e_out, o_out, rn_out, rp_out, bias = rest[pieces:]
    count = q.shape[0]
    size = kv[0].shape[1]

    @pl.when(pl.program_id(0) == 0)
    def _():
        query_place = info[4] + iota((1, count), 1)
        query_item = segment_of(info, query_place, row_len)
        for i in range(pieces):
            key_place = 4 * (info[8 + i] * size + iota((size, 1), 0))
            same = segment_of(info, key_place, row_len) == query_item
            near = jnp.abs(key_place - query_place) <= 2 * PWIN
            bias[i * size : (i + 1) * size] = jnp.where(same & near, 0.0, -1e30)

    kp = jnp.concatenate([piece[0] for piece in kv], axis=0)
    vt = jnp.concatenate([piece[1] for piece in kv], axis=0).T
    ones = jnp.ones((16, pieces * size), BF16)
    wide = min(256, count)
    for b in range(count // wide):
        cols = slice(b * wide, (b + 1) * wide)
        outs, near_scale, pool_scale = [], [], []
        for head in range(2):
            qh = head_half(q[cols, :], head)
            va = jnp.concatenate([vt[head * 64 : head * 64 + 64], ones], axis=0)
            s = nt(kp, qh) + bias[:, cols]
            near_top = st[0, head : head + 1, cols]
            top = jnp.maximum(jnp.max(s, axis=0, keepdims=True), near_top)
            e = jnp.exp(s - top).astype(BF16)
            e_out[head, :, cols] = e
            oa = nn(va, e)
            fade = jnp.exp(near_top - top)
            inverse = 1.0 / (fade * st[0, 2 + head : 3 + head, cols] + oa[64:65])
            outs.append((fade * o_near[head * 64 : head * 64 + 64, cols] + oa[:64]) * inverse)
            near_scale.append(jnp.broadcast_to(fade * inverse, (64, wide)))
            pool_scale.append(jnp.broadcast_to(inverse, (64, wide)))
        o_out[cols, :] = jnp.concatenate(outs, axis=0).T
        rn_out[cols, :] = jnp.concatenate(near_scale, axis=0).T
        rp_out[cols, :] = jnp.concatenate(pool_scale, axis=0).T


def normal_parts(v):
    bell = jnp.exp(v * v * -0.5)
    t = 1.0 / (1.0 + jnp.abs(v) * (0.3275911 * 0.7071067811865476))
    poly = t * (
        0.127414796 + t * (-0.142248368 + t * (0.7107068705 + t * (-0.7265760135 + t * 0.5307027145)))
    )
    tail = poly * bell
    return jnp.where(v < 0, tail, 1.0 - tail), v * bell * 0.3989422804014327


def normalized(values):
    shifted = values - jnp.mean(values, axis=1, keepdims=True)
    inverse = lax.rsqrt(jnp.mean(shifted * shifted, axis=1, keepdims=True) + 1e-05)
    return shifted * inverse, inverse


def norm_back(grad, gain, unit, inverse):
    e = grad * gain
    return inverse * (
        e
        - jnp.mean(e, axis=1, keepdims=True)
        - unit * jnp.mean(e * unit, axis=1, keepdims=True)
    )


def block_of(step, info, parts):
    ny = parts // 2
    back = step - parts
    mine = info[5]
    going_back = jnp.where(
        back < ny, 2 * back + 1 - mine, 2 * (back - ny) + mine
    )
    return jnp.where(step < parts, step, going_back)


def dense_kernel(
    info, o, rn, rp, tok, og, vecs, w_out, w_in, w_back,
    mixed, sum_grad, don, dop, in_keep, in_send, back_keep, back_send, out_keep, out_send, sums,
    att, first, unit_one, inv_one, low, low_t, act, slope, feed, feed_grad,
    *, parts,
):
    ny = parts // 2
    step = pl.program_id(0)
    width = w_in.shape[1]
    rc = in_keep.shape[1]
    mine = info[5]
    hidden = pl.ds(pl.multiple_of(block_of(step, info, parts) * width, width), width)
    gain_one, bias_one = vecs[0:1, :], vecs[1:2, :]
    gain_two, bias_two = vecs[2:3, :], vecs[3:4, :]

    def rows_of(y, core):
        return pl.ds(pl.multiple_of((2 * y + core) * rc, rc), rc)

    @pl.when(step == 0)
    def _():
        att[...] = o[...].astype(BF16)
        unit, inverse = normalized(tok[...].astype(F32) + nn(att[...], w_out[...]))
        unit_one[...] = unit
        inv_one[...] = jnp.broadcast_to(inverse, inv_one.shape)
        first[...] = unit * gain_one + bias_one
        low[...] = first[...].astype(BF16)
        low_t[...] = low[...].T
        feed[...] = jnp.zeros_like(feed)
        sums[...] = jnp.zeros_like(sums)

    @pl.when(step < parts)
    def _():
        inner = nn(low[...], w_in[...])
        phi, bell = normal_parts(inner)
        act[:, hidden] = (inner * phi).astype(BF16)
        slope[:, hidden] = (phi + bell).astype(slope.dtype)
        feed[...] += nn(act[:, hidden], w_back[...])

    @pl.when(step == parts - 1)
    def _():
        unit, inverse = normalized(first[...] + feed[...])
        mixed[...] = (unit * gain_two + bias_two).astype(BF16)
        upstream = og[...].astype(F32)
        sums[2:3] = jnp.sum(upstream * unit, axis=0, keepdims=True)
        sums[3:4] = jnp.sum(upstream, axis=0, keepdims=True)
        z_grad = norm_back(upstream, gain_two, unit, inverse)
        feed[...] = z_grad
        feed_grad[...] = z_grad.astype(BF16)

    @pl.when(step >= parts)
    def _():
        inner_grad = (nt(feed_grad[...], w_back[...]) * slope[:, hidden].astype(F32)).astype(BF16)
        act_t = act[:, hidden].T
        back = nn(act_t, feed_grad[...]).astype(BF16)

        @pl.when(step < parts + ny)
        def _():
            back_send[0] = back

        @pl.when(step >= parts + ny)
        def _():
            back_keep[0] = back

        for y in range(ny):
            in_send[y] = nn(low_t[rows_of(y, 1 - mine), :], inner_grad).astype(BF16)
            in_keep[y] = nn(low_t[rows_of(y, mine), :], inner_grad).astype(BF16)
        feed[...] += nt(inner_grad, w_in[...])

    @pl.when(step == 2 * parts - 1)
    def _():
        first_grad = feed[...]
        unit = unit_one[...]
        sums[0:1] = jnp.sum(first_grad * unit, axis=0, keepdims=True)
        sums[1:2] = jnp.sum(first_grad, axis=0, keepdims=True)
        total = norm_back(first_grad, gain_one, unit, inv_one[:, 0:1])
        sum_grad[...] = total
        branch_grad = total.astype(BF16)
        attended_grad = nt(branch_grad, w_out[...])
        don[...] = (attended_grad * rn[...]).astype(BF16)
        dop[...] = (attended_grad * rp[...]).astype(BF16)
        low_t[...] = att[...].T
        for y in range(ny):
            out_send[y] = nn(low_t[rows_of(y, 1 - mine), :], branch_grad).astype(BF16)
            out_keep[y] = nn(low_t[rows_of(y, mine), :], branch_grad).astype(BF16)


def score_delta(grad, attended):
    pick = ((iota((8, LANES), 1) // 64) == iota((8, LANES), 0)).astype(F32)
    return nt(pick, grad.astype(F32) * attended, precision=lax.Precision.HIGHEST)


def pool_backward_kernel(info, q, grad, o, e, *rest, pieces):
    kv = rest[:pieces]
    keep, send, dq_out, dk, dv = rest[pieces:]
    ny = pieces // 2
    count = q.shape[0]
    size = kv[0].shape[1]
    delta = score_delta(grad[...], o[...])
    kp = jnp.concatenate([piece[0] for piece in kv], axis=0)
    kt = kp.T
    vp = jnp.concatenate([piece[1] for piece in kv], axis=0)
    wide = min(256, count)
    for head in range(2):
        for b in range(count // wide):
            cols = slice(b * wide, (b + 1) * wide)
            gh = head_half(grad[cols, :], head)
            qh = head_half(q[cols, :], head)
            low = e[head, :, cols]
            dp = nt(vp, gh) - delta[head : head + 1, cols]
            ds = (low.astype(F32) * dp).astype(BF16)
            key_part = nn(ds, qh)
            value_part = nn(low, gh)
            if head == 0 and b == 0:
                dk[...] = key_part
                dv[...] = value_part
            else:
                dk[...] += key_part
                dv[...] += value_part
            dq_out[head * 64 : head * 64 + 64, cols] = nn(kt[head * 64 : head * 64 + 64], ds)
    for i in range(pieces):
        target = keep if i < ny else send
        after = pl.ds(pl.multiple_of(info[8 + pieces + i] * size, size), EXTRA)
        for which, total in ((0, dk), (1, dv)):
            target[i % ny, which, 0:size] = total[i * size : (i + 1) * size].astype(BF16)
            target[i % ny, which, size:] = total[after, :].astype(BF16)


def near_backward_kernel(q, grad, o, e, k, v, dq_pool, own, before, behind, dq_out, dk, dv):
    count = q.shape[0]
    delta = score_delta(grad[...], o[...])
    kt = k[...].T
    dk[...] = jnp.zeros_like(dk)
    dv[...] = jnp.zeros_like(dv)
    for b in range(count // QB):
        cols = slice(b * QB, (b + 1) * QB)
        keys = slice(b * QB, (b + 2) * QB)
        lows, scores, grads, queries, dqs = [], [], [], [], []
        for head in range(2):
            gh = head_half(grad[cols, :], head)
            low = e[head, b]
            dp = nt(v[keys, :], gh) - delta[head : head + 1, cols]
            ds = (low.astype(F32) * dp).astype(BF16)
            dqs.append(nn(kt[head * 64 : head * 64 + 64, keys], ds))
            lows.append(low)
            scores.append(ds)
            grads.append(gh)
            queries.append(head_half(q[cols, :], head))
        dk[keys, :] += nn(jnp.concatenate(scores, axis=1), jnp.concatenate(queries, axis=0))
        dv[keys, :] += nn(jnp.concatenate(lows, axis=1), jnp.concatenate(grads, axis=0))
        total = (jnp.concatenate(dqs, axis=0) + dq_pool[:, cols]) * 0.125
        dq_out[cols, :] = total.T.astype(BF16)
    for which, total in ((0, dk), (1, dv)):
        before[which] = total[0:HALF].astype(BF16)
        own[which] = total[HALF : HALF + count]
        behind[which] = total[HALF + count :].astype(BF16)


def query_grad_kernel(info, tt, dq, wq, sum_grad, keep, send, part):
    ny, rc = keep.shape[0], keep.shape[1]
    mine = info[5]
    for y in range(ny):
        for target, core in ((send, 1 - mine), (keep, mine)):
            rows = pl.ds(pl.multiple_of((2 * y + core) * rc, rc), rc)
            target[y] = nn(tt[rows, :], dq[...]).astype(BF16)
    part[...] = sum_grad[...] + nt(dq[...], wq[...])


def key_grad_kernel(info, tt, own, above, below, k, v, wk, wv, part, sums, taps, *rest, row_len, pieces):
    pooled = rest[:pieces]
    keep, send, tokens_grad, acc, cells, g, small, small_t, k_low, v_low = rest[pieces:]
    ny, rc = keep.shape[0], keep.shape[1]
    count = part.shape[0]
    size = count // 4
    mine = info[5]
    small[...] = jnp.zeros_like(small)
    small[0:8] = sums[...]
    masks = [tap_mask(info, tap, 0, size, row_len) for tap in range(5)]
    next_masks = [tap_mask(info, tap, 1, size, row_len) for tap in range(2)]
    moves = ((2, 0, 0), (3, 1, 0), (4, 2, 0), (0, 2, 1), (1, 3, 1))
    for which, source, low in ((0, k, k_low), (1, v, v_low)):
        for c in range(D // LANES):
            lanes = slice(c * LANES, (c + 1) * LANES)
            grad = acc.at[c]
            grad[...] = own[which, :, lanes]
            grad[0:HALF, :] += below[which, :, lanes].astype(F32)
            grad[count - HALF :, :] += above[which, :, lanes].astype(F32)
            cells[...] = source[:, lanes].astype(F32)
            total = pooled[0][0, which, :, lanes].astype(F32)
            for piece in pooled[1:]:
                total = total + piece[0, which, :, lanes].astype(F32)
            g[...] = total
            for tap, place, shift in moves:
                mask = next_masks[tap] if shift else masks[tap]
                spread = g[shift : shift + size, :] * mask * taps[tap : tap + 1, lanes]
                grad[pl.ds(place, size, stride=4), :] += spread
            for tap in range(5):
                taken = cells[pl.ds(HALF + tap - 2, size, stride=4), :]
                product = g[0:size, :] * masks[tap] * taken
                small[8 + tap : 9 + tap, lanes] += jnp.sum(product, axis=0, keepdims=True)
            low[:, lanes] = grad[...].astype(BF16)
    small_t[...] = small[...].T.astype(BF16)
    for y in range(ny):
        for target, core in ((send, 1 - mine), (keep, mine)):
            rows = pl.ds(pl.multiple_of((2 * y + core) * rc, rc), rc)
            target[y, :, 0:D] = nn(tt[rows, :], k_low[...]).astype(BF16)
            target[y, :, D : 2 * D] = nn(tt[rows, :], v_low[...]).astype(BF16)
            target[y, :, 2 * D :] = small_t[rows, :]
    total = part[...] + nt(k_low[...], wk[...])
    tokens_grad[...] = (total + nt(v_low[...], wv[...])).astype(BF16)


def hop_pairs(axis, count, stride, hop):
    pairs = []
    for device in range(lax.axis_size(axis)):
        place = (device // stride) % count
        pairs.append((device, device + ((place + hop) % count - place) * stride))
    return pairs


def swap_stage(parts, dim, axis, count, stride):
    mine = (lax.axis_index(axis) // stride) % count
    total = lax.dynamic_index_in_dim(parts, mine, dim, keepdims=False)
    for hop in range(1, count):
        block = lax.dynamic_index_in_dim(parts, (mine + hop) % count, dim, keepdims=False)
        moved = lax.ppermute(block.astype(BF16), axis, hop_pairs(axis, count, stride, hop))
        total = total + moved.astype(F32)
    return total


def scatter_sum(keep, send, seq_first):
    seq, dp = lax.axis_size("seq"), lax.axis_size("dp")
    moved = lax.ppermute(send, "seq", hop_pairs("seq", 2, 1, 1))
    parts = keep.astype(F32) + moved.astype(F32)
    near = 2 if dp % 2 == 0 else 1
    parts = parts.reshape(seq // 2, dp // near, near, parts.shape[1] // dp, parts.shape[2])
    if seq_first:
        parts = swap_stage(parts, 0, "seq", seq // 2, 2)
        parts = swap_stage(parts, 1, "dp", near, 1)
    else:
        parts = swap_stage(parts, 2, "dp", near, 1)
        parts = swap_stage(parts, 0, "seq", seq // 2, 2)
    return swap_stage(parts, 0, "dp", dp // near, near)


def shifted(block, by):
    size = lax.axis_size("seq")
    return lax.ppermute(block, "seq", [(i, i + by) for i in range(size) if 0 <= i + by < size])


def call(kernel, info, args, in_specs, outs, out_specs, grid, scratch, flops, vmem, name):
    moved = sum(a.size * a.dtype.itemsize for a in list(args) + list(outs))
    return pl.pallas_call(
        kernel,
        grid_spec=pltpu.PrefetchScalarGridSpec(
            num_scalar_prefetch=1,
            grid=grid,
            in_specs=in_specs,
            out_specs=out_specs,
            scratch_shapes=scratch,
        ),
        out_shape=outs,
        compiler_params=pltpu.CompilerParams(
            vmem_limit_bytes=vmem * MB, dimension_semantics=("arbitrary",) * len(grid)
        ),
        cost_estimate=pl.CostEstimate(flops=flops, bytes_accessed=moved, transcendentals=0),
        name=name,
    )(info, *args)


def whole(array):
    rank = len(array.shape)
    return pl.BlockSpec(array.shape, lambda i, info: (0,) * rank)


def columns(array, width=LANES):
    rank = len(array.shape)
    return pl.BlockSpec(array.shape[:-1] + (width,), lambda i, info: (0,) * (rank - 1) + (i,))


def leading(array, size):
    rank = len(array.shape)
    return pl.BlockSpec((size,) + array.shape[1:], lambda i, info: (i,) + (0,) * (rank - 1))


def per_device(
    tokens,
    item_lengths,
    w_query,
    w_key,
    w_value,
    w_out,
    w_in,
    w_back,
    norm1_gain,
    norm1_bias,
    norm2_gain,
    norm2_bias,
    pool_weight,
    out_grad,
):
    _, count, _ = tokens.shape
    seq = lax.axis_size("seq")
    ny = seq // 2
    row_len = count * seq
    span = count + 2 * HALF
    size = count // 4
    rc = D // seq
    here = lax.axis_index("seq")
    core, y = here % 2, here // 2
    owners = []
    for other in range(2):
        for hop in range(ny):
            owners.append(((y + hop) % ny) * 2 + jnp.bitwise_xor(core, other))
    afters = []
    for owner in owners:
        after = jnp.minimum(owner + 1, seq - 1)
        afters.append(jnp.bitwise_xor(after % 2, core) * ny + (after // 2 - y) % ny)
    zero = jnp.zeros((), jnp.int32)
    info = jnp.concatenate(
        [
            jnp.cumsum(item_lengths[0]).astype(jnp.int32),
            jnp.stack([here * count, core, y, zero] + owners + afters).astype(jnp.int32),
        ]
    )
    tok = tokens[0]
    og = out_grad[0]
    left = shifted(tok[count - HALF :], 1)
    right = shifted(tok[:HALF], -1)
    taps = jnp.pad(pool_weight.T, ((0, 3), (0, 0)))
    vecs = jnp.concatenate(
        [jnp.stack([norm1_gain, norm1_bias, norm2_gain, norm2_bias]), jnp.zeros((4, D), F32)]
    )

    def shape(dims, kind):
        return jax.ShapeDtypeStruct(dims, kind)

    args = (tok, left, right, w_query, w_key, w_value, taps)
    outs = (
        shape((count, D), BF16),
        shape((span, D), BF16),
        shape((span, D), BF16),
        shape((2, size, D), BF16),
        shape((D, count), BF16),
    )
    queries, keys, values, pool_own, tok_t = call(
        partial(project_kernel, row_len=row_len),
        info,
        args,
        [whole(a) for a in args],
        outs,
        [whole(a) for a in outs],
        (1,),
        [
            pltpu.VMEM((span, D), BF16),
            pltpu.VMEM((D // LANES, span, LANES), F32),
        ],
        2 * D * D * (count + 2 * span),
        40,
        "project",
    )

    pieces = [pool_own]
    for hop in range(1, ny):
        pieces.append(lax.ppermute(pool_own, "seq", hop_pairs("seq", ny, 2, ny - hop)))
    pieces = pieces + [lax.ppermute(piece, "seq", hop_pairs("seq", 2, 1, 1)) for piece in pieces]

    blocks = count // QB
    args = (queries, keys, values)
    outs = (
        shape((H, blocks, 2 * QB, QB), BF16),
        shape((D, count), F32),
        shape((PAIRS, 8, count), F32),
    )
    near_e, o_near, stats = call(
        partial(near_forward_kernel, row_len=row_len),
        info,
        args,
        [columns(a) for a in args],
        outs,
        [leading(outs[0], 2), leading(outs[1], LANES), leading(outs[2], 1)],
        (PAIRS,),
        [pltpu.VMEM((blocks, 2 * QB, QB), F32)],
        4 * H * 256 * 256 * count,
        32,
        "near_forward",
    )

    pool_all = seq * size
    args = (queries, o_near, stats) + tuple(pieces)
    outs = (
        shape((H, pool_all, count), BF16),
        shape((count, D), F32),
        shape((count, D), F32),
        shape((count, D), F32),
    )
    pool_e, attention, near_scale, pool_scale = call(
        partial(pool_forward_kernel, row_len=row_len, pieces=seq),
        info,
        args,
        [columns(queries), leading(o_near, LANES), leading(stats, 1)] + [columns(p) for p in pieces],
        outs,
        [leading(outs[0], 2)] + [columns(a) for a in outs[1:]],
        (PAIRS,),
        [pltpu.VMEM((pool_all, count), F32)],
        4 * H * 512 * 256 * count,
        32,
        "pool_forward",
    )

    width = FF // seq
    args = (attention, near_scale, pool_scale, tok, og, vecs, w_out, w_in, w_back)
    half_in = shape((ny, rc, FF), BF16)
    half_back = shape((ny, width, D), BF16)
    half_out = shape((ny, rc, D), BF16)
    outs = (
        shape((count, D), BF16),
        shape((count, D), F32),
        shape((count, D), BF16),
        shape((count, D), BF16),
        half_in,
        half_in,
        half_back,
        half_back,
        half_out,
        half_out,
        shape((8, D), F32),
    )
    in_columns = pl.BlockSpec(
        (ny, rc, width),
        lambda i, info: (0, 0, block_of(jnp.maximum(i, seq), info, seq)),
    )
    (
        mixed,
        sum_grad,
        near_grad,
        pool_grad,
        in_keep,
        in_send,
        back_keep,
        back_send,
        out_keep,
        out_send,
        sums,
    ) = call(
        partial(dense_kernel, parts=seq),
        info,
        args,
        [whole(a) for a in args[:7]]
        + [
            pl.BlockSpec((D, width), lambda i, info: (0, block_of(i, info, seq))),
            pl.BlockSpec((width, D), lambda i, info: (block_of(i, info, seq), 0)),
        ],
        outs,
        [whole(a) for a in outs[:4]]
        + [
            in_columns,
            in_columns,
            pl.BlockSpec(
                (1, width, D), lambda i, info: (jnp.maximum(i - seq - ny, 0), 0, 0)
            ),
            pl.BlockSpec(
                (1, width, D), lambda i, info: (jnp.clip(i - seq, 0, ny - 1), 0, 0)
            ),
        ]
        + [whole(a) for a in outs[8:]],
        (2 * seq,),
        [
            pltpu.VMEM((count, D), BF16),
            pltpu.VMEM((count, D), F32),
            pltpu.VMEM((count, D), F32),
            pltpu.VMEM((count, LANES), F32),
            pltpu.VMEM((count, D), BF16),
            pltpu.VMEM((D, count), BF16),
            pltpu.VMEM((count, FF), BF16),
            pltpu.VMEM((count, FF), BF16),
            pltpu.VMEM((count, D), F32),
            pltpu.VMEM((count, D), BF16),
        ],
        2 * count * (3 * D * D + 6 * D * FF),
        58,
        "dense",
    )
    sum_in = scatter_sum(in_keep, in_send, True)
    sum_back = scatter_sum(back_keep, back_send, False)
    sum_out = scatter_sum(out_keep, out_send, True)

    args = (queries, pool_grad, attention, pool_e) + tuple(pieces)
    half_pool = shape((ny, 2, size + EXTRA, D), BF16)
    outs = (half_pool, half_pool, shape((D, count), F32))
    pool_keep, pool_send, dq_pool = call(
        partial(pool_backward_kernel, pieces=seq),
        info,
        args,
        [columns(a) for a in args[:3]] + [leading(pool_e, 2)] + [columns(p) for p in pieces],
        outs,
        [columns(half_pool), columns(half_pool), leading(outs[2], LANES)],
        (PAIRS,),
        [pltpu.VMEM((pool_all, LANES), F32), pltpu.VMEM((pool_all, LANES), F32)],
        8 * H * 512 * 256 * count,
        32,
        "pool_backward",
    )
    pool_moved = lax.ppermute(pool_send, "seq", hop_pairs("seq", 2, 1, 1))
    pooled = [pool_keep[0:1], pool_moved[0:1]]
    for hop in range(1, ny):
        both = pool_keep[hop : hop + 1].astype(F32) + pool_moved[hop : hop + 1].astype(F32)
        pooled.append(lax.ppermute(both.astype(BF16), "seq", hop_pairs("seq", ny, 2, hop)))

    args = (queries, near_grad, attention, near_e, keys, values, dq_pool)
    outs = (
        shape((2, count, D), F32),
        shape((2, HALF, D), BF16),
        shape((2, HALF, D), BF16),
        shape((count, D), BF16),
    )
    own, before, behind, query_grad = call(
        lambda info, *refs: near_backward_kernel(*refs),
        info,
        args,
        [columns(a) for a in args[:3]]
        + [leading(near_e, 2), columns(keys), columns(values), leading(dq_pool, LANES)],
        outs,
        [columns(a) for a in outs],
        (PAIRS,),
        [pltpu.VMEM((span, LANES), F32), pltpu.VMEM((span, LANES), F32)],
        8 * H * 256 * 256 * count,
        32,
        "near_backward",
    )
    above = shifted(before, -1)
    below = shifted(behind, 1)

    args = (tok_t, query_grad, w_query, sum_grad)
    outs = (half_out, half_out, shape((count, D), F32))
    query_keep, query_send, part = call(
        query_grad_kernel,
        info,
        args,
        [whole(a) for a in args],
        outs,
        [whole(a) for a in outs],
        (1,),
        [],
        4 * count * D * D,
        32,
        "query_grad",
    )
    sum_query = scatter_sum(query_keep, query_send, False)

    args = (tok_t, own, above, below, keys, values, w_key, w_value, part, sums, taps) + tuple(pooled)
    half_both = shape((ny, rc, 2 * D + LANES), BF16)
    outs = (half_both, half_both, shape((count, D), BF16))
    both_keep, both_send, tokens_grad = call(
        partial(key_grad_kernel, row_len=row_len, pieces=len(pooled)),
        info,
        args,
        [whole(a) for a in args],
        outs,
        [whole(a) for a in outs],
        (1,),
        [
            pltpu.VMEM((D // LANES, count, LANES), F32),
            pltpu.VMEM((span, LANES), F32),
            pltpu.VMEM((size + EXTRA, LANES), F32),
            pltpu.VMEM((LANES, D), F32),
            pltpu.VMEM((D, LANES), BF16),
            pltpu.VMEM((count, D), BF16),
            pltpu.VMEM((count, D), BF16),
        ],
        8 * count * D * D,
        56,
        "key_grad",
    )
    sum_key = scatter_sum(both_keep[:, :, :D], both_send[:, :, :D], True)
    sum_rest = scatter_sum(both_keep[:, :, D:], both_send[:, :, D:], False)
    vectors = sum_rest[:, D:]
    return (
        mixed[None],
        tokens_grad[None],
        sum_query,
        sum_key,
        sum_rest[:, :D],
        sum_out,
        sum_in,
        sum_back,
        vectors[:, 0],
        vectors[:, 1],
        vectors[:, 2],
        vectors[:, 3],
        vectors[:, 8:13],
    )


def solution(mesh):
    shards, copied = P("dp", "seq", None), P()
    spread = P(("seq", "dp"), None)
    vector = P(("seq", "dp"))
    return jax.shard_map(
        per_device,
        mesh=mesh,
        in_specs=(shards, P("dp", None)) + (copied,) * 11 + (shards,),
        out_specs=(shards, shards) + (spread,) * 6 + (vector,) * 4 + (spread,),
        check_vma=False,
    )
```

```python
from functools import partial

import jax
import jax.numpy as jnp
from jax import lax
from jax.experimental import pallas as pl
from jax.experimental.pallas import tpu as pltpu
from jax.sharding import PartitionSpec as P

D = 768
FF = 3072
H = 12
PAIRS = H // 2
HALF = 64
PWIN = 512
QB = 128
EXTRA = 16
LANES = 128
BF16 = jnp.bfloat16
F32 = jnp.float32
MB = 1 << 20


def nn(left, right):
    return jnp.dot(left, right, preferred_element_type=F32)


def nt(left, right, precision=None):
    return lax.dot_general(
        left, right, (((1,), (1,)), ((), ())), preferred_element_type=F32, precision=precision
    )


def iota(shape, dim):
    return lax.broadcasted_iota(jnp.int32, shape, dim)


def segment_of(info, place, row_len):
    item = jnp.zeros_like(place)
    for m in range(4):
        item = item + (place >= info[m]).astype(jnp.int32)
    return jnp.where((place >= 0) & (place < row_len), item, -2)


def head_half(block, head):
    lane = iota(block.shape, 1)
    return jnp.where((lane < 64) == (head == 0), block, jnp.zeros_like(block))


def tap_mask(info, tap, shift, count, row_len):
    center = info[4] + 4 * (iota((count, 1), 0) + shift)
    same = segment_of(info, center + tap - 2, row_len) == segment_of(info, center, row_len)
    return (same & (center < row_len)).astype(F32)


def folds(rows, width):
    return 2 if rows % 16 and rows % 8 == 0 and (width // 2) % LANES == 0 else 1


def folded(rows, width):
    fold = folds(rows, width)
    return (rows * fold, width // fold)


def fold_rows(block):
    rows, width = block.shape
    fold = folds(rows, width)
    part = width // fold
    return jnp.concatenate([block[:, i * part : (i + 1) * part] for i in range(fold)], axis=0)


def unfold_rows(block, rows):
    fold = block.shape[0] // rows
    return jnp.concatenate([block[i * rows : (i + 1) * rows] for i in range(fold)], axis=1)


def store_chunks(target, total, inner=()):
    nz, nx = target.shape[0], target.shape[1]
    rows = total.shape[0] // (nz * nx)
    for z in range(nz):
        for x in range(nx):
            start = (z * nx + x) * rows
            target[(z, x) + inner] = fold_rows(total[start : start + rows]).astype(BF16)


def project_kernel(info, tok, left, right, wq, wk, wv, taps, q_out, k_out, v_out, pool_out, tt_out, x, cells, *, row_len):
    count = tok.shape[0]
    x[0:HALF] = left[...]
    x[HALF : HALF + count] = tok[...]
    x[HALF + count :] = right[...]
    k_low = nn(x[...], wk[...]).astype(BF16)
    k_out[...] = k_low
    v_low = nn(x[...], wv[...]).astype(BF16)
    v_out[...] = v_low
    masks = [tap_mask(info, tap, 0, count // 4, row_len) for tap in range(5)]
    for which, low in ((0, k_low), (1, v_low)):
        wide = low.astype(F32)
        for c in range(D // LANES):
            lanes = slice(c * LANES, (c + 1) * LANES)
            cells[c] = wide[:, lanes]
            total = jnp.zeros((count // 4, LANES), F32)
            for tap in range(5):
                taken = cells.at[c][pl.ds(HALF + tap - 2, count // 4, stride=4), :]
                total = total + taken * masks[tap] * taps[tap : tap + 1, lanes]
            pool_out[which, :, lanes] = total.astype(BF16)
    q_out[...] = (nn(tok[...], wq[...]).astype(BF16).astype(F32) * 0.125).astype(BF16)
    tt_out[...] = tok[...].T


def near_forward_kernel(info, q, k, v, e_out, o_out, st_out, bias, *, row_len):
    count, span = q.shape[0], k.shape[0]
    blocks = count // QB

    @pl.when(pl.program_id(0) == 0)
    def _():
        for b in range(blocks):
            query_place = info[4] + b * QB + iota((1, QB), 1)
            key_place = info[4] - HALF + b * QB + iota((2 * QB, 1), 0)
            same = segment_of(info, key_place, row_len) == segment_of(info, query_place, row_len)
            near = jnp.abs(key_place - query_place) <= HALF
            bias[b] = jnp.where(same & near, 0.0, -1e30)

    vt = v[...].T
    ones = jnp.ones((16, span), BF16)
    st_out[...] = jnp.zeros_like(st_out)
    for head in range(2):
        qh = head_half(q[...], head)
        va = jnp.concatenate([vt[head * 64 : head * 64 + 64], ones], axis=0)
        for b in range(blocks):
            cols = slice(b * QB, (b + 1) * QB)
            keys = slice(b * QB, (b + 2) * QB)
            s = nt(k[keys, :], qh[cols]) + bias[b]
            top = jnp.max(s, axis=0, keepdims=True)
            e = jnp.exp(s - top).astype(BF16)
            e_out[head, b] = e
            oa = nn(va[:, keys], e)
            o_out[head * 64 : head * 64 + 64, cols] = oa[:64]
            st_out[0, head : head + 1, cols] = top
            st_out[0, 2 + head : 3 + head, cols] = oa[64:65]


def pool_forward_kernel(info, q, o_near, st, *rest, row_len, pieces):
    kv = rest[:pieces]
    e_out, o_out, rn_out, rp_out, bias = rest[pieces:]
    count = q.shape[0]
    size = kv[0].shape[1]

    @pl.when(pl.program_id(0) == 0)
    def _():
        query_place = info[4] + iota((1, count), 1)
        query_item = segment_of(info, query_place, row_len)
        for i in range(pieces):
            key_place = 4 * (info[8 + i] * size + iota((size, 1), 0))
            same = segment_of(info, key_place, row_len) == query_item
            near = jnp.abs(key_place - query_place) <= 2 * PWIN
            bias[i * size : (i + 1) * size] = jnp.where(same & near, 0.0, -1e30)

    kp = jnp.concatenate([piece[0] for piece in kv], axis=0)
    vt = jnp.concatenate([piece[1] for piece in kv], axis=0).T
    ones = jnp.ones((16, pieces * size), BF16)
    wide = min(256, count)
    for b in range(count // wide):
        cols = slice(b * wide, (b + 1) * wide)
        outs, near_scale, pool_scale = [], [], []
        for head in range(2):
            qh = head_half(q[cols, :], head)
            va = jnp.concatenate([vt[head * 64 : head * 64 + 64], ones], axis=0)
            s = nt(kp, qh) + bias[:, cols]
            near_top = st[0, head : head + 1, cols]
            top = jnp.maximum(jnp.max(s, axis=0, keepdims=True), near_top)
            e = jnp.exp(s - top).astype(BF16)
            e_out[head, :, cols] = e
            oa = nn(va, e)
            fade = jnp.exp(near_top - top)
            inverse = 1.0 / (fade * st[0, 2 + head : 3 + head, cols] + oa[64:65])
            outs.append((fade * o_near[head * 64 : head * 64 + 64, cols] + oa[:64]) * inverse)
            near_scale.append(jnp.broadcast_to(fade * inverse, (64, wide)))
            pool_scale.append(jnp.broadcast_to(inverse, (64, wide)))
        o_out[cols, :] = jnp.concatenate(outs, axis=0).T
        rn_out[cols, :] = jnp.concatenate(near_scale, axis=0).T
        rp_out[cols, :] = jnp.concatenate(pool_scale, axis=0).T


def normal_parts(v):
    bell = jnp.exp(v * v * -0.5)
    t = 1.0 / (1.0 + jnp.abs(v) * (0.3275911 * 0.7071067811865476))
    poly = t * (
        0.127414796 + t * (-0.142248368 + t * (0.7107068705 + t * (-0.7265760135 + t * 0.5307027145)))
    )
    tail = poly * bell
    return jnp.where(v < 0, tail, 1.0 - tail), v * bell * 0.3989422804014327


def normalized(values):
    shifted = values - jnp.mean(values, axis=1, keepdims=True)
    inverse = lax.rsqrt(jnp.mean(shifted * shifted, axis=1, keepdims=True) + 1e-05)
    return shifted * inverse, inverse


def norm_back(grad, gain, unit, inverse):
    e = grad * gain
    return inverse * (
        e
        - jnp.mean(e, axis=1, keepdims=True)
        - unit * jnp.mean(e * unit, axis=1, keepdims=True)
    )


def block_of(step, info, parts):
    ny = parts // 2
    back = step - parts
    mine = info[5]
    going_back = jnp.where(
        back < ny, 2 * back + 1 - mine, 2 * (back - ny) + mine
    )
    return jnp.where(step < parts, step, going_back)


def dense_kernel(
    info, o, rn, rp, tok, og, vecs, w_out, w_in, w_back,
    mixed, sum_grad, don, dop, in_keep, in_send, back_keep, back_send, out_keep, out_send, sums,
    att, first, unit_one, inv_one, low, low_t, act, slope, feed, feed_grad,
    *, parts,
):
    ny = parts // 2
    step = pl.program_id(0)
    width = w_in.shape[1]
    rc = D // parts
    mine = info[5]
    hidden = pl.ds(pl.multiple_of(block_of(step, info, parts) * width, width), width)
    gain_one, bias_one = vecs[0:1, :], vecs[1:2, :]
    gain_two, bias_two = vecs[2:3, :], vecs[3:4, :]

    def rows_of(y, core):
        return pl.ds(pl.multiple_of((2 * y + core) * rc, rc), rc)

    @pl.when(step == 0)
    def _():
        att[...] = o[...].astype(BF16)
        unit, inverse = normalized(tok[...].astype(F32) + nn(att[...], w_out[...]))
        unit_one[...] = unit
        inv_one[...] = jnp.broadcast_to(inverse, inv_one.shape)
        first[...] = unit * gain_one + bias_one
        low[...] = first[...].astype(BF16)
        low_t[...] = low[...].T
        feed[...] = jnp.zeros_like(feed)
        sums[...] = jnp.zeros_like(sums)

    @pl.when(step < parts)
    def _():
        inner = nn(low[...], w_in[...])
        phi, bell = normal_parts(inner)
        act[:, hidden] = (inner * phi).astype(BF16)
        slope[:, hidden] = (phi + bell).astype(slope.dtype)
        feed[...] += nn(act[:, hidden], w_back[...])

    @pl.when(step == parts - 1)
    def _():
        unit, inverse = normalized(first[...] + feed[...])
        mixed[...] = (unit * gain_two + bias_two).astype(BF16)
        upstream = og[...].astype(F32)
        sums[2:3] = jnp.sum(upstream * unit, axis=0, keepdims=True)
        sums[3:4] = jnp.sum(upstream, axis=0, keepdims=True)
        z_grad = norm_back(upstream, gain_two, unit, inverse)
        feed[...] = z_grad
        feed_grad[...] = z_grad.astype(BF16)

    @pl.when(step >= parts)
    def _():
        inner_grad = (nt(feed_grad[...], w_back[...]) * slope[:, hidden].astype(F32)).astype(BF16)
        act_t = act[:, hidden].T
        back = nn(act_t, feed_grad[...])

        @pl.when(step < parts + ny)
        def _():
            store_chunks(back_send.at[0], back)

        @pl.when(step >= parts + ny)
        def _():
            store_chunks(back_keep.at[0], back)

        for y in range(ny):
            store_chunks(in_send.at[y], nn(low_t[rows_of(y, 1 - mine), :], inner_grad), (0,))
            store_chunks(in_keep.at[y], nn(low_t[rows_of(y, mine), :], inner_grad), (0,))
        feed[...] += nt(inner_grad, w_in[...])

    @pl.when(step == 2 * parts - 1)
    def _():
        first_grad = feed[...]
        unit = unit_one[...]
        sums[0:1] = jnp.sum(first_grad * unit, axis=0, keepdims=True)
        sums[1:2] = jnp.sum(first_grad, axis=0, keepdims=True)
        total = norm_back(first_grad, gain_one, unit, inv_one[:, 0:1])
        sum_grad[...] = total
        branch_grad = total.astype(BF16)
        attended_grad = nt(branch_grad, w_out[...])
        don[...] = (attended_grad * rn[...]).astype(BF16)
        dop[...] = (attended_grad * rp[...]).astype(BF16)
        low_t[...] = att[...].T
        for y in range(ny):
            store_chunks(out_send.at[y], nn(low_t[rows_of(y, 1 - mine), :], branch_grad))
            store_chunks(out_keep.at[y], nn(low_t[rows_of(y, mine), :], branch_grad))


def score_delta(grad, attended):
    pick = ((iota((8, LANES), 1) // 64) == iota((8, LANES), 0)).astype(F32)
    return nt(pick, grad.astype(F32) * attended, precision=lax.Precision.HIGHEST)


def pool_backward_kernel(info, q, grad, o, e, *rest, pieces):
    kv = rest[:pieces]
    keep, send, dq_out, dk, dv = rest[pieces:]
    ny = pieces // 2
    count = q.shape[0]
    size = kv[0].shape[1]
    delta = score_delta(grad[...], o[...])
    kp = jnp.concatenate([piece[0] for piece in kv], axis=0)
    kt = kp.T
    vp = jnp.concatenate([piece[1] for piece in kv], axis=0)
    wide = min(256, count)
    for head in range(2):
        for b in range(count // wide):
            cols = slice(b * wide, (b + 1) * wide)
            gh = head_half(grad[cols, :], head)
            qh = head_half(q[cols, :], head)
            low = e[head, :, cols]
            dp = nt(vp, gh) - delta[head : head + 1, cols]
            ds = (low.astype(F32) * dp).astype(BF16)
            key_part = nn(ds, qh)
            value_part = nn(low, gh)
            if head == 0 and b == 0:
                dk[...] = key_part
                dv[...] = value_part
            else:
                dk[...] += key_part
                dv[...] += value_part
            dq_out[head * 64 : head * 64 + 64, cols] = nn(kt[head * 64 : head * 64 + 64], ds)
    for i in range(pieces):
        target = keep if i < ny else send
        after = pl.ds(pl.multiple_of(info[8 + pieces + i] * size, size), EXTRA)
        for which, total in ((0, dk), (1, dv)):
            target[i % ny, which, 0:size] = total[i * size : (i + 1) * size].astype(BF16)
            target[i % ny, which, size:] = total[after, :].astype(BF16)


def near_backward_kernel(q, grad, o, e, k, v, dq_pool, own, before, behind, dq_out, dk, dv):
    count = q.shape[0]
    delta = score_delta(grad[...], o[...])
    kt = k[...].T
    dk[...] = jnp.zeros_like(dk)
    dv[...] = jnp.zeros_like(dv)
    for b in range(count // QB):
        cols = slice(b * QB, (b + 1) * QB)
        keys = slice(b * QB, (b + 2) * QB)
        lows, scores, grads, queries, dqs = [], [], [], [], []
        for head in range(2):
            gh = head_half(grad[cols, :], head)
            low = e[head, b]
            dp = nt(v[keys, :], gh) - delta[head : head + 1, cols]
            ds = (low.astype(F32) * dp).astype(BF16)
            dqs.append(nn(kt[head * 64 : head * 64 + 64, keys], ds))
            lows.append(low)
            scores.append(ds)
            grads.append(gh)
            queries.append(head_half(q[cols, :], head))
        dk[keys, :] += nn(jnp.concatenate(scores, axis=1), jnp.concatenate(queries, axis=0))
        dv[keys, :] += nn(jnp.concatenate(lows, axis=1), jnp.concatenate(grads, axis=0))
        total = (jnp.concatenate(dqs, axis=0) + dq_pool[:, cols]) * 0.125
        dq_out[cols, :] = total.T.astype(BF16)
    for which, total in ((0, dk), (1, dv)):
        before[which] = total[0:HALF].astype(BF16)
        own[which] = total[HALF : HALF + count]
        behind[which] = total[HALF + count :].astype(BF16)


def query_grad_kernel(info, tt, dq, wq, sum_grad, keep, send, part):
    ny = keep.shape[0]
    rc = D // (2 * ny)
    mine = info[5]
    for y in range(ny):
        for target, core in ((send, 1 - mine), (keep, mine)):
            rows = pl.ds(pl.multiple_of((2 * y + core) * rc, rc), rc)
            store_chunks(target.at[y], nn(tt[rows, :], dq[...]))
    part[...] = sum_grad[...] + nt(dq[...], wq[...])


def key_grad_kernel(info, tt, own, above, below, k, v, wk, wv, part, sums, taps, *rest, row_len, pieces):
    pooled = rest[:pieces]
    k_keep, k_send, v_keep, v_send, s_keep, s_send, tokens_grad = rest[pieces : pieces + 7]
    acc, cells, g, small, small_t, k_low, v_low = rest[pieces + 7 :]
    ny, nz, nx = k_keep.shape[:3]
    rc = D // (2 * ny)
    few = rc // (nz * nx)
    count = part.shape[0]
    size = count // 4
    mine = info[5]
    small[...] = jnp.zeros_like(small)
    small[0:8] = sums[...]
    masks = [tap_mask(info, tap, 0, size, row_len) for tap in range(5)]
    next_masks = [tap_mask(info, tap, 1, size, row_len) for tap in range(2)]
    moves = ((2, 0, 0), (3, 1, 0), (4, 2, 0), (0, 2, 1), (1, 3, 1))
    for which, source, low in ((0, k, k_low), (1, v, v_low)):
        for c in range(D // LANES):
            lanes = slice(c * LANES, (c + 1) * LANES)
            grad = acc.at[c]
            grad[...] = own[which, :, lanes]
            grad[0:HALF, :] += below[which, :, lanes].astype(F32)
            grad[count - HALF :, :] += above[which, :, lanes].astype(F32)
            cells[...] = source[:, lanes].astype(F32)
            total = pooled[0][0, which, :, lanes].astype(F32)
            for piece in pooled[1:]:
                total = total + piece[0, which, :, lanes].astype(F32)
            g[...] = total
            for tap, place, shift in moves:
                mask = next_masks[tap] if shift else masks[tap]
                spread = g[shift : shift + size, :] * mask * taps[tap : tap + 1, lanes]
                grad[pl.ds(place, size, stride=4), :] += spread
            for tap in range(5):
                taken = cells[pl.ds(HALF + tap - 2, size, stride=4), :]
                product = g[0:size, :] * masks[tap] * taken
                small[8 + tap : 9 + tap, lanes] += jnp.sum(product, axis=0, keepdims=True)
            low[:, lanes] = grad[...].astype(BF16)
    small_t[...] = small[...].T
    for y in range(ny):
        sides = ((k_send, v_send, s_send, 1 - mine), (k_keep, v_keep, s_keep, mine))
        for k_part, v_part, s_part, core in sides:
            rows = pl.ds(pl.multiple_of((2 * y + core) * rc, rc), rc)
            store_chunks(k_part.at[y], nn(tt[rows, :], k_low[...]))
            store_chunks(v_part.at[y], nn(tt[rows, :], v_low[...]))
            vectors = small_t[rows, :]
            for z in range(nz):
                for x in range(nx):
                    start = (z * nx + x) * few
                    s_part[y, z, x] = jnp.zeros(s_part.shape[3:], BF16)
                    s_part[y, z, x, 0:few] = vectors[start : start + few].astype(BF16)
    total = part[...] + nt(k_low[...], wk[...])
    tokens_grad[...] = (total + nt(v_low[...], wv[...])).astype(BF16)


def hop_pairs(axis, count, stride, hop):
    pairs = []
    for device in range(lax.axis_size(axis)):
        place = (device // stride) % count
        pairs.append((device, device + ((place + hop) % count - place) * stride))
    return pairs


MESH_ID = pl.DeviceIdType.MESH


class Summed:
    def __init__(self, seq_first, keep, send, bufs):
        self.seq_first = seq_first
        self.keep, self.send = keep, send
        self.core_in, self.one_in, self.two_in, self.three_in, self.out_sem, self.in_sem = bufs
        self.ny, self.nz, self.nx = keep.shape[:3]
        here, row = lax.axis_index("seq"), lax.axis_index("dp")
        self.y, self.core = here // 2, here % 2
        self.z, self.x = row // self.nx, row % self.nx
        self.row, self.here = row, here

    def copy(self, src, dst, slot, device):
        return pltpu.make_async_remote_copy(
            src_ref=src,
            dst_ref=dst,
            send_sem=self.out_sem.at[slot],
            recv_sem=self.in_sem.at[slot],
            device_id=device,
            device_id_type=MESH_ID,
        )

    def core_copies(self):
        partner = (self.y * 2 + 1 - self.core, self.row)
        copies = []
        for i in range(self.ny):
            block = (self.y + 1 + i) % self.ny
            copies.append(self.copy(self.send.at[block], self.core_in.at[block], i, partner))
        return copies

    def y_copies(self, two):
        copies = []
        for hop in range(1, self.ny):
            other = (self.y + hop) % self.ny
            device = (other * 2 + self.core, self.row)
            source = self.keep.at[other, :, self.x] if two else self.keep.at[other]
            into = self.two_in if two else self.one_in
            slot = (self.ny + self.nx - 1 if two else self.ny) + hop - 1
            copies.append(self.copy(source, into.at[hop - 1], slot, device))
        return copies

    def x_copies(self, two):
        copies = []
        for hop in range(1, self.nx):
            other = (self.x + hop) % self.nx
            device = (self.here, self.z * self.nx + other)
            source = self.keep.at[self.y, :, other] if two else self.keep.at[:, :, other]
            into = self.two_in if two else self.one_in
            slot = (2 * self.ny - 1 if two else self.ny) + hop - 1
            copies.append(self.copy(source, into.at[hop - 1], slot, device))
        return copies

    def one_copies(self):
        return self.y_copies(False) if self.seq_first else self.x_copies(False)

    def two_copies(self):
        return self.x_copies(True) if self.seq_first else self.y_copies(True)

    def three_copies(self):
        copies = []
        for hop in range(1, self.nz):
            other = (self.z + hop) % self.nz
            device = (self.here, other * self.nx + self.x)
            slot = 2 * self.ny + self.nx - 2 + hop - 1
            source = self.keep.at[self.y, other, self.x]
            copies.append(self.copy(source, self.three_in.at[hop - 1], slot, device))
        return copies

    def start(self):
        for copy in self.core_copies():
            copy.start()

    def add_core(self):
        copies = self.core_copies()
        for i, copy in enumerate(copies):
            block = (self.y + 1 + i) % self.ny
            copy.wait_recv()
            self.keep[block] = self.keep[block] + self.core_in[block]
            if self.seq_first and i < self.ny - 1:
                self.one_copies()[i].start()
        if not self.seq_first:
            for copy in self.one_copies():
                copy.start()

    def add_one(self):
        for hop, copy in enumerate(self.one_copies()):
            copy.wait_recv()
            if self.seq_first:
                self.keep[self.y] = self.keep[self.y] + self.one_in[hop]
            else:
                for y in range(self.ny):
                    for z in range(self.nz):
                        total = self.keep[y, z, self.x] + self.one_in[hop, y, z]
                        self.keep[y, z, self.x] = total
        for copy in self.two_copies():
            copy.start()

    def add_two(self):
        for hop, copy in enumerate(self.two_copies()):
            copy.wait_recv()
            for z in range(self.nz):
                total = self.keep[self.y, z, self.x] + self.two_in[hop, z]
                self.keep[self.y, z, self.x] = total
        for copy in self.three_copies():
            copy.start()

    def total(self):
        total = self.keep[self.y, self.z, self.x].astype(F32)
        for hop, copy in enumerate(self.three_copies()):
            copy.wait_recv()
            total = total + self.three_in[hop].astype(F32)
        return total

    def finish(self):
        copies = self.core_copies() + self.one_copies() + self.two_copies() + self.three_copies()
        for copy in copies:
            copy.wait_send()


def summed_scratch(shape, seq_first):
    ny, nz, nx = shape[:3]
    chunk = shape[3:]
    one = (ny - 1, nz, nx) if seq_first else (nx - 1, ny, nz)
    two = (nx - 1, nz) if seq_first else (ny - 1, nz)
    slots = 2 * ny + nx + nz - 3
    return [
        pltpu.VMEM(shape, BF16),
        pltpu.VMEM(one + chunk, BF16),
        pltpu.VMEM(two + chunk, BF16),
        pltpu.VMEM((nz - 1,) + chunk, BF16),
        pltpu.SemaphoreType.DMA((slots,)),
        pltpu.SemaphoreType.DMA((slots,)),
    ]


def greet(ny, nz, nx):
    here, row = lax.axis_index("seq"), lax.axis_index("dp")
    y, core, z, x = here // 2, here % 2, row // nx, row % nx
    peers = [(y * 2 + 1 - core, row)]
    peers += [(((y + hop) % ny) * 2 + core, row) for hop in range(1, ny)]
    peers += [(here, z * nx + (x + hop) % nx) for hop in range(1, nx)]
    peers += [(here, ((z + hop) % nz) * nx + x) for hop in range(1, nz)]
    barrier = pltpu.get_barrier_semaphore()
    for peer in peers:
        pl.semaphore_signal(barrier, inc=1, device_id=peer, device_id_type=MESH_ID)
    pl.semaphore_wait(barrier, len(peers))


def sum_kernel(*refs, order, grid):
    n = len(order)
    keeps, sends, outs = refs[:n], refs[n : 2 * n], refs[2 * n : 3 * n]
    rest = refs[3 * n :]
    held, local = rest[:n], rest[n]
    greet(*grid)
    units = []
    for i in range(n):
        units.append(Summed(order[i], held[i], sends[i], rest[n + 1 + 6 * i : n + 7 + 6 * i]))
    loads = [pltpu.make_async_copy(keeps[i], held[i], local.at[i]) for i in range(n)]
    for unit, load in zip(units, loads):
        unit.start()
        load.start()
    for unit, load in zip(units, loads):
        load.wait()
        unit.add_core()
    for unit in units:
        unit.add_one()
    for unit in units:
        unit.add_two()
    for unit, out in zip(units, outs):
        out[...] = unit.total()
    for unit in units:
        unit.finish()


def sum_all(keeps, sends, order):
    grid = keeps[0].shape[:3]
    outs = tuple(jax.ShapeDtypeStruct(a.shape[3:], F32) for a in keeps)
    scratch = [pltpu.VMEM(a.shape, BF16) for a in keeps] + [pltpu.SemaphoreType.DMA((len(order),))]
    for a, seq_first in zip(keeps, order):
        scratch += summed_scratch(a.shape, seq_first)
    return pl.pallas_call(
        partial(sum_kernel, order=order, grid=grid),
        out_shape=outs,
        in_specs=[pl.BlockSpec(memory_space=pl.ANY)] * (2 * len(order)),
        out_specs=[pl.BlockSpec(memory_space=pltpu.VMEM)] * len(order),
        scratch_shapes=scratch,
        compiler_params=pltpu.CompilerParams(
            collective_id=0, has_side_effects=True, vmem_limit_bytes=56 * MB
        ),
        name="sum_all",
    )(*keeps, *sends)


def shifted(block, by):
    size = lax.axis_size("seq")
    return lax.ppermute(block, "seq", [(i, i + by) for i in range(size) if 0 <= i + by < size])


def call(kernel, info, args, in_specs, outs, out_specs, grid, scratch, flops, vmem, name):
    moved = sum(a.size * a.dtype.itemsize for a in list(args) + list(outs))
    return pl.pallas_call(
        kernel,
        grid_spec=pltpu.PrefetchScalarGridSpec(
            num_scalar_prefetch=1,
            grid=grid,
            in_specs=in_specs,
            out_specs=out_specs,
            scratch_shapes=scratch,
        ),
        out_shape=outs,
        compiler_params=pltpu.CompilerParams(
            vmem_limit_bytes=vmem * MB, dimension_semantics=("arbitrary",) * len(grid)
        ),
        cost_estimate=pl.CostEstimate(flops=flops, bytes_accessed=moved, transcendentals=0),
        name=name,
    )(info, *args)


def whole(array):
    rank = len(array.shape)
    return pl.BlockSpec(array.shape, lambda i, info: (0,) * rank)


def columns(array, width=LANES):
    rank = len(array.shape)
    return pl.BlockSpec(array.shape[:-1] + (width,), lambda i, info: (0,) * (rank - 1) + (i,))


def leading(array, size):
    rank = len(array.shape)
    return pl.BlockSpec((size,) + array.shape[1:], lambda i, info: (i,) + (0,) * (rank - 1))


def per_device(
    tokens,
    item_lengths,
    w_query,
    w_key,
    w_value,
    w_out,
    w_in,
    w_back,
    norm1_gain,
    norm1_bias,
    norm2_gain,
    norm2_bias,
    pool_weight,
    out_grad,
):
    _, count, _ = tokens.shape
    seq = lax.axis_size("seq")
    ny = seq // 2
    row_len = count * seq
    span = count + 2 * HALF
    size = count // 4
    here = lax.axis_index("seq")
    core, y = here % 2, here // 2
    owners = []
    for other in range(2):
        for hop in range(ny):
            owners.append(((y + hop) % ny) * 2 + jnp.bitwise_xor(core, other))
    afters = []
    for owner in owners:
        after = jnp.minimum(owner + 1, seq - 1)
        afters.append(jnp.bitwise_xor(after % 2, core) * ny + (after // 2 - y) % ny)
    zero = jnp.zeros((), jnp.int32)
    info = jnp.concatenate(
        [
            jnp.cumsum(item_lengths[0]).astype(jnp.int32),
            jnp.stack([here * count, core, y, zero] + owners + afters).astype(jnp.int32),
        ]
    )
    tok = tokens[0]
    og = out_grad[0]
    left = shifted(tok[count - HALF :], 1)
    right = shifted(tok[:HALF], -1)
    taps = jnp.pad(pool_weight.T, ((0, 3), (0, 0)))
    vecs = jnp.concatenate(
        [jnp.stack([norm1_gain, norm1_bias, norm2_gain, norm2_bias]), jnp.zeros((4, D), F32)]
    )

    def shape(dims, kind):
        return jax.ShapeDtypeStruct(dims, kind)

    args = (tok, left, right, w_query, w_key, w_value, taps)
    outs = (
        shape((count, D), BF16),
        shape((span, D), BF16),
        shape((span, D), BF16),
        shape((2, size, D), BF16),
        shape((D, count), BF16),
    )
    queries, keys, values, pool_own, tok_t = call(
        partial(project_kernel, row_len=row_len),
        info,
        args,
        [whole(a) for a in args],
        outs,
        [whole(a) for a in outs],
        (1,),
        [
            pltpu.VMEM((span, D), BF16),
            pltpu.VMEM((D // LANES, span, LANES), F32),
        ],
        2 * D * D * (count + 2 * span),
        40,
        "project",
    )

    pieces = [pool_own]
    for hop in range(1, ny):
        pieces.append(lax.ppermute(pool_own, "seq", hop_pairs("seq", ny, 2, ny - hop)))
    pieces = pieces + [lax.ppermute(piece, "seq", hop_pairs("seq", 2, 1, 1)) for piece in pieces]

    blocks = count // QB
    args = (queries, keys, values)
    outs = (
        shape((H, blocks, 2 * QB, QB), BF16),
        shape((D, count), F32),
        shape((PAIRS, 8, count), F32),
    )
    near_e, o_near, stats = call(
        partial(near_forward_kernel, row_len=row_len),
        info,
        args,
        [columns(a) for a in args],
        outs,
        [leading(outs[0], 2), leading(outs[1], LANES), leading(outs[2], 1)],
        (PAIRS,),
        [pltpu.VMEM((blocks, 2 * QB, QB), F32)],
        4 * H * 256 * 256 * count,
        32,
        "near_forward",
    )

    pool_all = seq * size
    args = (queries, o_near, stats) + tuple(pieces)
    outs = (
        shape((H, pool_all, count), BF16),
        shape((count, D), F32),
        shape((count, D), F32),
        shape((count, D), F32),
    )
    pool_e, attention, near_scale, pool_scale = call(
        partial(pool_forward_kernel, row_len=row_len, pieces=seq),
        info,
        args,
        [columns(queries), leading(o_near, LANES), leading(stats, 1)] + [columns(p) for p in pieces],
        outs,
        [leading(outs[0], 2)] + [columns(a) for a in outs[1:]],
        (PAIRS,),
        [pltpu.VMEM((pool_all, count), F32)],
        4 * H * 512 * 256 * count,
        32,
        "pool_forward",
    )

    width = FF // seq
    args = (attention, near_scale, pool_scale, tok, og, vecs, w_out, w_in, w_back)
    dp = lax.axis_size("dp")
    nx = 2 if dp % 2 == 0 else 1
    nz = dp // nx
    rows = D // (seq * dp)
    half_in = shape((ny, nz, nx, seq) + folded(rows, width), BF16)
    half_back = shape((ny, nz, nx) + folded(FF // (seq * dp), D), BF16)
    half_out = shape((ny, nz, nx) + folded(rows, D), BF16)
    outs = (
        shape((count, D), BF16),
        shape((count, D), F32),
        shape((count, D), BF16),
        shape((count, D), BF16),
        half_in,
        half_in,
        half_back,
        half_back,
        half_out,
        half_out,
        shape((8, D), F32),
    )
    in_columns = pl.BlockSpec(
        (ny, nz, nx, 1) + half_in.shape[4:],
        lambda i, info: (0, 0, 0, block_of(jnp.maximum(i, seq), info, seq), 0, 0),
    )
    (
        mixed,
        sum_grad,
        near_grad,
        pool_grad,
        in_keep,
        in_send,
        back_keep,
        back_send,
        out_keep,
        out_send,
        sums,
    ) = call(
        partial(dense_kernel, parts=seq),
        info,
        args,
        [whole(a) for a in args[:7]]
        + [
            pl.BlockSpec((D, width), lambda i, info: (0, block_of(i, info, seq))),
            pl.BlockSpec((width, D), lambda i, info: (block_of(i, info, seq), 0)),
        ],
        outs,
        [whole(a) for a in outs[:4]]
        + [
            in_columns,
            in_columns,
            pl.BlockSpec(
                (1,) + half_back.shape[1:],
                lambda i, info: (jnp.maximum(i - seq - ny, 0), 0, 0, 0, 0),
            ),
            pl.BlockSpec(
                (1,) + half_back.shape[1:],
                lambda i, info: (jnp.clip(i - seq, 0, ny - 1), 0, 0, 0, 0),
            ),
        ]
        + [whole(a) for a in outs[8:]],
        (2 * seq,),
        [
            pltpu.VMEM((count, D), BF16),
            pltpu.VMEM((count, D), F32),
            pltpu.VMEM((count, D), F32),
            pltpu.VMEM((count, LANES), F32),
            pltpu.VMEM((count, D), BF16),
            pltpu.VMEM((D, count), BF16),
            pltpu.VMEM((count, FF), BF16),
            pltpu.VMEM((count, FF), BF16),
            pltpu.VMEM((count, D), F32),
            pltpu.VMEM((count, D), BF16),
        ],
        2 * count * (3 * D * D + 6 * D * FF),
        58,
        "dense",
    )

    args = (queries, pool_grad, attention, pool_e) + tuple(pieces)
    half_pool = shape((ny, 2, size + EXTRA, D), BF16)
    outs = (half_pool, half_pool, shape((D, count), F32))
    pool_keep, pool_send, dq_pool = call(
        partial(pool_backward_kernel, pieces=seq),
        info,
        args,
        [columns(a) for a in args[:3]] + [leading(pool_e, 2)] + [columns(p) for p in pieces],
        outs,
        [columns(half_pool), columns(half_pool), leading(outs[2], LANES)],
        (PAIRS,),
        [pltpu.VMEM((pool_all, LANES), F32), pltpu.VMEM((pool_all, LANES), F32)],
        8 * H * 512 * 256 * count,
        32,
        "pool_backward",
    )
    pool_moved = lax.ppermute(pool_send, "seq", hop_pairs("seq", 2, 1, 1))
    pooled = [pool_keep[0:1], pool_moved[0:1]]
    for hop in range(1, ny):
        both = pool_keep[hop : hop + 1].astype(F32) + pool_moved[hop : hop + 1].astype(F32)
        pooled.append(lax.ppermute(both.astype(BF16), "seq", hop_pairs("seq", ny, 2, hop)))

    args = (queries, near_grad, attention, near_e, keys, values, dq_pool)
    outs = (
        shape((2, count, D), F32),
        shape((2, HALF, D), BF16),
        shape((2, HALF, D), BF16),
        shape((count, D), BF16),
    )
    own, before, behind, query_grad = call(
        lambda info, *refs: near_backward_kernel(*refs),
        info,
        args,
        [columns(a) for a in args[:3]]
        + [leading(near_e, 2), columns(keys), columns(values), leading(dq_pool, LANES)],
        outs,
        [columns(a) for a in outs],
        (PAIRS,),
        [pltpu.VMEM((span, LANES), F32), pltpu.VMEM((span, LANES), F32)],
        8 * H * 256 * 256 * count,
        32,
        "near_backward",
    )
    above = shifted(before, -1)
    below = shifted(behind, 1)

    args = (tok_t, query_grad, w_query, sum_grad)
    outs = (half_out, half_out, shape((count, D), F32))
    query_keep, query_send, part = call(
        query_grad_kernel,
        info,
        args,
        [whole(a) for a in args],
        outs,
        [whole(a) for a in outs],
        (1,),
        [],
        4 * count * D * D,
        32,
        "query_grad",
    )

    args = (tok_t, own, above, below, keys, values, w_key, w_value, part, sums, taps) + tuple(pooled)
    half_small = shape((ny, nz, nx, -(-rows // 16) * 16, LANES), BF16)
    outs = (half_out, half_out, half_out, half_out, half_small, half_small, shape((count, D), BF16))
    key_keep, key_send, value_keep, value_send, small_keep, small_send, tokens_grad = call(
        partial(key_grad_kernel, row_len=row_len, pieces=len(pooled)),
        info,
        args,
        [whole(a) for a in args],
        outs,
        [whole(a) for a in outs],
        (1,),
        [
            pltpu.VMEM((D // LANES, count, LANES), F32),
            pltpu.VMEM((span, LANES), F32),
            pltpu.VMEM((size + EXTRA, LANES), F32),
            pltpu.VMEM((LANES, D), F32),
            pltpu.VMEM((D, LANES), F32),
            pltpu.VMEM((count, D), BF16),
            pltpu.VMEM((count, D), BF16),
        ],
        8 * count * D * D,
        56,
        "key_grad",
    )
    totals = sum_all(
        (in_keep, back_keep, out_keep, query_keep, key_keep, value_keep, small_keep),
        (in_send, back_send, out_send, query_send, key_send, value_send, small_send),
        (True, False, True, False, True, False, False),
    )
    sum_in = jnp.concatenate([unfold_rows(totals[0][g], rows) for g in range(seq)], axis=1)
    sum_back = unfold_rows(totals[1], FF // (seq * dp))
    sum_out, sum_query, sum_key, sum_value = (unfold_rows(t, rows) for t in totals[2:6])
    vectors = totals[6][:rows]
    return (
        mixed[None],
        tokens_grad[None],
        sum_query,
        sum_key,
        sum_value,
        sum_out,
        sum_in,
        sum_back,
        vectors[:, 0],
        vectors[:, 1],
        vectors[:, 2],
        vectors[:, 3],
        vectors[:, 8:13],
    )


def solution(mesh):
    shards, copied = P("dp", "seq", None), P()
    spread = P(("seq", "dp"), None)
    vector = P(("seq", "dp"))
    return jax.shard_map(
        per_device,
        mesh=mesh,
        in_specs=(shards, P("dp", None)) + (copied,) * 11 + (shards,),
        out_specs=(shards, shards) + (spread,) * 6 + (vector,) * 4 + (spread,),
        check_vma=False,
    )
```

```python
from functools import partial

import jax
import jax.numpy as jnp
from jax import lax
from jax.experimental import pallas as pl
from jax.experimental.pallas import tpu as pltpu
from jax.sharding import PartitionSpec as P

D = 768
FF = 3072
H = 12
PAIRS = H // 2
HALF = 64
PWIN = 512
QB = 128
EXTRA = 16
LANES = 128
BF16 = jnp.bfloat16
F32 = jnp.float32
MB = 1 << 20


def nn(left, right):
    return jnp.dot(left, right, preferred_element_type=F32)


def nt(left, right, precision=None):
    return lax.dot_general(
        left, right, (((1,), (1,)), ((), ())), preferred_element_type=F32, precision=precision
    )


def iota(shape, dim):
    return lax.broadcasted_iota(jnp.int32, shape, dim)


def segment_of(info, place, row_len):
    item = jnp.zeros_like(place)
    for m in range(4):
        item = item + (place >= info[m]).astype(jnp.int32)
    return jnp.where((place >= 0) & (place < row_len), item, -2)


def head_half(block, head):
    lane = iota(block.shape, 1)
    return jnp.where((lane < 64) == (head == 0), block, jnp.zeros_like(block))


def tap_mask(info, tap, shift, count, row_len):
    center = info[4] + 4 * (iota((count, 1), 0) + shift)
    same = segment_of(info, center + tap - 2, row_len) == segment_of(info, center, row_len)
    return (same & (center < row_len)).astype(F32)


def folds(rows, width):
    return 2 if rows % 16 and rows % 8 == 0 and (width // 2) % LANES == 0 else 1


def folded(rows, width):
    fold = folds(rows, width)
    return (rows * fold, width // fold)


def fold_rows(block):
    rows, width = block.shape
    fold = folds(rows, width)
    part = width // fold
    return jnp.concatenate([block[:, i * part : (i + 1) * part] for i in range(fold)], axis=0)


def unfold_rows(block, rows):
    fold = block.shape[0] // rows
    return jnp.concatenate([block[i * rows : (i + 1) * rows] for i in range(fold)], axis=1)


def store_chunks(target, total):
    nz, nx = target.shape[0], target.shape[1]
    rows = total.shape[0] // (nz * nx)
    for z in range(nz):
        for x in range(nx):
            start = (z * nx + x) * rows
            target[z, x] = fold_rows(total[start : start + rows]).astype(BF16)


def store_blocks(target, total):
    units, _, nz, nx, part, wide = target.shape
    rows = total.shape[0] // (nz * nx)
    across = total.shape[1] // wide
    for z in range(nz):
        for x in range(nx):
            start = (z * nx + x) * rows
            for unit in range(units):
                top = start + (unit // across) * part
                left = (unit % across) * wide
                target[unit, 0, z, x] = total[top : top + part, left : left + wide].astype(BF16)


def project_kernel(info, tok, left, right, wq, wk, wv, taps, q_out, k_out, v_out, pool_out, tt_out, mask_out, x, cells, *, row_len):
    count = tok.shape[0]
    x[0:HALF] = left[...]
    x[HALF : HALF + count] = tok[...]
    x[HALF + count :] = right[...]
    k_low = nn(x[...], wk[...]).astype(BF16)
    k_out[...] = k_low
    v_low = nn(x[...], wv[...]).astype(BF16)
    v_out[...] = v_low
    masks = [tap_mask(info, tap, 0, count // 4, row_len) for tap in range(5)]
    for which, low in ((0, k_low), (1, v_low)):
        wide = low.astype(F32)
        for c in range(D // LANES):
            lanes = slice(c * LANES, (c + 1) * LANES)
            cells[c] = wide[:, lanes]
            total = jnp.zeros((count // 4, LANES), F32)
            for tap in range(5):
                taken = cells.at[c][pl.ds(HALF + tap - 2, count // 4, stride=4), :]
                total = total + taken * masks[tap] * taps[tap : tap + 1, lanes]
            pool_out[which, :, lanes] = total.astype(BF16)
    q_out[...] = (nn(tok[...], wq[...]).astype(BF16).astype(F32) * 0.125).astype(BF16)
    tt_out[...] = tok[...].T
    lane = iota((count // 4, LANES), 1)
    for shift in range(2):
        total = jnp.zeros((count // 4, LANES), F32)
        for tap in range(5):
            mask = tap_mask(info, tap, shift, count // 4, row_len)
            total = jnp.where(lane == tap, mask, total)
        mask_out[shift] = total


def near_forward_kernel(info, q, k, v, e_out, o_out, st_out, bias, *, row_len):
    count, span = q.shape[0], k.shape[0]
    blocks = count // QB

    @pl.when(pl.program_id(0) == 0)
    def _():
        for b in range(blocks):
            query_place = info[4] + b * QB + iota((1, QB), 1)
            key_place = info[4] - HALF + b * QB + iota((2 * QB, 1), 0)
            same = segment_of(info, key_place, row_len) == segment_of(info, query_place, row_len)
            near = jnp.abs(key_place - query_place) <= HALF
            bias[b] = jnp.where(same & near, 0.0, -1e30)

    vt = v[...].T
    ones = jnp.ones((16, span), BF16)
    st_out[...] = jnp.zeros_like(st_out)
    for head in range(2):
        qh = head_half(q[...], head)
        va = jnp.concatenate([vt[head * 64 : head * 64 + 64], ones], axis=0)
        for b in range(blocks):
            cols = slice(b * QB, (b + 1) * QB)
            keys = slice(b * QB, (b + 2) * QB)
            s = nt(k[keys, :], qh[cols]) + bias[b]
            top = jnp.max(s, axis=0, keepdims=True)
            e = jnp.exp(s - top).astype(BF16)
            e_out[head, b] = e
            oa = nn(va[:, keys], e)
            o_out[head * 64 : head * 64 + 64, cols] = oa[:64]
            st_out[0, head : head + 1, cols] = top
            st_out[0, 2 + head : 3 + head, cols] = oa[64:65]


def pool_forward_kernel(info, q, o_near, st, *rest, row_len, pieces):
    kv = rest[:pieces]
    e_out, o_out, rn_out, rp_out, bias = rest[pieces:]
    count = q.shape[0]
    size = kv[0].shape[1]

    @pl.when(pl.program_id(0) == 0)
    def _():
        query_place = info[4] + iota((1, count), 1)
        query_item = segment_of(info, query_place, row_len)
        for i in range(pieces):
            key_place = 4 * (info[8 + i] * size + iota((size, 1), 0))
            same = segment_of(info, key_place, row_len) == query_item
            near = jnp.abs(key_place - query_place) <= 2 * PWIN
            bias[i * size : (i + 1) * size] = jnp.where(same & near, 0.0, -1e30)

    kp = jnp.concatenate([piece[0] for piece in kv], axis=0)
    vt = jnp.concatenate([piece[1] for piece in kv], axis=0).T
    ones = jnp.ones((16, pieces * size), BF16)
    wide = min(256, count)
    for b in range(count // wide):
        cols = slice(b * wide, (b + 1) * wide)
        outs, near_scale, pool_scale = [], [], []
        for head in range(2):
            qh = head_half(q[cols, :], head)
            va = jnp.concatenate([vt[head * 64 : head * 64 + 64], ones], axis=0)
            s = nt(kp, qh) + bias[:, cols]
            near_top = st[0, head : head + 1, cols]
            top = jnp.maximum(jnp.max(s, axis=0, keepdims=True), near_top)
            e = jnp.exp(s - top).astype(BF16)
            e_out[head, :, cols] = e
            oa = nn(va, e)
            fade = jnp.exp(near_top - top)
            inverse = 1.0 / (fade * st[0, 2 + head : 3 + head, cols] + oa[64:65])
            outs.append((fade * o_near[head * 64 : head * 64 + 64, cols] + oa[:64]) * inverse)
            near_scale.append(jnp.broadcast_to(fade * inverse, (64, wide)))
            pool_scale.append(jnp.broadcast_to(inverse, (64, wide)))
        o_out[cols, :] = jnp.concatenate(outs, axis=0).T
        rn_out[cols, :] = jnp.concatenate(near_scale, axis=0).T
        rp_out[cols, :] = jnp.concatenate(pool_scale, axis=0).T


def normal_parts(v):
    bell = jnp.exp(v * v * -0.5)
    t = 1.0 / (1.0 + jnp.abs(v) * (0.3275911 * 0.7071067811865476))
    poly = t * (
        0.127414796 + t * (-0.142248368 + t * (0.7107068705 + t * (-0.7265760135 + t * 0.5307027145)))
    )
    tail = poly * bell
    return jnp.where(v < 0, tail, 1.0 - tail), v * bell * 0.3989422804014327


def normalized(values):
    shifted = values - jnp.mean(values, axis=1, keepdims=True)
    inverse = lax.rsqrt(jnp.mean(shifted * shifted, axis=1, keepdims=True) + 1e-05)
    return shifted * inverse, inverse


def norm_back(grad, gain, unit, inverse):
    e = grad * gain
    return inverse * (
        e
        - jnp.mean(e, axis=1, keepdims=True)
        - unit * jnp.mean(e * unit, axis=1, keepdims=True)
    )


def block_of(step, info, parts):
    ny = parts // 2
    back = step - parts
    mine = info[5]
    going_back = jnp.where(
        back < ny, 2 * back + 1 - mine, 2 * (back - ny) + mine
    )
    return jnp.where(step < parts, step, going_back)


def dense_kernel(
    info, o, rn, rp, tok, og, vecs, w_out, w_in, w_back,
    mixed, sum_grad, don, dop, in_keep, in_send, back_keep, back_send, out_keep, out_send, sums,
    att, first, unit_one, inv_one, low, low_t, act, slope, feed, feed_grad,
    *, parts,
):
    ny = parts // 2
    step = pl.program_id(0)
    width = w_in.shape[1]
    rc = D // parts
    mine = info[5]
    hidden = pl.ds(pl.multiple_of(block_of(step, info, parts) * width, width), width)
    gain_one, bias_one = vecs[0:1, :], vecs[1:2, :]
    gain_two, bias_two = vecs[2:3, :], vecs[3:4, :]

    def rows_of(y, core):
        return pl.ds(pl.multiple_of((2 * y + core) * rc, rc), rc)

    @pl.when(step == 0)
    def _():
        att[...] = o[...].astype(BF16)
        unit, inverse = normalized(tok[...].astype(F32) + nn(att[...], w_out[...]))
        unit_one[...] = unit
        inv_one[...] = jnp.broadcast_to(inverse, inv_one.shape)
        first[...] = unit * gain_one + bias_one
        low[...] = first[...].astype(BF16)
        low_t[...] = low[...].T
        feed[...] = jnp.zeros_like(feed)
        sums[...] = jnp.zeros_like(sums)

    @pl.when(step < parts)
    def _():
        inner = nn(low[...], w_in[...])
        phi, bell = normal_parts(inner)
        act[:, hidden] = (inner * phi).astype(BF16)
        slope[:, hidden] = (phi + bell).astype(slope.dtype)
        feed[...] += nn(act[:, hidden], w_back[...])

    @pl.when(step == parts - 1)
    def _():
        unit, inverse = normalized(first[...] + feed[...])
        mixed[...] = (unit * gain_two + bias_two).astype(BF16)
        upstream = og[...].astype(F32)
        sums[2:3] = jnp.sum(upstream * unit, axis=0, keepdims=True)
        sums[3:4] = jnp.sum(upstream, axis=0, keepdims=True)
        z_grad = norm_back(upstream, gain_two, unit, inverse)
        feed[...] = z_grad
        feed_grad[...] = z_grad.astype(BF16)

    @pl.when(step >= parts)
    def _():
        inner_grad = (nt(feed_grad[...], w_back[...]) * slope[:, hidden].astype(F32)).astype(BF16)
        act_t = act[:, hidden].T
        back = nn(act_t, feed_grad[...])

        @pl.when(step < parts + ny)
        def _():
            store_blocks(back_send, back)

        @pl.when(step >= parts + ny)
        def _():
            store_blocks(back_keep, back)

        for y in range(ny):
            store_chunks(in_send.at[0, y], nn(low_t[rows_of(y, 1 - mine), :], inner_grad))
            store_chunks(in_keep.at[0, y], nn(low_t[rows_of(y, mine), :], inner_grad))
        feed[...] += nt(inner_grad, w_in[...])

    @pl.when(step == 2 * parts - 1)
    def _():
        first_grad = feed[...]
        unit = unit_one[...]
        sums[0:1] = jnp.sum(first_grad * unit, axis=0, keepdims=True)
        sums[1:2] = jnp.sum(first_grad, axis=0, keepdims=True)
        total = norm_back(first_grad, gain_one, unit, inv_one[:, 0:1])
        sum_grad[...] = total
        branch_grad = total.astype(BF16)
        attended_grad = nt(branch_grad, w_out[...])
        don[...] = (attended_grad * rn[...]).astype(BF16)
        dop[...] = (attended_grad * rp[...]).astype(BF16)
        low_t[...] = att[...].T
        for y in range(ny):
            store_chunks(out_send.at[y], nn(low_t[rows_of(y, 1 - mine), :], branch_grad))
            store_chunks(out_keep.at[y], nn(low_t[rows_of(y, mine), :], branch_grad))


def score_delta(grad, attended):
    pick = ((iota((8, LANES), 1) // 64) == iota((8, LANES), 0)).astype(F32)
    return nt(pick, grad.astype(F32) * attended, precision=lax.Precision.HIGHEST)


def hop_pairs(axis, count, stride, hop):
    pairs = []
    for device in range(lax.axis_size(axis)):
        place = (device // stride) % count
        pairs.append((device, device + ((place + hop) % count - place) * stride))
    return pairs


MESH_ID = pl.DeviceIdType.MESH


class Summed:
    def __init__(self, seq_first, sends, keep, core_in, one_in, two_in, three_in, out_sem, in_sem):
        self.seq_first = seq_first
        self.sends, self.keep = sends, keep
        self.core_in, self.one_in, self.two_in, self.three_in = core_in, one_in, two_in, three_in
        self.out_sem, self.in_sem = out_sem, in_sem
        self.units, self.ny, self.nz, self.nx = keep.shape[:4]
        self.here, self.row = lax.axis_index("seq"), lax.axis_index("dp")
        self.y, self.mine = self.here // 2, self.here % 2
        self.z, self.x = self.row // self.nx, self.row % self.nx

    def copy(self, u, src, dst, slot, device):
        return pltpu.make_async_remote_copy(
            src_ref=src,
            dst_ref=dst,
            send_sem=self.out_sem.at[u, slot],
            recv_sem=self.in_sem.at[u, slot],
            device_id=device,
            device_id_type=MESH_ID,
        )

    def core_copy(self, u, i):
        block = (self.y + 1 + i) % self.ny
        partner = (self.y * 2 + 1 - self.mine, self.row)
        return self.copy(u, self.sends[u].at[block], self.core_in.at[u, block], i, partner)

    def y_copy(self, u, hop, two):
        other = (self.y + hop) % self.ny
        device = (other * 2 + self.mine, self.row)
        if two:
            slot = self.ny + self.nx - 1 + hop - 1
            return self.copy(u, self.keep.at[u, other, :, self.x], self.two_in.at[u, hop - 1], slot, device)
        return self.copy(u, self.keep.at[u, other], self.one_in.at[u, hop - 1], self.ny + hop - 1, device)

    def x_copy(self, u, hop, two):
        other = (self.x + hop) % self.nx
        device = (self.here, self.z * self.nx + other)
        if two:
            slot = 2 * self.ny - 1 + hop - 1
            return self.copy(u, self.keep.at[u, self.y, :, other], self.two_in.at[u, hop - 1], slot, device)
        return self.copy(u, self.keep.at[u, :, :, other], self.one_in.at[u, hop - 1], self.ny + hop - 1, device)

    def z_copy(self, u, hop):
        other = (self.z + hop) % self.nz
        device = (self.here, other * self.nx + self.x)
        slot = 2 * self.ny + self.nx - 2 + hop - 1
        return self.copy(u, self.keep.at[u, self.y, other, self.x], self.three_in.at[u, hop - 1], slot, device)

    def one_copies(self, u):
        if self.seq_first:
            return [partial(self.y_copy, u, hop, False) for hop in range(1, self.ny)]
        return [partial(self.x_copy, u, hop, False) for hop in range(1, self.nx)]

    def two_copies(self, u):
        if self.seq_first:
            return [partial(self.x_copy, u, hop, True) for hop in range(1, self.nx)]
        return [partial(self.y_copy, u, hop, True) for hop in range(1, self.ny)]

    def three_copies(self, u):
        return [partial(self.z_copy, u, hop) for hop in range(1, self.nz)]

    def start(self, u):
        for i in range(self.ny):
            self.core_copy(u, i).start()

    def core(self, u):
        ones = self.one_copies(u)
        for i in range(self.ny):
            block = (self.y + 1 + i) % self.ny
            self.core_copy(u, i).wait_recv()
            for z in range(self.nz):
                self.keep[u, block, z] = self.keep[u, block, z] + self.core_in[u, block, z]
            if self.seq_first and i < self.ny - 1:
                ones[i]().start()
        if not self.seq_first:
            for copy in ones:
                copy().start()

    def one(self, u):
        for hop, copy in enumerate(self.one_copies(u)):
            copy().wait_recv()
            for z in range(self.nz):
                if self.seq_first:
                    total = self.keep[u, self.y, z] + self.one_in[u, hop, z]
                    self.keep[u, self.y, z] = total
                else:
                    for y in range(self.ny):
                        total = self.keep[u, y, z, self.x] + self.one_in[u, hop, y, z]
                        self.keep[u, y, z, self.x] = total
        for copy in self.two_copies(u):
            copy().start()

    def two(self, u):
        for hop, copy in enumerate(self.two_copies(u)):
            copy().wait_recv()
            for z in range(self.nz):
                total = self.keep[u, self.y, z, self.x] + self.two_in[u, hop, z]
                self.keep[u, self.y, z, self.x] = total
        for copy in self.three_copies(u):
            copy().start()

    def three(self, u):
        total = self.keep[u, self.y, self.z, self.x].astype(F32)
        for hop, copy in enumerate(self.three_copies(u)):
            copy().wait_recv()
            total = total + self.three_in[u, hop].astype(F32)
        return total

    def finish(self, u):
        for i in range(self.ny):
            self.core_copy(u, i).wait_send()
        for copy in self.one_copies(u) + self.two_copies(u) + self.three_copies(u):
            copy().wait_send()


def summed_scratch(units, shape, seq_first):
    ny, nz, nx = shape[:3]
    chunk = shape[3:]
    one = (units, ny - 1, nz, nx) if seq_first else (units, nx - 1, ny, nz)
    two = (units, nx - 1, nz) if seq_first else (units, ny - 1, nz)
    slots = 2 * ny + nx + nz - 3
    return [
        pltpu.VMEM((units,) + shape, BF16),
        pltpu.VMEM((units,) + shape, BF16),
        pltpu.VMEM(one + chunk, BF16),
        pltpu.VMEM(two + chunk, BF16),
        pltpu.VMEM((units, nz - 1) + chunk, BF16),
        pltpu.SemaphoreType.DMA((units, slots)),
        pltpu.SemaphoreType.DMA((units, slots)),
    ]


def greet(peers):
    barrier = pltpu.get_barrier_semaphore()
    for peer in peers:
        pl.semaphore_signal(barrier, inc=1, device_id=peer, device_id_type=MESH_ID)
    pl.semaphore_wait(barrier, len(peers))


def events(units_in, units_back):
    last = 3 * PAIRS
    table = []
    pairs = max(units_in, units_back)
    for u in range(pairs):
        for stack, count in (("in", units_in), ("back", units_back)):
            if u < count:
                table.append((min(2 + 3 * u, last), stack, u, "core"))
                table.append((min(8 + 4 * u, last), stack, u, "one"))
                table.append((min(11 + 4 * u, last), stack, u, "two"))
                table.append((min(15 + 4 * u, last), stack, u, "three"))
    table.append((14, "sqy", 0, "core"))
    table.append((15, "sqx", 0, "core"))
    rank = {"core": 0, "one": 1, "two": 2, "three": 3}
    table.sort(key=lambda row: (row[0], row[2] + rank[row[3]]))
    tail = [
        ("sqy", 1, "core"), ("sqx", 1, "core"), ("small", 0, "core"),
        ("sqy", 0, "one"), ("sqx", 0, "one"),
        ("sqy", 1, "one"), ("sqx", 1, "one"), ("small", 0, "one"),
        ("sqy", 0, "two"), ("sqx", 0, "two"),
        ("sqy", 1, "two"), ("sqx", 1, "two"), ("small", 0, "two"),
        ("sqy", 0, "three"), ("sqx", 0, "three"),
        ("sqy", 1, "three"), ("sqx", 1, "three"), ("small", 0, "three"),
    ]
    return table, tail


class Refs:
    pass


def backward_kernel(*refs, names, pieces):
    r = Refs()
    for name, ref in zip(names, refs):
        setattr(r, name, ref)
    kv = [getattr(r, "piece%d" % i) for i in range(pieces)]
    seq, ny = pieces, pieces // 2
    step = pl.program_id(0)
    count = r.q.shape[0]
    size = count // 4
    nz, nx = r.in_keep.shape[2:4]
    here, row = lax.axis_index("seq"), lax.axis_index("dp")
    y, core = here // 2, here % 2
    partner = (y * 2 + 1 - core, row)
    right, left = ((here + 1) % seq, row), ((here + seq - 1) % seq, row)
    stacks = {}
    sends = {
        "in": [r.in_send.at[u] for u in range(r.in_send.shape[0])],
        "back": [r.back_send.at[u] for u in range(r.back_send.shape[0])],
        "sqy": [r.out_send, r.k_send],
        "sqx": [r.q_send, r.v_send],
        "small": [r.s_send],
    }
    for name, seq_first in STACKS:
        bufs = [getattr(r, name + "_" + part) for part in BUFFERS]
        stacks[name] = Summed(seq_first, sends[name], *bufs)

    def copy(src, dst, out_sem, in_sem, device):
        return pltpu.make_async_remote_copy(
            src_ref=src, dst_ref=dst, send_sem=out_sem, recv_sem=in_sem,
            device_id=device, device_id_type=MESH_ID,
        )

    def pool_core(p):
        return copy(r.p_send.at[p], r.p_in.at[p], r.p_sem.at[0, p, 0], r.p_sem.at[1, p, 0], partner)

    def pool_y(p, hop):
        device = (((y + hop) % ny) * 2 + core, row)
        return copy(
            r.p_keep.at[p, hop], r.p_y.at[p, hop - 1], r.p_sem.at[0, p, hop], r.p_sem.at[1, p, hop], device
        )

    def halo(p, side):
        device = right if side else left
        return copy(
            r.h_out.at[p, side], r.h_in.at[p, side], r.h_sem.at[0, p, side], r.h_sem.at[1, p, side], device
        )

    loads = [
        pltpu.make_async_copy(r.out_keep, r.sqy_sum.at[0], r.l_sem.at[0]),
        pltpu.make_async_copy(r.in_keep, r.in_sum, r.l_sem.at[1]),
        pltpu.make_async_copy(r.back_keep, r.back_sum, r.l_sem.at[2]),
        pltpu.make_async_copy(r.tt_any, r.tt, r.l_sem.at[3]),
        pltpu.make_async_copy(r.wq_any, r.wq, r.l_sem.at[4]),
        pltpu.make_async_copy(r.wk_any, r.wk, r.l_sem.at[5]),
        pltpu.make_async_copy(r.wv_any, r.wv, r.l_sem.at[6]),
        pltpu.make_async_copy(r.sg_any, r.sg, r.l_sem.at[7]),
    ]

    @pl.when(step == 0)
    def _():
        z, x = row // nx, row % nx
        peers = [partner, right, left]
        peers += [(((y + hop) % ny) * 2 + core, row) for hop in range(1, ny)]
        peers += [(here, z * nx + (x + hop) % nx) for hop in range(1, nx)]
        peers += [(here, ((z + hop) % nz) * nx + x) for hop in range(1, nz)]
        greet(peers)
        for u in range(max(len(sends["in"]), len(sends["back"]))):
            for name in ("in", "back"):
                if u < len(sends[name]):
                    stacks[name].start(u)
        stacks["sqy"].start(0)
        for load in loads:
            load.start()

    @pl.when(step < PAIRS)
    def _():
        p = step
        delta = score_delta(r.dop[...], r.o[...])
        kp = jnp.concatenate([piece[0] for piece in kv], axis=0)
        kt = kp.T
        vp = jnp.concatenate([piece[1] for piece in kv], axis=0)
        wide = min(256, count)
        for head in range(2):
            for b in range(count // wide):
                cols = slice(b * wide, (b + 1) * wide)
                gh = head_half(r.dop[cols, :], head)
                qh = head_half(r.q[cols, :], head)
                low = r.pool_e[head, :, cols]
                dp = nt(vp, gh) - delta[head : head + 1, cols]
                ds = (low.astype(F32) * dp).astype(BF16)
                key_part = nn(ds, qh)
                value_part = nn(low, gh)
                if head == 0 and b == 0:
                    r.dk[0 : seq * size] = key_part
                    r.dv[0 : seq * size] = value_part
                else:
                    r.dk[0 : seq * size] += key_part
                    r.dv[0 : seq * size] += value_part
                r.dq_pool[p, head * 64 : head * 64 + 64, cols] = nn(kt[head * 64 : head * 64 + 64], ds)
        for i in range(pieces):
            target = r.p_keep if i < ny else r.p_send
            after = (((y + i % ny) % ny) * 2 + (core + i // ny) % 2 + 1) % seq
            index = ((after % 2 - core + 2) % 2) * ny + (after // 2 - y + ny) % ny
            rows = pl.ds(pl.multiple_of(index * size, size), EXTRA)
            for which, total in ((0, r.dk), (1, r.dv)):
                target[p, i % ny, which, 0:size] = total[i * size : (i + 1) * size].astype(BF16)
                target[p, i % ny, which, size:] = total[rows, :].astype(BF16)
        pool_core(p).start()

    @pl.when((step > 0) & (step <= PAIRS))
    def _():
        p = step - 1
        pool_core(p).wait_recv()
        for hop in range(1, ny):
            for which in range(2):
                r.p_keep[p, hop, which] = r.p_keep[p, hop, which] + r.p_in[p, hop, which]
            pool_y(p, hop).start()

    @pl.when((step >= PAIRS) & (step < 2 * PAIRS))
    def _():
        p = step - PAIRS
        delta = score_delta(r.don[...], r.o[...])
        kt = r.keys[...].T
        r.dk[0 : count + 2 * HALF] = jnp.zeros((count + 2 * HALF, LANES), F32)
        r.dv[0 : count + 2 * HALF] = jnp.zeros((count + 2 * HALF, LANES), F32)
        for b in range(count // QB):
            cols = slice(b * QB, (b + 1) * QB)
            keys = slice(b * QB, (b + 2) * QB)
            lows, scores, grads, queries, dqs = [], [], [], [], []
            for head in range(2):
                gh = head_half(r.don[cols, :], head)
                low = r.near_e[head, b]
                dp = nt(r.values[keys, :], gh) - delta[head : head + 1, cols]
                ds = (low.astype(F32) * dp).astype(BF16)
                dqs.append(nn(kt[head * 64 : head * 64 + 64, keys], ds))
                lows.append(low)
                scores.append(ds)
                grads.append(gh)
                queries.append(head_half(r.q[cols, :], head))
            r.dk[keys, :] += nn(jnp.concatenate(scores, axis=1), jnp.concatenate(queries, axis=0))
            r.dv[keys, :] += nn(jnp.concatenate(lows, axis=1), jnp.concatenate(grads, axis=0))
            total = (jnp.concatenate(dqs, axis=0) + r.dq_pool[p, :, cols]) * 0.125
            lanes = pl.ds(pl.multiple_of(p * LANES, LANES), LANES)
            r.dq[cols, lanes] = total.T.astype(BF16)
        for which, total in ((0, r.dk), (1, r.dv)):
            r.h_out[p, 0, which] = total[0:HALF].astype(BF16)
            r.acc[which, p] = total[HALF : HALF + count]
            r.h_out[p, 1, which] = total[HALF + count : 2 * HALF + count].astype(BF16)

        @pl.when(here > 0)
        def _():
            halo(p, 0).start()

        @pl.when(here < seq - 1)
        def _():
            halo(p, 1).start()

    def rows_of(block, mine):
        rc = D // seq
        return pl.ds(pl.multiple_of((2 * block + mine) * rc, rc), rc)

    @pl.when(step == 2 * PAIRS)
    def _():
        for load in loads[3:]:
            load.wait()
        for block in range(ny):
            store_chunks(r.q_send.at[block], nn(r.tt[rows_of(block, 1 - core), :], r.dq[...]))
        stacks["sqx"].start(0)
        for block in range(ny):
            store_chunks(r.sqx_sum.at[0, block], nn(r.tt[rows_of(block, core), :], r.dq[...]))
        r.sg[...] += nt(r.dq[...], r.wq[...])

    @pl.when((step >= 2 * PAIRS) & (step < 3 * PAIRS))
    def _():
        p = step - 2 * PAIRS
        lanes = pl.ds(pl.multiple_of(p * LANES, LANES), LANES)
        for hop in range(1, ny):
            pool_y(p, hop).wait_recv()

        @pl.when(here < seq - 1)
        def _():
            halo(p, 0).wait_recv()
            for which in range(2):
                r.acc[which, p, count - HALF :, :] += r.h_in[p, 0, which].astype(F32)

        @pl.when(here > 0)
        def _():
            halo(p, 1).wait_recv()
            for which in range(2):
                r.acc[which, p, 0:HALF, :] += r.h_in[p, 1, which].astype(F32)

        moves = ((2, 0, 0), (3, 1, 0), (4, 2, 0), (0, 2, 1), (1, 3, 1))
        sums = [jnp.zeros((1, LANES), F32)] * 5
        for which, source, low in ((0, r.keys, r.k_low), (1, r.values, r.v_low)):
            grad = r.acc.at[which, p]
            r.cells[...] = source[...].astype(F32)
            total = r.p_keep[p, 0, which].astype(F32) + r.p_in[p, 0, which].astype(F32)
            for hop in range(1, ny):
                total = total + r.p_y[p, hop - 1, which].astype(F32)
            r.g[...] = total
            for tap, place, shift in moves:
                mask = r.masks[shift, :, tap : tap + 1]
                spread = r.g[shift : shift + size, :] * mask * r.taps[tap : tap + 1, :]
                grad[pl.ds(place, size, stride=4), :] += spread
            for tap in range(5):
                taken = r.cells[pl.ds(HALF + tap - 2, size, stride=4), :]
                product = r.g[0:size, :] * r.masks[0, :, tap : tap + 1] * taken
                sums[tap] = sums[tap] + jnp.sum(product, axis=0, keepdims=True)
            low[:, lanes] = grad[...].astype(BF16)
        for tap in range(5):
            r.small[8 + tap : 9 + tap, lanes] = sums[tap]

    last = 3 * PAIRS

    @pl.when(step == last)
    def _():
        for name, index, send, low in (("sqy", 1, r.k_send, r.k_low), ("sqx", 1, r.v_send, r.v_low)):
            keep = stacks[name].keep
            for block in range(ny):
                store_chunks(send.at[block], nn(r.tt[rows_of(block, 1 - core), :], low[...]))
            stacks[name].start(index)
            for block in range(ny):
                store_chunks(keep.at[index, block], nn(r.tt[rows_of(block, core), :], low[...]))
        r.small[0:8] = r.sums[...]
        r.small[13:] = jnp.zeros((LANES - 13, D), F32)
        r.small_t[...] = r.small[...].T
        few = D // (seq * nz * nx)
        for block in range(ny):
            for part, mine in ((r.s_send.at[block], 1 - core), (r.small_sum.at[0, block], core)):
                vectors = r.small_t[rows_of(block, mine), :]
                for z in range(nz):
                    for x in range(nx):
                        start = (z * nx + x) * few
                        part[z, x] = jnp.zeros(part.shape[2:], BF16)
                        part[z, x, 0:few] = vectors[start : start + few].astype(BF16)
        stacks["small"].start(0)
        total = r.sg[...] + nt(r.k_low[...], r.wk[...])
        r.tokens_grad[...] = (total + nt(r.v_low[...], r.wv[...])).astype(BF16)

    results = {
        "in": [r.t_in.at[u] for u in range(r.t_in.shape[0])],
        "back": [r.t_back.at[u] for u in range(r.t_back.shape[0])],
        "sqy": [r.t_out, r.t_key],
        "sqx": [r.t_query, r.t_value],
        "small": [r.t_small],
    }

    def run(name, u, stage):
        done = getattr(stacks[name], stage)(u)
        if stage == "three":
            results[name][u][...] = done

    table, tail = events(len(sends["in"]), len(sends["back"]))
    for when in range(last + 1):
        rows = [event[1:] for event in table if event[0] == when]
        if when == last:
            rows = rows + tail
        if rows:

            @pl.when(step == when)
            def _(when=when, rows=rows):
                if when == 2:
                    for load in loads[:3]:
                        load.wait()
                for row in rows:
                    run(*row)

    @pl.when(step == last)
    def _():
        for name, _ in STACKS:
            for u in range(len(sends[name])):
                stacks[name].finish(u)
        for p in range(PAIRS):
            pool_core(p).wait_send()
            for hop in range(1, ny):
                pool_y(p, hop).wait_send()

        @pl.when(here > 0)
        def _():
            for p in range(PAIRS):
                halo(p, 0).wait_send()

        @pl.when(here < seq - 1)
        def _():
            for p in range(PAIRS):
                halo(p, 1).wait_send()


STACKS = (("in", True), ("back", False), ("sqy", True), ("sqx", False), ("small", False))
BUFFERS = ("sum", "core", "first", "second", "third", "out", "inn")


def unpack_kernel(t_in, t_back, t_query, t_key, t_value, t_out, t_small, tg, *outs):
    tokens_grad, query, key, value, out, inn, back = outs[:7]
    rows = query.shape[0]
    tokens_grad[...] = tg[...]
    for source, target in ((t_query, query), (t_key, key), (t_value, value), (t_out, out)):
        target[...] = unfold_rows(source[...], rows)
    width = inn.shape[1] // t_in.shape[0]
    for u in range(t_in.shape[0]):
        inn[:, u * width : (u + 1) * width] = unfold_rows(t_in[u], rows)
    units, part, wide = t_back.shape
    across = back.shape[1] // wide
    for u in range(units):
        top, start = (u // across) * part, (u % across) * wide
        back[top : top + part, start : start + wide] = t_back[u]
    small = t_small[...]
    pad = LANES - small.shape[0]
    turned = jnp.concatenate([small, jnp.zeros((pad, LANES), F32)], axis=0).T
    for i in range(4):
        outs[7 + i][...] = turned[i : i + 1, 0:rows]
    outs[11][...] = small[0:rows, 8:13]


def shifted(block, by):
    size = lax.axis_size("seq")
    return lax.ppermute(block, "seq", [(i, i + by) for i in range(size) if 0 <= i + by < size])


def call(kernel, info, args, in_specs, outs, out_specs, grid, scratch, flops, name):
    moved = sum(a.size * a.dtype.itemsize for a in list(args) + list(outs))
    return pl.pallas_call(
        kernel,
        grid_spec=pltpu.PrefetchScalarGridSpec(
            num_scalar_prefetch=1,
            grid=grid,
            in_specs=in_specs,
            out_specs=out_specs,
            scratch_shapes=scratch,
        ),
        out_shape=outs,
        compiler_params=pltpu.CompilerParams(
            vmem_limit_bytes=60 * MB, dimension_semantics=("arbitrary",) * len(grid)
        ),
        cost_estimate=pl.CostEstimate(flops=flops, bytes_accessed=moved, transcendentals=0),
        name=name,
    )(info, *args)


def whole(array):
    rank = len(array.shape)
    return pl.BlockSpec(array.shape, lambda i, info: (0,) * rank)


def columns(array, width=LANES):
    rank = len(array.shape)
    return pl.BlockSpec(array.shape[:-1] + (width,), lambda i, info: (0,) * (rank - 1) + (i,))


def leading(array, size):
    rank = len(array.shape)
    return pl.BlockSpec((size,) + array.shape[1:], lambda i, info: (i,) + (0,) * (rank - 1))


def per_device(
    tokens,
    item_lengths,
    w_query,
    w_key,
    w_value,
    w_out,
    w_in,
    w_back,
    norm1_gain,
    norm1_bias,
    norm2_gain,
    norm2_bias,
    pool_weight,
    out_grad,
):
    _, count, _ = tokens.shape
    seq = lax.axis_size("seq")
    ny = seq // 2
    row_len = count * seq
    span = count + 2 * HALF
    size = count // 4
    here = lax.axis_index("seq")
    core, y = here % 2, here // 2
    owners = []
    for other in range(2):
        for hop in range(ny):
            owners.append(((y + hop) % ny) * 2 + jnp.bitwise_xor(core, other))
    afters = []
    for owner in owners:
        after = jnp.minimum(owner + 1, seq - 1)
        afters.append(jnp.bitwise_xor(after % 2, core) * ny + (after // 2 - y) % ny)
    zero = jnp.zeros((), jnp.int32)
    info = jnp.concatenate(
        [
            jnp.cumsum(item_lengths[0]).astype(jnp.int32),
            jnp.stack([here * count, core, y, zero] + owners + afters).astype(jnp.int32),
        ]
    )
    tok = tokens[0]
    og = out_grad[0]
    left = shifted(tok[count - HALF :], 1)
    right = shifted(tok[:HALF], -1)
    taps = jnp.pad(pool_weight.T, ((0, 3), (0, 0)))
    vecs = jnp.concatenate(
        [jnp.stack([norm1_gain, norm1_bias, norm2_gain, norm2_bias]), jnp.zeros((4, D), F32)]
    )

    def shape(dims, kind):
        return jax.ShapeDtypeStruct(dims, kind)

    args = (tok, left, right, w_query, w_key, w_value, taps)
    outs = (
        shape((count, D), BF16),
        shape((span, D), BF16),
        shape((span, D), BF16),
        shape((2, size, D), BF16),
        shape((D, count), BF16),
        shape((2, size, LANES), F32),
    )
    queries, keys, values, pool_own, tok_t, tap_masks = call(
        partial(project_kernel, row_len=row_len),
        info,
        args,
        [whole(a) for a in args],
        outs,
        [whole(a) for a in outs],
        (1,),
        [
            pltpu.VMEM((span, D), BF16),
            pltpu.VMEM((D // LANES, span, LANES), F32),
        ],
        2 * D * D * (count + 2 * span),
        "project",
    )

    pieces = [pool_own]
    for hop in range(1, ny):
        pieces.append(lax.ppermute(pool_own, "seq", hop_pairs("seq", ny, 2, ny - hop)))
    pieces = pieces + [lax.ppermute(piece, "seq", hop_pairs("seq", 2, 1, 1)) for piece in pieces]

    blocks = count // QB
    args = (queries, keys, values)
    outs = (
        shape((H, blocks, 2 * QB, QB), BF16),
        shape((D, count), F32),
        shape((PAIRS, 8, count), F32),
    )
    near_e, o_near, stats = call(
        partial(near_forward_kernel, row_len=row_len),
        info,
        args,
        [columns(a) for a in args],
        outs,
        [leading(outs[0], 2), leading(outs[1], LANES), leading(outs[2], 1)],
        (PAIRS,),
        [pltpu.VMEM((blocks, 2 * QB, QB), F32)],
        4 * H * 256 * 256 * count,
        "near_forward",
    )

    pool_all = seq * size
    args = (queries, o_near, stats) + tuple(pieces)
    outs = (
        shape((H, pool_all, count), BF16),
        shape((count, D), F32),
        shape((count, D), F32),
        shape((count, D), F32),
    )
    pool_e, attention, near_scale, pool_scale = call(
        partial(pool_forward_kernel, row_len=row_len, pieces=seq),
        info,
        args,
        [columns(queries), leading(o_near, LANES), leading(stats, 1)] + [columns(p) for p in pieces],
        outs,
        [leading(outs[0], 2)] + [columns(a) for a in outs[1:]],
        (PAIRS,),
        [pltpu.VMEM((pool_all, count), F32)],
        4 * H * 512 * 256 * count,
        "pool_forward",
    )

    width = FF // seq
    args = (attention, near_scale, pool_scale, tok, og, vecs, w_out, w_in, w_back)
    dp = lax.axis_size("dp")
    nx = 2 if dp % 2 == 0 else 1
    nz = dp // nx
    rows = D // (seq * dp)
    back_rows = FF // (seq * dp)
    down = 2 if back_rows % 32 == 0 else 1
    half_in = shape((seq, ny, nz, nx) + folded(rows, width), BF16)
    half_back = shape((2 * down, ny, nz, nx, back_rows // down, D // 2), BF16)
    half_out = shape((ny, nz, nx) + folded(rows, D), BF16)
    outs = (
        shape((count, D), BF16),
        shape((count, D), F32),
        shape((count, D), BF16),
        shape((count, D), BF16),
        half_in,
        half_in,
        half_back,
        half_back,
        half_out,
        half_out,
        shape((8, D), F32),
    )
    in_columns = pl.BlockSpec(
        (1,) + half_in.shape[1:],
        lambda i, info: (block_of(jnp.maximum(i, seq), info, seq), 0, 0, 0, 0, 0),
    )
    (
        mixed,
        sum_grad,
        near_grad,
        pool_grad,
        in_keep,
        in_send,
        back_keep,
        back_send,
        out_keep,
        out_send,
        sums,
    ) = call(
        partial(dense_kernel, parts=seq),
        info,
        args,
        [whole(a) for a in args[:7]]
        + [
            pl.BlockSpec((D, width), lambda i, info: (0, block_of(i, info, seq))),
            pl.BlockSpec((width, D), lambda i, info: (block_of(i, info, seq), 0)),
        ],
        outs,
        [whole(a) for a in outs[:4]]
        + [
            in_columns,
            in_columns,
            pl.BlockSpec(
                (2 * down, 1) + half_back.shape[2:],
                lambda i, info: (0, jnp.maximum(i - seq - ny, 0), 0, 0, 0, 0),
            ),
            pl.BlockSpec(
                (2 * down, 1) + half_back.shape[2:],
                lambda i, info: (0, jnp.clip(i - seq, 0, ny - 1), 0, 0, 0, 0),
            ),
        ]
        + [whole(a) for a in outs[8:]],
        (2 * seq,),
        [
            pltpu.VMEM((count, D), BF16),
            pltpu.VMEM((count, D), F32),
            pltpu.VMEM((count, D), F32),
            pltpu.VMEM((count, LANES), F32),
            pltpu.VMEM((count, D), BF16),
            pltpu.VMEM((D, count), BF16),
            pltpu.VMEM((count, FF), BF16),
            pltpu.VMEM((count, FF), BF16),
            pltpu.VMEM((count, D), F32),
            pltpu.VMEM((count, D), BF16),
        ],
        2 * count * (3 * D * D + 6 * D * FF),
        "dense",
    )

    half_small = shape((ny, nz, nx, -(-rows // 16) * 16, LANES), BF16)
    half_pool = (PAIRS, ny, 2, size + EXTRA, LANES)
    blocks_in = []

    def block(name, array, spec):
        blocks_in.append((name, array, spec))

    def col_spec(array, index):
        lead = (0,) * (len(array.shape) - 1)
        return pl.BlockSpec(array.shape[:-1] + (LANES,), lambda i: lead + (index(i),))

    def lead_spec(array, index):
        rest = (0,) * (len(array.shape) - 1)
        return pl.BlockSpec((2,) + array.shape[1:], lambda i: (index(i),) + rest)

    def all_spec(array):
        rest = (0,) * len(array.shape)
        return pl.BlockSpec(array.shape, lambda i: rest)

    def in_pool(i):
        return jnp.minimum(i, PAIRS - 1)

    def in_near(i):
        return jnp.clip(i - PAIRS, 0, PAIRS - 1)

    def in_both(i):
        return jnp.minimum(i, 2 * PAIRS - 1) % PAIRS

    def in_late(i):
        return jnp.where(i < PAIRS, 0, jnp.minimum(i - PAIRS, 2 * PAIRS - 1) % PAIRS)

    block("q", queries, col_spec(queries, in_both))
    block("o", attention, col_spec(attention, in_both))
    block("dop", pool_grad, col_spec(pool_grad, in_pool))
    block("don", near_grad, col_spec(near_grad, in_near))
    block("pool_e", pool_e, lead_spec(pool_e, in_pool))
    block("near_e", near_e, lead_spec(near_e, in_near))
    block("keys", keys, col_spec(keys, in_late))
    block("values", values, col_spec(values, in_late))
    for i, piece in enumerate(pieces):
        block("piece%d" % i, piece, col_spec(piece, in_pool))
    block("masks", tap_masks, all_spec(tap_masks))
    block("taps", taps, col_spec(taps, in_late))
    block("sums", sums, all_spec(sums))
    anywhere = pl.BlockSpec(memory_space=pl.ANY)
    for name, array in (
        ("in_keep", in_keep),
        ("in_send", in_send),
        ("back_keep", back_keep),
        ("back_send", back_send),
        ("out_keep", out_keep),
        ("out_send", out_send),
        ("tt_any", tok_t),
        ("wq_any", w_query),
        ("wk_any", w_key),
        ("wv_any", w_value),
        ("sg_any", sum_grad),
    ):
        block(name, array, anywhere)
    outs = [
        ("t_in", shape((half_in.shape[0],) + half_in.shape[4:], F32)),
        ("t_back", shape((half_back.shape[0],) + half_back.shape[4:], F32)),
        ("t_query", shape(half_out.shape[3:], F32)),
        ("t_key", shape(half_out.shape[3:], F32)),
        ("t_value", shape(half_out.shape[3:], F32)),
        ("t_out", shape(half_out.shape[3:], F32)),
        ("t_small", shape(half_small.shape[3:], F32)),
        ("tokens_grad", shape((count, D), BF16)),
    ]
    tall = max(pool_all, span)
    scratch = [
        ("dk", pltpu.VMEM((tall, LANES), F32)),
        ("dv", pltpu.VMEM((tall, LANES), F32)),
        ("dq_pool", pltpu.VMEM((PAIRS, LANES, count), F32)),
        ("dq", pltpu.VMEM((count, D), BF16)),
        ("acc", pltpu.VMEM((2, PAIRS, count, LANES), F32)),
        ("k_low", pltpu.VMEM((count, D), BF16)),
        ("v_low", pltpu.VMEM((count, D), BF16)),
        ("cells", pltpu.VMEM((span, LANES), F32)),
        ("g", pltpu.VMEM((size + EXTRA, LANES), F32)),
        ("small", pltpu.VMEM((LANES, D), F32)),
        ("small_t", pltpu.VMEM((D, LANES), F32)),
        ("p_keep", pltpu.VMEM(half_pool, BF16)),
        ("p_send", pltpu.VMEM(half_pool, BF16)),
        ("p_in", pltpu.VMEM(half_pool, BF16)),
        ("p_y", pltpu.VMEM((PAIRS, ny - 1) + half_pool[2:], BF16)),
        ("h_out", pltpu.VMEM((PAIRS, 2, 2, HALF, LANES), BF16)),
        ("h_in", pltpu.VMEM((PAIRS, 2, 2, HALF, LANES), BF16)),
        ("p_sem", pltpu.SemaphoreType.DMA((2, PAIRS, ny))),
        ("h_sem", pltpu.SemaphoreType.DMA((2, PAIRS, 2))),
        ("l_sem", pltpu.SemaphoreType.DMA((8,))),
        ("tt", pltpu.VMEM((D, count), BF16)),
        ("wq", pltpu.VMEM((D, D), BF16)),
        ("wk", pltpu.VMEM((D, D), BF16)),
        ("wv", pltpu.VMEM((D, D), BF16)),
        ("sg", pltpu.VMEM((count, D), F32)),
        ("q_send", pltpu.VMEM(half_out.shape, BF16)),
        ("k_send", pltpu.VMEM(half_out.shape, BF16)),
        ("v_send", pltpu.VMEM(half_out.shape, BF16)),
        ("s_send", pltpu.VMEM(half_small.shape, BF16)),
    ]
    sizes = {
        "in": (half_in.shape[0], half_in.shape[1:]),
        "back": (half_back.shape[0], half_back.shape[1:]),
        "sqy": (2, half_out.shape),
        "sqx": (2, half_out.shape),
        "small": (1, half_small.shape),
    }
    for name, seq_first in STACKS:
        bufs = summed_scratch(sizes[name][0], sizes[name][1], seq_first)
        scratch += [(name + "_" + part, buf) for part, buf in zip(BUFFERS, bufs)]
    names = [entry[0] for entry in blocks_in] + [entry[0] for entry in outs + scratch]
    moved = sum(entry[1].size * entry[1].dtype.itemsize for entry in blocks_in)
    totals = pl.pallas_call(
        partial(backward_kernel, names=names, pieces=seq),
        grid_spec=pltpu.PrefetchScalarGridSpec(
            num_scalar_prefetch=0,
            grid=(3 * PAIRS + 1,),
            in_specs=[entry[2] for entry in blocks_in],
            out_specs=[all_spec(entry[1]) for entry in outs],
            scratch_shapes=[entry[1] for entry in scratch],
        ),
        out_shape=[entry[1] for entry in outs],
        compiler_params=pltpu.CompilerParams(
            collective_id=0,
            has_side_effects=True,
            vmem_limit_bytes=60 * MB,
            dimension_semantics=("arbitrary",),
        ),
        cost_estimate=pl.CostEstimate(
            flops=8 * H * 768 * 256 * count + 12 * count * D * D, bytes_accessed=moved, transcendentals=0
        ),
        name="backward",
    )(*[entry[1] for entry in blocks_in])

    outs = (
        shape((count, D), BF16),
        shape((rows, D), F32),
        shape((rows, D), F32),
        shape((rows, D), F32),
        shape((rows, D), F32),
        shape((rows, FF), F32),
        shape((back_rows, D), F32),
        shape((1, rows), F32),
        shape((1, rows), F32),
        shape((1, rows), F32),
        shape((1, rows), F32),
        shape((rows, 5), F32),
    )
    done = call(
        lambda info, *refs: unpack_kernel(*refs),
        info,
        tuple(totals),
        [whole(a) for a in totals],
        outs,
        [whole(a) for a in outs],
        (1,),
        [],
        0,
        "unpack",
    )
    return (
        mixed[None],
        done[0][None],
        done[1],
        done[2],
        done[3],
        done[4],
        done[5],
        done[6],
        done[7].reshape(rows),
        done[8].reshape(rows),
        done[9].reshape(rows),
        done[10].reshape(rows),
        done[11],
    )


def solution(mesh):
    shards, copied = P("dp", "seq", None), P()
    spread = P(("seq", "dp"), None)
    vector = P(("seq", "dp"))
    return jax.shard_map(
        per_device,
        mesh=mesh,
        in_specs=(shards, P("dp", None)) + (copied,) * 11 + (shards,),
        out_specs=(shards, shards) + (spread,) * 6 + (vector,) * 4 + (spread,),
        check_vma=False,
    )
```

```python
import itertools
from functools import partial

import jax
import jax.numpy as jnp
from jax import lax
from jax.experimental import pallas as pl
from jax.experimental.pallas import tpu as pltpu
from jax.sharding import PartitionSpec as P

D = 768
FF = 3072
H = 12
PAIRS = H // 2
HALF = 64
PWIN = 512
QB = 128
EXTRA = 16
LANES = 128
BF16 = jnp.bfloat16
F32 = jnp.float32
MB = 1 << 20


def nn(left, right):
    return jnp.dot(left, right, preferred_element_type=F32)


def nt(left, right, precision=None):
    return lax.dot_general(
        left, right, (((1,), (1,)), ((), ())), preferred_element_type=F32, precision=precision
    )


def iota(shape, dim):
    return lax.broadcasted_iota(jnp.int32, shape, dim)


def segment_of(info, place, row_len):
    item = jnp.zeros_like(place)
    for m in range(4):
        item = item + (place >= info[m]).astype(jnp.int32)
    return jnp.where((place >= 0) & (place < row_len), item, -2)


def head_half(block, head):
    lane = iota(block.shape, 1)
    return jnp.where((lane < 64) == (head == 0), block, jnp.zeros_like(block))


def tap_mask(info, tap, shift, count, row_len):
    center = info[4] + 4 * (iota((count, 1), 0) + shift)
    same = segment_of(info, center + tap - 2, row_len) == segment_of(info, center, row_len)
    return (same & (center < row_len)).astype(F32)


def folds(rows, width):
    return 2 if rows % 16 and rows % 8 == 0 and (width // 2) % LANES == 0 else 1


def folded(rows, width):
    fold = folds(rows, width)
    return (rows * fold, width // fold)


def fold_rows(block):
    rows, width = block.shape
    fold = folds(rows, width)
    part = width // fold
    return jnp.concatenate([block[:, i * part : (i + 1) * part] for i in range(fold)], axis=0)


def unfold_rows(block, rows):
    fold = block.shape[0] // rows
    return jnp.concatenate([block[i * rows : (i + 1) * rows] for i in range(fold)], axis=1)


def store_chunks(target, total):
    nz, nx = target.shape[0], target.shape[1]
    rows = total.shape[0] // (nz * nx)
    for z in range(nz):
        for x in range(nx):
            start = (z * nx + x) * rows
            target[z, x] = fold_rows(total[start : start + rows]).astype(BF16)


def store_blocks(targets, block, total):
    _, nz, nx, part, wide = targets[0].shape
    rows = total.shape[0] // (nz * nx)
    across = total.shape[1] // wide
    for z in range(nz):
        for x in range(nx):
            start = (z * nx + x) * rows
            for unit, target in enumerate(targets):
                top = start + (unit // across) * part
                left = (unit % across) * wide
                target[block, z, x] = total[top : top + part, left : left + wide].astype(BF16)


def project_kernel(info, tok, left, right, wq, wk, wv, taps, q_out, k_out, v_out, pool_out, tt_out, mask_out, x, cells, *, row_len):
    count = tok.shape[0]
    x[0:HALF] = left[...]
    x[HALF : HALF + count] = tok[...]
    x[HALF + count :] = right[...]
    k_low = nn(x[...], wk[...]).astype(BF16)
    k_out[...] = k_low
    v_low = nn(x[...], wv[...]).astype(BF16)
    v_out[...] = v_low
    masks = [tap_mask(info, tap, 0, count // 4, row_len) for tap in range(5)]
    for which, low in ((0, k_low), (1, v_low)):
        wide = low.astype(F32)
        for c in range(D // LANES):
            lanes = slice(c * LANES, (c + 1) * LANES)
            cells[c] = wide[:, lanes]
            total = jnp.zeros((count // 4, LANES), F32)
            for tap in range(5):
                taken = cells.at[c][pl.ds(HALF + tap - 2, count // 4, stride=4), :]
                total = total + taken * masks[tap] * taps[tap : tap + 1, lanes]
            pool_out[which, :, lanes] = total.astype(BF16)
    q_out[...] = (nn(tok[...], wq[...]).astype(BF16).astype(F32) * 0.125).astype(BF16)
    tt_out[...] = tok[...].T
    lane = iota((count // 4, LANES), 1)
    for shift in range(2):
        total = jnp.zeros((count // 4, LANES), F32)
        for tap in range(5):
            mask = tap_mask(info, tap, shift, count // 4, row_len)
            total = jnp.where(lane == tap, mask, total)
        mask_out[shift] = total


def near_forward_kernel(info, q, k, v, e_out, o_out, st_out, bias, *, row_len):
    count, span = q.shape[0], k.shape[0]
    blocks = count // QB

    @pl.when(pl.program_id(0) == 0)
    def _():
        for b in range(blocks):
            query_place = info[4] + b * QB + iota((1, QB), 1)
            key_place = info[4] - HALF + b * QB + iota((2 * QB, 1), 0)
            same = segment_of(info, key_place, row_len) == segment_of(info, query_place, row_len)
            near = jnp.abs(key_place - query_place) <= HALF
            bias[b] = jnp.where(same & near, 0.0, -1e30)

    vt = v[...].T
    ones = jnp.ones((16, span), BF16)
    st_out[...] = jnp.zeros_like(st_out)
    for head in range(2):
        qh = head_half(q[...], head)
        va = jnp.concatenate([vt[head * 64 : head * 64 + 64], ones], axis=0)
        for b in range(blocks):
            cols = slice(b * QB, (b + 1) * QB)
            keys = slice(b * QB, (b + 2) * QB)
            s = nt(k[keys, :], qh[cols]) + bias[b]
            top = jnp.max(s, axis=0, keepdims=True)
            e = jnp.exp(s - top).astype(BF16)
            e_out[head, b] = e
            oa = nn(va[:, keys], e)
            o_out[head * 64 : head * 64 + 64, cols] = oa[:64]
            st_out[0, head : head + 1, cols] = top
            st_out[0, 2 + head : 3 + head, cols] = oa[64:65]


def pool_forward_kernel(info, q, o_near, st, *rest, row_len, pieces):
    kv = rest[:pieces]
    e_out, o_out, rn_out, rp_out, bias = rest[pieces:]
    count = q.shape[0]
    size = kv[0].shape[1]

    @pl.when(pl.program_id(0) == 0)
    def _():
        query_place = info[4] + iota((1, count), 1)
        query_item = segment_of(info, query_place, row_len)
        for i in range(pieces):
            key_place = 4 * (info[8 + i] * size + iota((size, 1), 0))
            same = segment_of(info, key_place, row_len) == query_item
            near = jnp.abs(key_place - query_place) <= 2 * PWIN
            bias[i * size : (i + 1) * size] = jnp.where(same & near, 0.0, -1e30)

    kp = jnp.concatenate([piece[0] for piece in kv], axis=0)
    vt = jnp.concatenate([piece[1] for piece in kv], axis=0).T
    ones = jnp.ones((16, pieces * size), BF16)
    wide = min(256, count)
    for b in range(count // wide):
        cols = slice(b * wide, (b + 1) * wide)
        outs, near_scale, pool_scale = [], [], []
        for head in range(2):
            qh = head_half(q[cols, :], head)
            va = jnp.concatenate([vt[head * 64 : head * 64 + 64], ones], axis=0)
            s = nt(kp, qh) + bias[:, cols]
            near_top = st[0, head : head + 1, cols]
            top = jnp.maximum(jnp.max(s, axis=0, keepdims=True), near_top)
            e = jnp.exp(s - top).astype(BF16)
            e_out[head, :, cols] = e
            oa = nn(va, e)
            fade = jnp.exp(near_top - top)
            inverse = 1.0 / (fade * st[0, 2 + head : 3 + head, cols] + oa[64:65])
            outs.append((fade * o_near[head * 64 : head * 64 + 64, cols] + oa[:64]) * inverse)
            near_scale.append(jnp.broadcast_to(fade * inverse, (64, wide)))
            pool_scale.append(jnp.broadcast_to(inverse, (64, wide)))
        o_out[cols, :] = jnp.concatenate(outs, axis=0).T
        rn_out[cols, :] = jnp.concatenate(near_scale, axis=0).T
        rp_out[cols, :] = jnp.concatenate(pool_scale, axis=0).T


def normal_parts(v):
    bell = jnp.exp(v * v * -0.5)
    t = 1.0 / (1.0 + jnp.abs(v) * (0.3275911 * 0.7071067811865476))
    poly = t * (
        0.127414796 + t * (-0.142248368 + t * (0.7107068705 + t * (-0.7265760135 + t * 0.5307027145)))
    )
    tail = poly * bell
    return jnp.where(v < 0, tail, 1.0 - tail), v * bell * 0.3989422804014327


def normalized(values):
    shifted = values - jnp.mean(values, axis=1, keepdims=True)
    inverse = lax.rsqrt(jnp.mean(shifted * shifted, axis=1, keepdims=True) + 1e-05)
    return shifted * inverse, inverse


def dense_kernel(
    info, o, tok, og, vecs, w_out, w_in, w_back,
    mixed, act, slope, low_t, feed_grad, z_grad, unit_out, inv_out, att_t, sums,
    first, low, feed,
):
    step = pl.program_id(0)
    gain_one, bias_one = vecs[0:1, :], vecs[1:2, :]
    gain_two, bias_two = vecs[2:3, :], vecs[3:4, :]

    @pl.when(step == 0)
    def _():
        att = o[...].astype(BF16)
        att_t[...] = att.T
        unit, inverse = normalized(tok[...].astype(F32) + nn(att, w_out[...]))
        for c in range(PAIRS):
            unit_out[c] = unit[:, c * LANES : (c + 1) * LANES]
        inv_out[...] = jnp.broadcast_to(inverse, inv_out.shape)
        first[...] = unit * gain_one + bias_one
        low[...] = first[...].astype(BF16)
        low_t[...] = low[...].T
        feed[...] = jnp.zeros_like(feed)

    inner = nn(low[...], w_in[...])
    phi, bell = normal_parts(inner)
    act[...] = (inner * phi).astype(BF16)
    slope[...] = (phi + bell).astype(BF16)
    feed[...] += nn(act[...], w_back[...])

    @pl.when(step == CHUNKS - 1)
    def _():
        unit, inverse = normalized(first[...] + feed[...])
        mixed[...] = (unit * gain_two + bias_two).astype(BF16)
        upstream = og[...].astype(F32)
        sums[...] = jnp.zeros_like(sums)
        sums[2:3] = jnp.sum(upstream * unit, axis=0, keepdims=True)
        sums[3:4] = jnp.sum(upstream, axis=0, keepdims=True)
        e = upstream * gain_two
        centred = e - jnp.mean(e, axis=1, keepdims=True)
        total = inverse * (centred - unit * jnp.mean(e * unit, axis=1, keepdims=True))
        z_grad[...] = total
        feed_grad[...] = total.astype(BF16)


def score_delta(grad, attended):
    pick = ((iota((8, LANES), 1) // 64) == iota((8, LANES), 0)).astype(F32)
    return nt(pick, grad.astype(F32) * attended, precision=lax.Precision.HIGHEST)


def hop_pairs(axis, count, stride, hop):
    pairs = []
    for device in range(lax.axis_size(axis)):
        place = (device // stride) % count
        pairs.append((device, device + ((place + hop) % count - place) * stride))
    return pairs


MESH_ID = pl.DeviceIdType.MESH


class Summed:
    def __init__(self, order, send_of, keep, core_in, first, second, third, out_sem, in_sem):
        self.order, self.send_of = order, send_of
        self.keep, self.core_in = keep, core_in
        self.bufs = (first, second, third)
        self.out_sem, self.in_sem = out_sem, in_sem
        self.units = keep.shape[0]
        self.count = dict(zip("yzx", keep.shape[1:4]))
        self.here, self.row = lax.axis_index("seq"), lax.axis_index("dp")
        self.mine = self.here % 2
        nx = self.count["x"]
        self.own = {"y": self.here // 2, "z": self.row // nx, "x": self.row % nx}
        self.base = {"y": 1}
        self.base["x"] = self.base["y"] + self.count["y"] - 1
        self.base["z"] = self.base["x"] + nx - 1

    def copy(self, u, src, dst, slot, device):
        return pltpu.make_async_remote_copy(
            src_ref=src,
            dst_ref=dst,
            send_sem=self.out_sem.at[u, slot],
            recv_sem=self.in_sem.at[u, slot],
            device_id=device,
            device_id_type=MESH_ID,
        )

    def core_copy(self, u):
        partner = (self.own["y"] * 2 + 1 - self.mine, self.row)
        return self.copy(u, self.send_of(u), self.core_in.at[u], 0, partner)

    def hop_copy(self, u, stage, hop):
        axis = self.order[stage]
        other = (self.own[axis] + hop) % self.count[axis]
        place = dict(self.own)
        place[axis] = other
        device = (place["y"] * 2 + self.mine, place["z"] * self.count["x"] + place["x"])
        index = []
        for dim in "yzx":
            known = dim in self.order[: stage + 1]
            index.append(place[dim] if known else slice(None))
        source = self.keep.at[(u,) + tuple(index)]
        slot = self.base[axis] + hop - 1
        return self.copy(u, source, self.bufs[stage].at[u, hop - 1], slot, device)

    def hops(self, stage):
        return range(1, self.count[self.order[stage]])

    def start(self, u):
        self.core_copy(u).start()

    def core(self, u):
        self.core_copy(u).wait_recv()
        for y in range(self.count["y"]):
            for z in range(self.count["z"]):
                self.keep[u, y, z] = self.keep[u, y, z] + self.core_in[u, y, z]
        for hop in self.hops(0):
            self.hop_copy(u, 0, hop).start()

    def add(self, u, stage):
        left = [dim for dim in "yzx" if dim not in self.order[: stage + 1]]
        for hop in self.hops(stage):
            self.hop_copy(u, stage, hop).wait_recv()
            for place in itertools.product(*[range(self.count[dim]) for dim in left]):
                at = dict(self.own)
                at.update(zip(left, place))
                index = (u,) + tuple(at[dim] for dim in "yzx")
                self.keep[index] = self.keep[index] + self.bufs[stage][(u, hop - 1) + place]
        for hop in self.hops(stage + 1):
            self.hop_copy(u, stage + 1, hop).start()

    def one(self, u):
        self.add(u, 0)

    def two(self, u):
        self.add(u, 1)

    def three(self, u):
        total = self.keep[(u,) + tuple(self.own[dim] for dim in "yzx")].astype(F32)
        for hop in self.hops(2):
            self.hop_copy(u, 2, hop).wait_recv()
            total = total + self.bufs[2][u, hop - 1].astype(F32)
        return total

    def sent_core(self, u):
        self.core_copy(u).wait_send()

    def sent(self, u):
        for stage in range(3):
            for hop in self.hops(stage):
                self.hop_copy(u, stage, hop).wait_send()


def summed_scratch(units, shape, order):
    count = dict(zip("yzx", shape[:3]))
    chunk = shape[3:]
    bufs = [pltpu.VMEM((units,) + shape, BF16), pltpu.VMEM((units,) + shape, BF16)]
    for stage in range(3):
        left = tuple(count[dim] for dim in "yzx" if dim not in order[: stage + 1])
        bufs.append(pltpu.VMEM((units, max(count[order[stage]] - 1, 1)) + left + chunk, BF16))
    slots = count["y"] + count["x"] + count["z"] - 2
    bufs += [pltpu.SemaphoreType.DMA((units, slots)), pltpu.SemaphoreType.DMA((units, slots))]
    return bufs


def greet(peers):
    barrier = pltpu.get_barrier_semaphore()
    for peer in peers:
        pl.semaphore_signal(barrier, inc=1, device_id=peer, device_id_type=MESH_ID)
    pl.semaphore_wait(barrier, len(peers))


CHUNKS = FF // D
BUFFERS = ("sum", "core", "first", "second", "third", "out", "inn")
POOL = CHUNKS + 1
NEAR = POOL + PAIRS
LATE = NEAR + PAIRS
LAST = LATE + PAIRS
ORDERS = {
    "in0": "zxy",
    "in1": "xzy",
    "in2": "yzx",
    "in3": "yzx",
    "b0": "xzy",
    "b1": "xzy",
    "b2": "zxy",
    "b3": "xyz",
    "out": "yzx",
    "q": "xyz",
    "k": "xyz",
    "v": "yxz",
    "small": "yzx",
}
PLAN = {
    1: (
        ("in0", 0),
    ),
    3: (
        ("in1", 0),
    ),
    4: (
        ("b0", 0),
        ("in3", 0),
        ("b2", 0),
    ),
    8: (
        ("out", 0),
    ),
    9: (
        ("b1", 0),
    ),
    10: (
        ("in1", 1),
    ),
    11: (
        ("b0", 1),
    ),
    13: (
        ("b3", 0),
    ),
    14: (
        ("b1", 1),
    ),
    15: (
        ("in2", 0),
    ),
    17: (
        ("query", 0),
        ("in3", 1),
    ),
    19: (
        ("q", 0),
    ),
    20: (
        ("in2", 1),
        ("b3", 1),
    ),
    23: (
        ("in0", 1),
        ("b1", 2),
        ("q", 1),
        ("in3", 2),
        ("out", 1),
        ("k", 0),
        ("small", 0),
        ("v", 0),
        ("tokens", 0),
        ("b3", 2),
        ("small", 1),
        ("q", 2),
        ("k", 1),
        ("b2", 1),
        ("v", 1),
        ("small", 2),
        ("b0", 2),
        ("b2", 2),
        ("k", 2),
        ("q", 3),
        ("in0", 2),
        ("in3", 3),
        ("b1", 3),
        ("in2", 2),
        ("small", 3),
        ("out", 2),
        ("in1", 2),
        ("v", 2),
        ("out", 3),
        ("b3", 3),
        ("in0", 3),
        ("in1", 3),
        ("in2", 3),
        ("b0", 3),
        ("b2", 3),
        ("k", 3),
        ("v", 3),
    ),
}

class Refs:
    pass


def backward_kernel(*refs, names, pieces):
    r = Refs()
    for name, ref in zip(names, refs):
        setattr(r, name, ref)
    kv = [getattr(r, "piece%d" % i) for i in range(pieces)]
    seq, ny = pieces, pieces // 2
    step = pl.program_id(0)
    count = r.q.shape[0]
    size = count // 4
    nz, nx = r.b_send.shape[2:4]
    here, row = lax.axis_index("seq"), lax.axis_index("dp")
    y, core = here // 2, here % 2
    partner = (y * 2 + 1 - core, row)
    right, left = ((here + 1) % seq, row), ((here + seq - 1) % seq, row)
    units_back = r.b_send.shape[0]
    senders = {"small": r.s_send}
    for f in range(CHUNKS):
        senders["in%d" % f] = r.a_send.at[f]
    for place, name in enumerate(("out", "q", "k", "v")):
        senders[name] = r.a_send.at[place]
    for u in range(units_back):
        senders["b%d" % u] = r.b_send.at[u]
    sums = {}
    for name in senders:
        bufs = [getattr(r, name + "_" + part) for part in BUFFERS]
        sums[name] = Summed(ORDERS[name], lambda u, name=name: senders[name], *bufs)

    def copy(src, dst, out_sem, in_sem, device):
        return pltpu.make_async_remote_copy(
            src_ref=src, dst_ref=dst, send_sem=out_sem, recv_sem=in_sem,
            device_id=device, device_id_type=MESH_ID,
        )

    def pool_core(p):
        return copy(r.p_send.at[p], r.p_in.at[p], r.p_sem.at[0, p, 0], r.p_sem.at[1, p, 0], partner)

    def pool_y(p, hop):
        device = (((y + hop) % ny) * 2 + core, row)
        return copy(
            r.p_keep.at[p, hop], r.p_y.at[p, hop - 1], r.p_sem.at[0, p, hop], r.p_sem.at[1, p, hop], device
        )

    def halo(p, side):
        device = right if side else left
        return copy(
            r.h_out.at[p, side], r.h_in.at[p, side], r.h_sem.at[0, p, side], r.h_sem.at[1, p, side], device
        )

    def chunk_loads(f):
        slot = f % 2
        part = pl.ds(pl.multiple_of(f * D, D), D)
        return [
            pltpu.make_async_copy(r.win_any.at[:, part], r.wbuf.at[slot], r.l_sem.at[0, slot]),
            pltpu.make_async_copy(r.wback_any.at[part, :], r.wbuf.at[2 + slot], r.l_sem.at[1, slot]),
            pltpu.make_async_copy(r.act_any.at[:, part], r.tbuf.at[slot], r.l_sem.at[2, slot]),
            pltpu.make_async_copy(r.slope_any.at[:, part], r.tbuf.at[2 + slot], r.l_sem.at[3, slot]),
        ]

    load_feed = [
        pltpu.make_async_copy(r.fg_any, r.fg, r.l_sem.at[4, 0]),
        pltpu.make_async_copy(r.lowt_any, r.lt, r.l_sem.at[4, 1]),
        pltpu.make_async_copy(r.zg_any, r.sg, r.l_sem.at[5, 0]),
    ]
    load_unit = pltpu.make_async_copy(r.unit_any, r.acc.at[0], r.l_sem.at[5, 1])
    load_wout = pltpu.make_async_copy(r.wout_any, r.wbuf.at[0], r.l_sem.at[6, 0])
    load_att = pltpu.make_async_copy(r.att_any, r.att, r.l_sem.at[6, 1])
    load_wq = pltpu.make_async_copy(r.wq_any, r.wbuf.at[1], r.l_sem.at[7, 0])
    load_wk = pltpu.make_async_copy(r.wk_any, r.wbuf.at[2], r.l_sem.at[7, 1])
    load_wv = pltpu.make_async_copy(r.wv_any, r.wbuf.at[3], r.l_sem.at[8, 0])
    load_tt = pltpu.make_async_copy(r.tt_any, r.lt, r.l_sem.at[8, 1])

    def rows_of(block, mine):
        rc = D // seq
        return pl.ds(pl.multiple_of((2 * block + mine) * rc, rc), rc)

    @pl.when(step == 0)
    def _():
        for load in chunk_loads(0) + load_feed + [load_unit, load_att]:
            load.start()
        z, x = row // nx, row % nx
        peers = [partner, right, left]
        peers += [(((y + hop) % ny) * 2 + core, row) for hop in range(1, ny)]
        peers += [(here, z * nx + (x + hop) % nx) for hop in range(1, nx)]
        peers += [(here, ((z + hop) % nz) * nx + x) for hop in range(1, nz)]
        greet(peers)
        for load in load_feed:
            load.wait()

    @pl.when(step < CHUNKS)
    def _():
        f = step
        slot = f % 2
        for load in chunk_loads(f):
            load.wait()

        @pl.when(f < CHUNKS - 1)
        def _():
            for load in chunk_loads(f + 1):
                load.start()

        @pl.when(f == CHUNKS - 1)
        def _():
            load_wout.start()

        slope = r.tbuf[2 + slot].astype(F32)
        inner_grad = (nt(r.fg[...], r.wbuf[2 + slot]) * slope).astype(BF16)
        for block in range(ny):
            store_chunks(r.a_send.at[f, block], nn(r.lt[rows_of(block, 1 - core), :], inner_grad))

        kept = [nn(r.lt[rows_of(block, core), :], inner_grad) for block in range(ny)]
        for i in range(CHUNKS):

            @pl.when(f == i)
            def _(i=i):
                sums["in%d" % i].start(0)
                for block in range(ny):
                    store_chunks(sums["in%d" % i].keep.at[0, block], kept[block])

        r.sg[...] += nt(inner_grad, r.wbuf[slot])
        back = nn(r.tbuf[slot].T, r.fg[...])
        part = FF // seq
        for sub in range(D // part):
            block = f * (D // part) + sub
            piece = back[sub * part : (sub + 1) * part]

            @pl.when(block % 2 == core)
            def _(block=block, piece=piece):
                keeps = [sums["b%d" % u].keep.at[0] for u in range(units_back)]
                store_blocks(keeps, block // 2, piece)

            @pl.when(block % 2 != core)
            def _(block=block, piece=piece):
                store_blocks([r.b_send.at[u] for u in range(units_back)], block // 2, piece)

        @pl.when(f == CHUNKS - 1)
        def _():
            for u in range(units_back):
                sums["b%d" % u].start(0)

    @pl.when(step == CHUNKS)
    def _():
        load_wq.start()
        load_wk.start()
        load_wv.start()
        load_unit.wait()
        inverse = r.inv[:, 0:1]
        total = jnp.zeros((count, LANES), F32)
        total_unit = jnp.zeros((count, LANES), F32)
        r.small[...] = jnp.zeros_like(r.small)
        r.small[0:8] = r.sums[...]
        for c in range(PAIRS):
            lanes = slice(c * LANES, (c + 1) * LANES)
            grad, unit = r.sg[:, lanes], r.acc[0, c]
            r.small[0:1, lanes] = jnp.sum(grad * unit, axis=0, keepdims=True)
            r.small[1:2, lanes] = jnp.sum(grad, axis=0, keepdims=True)
            e = grad * r.vecs[0:1, lanes]
            total = total + e
            total_unit = total_unit + e * unit
        mean = jnp.sum(total, axis=1, keepdims=True) * (1.0 / D)
        mean_unit = jnp.sum(total_unit, axis=1, keepdims=True) * (1.0 / D)
        for c in range(PAIRS):
            lanes = slice(c * LANES, (c + 1) * LANES)
            e = r.sg[:, lanes] * r.vecs[0:1, lanes]
            r.sg[:, lanes] = inverse * (e - mean - r.acc[0, c] * mean_unit)
        branch_grad = r.sg[...].astype(BF16)
        load_att.wait()
        load_wout.wait()
        sums["in0"].sent_core(0)
        for block in range(ny):
            store_chunks(r.a_send.at[0, block], nn(r.att[rows_of(block, 1 - core), :], branch_grad))
        sums["out"].start(0)
        for block in range(ny):
            store_chunks(sums["out"].keep.at[0, block], nn(r.att[rows_of(block, core), :], branch_grad))
        load_tt.start()
        attended_grad = nt(branch_grad, r.wbuf[0])
        for c in range(PAIRS):
            r.acc[1, c] = attended_grad[:, c * LANES : (c + 1) * LANES]

    @pl.when((step >= POOL) & (step < NEAR))
    def _():
        p = step - POOL
        r.gb[...] = (r.acc[1, p] * r.rp[...]).astype(BF16)
        delta = score_delta(r.gb[...], r.o[...])
        kp = jnp.concatenate([piece[0] for piece in kv], axis=0)
        kt = kp.T
        vp = jnp.concatenate([piece[1] for piece in kv], axis=0)
        wide = min(256, count)
        for head in range(2):
            for b in range(count // wide):
                cols = slice(b * wide, (b + 1) * wide)
                gh = head_half(r.gb[cols, :], head)
                qh = head_half(r.q[cols, :], head)
                low = r.pool_e[head, :, cols]
                dp = nt(vp, gh) - delta[head : head + 1, cols]
                ds = (low.astype(F32) * dp).astype(BF16)
                key_part = nn(ds, qh)
                value_part = nn(low, gh)
                if head == 0 and b == 0:
                    r.dk[0 : seq * size] = key_part
                    r.dv[0 : seq * size] = value_part
                else:
                    r.dk[0 : seq * size] += key_part
                    r.dv[0 : seq * size] += value_part
                r.dq_pool[p, head * 64 : head * 64 + 64, cols] = nn(kt[head * 64 : head * 64 + 64], ds)
        for i in range(pieces):
            target = r.p_keep if i < ny else r.p_send
            after = (((y + i % ny) % ny) * 2 + (core + i // ny) % 2 + 1) % seq
            index = ((after % 2 - core + 2) % 2) * ny + (after // 2 - y + ny) % ny
            rows = pl.ds(pl.multiple_of(index * size, size), EXTRA)
            for which, total in ((0, r.dk), (1, r.dv)):
                target[p, i % ny, which, 0:size] = total[i * size : (i + 1) * size].astype(BF16)
                target[p, i % ny, which, size:] = total[rows, :].astype(BF16)
        pool_core(p).start()

    @pl.when((step > POOL) & (step <= NEAR))
    def _():
        p = step - POOL - 1
        pool_core(p).wait_recv()
        for hop in range(1, ny):
            for which in range(2):
                r.p_keep[p, hop, which] = r.p_keep[p, hop, which] + r.p_in[p, hop, which]
            pool_y(p, hop).start()

    @pl.when((step >= NEAR) & (step < LATE))
    def _():
        p = step - NEAR
        r.gb[...] = (r.acc[1, p] * r.rn[...]).astype(BF16)
        delta = score_delta(r.gb[...], r.o[...])
        kt = r.keys[...].T
        r.dk[0 : count + 2 * HALF] = jnp.zeros((count + 2 * HALF, LANES), F32)
        r.dv[0 : count + 2 * HALF] = jnp.zeros((count + 2 * HALF, LANES), F32)
        for b in range(count // QB):
            cols = slice(b * QB, (b + 1) * QB)
            keys = slice(b * QB, (b + 2) * QB)
            lows, scores, grads, queries, dqs = [], [], [], [], []
            for head in range(2):
                gh = head_half(r.gb[cols, :], head)
                low = r.near_e[head, b]
                dp = nt(r.values[keys, :], gh) - delta[head : head + 1, cols]
                ds = (low.astype(F32) * dp).astype(BF16)
                dqs.append(nn(kt[head * 64 : head * 64 + 64, keys], ds))
                lows.append(low)
                scores.append(ds)
                grads.append(gh)
                queries.append(head_half(r.q[cols, :], head))
            r.dk[keys, :] += nn(jnp.concatenate(scores, axis=1), jnp.concatenate(queries, axis=0))
            r.dv[keys, :] += nn(jnp.concatenate(lows, axis=1), jnp.concatenate(grads, axis=0))
            total = (jnp.concatenate(dqs, axis=0) + r.dq_pool[p, :, cols]) * 0.125
            lanes = pl.ds(pl.multiple_of(p * LANES, LANES), LANES)
            r.tbuf[0, cols, lanes] = total.T.astype(BF16)
        for which, total in ((0, r.dk), (1, r.dv)):
            r.h_out[p, 0, which] = total[0:HALF].astype(BF16)
            r.acc[which, p] = total[HALF : HALF + count]
            r.h_out[p, 1, which] = total[HALF + count : 2 * HALF + count].astype(BF16)

        @pl.when(here > 0)
        def _():
            halo(p, 0).start()

        @pl.when(here < seq - 1)
        def _():
            halo(p, 1).start()

    def query_gradient():
        load_tt.wait()
        sums["in1"].sent_core(0)
        for block in range(ny):
            store_chunks(r.a_send.at[1, block], nn(r.lt[rows_of(block, 1 - core), :], r.tbuf[0]))
        sums["q"].start(0)
        for block in range(ny):
            store_chunks(sums["q"].keep.at[0, block], nn(r.lt[rows_of(block, core), :], r.tbuf[0]))

    def tokens_gradient():
        for load in (load_wq, load_wk, load_wv):
            load.wait()
        total = r.sg[...] + nt(r.tbuf[0], r.wbuf[1])
        total = total + nt(r.tbuf[1], r.wbuf[2])
        r.tokens_grad[...] = (total + nt(r.tbuf[2], r.wbuf[3])).astype(BF16)

    @pl.when((step >= LATE) & (step < LAST))
    def _():
        p = step - LATE
        lanes = pl.ds(pl.multiple_of(p * LANES, LANES), LANES)
        for hop in range(1, ny):
            pool_y(p, hop).wait_recv()

        @pl.when(here < seq - 1)
        def _():
            halo(p, 0).wait_recv()
            for which in range(2):
                r.acc[which, p, count - HALF :, :] += r.h_in[p, 0, which].astype(F32)

        @pl.when(here > 0)
        def _():
            halo(p, 1).wait_recv()
            for which in range(2):
                r.acc[which, p, 0:HALF, :] += r.h_in[p, 1, which].astype(F32)

        moves = ((2, 0, 0), (3, 1, 0), (4, 2, 0), (0, 2, 1), (1, 3, 1))
        sums = [jnp.zeros((1, LANES), F32)] * 5
        for which, source in ((0, r.keys), (1, r.values)):
            grad = r.acc.at[which, p]
            r.cells[...] = source[...].astype(F32)
            total = r.p_keep[p, 0, which].astype(F32) + r.p_in[p, 0, which].astype(F32)
            for hop in range(1, ny):
                total = total + r.p_y[p, hop - 1, which].astype(F32)
            r.g[...] = total
            for tap, place, shift in moves:
                mask = r.masks[shift, :, tap : tap + 1]
                spread = r.g[shift : shift + size, :] * mask * r.taps[tap : tap + 1, :]
                grad[pl.ds(place, size, stride=4), :] += spread
            for tap in range(5):
                taken = r.cells[pl.ds(HALF + tap - 2, size, stride=4), :]
                product = r.g[0:size, :] * r.masks[0, :, tap : tap + 1] * taken
                sums[tap] = sums[tap] + jnp.sum(product, axis=0, keepdims=True)
            r.tbuf[1 + which, :, lanes] = grad[...].astype(BF16)
        for tap in range(5):
            r.small[8 + tap : 9 + tap, lanes] = sums[tap]

    @pl.when(step == LAST)
    def _():
        for name, place, low in (("k", 2, 1), ("v", 3, 2)):
            sums["in%d" % place].sent_core(0)
            for block in range(ny):
                rows = rows_of(block, 1 - core)
                store_chunks(r.a_send.at[place, block], nn(r.lt[rows, :], r.tbuf[low]))
            sums[name].start(0)
            keep = sums[name].keep
            for block in range(ny):
                store_chunks(keep.at[0, block], nn(r.lt[rows_of(block, core), :], r.tbuf[low]))
        r.small_t[...] = r.small[...].T
        few = D // (seq * nz * nx)
        for block in range(ny):
            for part, mine in ((r.s_send.at[block], 1 - core), (sums["small"].keep.at[0, block], core)):
                vectors = r.small_t[rows_of(block, mine), :]
                for z in range(nz):
                    for x in range(nx):
                        start = (z * nx + x) * few
                        part[z, x] = jnp.zeros(part.shape[2:], BF16)
                        part[z, x, 0:few] = vectors[start : start + few].astype(BF16)
        sums["small"].start(0)

    results = {"out": r.t_out, "q": r.t_query, "k": r.t_key, "v": r.t_value, "small": r.t_small}
    for f in range(CHUNKS):
        results["in%d" % f] = r.t_in.at[f]
    for u in range(units_back):
        results["b%d" % u] = r.t_back.at[u]

    def run(name, stage):
        if name == "query":
            query_gradient()
        elif name == "tokens":
            tokens_gradient()
        elif name in sums:
            done = getattr(sums[name], ("core", "one", "two", "three")[stage])(0)
            if stage == 3:
                results[name][...] = done

    for when, todo in PLAN.items():

        @pl.when(step == when)
        def _(todo=todo):
            for name, stage in todo:
                run(name, stage)

    @pl.when(step == LAST)
    def _():
        reused = ["in%d" % f for f in range(CHUNKS)]
        for name in sums:
            if name not in reused:
                sums[name].sent_core(0)
            sums[name].sent(0)
        for p in range(PAIRS):
            pool_core(p).wait_send()
            for hop in range(1, ny):
                pool_y(p, hop).wait_send()

        @pl.when(here > 0)
        def _():
            for p in range(PAIRS):
                halo(p, 0).wait_send()

        @pl.when(here < seq - 1)
        def _():
            for p in range(PAIRS):
                halo(p, 1).wait_send()


def unpack_kernel(t_in, t_back, t_query, t_key, t_value, t_out, t_small, tg, *outs):
    tokens_grad, query, key, value, out, inn, back = outs[:7]
    rows = query.shape[0]
    tokens_grad[...] = tg[...]
    for source, target in ((t_query, query), (t_key, key), (t_value, value), (t_out, out)):
        target[...] = unfold_rows(source[...], rows)
    for u in range(CHUNKS):
        inn[:, u * D : (u + 1) * D] = unfold_rows(t_in[u], rows)
    units, part, wide = t_back.shape
    across = back.shape[1] // wide
    for u in range(units):
        top, start = (u // across) * part, (u % across) * wide
        back[top : top + part, start : start + wide] = t_back[u]
    small = t_small[...]
    pad = LANES - small.shape[0]
    turned = jnp.concatenate([small, jnp.zeros((pad, LANES), F32)], axis=0).T
    for i in range(4):
        outs[7 + i][...] = turned[i : i + 1, 0:rows]
    outs[11][...] = small[0:rows, 8:13]


def shifted(block, by):
    size = lax.axis_size("seq")
    return lax.ppermute(block, "seq", [(i, i + by) for i in range(size) if 0 <= i + by < size])


def call(kernel, info, args, in_specs, outs, out_specs, grid, scratch, flops, name):
    moved = sum(a.size * a.dtype.itemsize for a in list(args) + list(outs))
    return pl.pallas_call(
        kernel,
        grid_spec=pltpu.PrefetchScalarGridSpec(
            num_scalar_prefetch=1,
            grid=grid,
            in_specs=in_specs,
            out_specs=out_specs,
            scratch_shapes=scratch,
        ),
        out_shape=outs,
        compiler_params=pltpu.CompilerParams(
            vmem_limit_bytes=60 * MB, dimension_semantics=("arbitrary",) * len(grid)
        ),
        cost_estimate=pl.CostEstimate(flops=flops, bytes_accessed=moved, transcendentals=0),
        name=name,
    )(info, *args)


def whole(array):
    rank = len(array.shape)
    return pl.BlockSpec(array.shape, lambda i, info: (0,) * rank)


def columns(array, width=LANES):
    rank = len(array.shape)
    return pl.BlockSpec(array.shape[:-1] + (width,), lambda i, info: (0,) * (rank - 1) + (i,))


def leading(array, size):
    rank = len(array.shape)
    return pl.BlockSpec((size,) + array.shape[1:], lambda i, info: (i,) + (0,) * (rank - 1))


def per_device(
    tokens,
    item_lengths,
    w_query,
    w_key,
    w_value,
    w_out,
    w_in,
    w_back,
    norm1_gain,
    norm1_bias,
    norm2_gain,
    norm2_bias,
    pool_weight,
    out_grad,
):
    _, count, _ = tokens.shape
    seq = lax.axis_size("seq")
    ny = seq // 2
    row_len = count * seq
    span = count + 2 * HALF
    size = count // 4
    here = lax.axis_index("seq")
    core, y = here % 2, here // 2
    owners = []
    for other in range(2):
        for hop in range(ny):
            owners.append(((y + hop) % ny) * 2 + jnp.bitwise_xor(core, other))
    afters = []
    for owner in owners:
        after = jnp.minimum(owner + 1, seq - 1)
        afters.append(jnp.bitwise_xor(after % 2, core) * ny + (after // 2 - y) % ny)
    zero = jnp.zeros((), jnp.int32)
    info = jnp.concatenate(
        [
            jnp.cumsum(item_lengths[0]).astype(jnp.int32),
            jnp.stack([here * count, core, y, zero] + owners + afters).astype(jnp.int32),
        ]
    )
    tok = tokens[0]
    og = out_grad[0]
    left = shifted(tok[count - HALF :], 1)
    right = shifted(tok[:HALF], -1)
    taps = jnp.pad(pool_weight.T, ((0, 3), (0, 0)))
    vecs = jnp.concatenate(
        [jnp.stack([norm1_gain, norm1_bias, norm2_gain, norm2_bias]), jnp.zeros((4, D), F32)]
    )

    def shape(dims, kind):
        return jax.ShapeDtypeStruct(dims, kind)

    args = (tok, left, right, w_query, w_key, w_value, taps)
    outs = (
        shape((count, D), BF16),
        shape((span, D), BF16),
        shape((span, D), BF16),
        shape((2, size, D), BF16),
        shape((D, count), BF16),
        shape((2, size, LANES), F32),
    )
    queries, keys, values, pool_own, tok_t, tap_masks = call(
        partial(project_kernel, row_len=row_len),
        info,
        args,
        [whole(a) for a in args],
        outs,
        [whole(a) for a in outs],
        (1,),
        [
            pltpu.VMEM((span, D), BF16),
            pltpu.VMEM((D // LANES, span, LANES), F32),
        ],
        2 * D * D * (count + 2 * span),
        "project",
    )

    pieces = [pool_own]
    for hop in range(1, ny):
        pieces.append(lax.ppermute(pool_own, "seq", hop_pairs("seq", ny, 2, ny - hop)))
    pieces = pieces + [lax.ppermute(piece, "seq", hop_pairs("seq", 2, 1, 1)) for piece in pieces]

    blocks = count // QB
    args = (queries, keys, values)
    outs = (
        shape((H, blocks, 2 * QB, QB), BF16),
        shape((D, count), F32),
        shape((PAIRS, 8, count), F32),
    )
    near_e, o_near, stats = call(
        partial(near_forward_kernel, row_len=row_len),
        info,
        args,
        [columns(a) for a in args],
        outs,
        [leading(outs[0], 2), leading(outs[1], LANES), leading(outs[2], 1)],
        (PAIRS,),
        [pltpu.VMEM((blocks, 2 * QB, QB), F32)],
        4 * H * 256 * 256 * count,
        "near_forward",
    )

    pool_all = seq * size
    args = (queries, o_near, stats) + tuple(pieces)
    outs = (
        shape((H, pool_all, count), BF16),
        shape((count, D), F32),
        shape((count, D), F32),
        shape((count, D), F32),
    )
    pool_e, attention, near_scale, pool_scale = call(
        partial(pool_forward_kernel, row_len=row_len, pieces=seq),
        info,
        args,
        [columns(queries), leading(o_near, LANES), leading(stats, 1)] + [columns(p) for p in pieces],
        outs,
        [leading(outs[0], 2)] + [columns(a) for a in outs[1:]],
        (PAIRS,),
        [pltpu.VMEM((pool_all, count), F32)],
        4 * H * 512 * 256 * count,
        "pool_forward",
    )

    dp = lax.axis_size("dp")
    nx = 2 if dp % 2 == 0 else 1
    nz = dp // nx
    rows = D // (seq * dp)
    back_rows = FF // (seq * dp)
    down = 2 if back_rows % 32 == 0 else 1
    half_one = shape((ny, nz, nx) + folded(rows, D), BF16)
    half_back = shape((2 * down, ny, nz, nx, back_rows // down, D // 2), BF16)
    args = (attention, tok, og, vecs, w_out, w_in, w_back)
    outs = (
        shape((count, D), BF16),
        shape((count, FF), BF16),
        shape((count, FF), BF16),
        shape((D, count), BF16),
        shape((count, D), BF16),
        shape((count, D), F32),
        shape((PAIRS, count, LANES), F32),
        shape((count, LANES), F32),
        shape((D, count), BF16),
        shape((8, D), F32),
    )
    mixed, act, slope, low_t, feed_grad, z_grad, unit_one, inv_one, att_t, sums = call(
        dense_kernel,
        info,
        args,
        [whole(a) for a in args[:5]]
        + [columns(w_in, D), pl.BlockSpec((D, D), lambda i, info: (i, 0))],
        outs,
        [whole(outs[0]), columns(outs[1], D), columns(outs[2], D)] + [whole(a) for a in outs[3:]],
        (CHUNKS,),
        [
            pltpu.VMEM((count, D), F32),
            pltpu.VMEM((count, D), BF16),
            pltpu.VMEM((count, D), F32),
        ],
        2 * count * (D * D + 2 * D * FF),
        "dense",
    )
    half_small = shape((ny, nz, nx, -(-rows // 16) * 16, LANES), BF16)
    half_pool = (PAIRS, ny, 2, size + EXTRA, LANES)
    blocks_in = []

    def block(name, array, spec):
        blocks_in.append((name, array, spec))

    def col_spec(array, index):
        lead = (0,) * (len(array.shape) - 1)
        return pl.BlockSpec(array.shape[:-1] + (LANES,), lambda i: lead + (index(i),))

    def lead_spec(array, index):
        rest = (0,) * (len(array.shape) - 1)
        return pl.BlockSpec((2,) + array.shape[1:], lambda i: (index(i),) + rest)

    def all_spec(array):
        rest = (0,) * len(array.shape)
        return pl.BlockSpec(array.shape, lambda i: rest)

    def in_pool(i):
        return jnp.clip(i - POOL, 0, PAIRS - 1)

    def in_near(i):
        return jnp.clip(i - NEAR, 0, PAIRS - 1)

    def in_both(i):
        return jnp.clip(i - POOL, 0, 2 * PAIRS - 1) % PAIRS

    def in_late(i):
        return jnp.clip(i - NEAR, 0, 2 * PAIRS - 1) % PAIRS

    block("q", queries, col_spec(queries, in_both))
    block("o", attention, col_spec(attention, in_both))
    block("rp", pool_scale, col_spec(pool_scale, in_pool))
    block("rn", near_scale, col_spec(near_scale, in_near))
    block("pool_e", pool_e, lead_spec(pool_e, in_pool))
    block("near_e", near_e, lead_spec(near_e, in_near))
    block("keys", keys, col_spec(keys, in_late))
    block("values", values, col_spec(values, in_late))
    for i, piece in enumerate(pieces):
        block("piece%d" % i, piece, col_spec(piece, in_pool))
    block("masks", tap_masks, all_spec(tap_masks))
    block("taps", taps, col_spec(taps, in_late))
    block("sums", sums, all_spec(sums))
    block("vecs", vecs, all_spec(vecs))
    block("inv", inv_one, all_spec(inv_one))
    anywhere = pl.BlockSpec(memory_space=pl.ANY)
    for name, array in (
        ("win_any", w_in),
        ("wback_any", w_back),
        ("act_any", act),
        ("slope_any", slope),
        ("fg_any", feed_grad),
        ("lowt_any", low_t),
        ("zg_any", z_grad),
        ("unit_any", unit_one),
        ("wout_any", w_out),
        ("att_any", att_t),
        ("tt_any", tok_t),
        ("wq_any", w_query),
        ("wk_any", w_key),
        ("wv_any", w_value),
    ):
        block(name, array, anywhere)
    outs = [
        ("t_in", shape((CHUNKS,) + half_one.shape[3:], F32)),
        ("t_back", shape((half_back.shape[0],) + half_back.shape[4:], F32)),
        ("t_query", shape(half_one.shape[3:], F32)),
        ("t_key", shape(half_one.shape[3:], F32)),
        ("t_value", shape(half_one.shape[3:], F32)),
        ("t_out", shape(half_one.shape[3:], F32)),
        ("t_small", shape(half_small.shape[3:], F32)),
        ("tokens_grad", shape((count, D), BF16)),
    ]
    tall = max(pool_all, span)
    scratch = [
        ("dk", pltpu.VMEM((tall, LANES), F32)),
        ("dv", pltpu.VMEM((tall, LANES), F32)),
        ("dq_pool", pltpu.VMEM((PAIRS, LANES, count), F32)),
        ("gb", pltpu.VMEM((count, LANES), BF16)),
        ("acc", pltpu.VMEM((2, PAIRS, count, LANES), F32)),
        ("tbuf", pltpu.VMEM((4, count, D), BF16)),
        ("wbuf", pltpu.VMEM((4, D, D), BF16)),
        ("fg", pltpu.VMEM((count, D), BF16)),
        ("lt", pltpu.VMEM((D, count), BF16)),
        ("att", pltpu.VMEM((D, count), BF16)),
        ("cells", pltpu.VMEM((span, LANES), F32)),
        ("g", pltpu.VMEM((size + EXTRA, LANES), F32)),
        ("small", pltpu.VMEM((LANES, D), F32)),
        ("small_t", pltpu.VMEM((D, LANES), F32)),
        ("p_keep", pltpu.VMEM(half_pool, BF16)),
        ("p_send", pltpu.VMEM(half_pool, BF16)),
        ("p_in", pltpu.VMEM(half_pool, BF16)),
        ("p_y", pltpu.VMEM((PAIRS, ny - 1) + half_pool[2:], BF16)),
        ("h_out", pltpu.VMEM((PAIRS, 2, 2, HALF, LANES), BF16)),
        ("h_in", pltpu.VMEM((PAIRS, 2, 2, HALF, LANES), BF16)),
        ("p_sem", pltpu.SemaphoreType.DMA((2, PAIRS, ny))),
        ("h_sem", pltpu.SemaphoreType.DMA((2, PAIRS, 2))),
        ("l_sem", pltpu.SemaphoreType.DMA((9, 2))),
        ("sg", pltpu.VMEM((count, D), F32)),
        ("a_send", pltpu.VMEM((CHUNKS,) + half_one.shape, BF16)),
        ("b_send", pltpu.VMEM(half_back.shape, BF16)),
        ("s_send", pltpu.VMEM(half_small.shape, BF16)),
    ]
    sizes = {name: half_one.shape for name in ORDERS}
    sizes["small"] = half_small.shape
    for u in range(CHUNKS):
        if u < half_back.shape[0]:
            sizes["b%d" % u] = half_back.shape[1:]
        else:
            del sizes["b%d" % u]
    for name, dims in sizes.items():
        bufs = summed_scratch(1, dims, ORDERS[name])
        scratch += [(name + "_" + part, buf) for part, buf in zip(BUFFERS, bufs)]
    names = [entry[0] for entry in blocks_in] + [entry[0] for entry in outs + scratch]
    moved = sum(entry[1].size * entry[1].dtype.itemsize for entry in blocks_in)
    totals = pl.pallas_call(
        partial(backward_kernel, names=names, pieces=seq),
        grid_spec=pltpu.PrefetchScalarGridSpec(
            num_scalar_prefetch=0,
            grid=(LAST + 1,),
            in_specs=[entry[2] for entry in blocks_in],
            out_specs=[all_spec(entry[1]) for entry in outs],
            scratch_shapes=[entry[1] for entry in scratch],
        ),
        out_shape=[entry[1] for entry in outs],
        compiler_params=pltpu.CompilerParams(
            collective_id=0,
            has_side_effects=True,
            vmem_limit_bytes=63 * MB,
            dimension_semantics=("arbitrary",),
        ),
        cost_estimate=pl.CostEstimate(
            flops=8 * H * 768 * 256 * count + 12 * count * D * D + 8 * count * D * FF, bytes_accessed=moved, transcendentals=0
        ),
        name="backward",
    )(*[entry[1] for entry in blocks_in])

    outs = (
        shape((count, D), BF16),
        shape((rows, D), F32),
        shape((rows, D), F32),
        shape((rows, D), F32),
        shape((rows, D), F32),
        shape((rows, FF), F32),
        shape((back_rows, D), F32),
        shape((1, rows), F32),
        shape((1, rows), F32),
        shape((1, rows), F32),
        shape((1, rows), F32),
        shape((rows, 5), F32),
    )
    done = call(
        lambda info, *refs: unpack_kernel(*refs),
        info,
        tuple(totals),
        [whole(a) for a in totals],
        outs,
        [whole(a) for a in outs],
        (1,),
        [],
        0,
        "unpack",
    )
    return (
        mixed[None],
        done[0][None],
        done[1],
        done[2],
        done[3],
        done[4],
        done[5],
        done[6],
        done[7].reshape(rows),
        done[8].reshape(rows),
        done[9].reshape(rows),
        done[10].reshape(rows),
        done[11],
    )


def solution(mesh):
    shards, copied = P("dp", "seq", None), P()
    spread = P(("seq", "dp"), None)
    vector = P(("seq", "dp"))
    return jax.shard_map(
        per_device,
        mesh=mesh,
        in_specs=(shards, P("dp", None)) + (copied,) * 11 + (shards,),
        out_specs=(shards, shards) + (spread,) * 6 + (vector,) * 4 + (spread,),
        check_vma=False,
    )
```

```python
import itertools
from functools import partial

import jax
import jax.numpy as jnp
from jax import lax
from jax.experimental import pallas as pl
from jax.experimental.pallas import tpu as pltpu
from jax.sharding import PartitionSpec as P

D = 768
FF = 3072
H = 12
PAIRS = H // 2
HALF = 64
PWIN = 512
QB = 128
EXTRA = 16
LANES = 128
BF16 = jnp.bfloat16
F32 = jnp.float32
MB = 1 << 20


def nn(left, right):
    return jnp.dot(left, right, preferred_element_type=F32)


def nt(left, right, precision=None):
    return lax.dot_general(
        left, right, (((1,), (1,)), ((), ())), preferred_element_type=F32, precision=precision
    )


def iota(shape, dim):
    return lax.broadcasted_iota(jnp.int32, shape, dim)


def segment_of(ends, place, row_len):
    item = jnp.zeros_like(place)
    for end in ends:
        item = item + (place >= end).astype(jnp.int32)
    return jnp.where((place >= 0) & (place < row_len), item, -2)


def head_half(block, head):
    lane = iota(block.shape, 1)
    return jnp.where((lane < 64) == (head == 0), block, jnp.zeros_like(block))


def tap_mask(ends, start, tap, shift, count, row_len):
    center = start + 4 * (iota((count, 1), 0) + shift)
    same = segment_of(ends, center + tap - 2, row_len) == segment_of(ends, center, row_len)
    return (same & (center < row_len)).astype(F32)


def folds(rows, width):
    return 2 if rows % 16 and rows % 8 == 0 and (width // 2) % LANES == 0 else 1


def folded(rows, width):
    fold = folds(rows, width)
    return (rows * fold, width // fold)


def fold_rows(block):
    rows, width = block.shape
    fold = folds(rows, width)
    part = width // fold
    return jnp.concatenate([block[:, i * part : (i + 1) * part] for i in range(fold)], axis=0)


def unfold_rows(block, rows):
    fold = block.shape[0] // rows
    return jnp.concatenate([block[i * rows : (i + 1) * rows] for i in range(fold)], axis=1)


def store_chunks(target, total):
    nz, nx = target.shape[0], target.shape[1]
    rows = total.shape[0] // (nz * nx)
    for z in range(nz):
        for x in range(nx):
            start = (z * nx + x) * rows
            target[z, x] = fold_rows(total[start : start + rows]).astype(BF16)


def store_blocks(targets, block, total):
    _, nz, nx, part, wide = targets[0].shape
    rows = total.shape[0] // (nz * nx)
    across = total.shape[1] // wide
    for z in range(nz):
        for x in range(nx):
            start = (z * nx + x) * rows
            for unit, target in enumerate(targets):
                top = start + (unit // across) * part
                left = (unit % across) * wide
                target[block, z, x] = total[top : top + part, left : left + wide].astype(BF16)


def normal_parts(v):
    bell = jnp.exp(v * v * -0.5)
    t = 1.0 / (1.0 + jnp.abs(v) * (0.3275911 * 0.7071067811865476))
    poly = t * (
        0.127414796 + t * (-0.142248368 + t * (0.7107068705 + t * (-0.7265760135 + t * 0.5307027145)))
    )
    tail = poly * bell
    return jnp.where(v < 0, tail, 1.0 - tail), v * bell * 0.3989422804014327


def normalized(values):
    shifted = values - jnp.mean(values, axis=1, keepdims=True)
    inverse = lax.rsqrt(jnp.mean(shifted * shifted, axis=1, keepdims=True) + 1e-05)
    return shifted * inverse, inverse


def dense_kernel(
    o, tok, og, vecs, w_out, w_in, w_back,
    mixed, act, slope, low_t, feed_grad, z_grad, unit_out, inv_out, att_t, sums,
    first, low, feed,
):
    step = pl.program_id(0)
    gain_one, bias_one = vecs[0:1, :], vecs[1:2, :]
    gain_two, bias_two = vecs[2:3, :], vecs[3:4, :]

    @pl.when(step == 0)
    def _():
        att = o[...].astype(BF16)
        att_t[...] = att.T
        unit, inverse = normalized(tok[...].astype(F32) + nn(att, w_out[...]))
        for c in range(PAIRS):
            unit_out[c] = unit[:, c * LANES : (c + 1) * LANES]
        inv_out[...] = jnp.broadcast_to(inverse, inv_out.shape)
        first[...] = unit * gain_one + bias_one
        low[...] = first[...].astype(BF16)
        low_t[...] = low[...].T
        feed[...] = jnp.zeros_like(feed)

    inner = nn(low[...], w_in[...])
    phi, bell = normal_parts(inner)
    act[...] = (inner * phi).astype(BF16)
    slope[...] = (phi + bell).astype(BF16)
    feed[...] += nn(act[...], w_back[...])

    @pl.when(step == CHUNKS - 1)
    def _():
        unit, inverse = normalized(first[...] + feed[...])
        mixed[...] = (unit * gain_two + bias_two).astype(BF16)
        upstream = og[...].astype(F32)
        sums[...] = jnp.zeros_like(sums)
        sums[2:3] = jnp.sum(upstream * unit, axis=0, keepdims=True)
        sums[3:4] = jnp.sum(upstream, axis=0, keepdims=True)
        e = upstream * gain_two
        centred = e - jnp.mean(e, axis=1, keepdims=True)
        total = inverse * (centred - unit * jnp.mean(e * unit, axis=1, keepdims=True))
        z_grad[...] = total
        feed_grad[...] = total.astype(BF16)


def score_delta(grad, attended):
    pick = ((iota((8, LANES), 1) // 64) == iota((8, LANES), 0)).astype(F32)
    return nt(pick, grad.astype(F32) * attended, precision=lax.Precision.HIGHEST)


def hop_pairs(axis, count, stride, hop):
    pairs = []
    for device in range(lax.axis_size(axis)):
        place = (device // stride) % count
        pairs.append((device, device + ((place + hop) % count - place) * stride))
    return pairs


MESH_ID = pl.DeviceIdType.MESH


class Summed:
    def __init__(self, order, send_of, keep, core_in, first, second, third, out_sem, in_sem):
        self.order, self.send_of = order, send_of
        self.keep, self.core_in = keep, core_in
        self.bufs = (first, second, third)
        self.out_sem, self.in_sem = out_sem, in_sem
        self.units = keep.shape[0]
        self.count = dict(zip("yzx", keep.shape[1:4]))
        self.here, self.row = lax.axis_index("seq"), lax.axis_index("dp")
        self.mine = self.here % 2
        nx = self.count["x"]
        self.own = {"y": self.here // 2, "z": self.row // nx, "x": self.row % nx}
        self.base = {"y": 1}
        self.base["x"] = self.base["y"] + self.count["y"] - 1
        self.base["z"] = self.base["x"] + nx - 1

    def copy(self, u, src, dst, slot, device):
        return pltpu.make_async_remote_copy(
            src_ref=src,
            dst_ref=dst,
            send_sem=self.out_sem.at[u, slot],
            recv_sem=self.in_sem.at[u, slot],
            device_id=device,
            device_id_type=MESH_ID,
        )

    def core_copy(self, u):
        partner = (self.own["y"] * 2 + 1 - self.mine, self.row)
        return self.copy(u, self.send_of(u), self.core_in.at[u], 0, partner)

    def hop_copy(self, u, stage, hop):
        axis = self.order[stage]
        other = (self.own[axis] + hop) % self.count[axis]
        place = dict(self.own)
        place[axis] = other
        device = (place["y"] * 2 + self.mine, place["z"] * self.count["x"] + place["x"])
        index = []
        for dim in "yzx":
            known = dim in self.order[: stage + 1]
            index.append(place[dim] if known else slice(None))
        source = self.keep.at[(u,) + tuple(index)]
        slot = self.base[axis] + hop - 1
        return self.copy(u, source, self.bufs[stage].at[u, hop - 1], slot, device)

    def hops(self, stage):
        return range(1, self.count[self.order[stage]])

    def start(self, u):
        self.core_copy(u).start()

    def core(self, u):
        self.core_copy(u).wait_recv()
        for y in range(self.count["y"]):
            for z in range(self.count["z"]):
                self.keep[u, y, z] = self.keep[u, y, z] + self.core_in[u, y, z]
        for hop in self.hops(0):
            self.hop_copy(u, 0, hop).start()

    def add(self, u, stage):
        left = [dim for dim in "yzx" if dim not in self.order[: stage + 1]]
        for hop in self.hops(stage):
            self.hop_copy(u, stage, hop).wait_recv()
            for place in itertools.product(*[range(self.count[dim]) for dim in left]):
                at = dict(self.own)
                at.update(zip(left, place))
                index = (u,) + tuple(at[dim] for dim in "yzx")
                self.keep[index] = self.keep[index] + self.bufs[stage][(u, hop - 1) + place]
        for hop in self.hops(stage + 1):
            self.hop_copy(u, stage + 1, hop).start()

    def one(self, u):
        self.add(u, 0)

    def two(self, u):
        self.add(u, 1)

    def three(self, u):
        total = self.keep[(u,) + tuple(self.own[dim] for dim in "yzx")].astype(F32)
        for hop in self.hops(2):
            self.hop_copy(u, 2, hop).wait_recv()
            total = total + self.bufs[2][u, hop - 1].astype(F32)
        return total

    def sent_core(self, u):
        self.core_copy(u).wait_send()

    def sent(self, u):
        for stage in range(3):
            for hop in self.hops(stage):
                self.hop_copy(u, stage, hop).wait_send()


def summed_scratch(units, shape, order):
    count = dict(zip("yzx", shape[:3]))
    chunk = shape[3:]
    bufs = [pltpu.VMEM((units,) + shape, BF16), pltpu.VMEM((units,) + shape, BF16)]
    for stage in range(3):
        left = tuple(count[dim] for dim in "yzx" if dim not in order[: stage + 1])
        bufs.append(pltpu.VMEM((units, max(count[order[stage]] - 1, 1)) + left + chunk, BF16))
    slots = count["y"] + count["x"] + count["z"] - 2
    bufs += [pltpu.SemaphoreType.DMA((units, slots)), pltpu.SemaphoreType.DMA((units, slots))]
    return bufs


def greet(peers):
    barrier = pltpu.get_barrier_semaphore()
    for peer in peers:
        pl.semaphore_signal(barrier, inc=1, device_id=peer, device_id_type=MESH_ID)
    pl.semaphore_wait(barrier, len(peers))


class Refs:
    pass


FORWARD_NEAR = 1
FORWARD_POOL = 1 + PAIRS
FORWARD_LAST = 2 * PAIRS


def forward_kernel(*refs, names):
    r = Refs()
    for name, ref in zip(names, refs):
        setattr(r, name, ref)
    seq, _, size, _ = r.pieces.shape
    ny = seq // 2
    count, row_len = 4 * size, 4 * size * seq
    span = count + 2 * HALF
    step = pl.program_id(0)
    here, row = lax.axis_index("seq"), lax.axis_index("dp")
    y, core = here // 2, here % 2
    start = here * count
    partner = (y * 2 + 1 - core, row)
    right, left = ((here + 1) % seq, row), ((here + seq - 1) % seq, row)
    ends = [r.lengths[0, 0]]
    for m in range(1, 4):
        ends.append(ends[-1] + r.lengths[0, m])

    def copy(src, dst, slot, device):
        return pltpu.make_async_remote_copy(
            src_ref=src, dst_ref=dst, send_sem=r.s_sem.at[slot], recv_sem=r.r_sem.at[slot],
            device_id=device, device_id_type=MESH_ID,
        )

    own = r.x.at[HALF : HALF + count]
    to_right = copy(r.tok.at[count - HALF :], r.x.at[0:HALF], 0, right)
    to_left = copy(r.tok.at[0:HALF], r.x.at[HALF + count :], 1, left)

    def to_y(hop):
        device = (((y + hop) % ny) * 2 + core, row)
        return copy(r.pieces.at[0], r.pieces.at[ny - hop], 1 + hop, device)

    def to_core(hop):
        return copy(r.pieces.at[hop], r.pieces.at[ny + hop], 1 + ny + hop, partner)

    loads = [
        pltpu.make_async_copy(r.tok, own, r.l_sem.at[0]),
        pltpu.make_async_copy(r.wk_any, r.wk, r.l_sem.at[1]),
        pltpu.make_async_copy(r.wv_any, r.wv, r.l_sem.at[2]),
        pltpu.make_async_copy(r.wq_any, r.wq, r.l_sem.at[3]),
    ]
    stores = [
        pltpu.make_async_copy(r.qs, r.q_out, r.l_sem.at[4]),
        pltpu.make_async_copy(r.ks, r.k_out, r.l_sem.at[5]),
        pltpu.make_async_copy(r.vs, r.v_out, r.l_sem.at[6]),
        pltpu.make_async_copy(r.tt, r.tt_out, r.l_sem.at[7]),
        pltpu.make_async_copy(r.mask, r.mask_out, r.l_sem.at[8]),
        pltpu.make_async_copy(r.tap, r.tap_out, r.l_sem.at[9]),
    ]
    store_pieces = pltpu.make_async_copy(r.pieces, r.pieces_out, r.l_sem.at[10])

    @pl.when(step == 0)
    def _():
        for load in loads:
            load.start()
        greet([partner, right, left] + [(((y + hop) % ny) * 2 + core, row) for hop in range(1, ny)])

        @pl.when(here < seq - 1)
        def _():
            to_right.start()

        @pl.when(here > 0)
        def _():
            to_left.start()

        @pl.when(here == 0)
        def _():
            r.x[0:HALF] = jnp.zeros((HALF, D), BF16)

        @pl.when(here == seq - 1)
        def _():
            r.x[HALF + count :] = jnp.zeros((HALF, D), BF16)

        pick = (iota((8, 5), 0) == iota((8, 5), 1)).astype(F32)
        r.tap[...] = nt(pick, r.pool_weight[...], precision=lax.Precision.HIGHEST)
        lane = iota((size, LANES), 1)
        masks = [[tap_mask(ends, start, tap, shift, size, row_len) for tap in range(5)] for shift in range(2)]
        for shift in range(2):
            total = jnp.zeros((size, LANES), F32)
            for tap in range(5):
                total = jnp.where(lane == tap, masks[shift][tap], total)
            r.mask[shift] = total
        loads[0].wait()
        inner = slice(HALF, HALF + count)
        for weight, load, cells in ((r.wk, loads[1], r.ks), (r.wv, loads[2], r.vs)):
            load.wait()
            cells[inner] = nn(r.x[inner], weight[...]).astype(BF16)

        @pl.when(here > 0)
        def _():
            to_right.wait_recv()

        @pl.when(here < seq - 1)
        def _():
            to_left.wait_recv()

        for weight, cells in ((r.wk, r.ks), (r.wv, r.vs)):
            for outer in (slice(0, HALF), slice(HALF + count, span)):
                cells[outer] = nn(r.x[outer], weight[...]).astype(BF16)
        for which, source in ((0, r.ks), (1, r.vs)):
            for c in range(PAIRS):
                lanes = slice(c * LANES, (c + 1) * LANES)
                r.cells[c] = source[:, lanes].astype(F32)
                total = jnp.zeros((size, LANES), F32)
                for tap in range(5):
                    taken = r.cells.at[c][pl.ds(HALF + tap - 2, size, stride=4), :]
                    total = total + taken * masks[0][tap] * r.tap[tap : tap + 1, lanes]
                r.pieces[0, which, :, lanes] = total.astype(BF16)
        for hop in range(1, ny):
            to_y(hop).start()
        to_core(0).start()
        loads[3].wait()
        r.qs[...] = (nn(r.x[inner], r.wq[...]).astype(BF16).astype(F32) * 0.125).astype(BF16)
        r.tt[...] = r.x[inner].T
        for store in stores:
            store.start()
        for b in range(count // QB):
            query_place = start + b * QB + iota((1, QB), 1)
            key_place = start - HALF + b * QB + iota((2 * QB, 1), 0)
            same = segment_of(ends, key_place, row_len) == segment_of(ends, query_place, row_len)
            near = jnp.abs(key_place - query_place) <= HALF
            r.near_bias[b] = jnp.where(same & near, 0.0, -1e30)

    @pl.when((step >= FORWARD_NEAR) & (step < FORWARD_POOL))
    def _():
        p = step - FORWARD_NEAR
        lanes = pl.ds(pl.multiple_of(p * LANES, LANES), LANES)
        vt = r.vs[:, lanes].T
        ones = jnp.ones((16, span), BF16)
        for head in range(2):
            qh = head_half(r.qs[:, lanes], head)
            va = jnp.concatenate([vt[head * 64 : head * 64 + 64], ones], axis=0)
            for b in range(count // QB):
                cols = slice(b * QB, (b + 1) * QB)
                keys = slice(b * QB, (b + 2) * QB)
                s = nt(r.ks[keys, lanes], qh[cols]) + r.near_bias[b]
                top = jnp.max(s, axis=0, keepdims=True)
                e = jnp.exp(s - top).astype(BF16)
                r.near_e[head, b] = e
                oa = nn(va[:, keys], e)
                r.o_near[p, head * 64 : head * 64 + 64, cols] = oa[:64]
                r.stats[p, head : head + 1, cols] = top
                r.stats[p, 2 + head : 3 + head, cols] = oa[64:65]

    @pl.when(step == FORWARD_POOL - 2)
    def _():
        query_place = start + iota((1, count), 1)
        query_item = segment_of(ends, query_place, row_len)
        for i in range(seq):
            owner = ((y + i % ny) % ny) * 2 + (core + i // ny) % 2
            key_place = 4 * (owner * size + iota((size, 1), 0))
            same = segment_of(ends, key_place, row_len) == query_item
            near = jnp.abs(key_place - query_place) <= 2 * PWIN
            r.pool_bias[i * size : (i + 1) * size] = jnp.where(same & near, 0.0, -1e30)

    @pl.when(step == FORWARD_POOL - 1)
    def _():
        for hop in range(1, ny):
            to_y(ny - hop).wait_recv()
            to_core(hop).start()

    @pl.when(step == FORWARD_POOL)
    def _():
        for hop in range(ny):
            to_core(hop).wait_recv()
        store_pieces.start()

    @pl.when(step >= FORWARD_POOL)
    def _():
        p = step - FORWARD_POOL
        lanes = pl.ds(pl.multiple_of(p * LANES, LANES), LANES)
        kp = jnp.concatenate([r.pieces[i, 0, :, lanes] for i in range(seq)], axis=0)
        vt = jnp.concatenate([r.pieces[i, 1, :, lanes] for i in range(seq)], axis=0).T
        ones = jnp.ones((16, seq * size), BF16)
        wide = min(256, count)
        for b in range(count // wide):
            cols = slice(b * wide, (b + 1) * wide)
            outs, near_scale, pool_scale = [], [], []
            for head in range(2):
                qh = head_half(r.qs[cols, lanes], head)
                va = jnp.concatenate([vt[head * 64 : head * 64 + 64], ones], axis=0)
                s = nt(kp, qh) + r.pool_bias[:, cols]
                near_top = r.stats[p, head : head + 1, cols]
                top = jnp.maximum(jnp.max(s, axis=0, keepdims=True), near_top)
                e = jnp.exp(s - top).astype(BF16)
                r.pool_e[head, :, cols] = e
                oa = nn(va, e)
                fade = jnp.exp(near_top - top)
                inverse = 1.0 / (fade * r.stats[p, 2 + head : 3 + head, cols] + oa[64:65])
                rows = slice(head * 64, head * 64 + 64)
                outs.append((fade * r.o_near[p, rows, cols] + oa[:64]) * inverse)
                near_scale.append(jnp.broadcast_to(fade * inverse, (64, wide)))
                pool_scale.append(jnp.broadcast_to(inverse, (64, wide)))
            r.o_out[cols, :] = jnp.concatenate(outs, axis=0).T
            r.rn_out[cols, :] = jnp.concatenate(near_scale, axis=0).T
            r.rp_out[cols, :] = jnp.concatenate(pool_scale, axis=0).T

    @pl.when(step == FORWARD_LAST)
    def _():
        for store in stores + [store_pieces]:
            store.wait()
        for hop in range(1, ny):
            to_y(hop).wait_send()
        for hop in range(ny):
            to_core(hop).wait_send()

        @pl.when(here < seq - 1)
        def _():
            to_right.wait_send()

        @pl.when(here > 0)
        def _():
            to_left.wait_send()


CHUNKS = FF // D
BUFFERS = ("sum", "core", "first", "second", "third", "out", "inn")
POOL = CHUNKS + 1
NEAR = POOL + PAIRS
LATE = NEAR + PAIRS
LAST = LATE + PAIRS
ORDERS = {
    "in0": "zxy",
    "in1": "xzy",
    "in2": "yzx",
    "in3": "yzx",
    "b0": "xzy",
    "b1": "xzy",
    "b2": "zxy",
    "b3": "xyz",
    "out": "yzx",
    "q": "xyz",
    "k": "xyz",
    "v": "yxz",
    "small": "yzx",
}
PLAN = {
    1: (
        ("in0", 0),
    ),
    3: (
        ("in1", 0),
    ),
    4: (
        ("b0", 0),
        ("in3", 0),
        ("b2", 0),
    ),
    8: (
        ("out", 0),
    ),
    9: (
        ("b1", 0),
    ),
    10: (
        ("in1", 1),
    ),
    11: (
        ("b0", 1),
    ),
    13: (
        ("b3", 0),
    ),
    14: (
        ("b1", 1),
    ),
    15: (
        ("in2", 0),
    ),
    17: (
        ("query", 0),
        ("in3", 1),
    ),
    19: (
        ("q", 0),
    ),
    20: (
        ("in2", 1),
        ("b3", 1),
    ),
    23: (
        ("in0", 1),
        ("b1", 2),
        ("q", 1),
        ("in3", 2),
        ("out", 1),
        ("k", 0),
        ("small", 0),
        ("v", 0),
        ("tokens", 0),
        ("b3", 2),
        ("small", 1),
        ("q", 2),
        ("k", 1),
        ("b2", 1),
        ("v", 1),
        ("small", 2),
        ("b0", 2),
        ("b2", 2),
        ("k", 2),
        ("q", 3),
        ("in0", 2),
        ("in3", 3),
        ("b1", 3),
        ("in2", 2),
        ("small", 3),
        ("out", 2),
        ("in1", 2),
        ("v", 2),
        ("out", 3),
        ("b3", 3),
        ("in0", 3),
        ("in1", 3),
        ("in2", 3),
        ("b0", 3),
        ("b2", 3),
        ("k", 3),
        ("v", 3),
    ),
}

def backward_kernel(*refs, names, pieces):
    r = Refs()
    for name, ref in zip(names, refs):
        setattr(r, name, ref)
    kv = [r.piece.at[i] for i in range(pieces)]
    seq, ny = pieces, pieces // 2
    step = pl.program_id(0)
    count = r.q.shape[0]
    size = count // 4
    nz, nx = r.b_send.shape[2:4]
    here, row = lax.axis_index("seq"), lax.axis_index("dp")
    y, core = here // 2, here % 2
    partner = (y * 2 + 1 - core, row)
    right, left = ((here + 1) % seq, row), ((here + seq - 1) % seq, row)
    units_back = r.b_send.shape[0]
    senders = {"small": r.s_send}
    for f in range(CHUNKS):
        senders["in%d" % f] = r.a_send.at[f]
    for place, name in enumerate(("out", "q", "k", "v")):
        senders[name] = r.a_send.at[place]
    for u in range(units_back):
        senders["b%d" % u] = r.b_send.at[u]
    sums = {}
    for name in senders:
        bufs = [getattr(r, name + "_" + part) for part in BUFFERS]
        sums[name] = Summed(ORDERS[name], lambda u, name=name: senders[name], *bufs)

    def copy(src, dst, out_sem, in_sem, device):
        return pltpu.make_async_remote_copy(
            src_ref=src, dst_ref=dst, send_sem=out_sem, recv_sem=in_sem,
            device_id=device, device_id_type=MESH_ID,
        )

    def pool_core(p):
        return copy(r.p_send.at[p], r.p_in.at[p], r.p_sem.at[0, p, 0], r.p_sem.at[1, p, 0], partner)

    def pool_y(p, hop):
        device = (((y + hop) % ny) * 2 + core, row)
        return copy(
            r.p_keep.at[p, hop], r.p_y.at[p, hop - 1], r.p_sem.at[0, p, hop], r.p_sem.at[1, p, hop], device
        )

    def halo(p, side):
        device = right if side else left
        return copy(
            r.h_out.at[p, side], r.h_in.at[p, side], r.h_sem.at[0, p, side], r.h_sem.at[1, p, side], device
        )

    def chunk_loads(f):
        slot = f % 2
        part = pl.ds(pl.multiple_of(f * D, D), D)
        return [
            pltpu.make_async_copy(r.win_any.at[:, part], r.wbuf.at[slot], r.l_sem.at[0, slot]),
            pltpu.make_async_copy(r.wback_any.at[part, :], r.wbuf.at[2 + slot], r.l_sem.at[1, slot]),
            pltpu.make_async_copy(r.act_any.at[:, part], r.tbuf.at[slot], r.l_sem.at[2, slot]),
            pltpu.make_async_copy(r.slope_any.at[:, part], r.tbuf.at[2 + slot], r.l_sem.at[3, slot]),
        ]

    load_feed = [
        pltpu.make_async_copy(r.fg_any, r.fg, r.l_sem.at[4, 0]),
        pltpu.make_async_copy(r.lowt_any, r.lt, r.l_sem.at[4, 1]),
        pltpu.make_async_copy(r.zg_any, r.sg, r.l_sem.at[5, 0]),
    ]
    load_unit = pltpu.make_async_copy(r.unit_any, r.acc.at[0], r.l_sem.at[5, 1])
    load_wout = pltpu.make_async_copy(r.wout_any, r.wbuf.at[0], r.l_sem.at[6, 0])
    load_att = pltpu.make_async_copy(r.att_any, r.att, r.l_sem.at[6, 1])
    load_wq = pltpu.make_async_copy(r.wq_any, r.wbuf.at[1], r.l_sem.at[7, 0])
    load_wk = pltpu.make_async_copy(r.wk_any, r.wbuf.at[2], r.l_sem.at[7, 1])
    load_wv = pltpu.make_async_copy(r.wv_any, r.wbuf.at[3], r.l_sem.at[8, 0])
    load_tt = pltpu.make_async_copy(r.tt_any, r.lt, r.l_sem.at[8, 1])

    def rows_of(block, mine):
        rc = D // seq
        return pl.ds(pl.multiple_of((2 * block + mine) * rc, rc), rc)

    @pl.when(step == 0)
    def _():
        for load in chunk_loads(0) + load_feed + [load_unit, load_att]:
            load.start()
        z, x = row // nx, row % nx
        peers = [partner, right, left]
        peers += [(((y + hop) % ny) * 2 + core, row) for hop in range(1, ny)]
        peers += [(here, z * nx + (x + hop) % nx) for hop in range(1, nx)]
        peers += [(here, ((z + hop) % nz) * nx + x) for hop in range(1, nz)]
        greet(peers)
        for load in load_feed:
            load.wait()

    @pl.when(step < CHUNKS)
    def _():
        f = step
        slot = f % 2
        for load in chunk_loads(f):
            load.wait()

        @pl.when(f < CHUNKS - 1)
        def _():
            for load in chunk_loads(f + 1):
                load.start()

        @pl.when(f == CHUNKS - 1)
        def _():
            load_wout.start()

        slope = r.tbuf[2 + slot].astype(F32)
        inner_grad = (nt(r.fg[...], r.wbuf[2 + slot]) * slope).astype(BF16)
        for block in range(ny):
            store_chunks(r.a_send.at[f, block], nn(r.lt[rows_of(block, 1 - core), :], inner_grad))

        kept = [nn(r.lt[rows_of(block, core), :], inner_grad) for block in range(ny)]
        for i in range(CHUNKS):

            @pl.when(f == i)
            def _(i=i):
                sums["in%d" % i].start(0)
                for block in range(ny):
                    store_chunks(sums["in%d" % i].keep.at[0, block], kept[block])

        r.sg[...] += nt(inner_grad, r.wbuf[slot])
        back = nn(r.tbuf[slot].T, r.fg[...])
        part = FF // seq
        for sub in range(D // part):
            block = f * (D // part) + sub
            piece = back[sub * part : (sub + 1) * part]

            @pl.when(block % 2 == core)
            def _(block=block, piece=piece):
                keeps = [sums["b%d" % u].keep.at[0] for u in range(units_back)]
                store_blocks(keeps, block // 2, piece)

            @pl.when(block % 2 != core)
            def _(block=block, piece=piece):
                store_blocks([r.b_send.at[u] for u in range(units_back)], block // 2, piece)

        @pl.when(f == CHUNKS - 1)
        def _():
            for u in range(units_back):
                sums["b%d" % u].start(0)

    @pl.when(step == CHUNKS)
    def _():
        load_wq.start()
        load_wk.start()
        load_wv.start()
        load_unit.wait()
        inverse = r.inv[:, 0:1]
        total = jnp.zeros((count, LANES), F32)
        total_unit = jnp.zeros((count, LANES), F32)
        r.small[...] = jnp.zeros_like(r.small)
        r.small[0:8] = r.sums[...]
        for c in range(PAIRS):
            lanes = slice(c * LANES, (c + 1) * LANES)
            grad, unit = r.sg[:, lanes], r.acc[0, c]
            r.small[0:1, lanes] = jnp.sum(grad * unit, axis=0, keepdims=True)
            r.small[1:2, lanes] = jnp.sum(grad, axis=0, keepdims=True)
            e = grad * r.vecs[0:1, lanes]
            total = total + e
            total_unit = total_unit + e * unit
        mean = jnp.sum(total, axis=1, keepdims=True) * (1.0 / D)
        mean_unit = jnp.sum(total_unit, axis=1, keepdims=True) * (1.0 / D)
        for c in range(PAIRS):
            lanes = slice(c * LANES, (c + 1) * LANES)
            e = r.sg[:, lanes] * r.vecs[0:1, lanes]
            r.sg[:, lanes] = inverse * (e - mean - r.acc[0, c] * mean_unit)
        branch_grad = r.sg[...].astype(BF16)
        load_att.wait()
        load_wout.wait()
        sums["in0"].sent_core(0)
        for block in range(ny):
            store_chunks(r.a_send.at[0, block], nn(r.att[rows_of(block, 1 - core), :], branch_grad))
        sums["out"].start(0)
        for block in range(ny):
            store_chunks(sums["out"].keep.at[0, block], nn(r.att[rows_of(block, core), :], branch_grad))
        load_tt.start()
        attended_grad = nt(branch_grad, r.wbuf[0])
        for c in range(PAIRS):
            r.acc[1, c] = attended_grad[:, c * LANES : (c + 1) * LANES]

    @pl.when((step >= POOL) & (step < NEAR))
    def _():
        p = step - POOL
        r.gb[...] = (r.acc[1, p] * r.rp[...]).astype(BF16)
        delta = score_delta(r.gb[...], r.o[...])
        kp = jnp.concatenate([piece[0] for piece in kv], axis=0)
        kt = kp.T
        vp = jnp.concatenate([piece[1] for piece in kv], axis=0)
        wide = min(256, count)
        for head in range(2):
            for b in range(count // wide):
                cols = slice(b * wide, (b + 1) * wide)
                gh = head_half(r.gb[cols, :], head)
                qh = head_half(r.q[cols, :], head)
                low = r.pool_e[head, :, cols]
                dp = nt(vp, gh) - delta[head : head + 1, cols]
                ds = (low.astype(F32) * dp).astype(BF16)
                key_part = nn(ds, qh)
                value_part = nn(low, gh)
                if head == 0 and b == 0:
                    r.dk[0 : seq * size] = key_part
                    r.dv[0 : seq * size] = value_part
                else:
                    r.dk[0 : seq * size] += key_part
                    r.dv[0 : seq * size] += value_part
                r.dq_pool[p, head * 64 : head * 64 + 64, cols] = nn(kt[head * 64 : head * 64 + 64], ds)
        for i in range(pieces):
            target = r.p_keep if i < ny else r.p_send
            after = (((y + i % ny) % ny) * 2 + (core + i // ny) % 2 + 1) % seq
            index = ((after % 2 - core + 2) % 2) * ny + (after // 2 - y + ny) % ny
            rows = pl.ds(pl.multiple_of(index * size, size), EXTRA)
            for which, total in ((0, r.dk), (1, r.dv)):
                target[p, i % ny, which, 0:size] = total[i * size : (i + 1) * size].astype(BF16)
                target[p, i % ny, which, size:] = total[rows, :].astype(BF16)
        pool_core(p).start()

    @pl.when((step > POOL) & (step <= NEAR))
    def _():
        p = step - POOL - 1
        pool_core(p).wait_recv()
        for hop in range(1, ny):
            for which in range(2):
                r.p_keep[p, hop, which] = r.p_keep[p, hop, which] + r.p_in[p, hop, which]
            pool_y(p, hop).start()

    @pl.when((step >= NEAR) & (step < LATE))
    def _():
        p = step - NEAR
        r.gb[...] = (r.acc[1, p] * r.rn[...]).astype(BF16)
        delta = score_delta(r.gb[...], r.o[...])
        kt = r.keys[...].T
        r.dk[0 : count + 2 * HALF] = jnp.zeros((count + 2 * HALF, LANES), F32)
        r.dv[0 : count + 2 * HALF] = jnp.zeros((count + 2 * HALF, LANES), F32)
        for b in range(count // QB):
            cols = slice(b * QB, (b + 1) * QB)
            keys = slice(b * QB, (b + 2) * QB)
            lows, scores, grads, queries, dqs = [], [], [], [], []
            for head in range(2):
                gh = head_half(r.gb[cols, :], head)
                low = r.near_e[head, b]
                dp = nt(r.values[keys, :], gh) - delta[head : head + 1, cols]
                ds = (low.astype(F32) * dp).astype(BF16)
                dqs.append(nn(kt[head * 64 : head * 64 + 64, keys], ds))
                lows.append(low)
                scores.append(ds)
                grads.append(gh)
                queries.append(head_half(r.q[cols, :], head))
            r.dk[keys, :] += nn(jnp.concatenate(scores, axis=1), jnp.concatenate(queries, axis=0))
            r.dv[keys, :] += nn(jnp.concatenate(lows, axis=1), jnp.concatenate(grads, axis=0))
            total = (jnp.concatenate(dqs, axis=0) + r.dq_pool[p, :, cols]) * 0.125
            lanes = pl.ds(pl.multiple_of(p * LANES, LANES), LANES)
            r.tbuf[0, cols, lanes] = total.T.astype(BF16)
        for which, total in ((0, r.dk), (1, r.dv)):
            r.h_out[p, 0, which] = total[0:HALF].astype(BF16)
            r.acc[which, p] = total[HALF : HALF + count]
            r.h_out[p, 1, which] = total[HALF + count : 2 * HALF + count].astype(BF16)

        @pl.when(here > 0)
        def _():
            halo(p, 0).start()

        @pl.when(here < seq - 1)
        def _():
            halo(p, 1).start()

    def query_gradient():
        load_tt.wait()
        sums["in1"].sent_core(0)
        for block in range(ny):
            store_chunks(r.a_send.at[1, block], nn(r.lt[rows_of(block, 1 - core), :], r.tbuf[0]))
        sums["q"].start(0)
        for block in range(ny):
            store_chunks(sums["q"].keep.at[0, block], nn(r.lt[rows_of(block, core), :], r.tbuf[0]))

    def tokens_gradient():
        for load in (load_wq, load_wk, load_wv):
            load.wait()
        total = r.sg[...] + nt(r.tbuf[0], r.wbuf[1])
        total = total + nt(r.tbuf[1], r.wbuf[2])
        r.tokens_grad[...] = (total + nt(r.tbuf[2], r.wbuf[3])).astype(BF16)

    @pl.when((step >= LATE) & (step < LAST))
    def _():
        p = step - LATE
        lanes = pl.ds(pl.multiple_of(p * LANES, LANES), LANES)
        for hop in range(1, ny):
            pool_y(p, hop).wait_recv()

        @pl.when(here < seq - 1)
        def _():
            halo(p, 0).wait_recv()
            for which in range(2):
                r.acc[which, p, count - HALF :, :] += r.h_in[p, 0, which].astype(F32)

        @pl.when(here > 0)
        def _():
            halo(p, 1).wait_recv()
            for which in range(2):
                r.acc[which, p, 0:HALF, :] += r.h_in[p, 1, which].astype(F32)

        moves = ((2, 0, 0), (3, 1, 0), (4, 2, 0), (0, 2, 1), (1, 3, 1))
        sums = [jnp.zeros((1, LANES), F32)] * 5
        for which, source in ((0, r.keys), (1, r.values)):
            grad = r.acc.at[which, p]
            r.cells[...] = source[...].astype(F32)
            total = r.p_keep[p, 0, which].astype(F32) + r.p_in[p, 0, which].astype(F32)
            for hop in range(1, ny):
                total = total + r.p_y[p, hop - 1, which].astype(F32)
            r.g[...] = total
            for tap, place, shift in moves:
                mask = r.masks[shift, :, tap : tap + 1]
                spread = r.g[shift : shift + size, :] * mask * r.taps[tap : tap + 1, :]
                grad[pl.ds(place, size, stride=4), :] += spread
            for tap in range(5):
                taken = r.cells[pl.ds(HALF + tap - 2, size, stride=4), :]
                product = r.g[0:size, :] * r.masks[0, :, tap : tap + 1] * taken
                sums[tap] = sums[tap] + jnp.sum(product, axis=0, keepdims=True)
            r.tbuf[1 + which, :, lanes] = grad[...].astype(BF16)
        for tap in range(5):
            r.small[8 + tap : 9 + tap, lanes] = sums[tap]

    @pl.when(step == LAST)
    def _():
        for name, place, low in (("k", 2, 1), ("v", 3, 2)):
            sums["in%d" % place].sent_core(0)
            for block in range(ny):
                rows = rows_of(block, 1 - core)
                store_chunks(r.a_send.at[place, block], nn(r.lt[rows, :], r.tbuf[low]))
            sums[name].start(0)
            keep = sums[name].keep
            for block in range(ny):
                store_chunks(keep.at[0, block], nn(r.lt[rows_of(block, core), :], r.tbuf[low]))
        r.small_t[...] = r.small[...].T
        few = D // (seq * nz * nx)
        for block in range(ny):
            for part, mine in ((r.s_send.at[block], 1 - core), (sums["small"].keep.at[0, block], core)):
                vectors = r.small_t[rows_of(block, mine), :]
                for z in range(nz):
                    for x in range(nx):
                        start = (z * nx + x) * few
                        part[z, x] = jnp.zeros(part.shape[2:], BF16)
                        part[z, x, 0:few] = vectors[start : start + few].astype(BF16)
        sums["small"].start(0)

    results = {"out": r.t_out, "q": r.t_query, "k": r.t_key, "v": r.t_value, "small": r.t_small}
    for f in range(CHUNKS):
        results["in%d" % f] = r.t_in.at[f]
    for u in range(units_back):
        results["b%d" % u] = r.t_back.at[u]

    def run(name, stage):
        if name == "query":
            query_gradient()
        elif name == "tokens":
            tokens_gradient()
        elif name in sums:
            done = getattr(sums[name], ("core", "one", "two", "three")[stage])(0)
            if stage == 3:
                results[name][...] = done

    for when, todo in PLAN.items():

        @pl.when(step == when)
        def _(todo=todo):
            for name, stage in todo:
                run(name, stage)

    @pl.when(step == LAST)
    def _():
        reused = ["in%d" % f for f in range(CHUNKS)]
        for name in sums:
            if name not in reused:
                sums[name].sent_core(0)
            sums[name].sent(0)
        for p in range(PAIRS):
            pool_core(p).wait_send()
            for hop in range(1, ny):
                pool_y(p, hop).wait_send()

        @pl.when(here > 0)
        def _():
            for p in range(PAIRS):
                halo(p, 0).wait_send()

        @pl.when(here < seq - 1)
        def _():
            for p in range(PAIRS):
                halo(p, 1).wait_send()


def unpack_kernel(t_in, t_back, t_query, t_key, t_value, t_out, t_small, tg, *outs):
    tokens_grad, query, key, value, out, inn, back = outs[:7]
    rows = query.shape[0]
    tokens_grad[...] = tg[...]
    for source, target in ((t_query, query), (t_key, key), (t_value, value), (t_out, out)):
        target[...] = unfold_rows(source[...], rows)
    for u in range(CHUNKS):
        inn[:, u * D : (u + 1) * D] = unfold_rows(t_in[u], rows)
    units, part, wide = t_back.shape
    across = back.shape[1] // wide
    for u in range(units):
        top, start = (u // across) * part, (u % across) * wide
        back[top : top + part, start : start + wide] = t_back[u]
    small = t_small[...]
    pad = LANES - small.shape[0]
    turned = jnp.concatenate([small, jnp.zeros((pad, LANES), F32)], axis=0).T
    for i in range(4):
        outs[7 + i][...] = turned[i : i + 1, 0:rows]
    outs[11][...] = small[0:rows, 8:13]


def call(kernel, args, in_specs, outs, out_specs, grid, scratch, flops, name):
    moved = sum(a.size * a.dtype.itemsize for a in list(args) + list(outs))
    return pl.pallas_call(
        kernel,
        grid_spec=pltpu.PrefetchScalarGridSpec(
            num_scalar_prefetch=0,
            grid=grid,
            in_specs=in_specs,
            out_specs=out_specs,
            scratch_shapes=scratch,
        ),
        out_shape=outs,
        compiler_params=pltpu.CompilerParams(
            vmem_limit_bytes=60 * MB, dimension_semantics=("arbitrary",) * len(grid)
        ),
        cost_estimate=pl.CostEstimate(flops=flops, bytes_accessed=moved, transcendentals=0),
        name=name,
    )(*args)


def whole(array):
    rank = len(array.shape)
    return pl.BlockSpec(array.shape, lambda i: (0,) * rank)


def columns(array, width=LANES):
    rank = len(array.shape)
    return pl.BlockSpec(array.shape[:-1] + (width,), lambda i: (0,) * (rank - 1) + (i,))


def leading(array, size):
    rank = len(array.shape)
    return pl.BlockSpec((size,) + array.shape[1:], lambda i: (i,) + (0,) * (rank - 1))


def per_device(
    tokens,
    item_lengths,
    w_query,
    w_key,
    w_value,
    w_out,
    w_in,
    w_back,
    norm1_gain,
    norm1_bias,
    norm2_gain,
    norm2_bias,
    pool_weight,
    out_grad,
):
    _, count, _ = tokens.shape
    seq = lax.axis_size("seq")
    ny = seq // 2
    row_len = count * seq
    span = count + 2 * HALF
    size = count // 4
    tok = tokens[0]
    og = out_grad[0]
    vecs = jnp.concatenate(
        [jnp.stack([norm1_gain, norm1_bias, norm2_gain, norm2_bias]), jnp.zeros((4, D), F32)]
    )

    def shape(dims, kind):
        return jax.ShapeDtypeStruct(dims, kind)

    blocks = count // QB
    pool_all = seq * size
    anywhere = pl.BlockSpec(memory_space=pl.ANY)

    def in_first(i):
        return jnp.clip(i - FORWARD_NEAR, 0, PAIRS - 1)

    def in_second(i):
        return jnp.clip(i - FORWARD_POOL, 0, PAIRS - 1)

    ins = [
        ("lengths", item_lengths, pl.BlockSpec(memory_space=pltpu.SMEM)),
        ("pool_weight", pool_weight, whole(pool_weight)),
        ("tok", tok, anywhere),
        ("wq_any", w_query, anywhere),
        ("wk_any", w_key, anywhere),
        ("wv_any", w_value, anywhere),
    ]
    near_shape = shape((H, blocks, 2 * QB, QB), BF16)
    pool_shape = shape((H, pool_all, count), BF16)
    wide_shape = shape((count, D), F32)
    outs = [
        ("q_out", shape((count, D), BF16), anywhere),
        ("k_out", shape((span, D), BF16), anywhere),
        ("v_out", shape((span, D), BF16), anywhere),
        ("tt_out", shape((D, count), BF16), anywhere),
        ("mask_out", shape((2, size, LANES), F32), anywhere),
        ("tap_out", shape((8, D), F32), anywhere),
        ("pieces_out", shape((seq, 2, size, D), BF16), anywhere),
        ("near_e", near_shape, pl.BlockSpec((2, blocks, 2 * QB, QB), lambda i: (in_first(i), 0, 0, 0))),
        ("pool_e", pool_shape, pl.BlockSpec((2, pool_all, count), lambda i: (in_second(i), 0, 0))),
        ("o_out", wide_shape, pl.BlockSpec((count, LANES), lambda i: (0, in_second(i)))),
        ("rn_out", wide_shape, pl.BlockSpec((count, LANES), lambda i: (0, in_second(i)))),
        ("rp_out", wide_shape, pl.BlockSpec((count, LANES), lambda i: (0, in_second(i)))),
    ]
    scratch = [
        ("x", pltpu.VMEM((span, D), BF16)),
        ("wq", pltpu.VMEM((D, D), BF16)),
        ("wk", pltpu.VMEM((D, D), BF16)),
        ("wv", pltpu.VMEM((D, D), BF16)),
        ("qs", pltpu.VMEM((count, D), BF16)),
        ("ks", pltpu.VMEM((span, D), BF16)),
        ("vs", pltpu.VMEM((span, D), BF16)),
        ("tt", pltpu.VMEM((D, count), BF16)),
        ("mask", pltpu.VMEM((2, size, LANES), F32)),
        ("tap", pltpu.VMEM((8, D), F32)),
        ("cells", pltpu.VMEM((PAIRS, span, LANES), F32)),
        ("pieces", pltpu.VMEM((seq, 2, size, D), BF16)),
        ("o_near", pltpu.VMEM((PAIRS, LANES, count), F32)),
        ("stats", pltpu.VMEM((PAIRS, 8, count), F32)),
        ("near_bias", pltpu.VMEM((blocks, 2 * QB, QB), F32)),
        ("pool_bias", pltpu.VMEM((pool_all, count), F32)),
        ("s_sem", pltpu.SemaphoreType.DMA((2 + seq,))),
        ("r_sem", pltpu.SemaphoreType.DMA((2 + seq,))),
        ("l_sem", pltpu.SemaphoreType.DMA((11,))),
    ]
    (queries, keys, values, tok_t, tap_masks, taps, pieces, near_e, pool_e, attention, near_scale, pool_scale) = (
        pl.pallas_call(
            partial(forward_kernel, names=[entry[0] for entry in ins + outs + scratch]),
            grid_spec=pltpu.PrefetchScalarGridSpec(
                num_scalar_prefetch=0,
                grid=(FORWARD_LAST + 1,),
                in_specs=[entry[2] for entry in ins],
                out_specs=[entry[2] for entry in outs],
                scratch_shapes=[entry[1] for entry in scratch],
            ),
            out_shape=[entry[1] for entry in outs],
            compiler_params=pltpu.CompilerParams(
                collective_id=1,
                has_side_effects=True,
                vmem_limit_bytes=60 * MB,
                dimension_semantics=("arbitrary",),
            ),
            cost_estimate=pl.CostEstimate(
                flops=4 * H * 768 * 256 * count + 6 * count * D * D, bytes_accessed=16 * MB, transcendentals=0
            ),
            name="forward",
        )(*[entry[1] for entry in ins])
    )

    dp = lax.axis_size("dp")
    nx = 2 if dp % 2 == 0 else 1
    nz = dp // nx
    rows = D // (seq * dp)
    back_rows = FF // (seq * dp)
    down = 2 if back_rows % 32 == 0 else 1
    half_one = shape((ny, nz, nx) + folded(rows, D), BF16)
    half_back = shape((2 * down, ny, nz, nx, back_rows // down, D // 2), BF16)
    args = (attention, tok, og, vecs, w_out, w_in, w_back)
    outs = (
        shape((count, D), BF16),
        shape((count, FF), BF16),
        shape((count, FF), BF16),
        shape((D, count), BF16),
        shape((count, D), BF16),
        shape((count, D), F32),
        shape((PAIRS, count, LANES), F32),
        shape((count, LANES), F32),
        shape((D, count), BF16),
        shape((8, D), F32),
    )
    mixed, act, slope, low_t, feed_grad, z_grad, unit_one, inv_one, att_t, sums = call(
        dense_kernel,
        args,
        [whole(a) for a in args[:5]]
        + [columns(w_in, D), pl.BlockSpec((D, D), lambda i: (i, 0))],
        outs,
        [whole(outs[0]), columns(outs[1], D), columns(outs[2], D)] + [whole(a) for a in outs[3:]],
        (CHUNKS,),
        [
            pltpu.VMEM((count, D), F32),
            pltpu.VMEM((count, D), BF16),
            pltpu.VMEM((count, D), F32),
        ],
        2 * count * (D * D + 2 * D * FF),
        "dense",
    )
    half_small = shape((ny, nz, nx, -(-rows // 16) * 16, LANES), BF16)
    half_pool = (PAIRS, ny, 2, size + EXTRA, LANES)
    blocks_in = []

    def block(name, array, spec):
        blocks_in.append((name, array, spec))

    def col_spec(array, index):
        lead = (0,) * (len(array.shape) - 1)
        return pl.BlockSpec(array.shape[:-1] + (LANES,), lambda i: lead + (index(i),))

    def lead_spec(array, index):
        rest = (0,) * (len(array.shape) - 1)
        return pl.BlockSpec((2,) + array.shape[1:], lambda i: (index(i),) + rest)

    def all_spec(array):
        rest = (0,) * len(array.shape)
        return pl.BlockSpec(array.shape, lambda i: rest)

    def in_pool(i):
        return jnp.clip(i - POOL, 0, PAIRS - 1)

    def in_near(i):
        return jnp.clip(i - NEAR, 0, PAIRS - 1)

    def in_both(i):
        return jnp.clip(i - POOL, 0, 2 * PAIRS - 1) % PAIRS

    def in_late(i):
        return jnp.clip(i - NEAR, 0, 2 * PAIRS - 1) % PAIRS

    block("q", queries, col_spec(queries, in_both))
    block("o", attention, col_spec(attention, in_both))
    block("rp", pool_scale, col_spec(pool_scale, in_pool))
    block("rn", near_scale, col_spec(near_scale, in_near))
    block("pool_e", pool_e, lead_spec(pool_e, in_pool))
    block("near_e", near_e, lead_spec(near_e, in_near))
    block("keys", keys, col_spec(keys, in_late))
    block("values", values, col_spec(values, in_late))
    block("piece", pieces, col_spec(pieces, in_pool))
    block("masks", tap_masks, all_spec(tap_masks))
    block("taps", taps, col_spec(taps, in_late))
    block("sums", sums, all_spec(sums))
    block("vecs", vecs, all_spec(vecs))
    block("inv", inv_one, all_spec(inv_one))
    for name, array in (
        ("win_any", w_in),
        ("wback_any", w_back),
        ("act_any", act),
        ("slope_any", slope),
        ("fg_any", feed_grad),
        ("lowt_any", low_t),
        ("zg_any", z_grad),
        ("unit_any", unit_one),
        ("wout_any", w_out),
        ("att_any", att_t),
        ("tt_any", tok_t),
        ("wq_any", w_query),
        ("wk_any", w_key),
        ("wv_any", w_value),
    ):
        block(name, array, anywhere)
    outs = [
        ("t_in", shape((CHUNKS,) + half_one.shape[3:], F32)),
        ("t_back", shape((half_back.shape[0],) + half_back.shape[4:], F32)),
        ("t_query", shape(half_one.shape[3:], F32)),
        ("t_key", shape(half_one.shape[3:], F32)),
        ("t_value", shape(half_one.shape[3:], F32)),
        ("t_out", shape(half_one.shape[3:], F32)),
        ("t_small", shape(half_small.shape[3:], F32)),
        ("tokens_grad", shape((count, D), BF16)),
    ]
    tall = max(pool_all, span)
    scratch = [
        ("dk", pltpu.VMEM((tall, LANES), F32)),
        ("dv", pltpu.VMEM((tall, LANES), F32)),
        ("dq_pool", pltpu.VMEM((PAIRS, LANES, count), F32)),
        ("gb", pltpu.VMEM((count, LANES), BF16)),
        ("acc", pltpu.VMEM((2, PAIRS, count, LANES), F32)),
        ("tbuf", pltpu.VMEM((4, count, D), BF16)),
        ("wbuf", pltpu.VMEM((4, D, D), BF16)),
        ("fg", pltpu.VMEM((count, D), BF16)),
        ("lt", pltpu.VMEM((D, count), BF16)),
        ("att", pltpu.VMEM((D, count), BF16)),
        ("cells", pltpu.VMEM((span, LANES), F32)),
        ("g", pltpu.VMEM((size + EXTRA, LANES), F32)),
        ("small", pltpu.VMEM((LANES, D), F32)),
        ("small_t", pltpu.VMEM((D, LANES), F32)),
        ("p_keep", pltpu.VMEM(half_pool, BF16)),
        ("p_send", pltpu.VMEM(half_pool, BF16)),
        ("p_in", pltpu.VMEM(half_pool, BF16)),
        ("p_y", pltpu.VMEM((PAIRS, ny - 1) + half_pool[2:], BF16)),
        ("h_out", pltpu.VMEM((PAIRS, 2, 2, HALF, LANES), BF16)),
        ("h_in", pltpu.VMEM((PAIRS, 2, 2, HALF, LANES), BF16)),
        ("p_sem", pltpu.SemaphoreType.DMA((2, PAIRS, ny))),
        ("h_sem", pltpu.SemaphoreType.DMA((2, PAIRS, 2))),
        ("l_sem", pltpu.SemaphoreType.DMA((9, 2))),
        ("sg", pltpu.VMEM((count, D), F32)),
        ("a_send", pltpu.VMEM((CHUNKS,) + half_one.shape, BF16)),
        ("b_send", pltpu.VMEM(half_back.shape, BF16)),
        ("s_send", pltpu.VMEM(half_small.shape, BF16)),
    ]
    sizes = {name: half_one.shape for name in ORDERS}
    sizes["small"] = half_small.shape
    for u in range(CHUNKS):
        if u < half_back.shape[0]:
            sizes["b%d" % u] = half_back.shape[1:]
        else:
            del sizes["b%d" % u]
    for name, dims in sizes.items():
        bufs = summed_scratch(1, dims, ORDERS[name])
        scratch += [(name + "_" + part, buf) for part, buf in zip(BUFFERS, bufs)]
    names = [entry[0] for entry in blocks_in] + [entry[0] for entry in outs + scratch]
    moved = sum(entry[1].size * entry[1].dtype.itemsize for entry in blocks_in)
    totals = pl.pallas_call(
        partial(backward_kernel, names=names, pieces=seq),
        grid_spec=pltpu.PrefetchScalarGridSpec(
            num_scalar_prefetch=0,
            grid=(LAST + 1,),
            in_specs=[entry[2] for entry in blocks_in],
            out_specs=[all_spec(entry[1]) for entry in outs],
            scratch_shapes=[entry[1] for entry in scratch],
        ),
        out_shape=[entry[1] for entry in outs],
        compiler_params=pltpu.CompilerParams(
            collective_id=0,
            has_side_effects=True,
            vmem_limit_bytes=63 * MB,
            dimension_semantics=("arbitrary",),
        ),
        cost_estimate=pl.CostEstimate(
            flops=8 * H * 768 * 256 * count + 12 * count * D * D + 8 * count * D * FF, bytes_accessed=moved, transcendentals=0
        ),
        name="backward",
    )(*[entry[1] for entry in blocks_in])

    outs = (
        shape((count, D), BF16),
        shape((rows, D), F32),
        shape((rows, D), F32),
        shape((rows, D), F32),
        shape((rows, D), F32),
        shape((rows, FF), F32),
        shape((back_rows, D), F32),
        shape((1, rows), F32),
        shape((1, rows), F32),
        shape((1, rows), F32),
        shape((1, rows), F32),
        shape((rows, 5), F32),
    )
    done = call(
        unpack_kernel,
        tuple(totals),
        [whole(a) for a in totals],
        outs,
        [whole(a) for a in outs],
        (1,),
        [],
        0,
        "unpack",
    )
    return (
        mixed[None],
        done[0][None],
        done[1],
        done[2],
        done[3],
        done[4],
        done[5],
        done[6],
        done[7].reshape(rows),
        done[8].reshape(rows),
        done[9].reshape(rows),
        done[10].reshape(rows),
        done[11],
    )


def solution(mesh):
    shards, copied = P("dp", "seq", None), P()
    spread = P(("seq", "dp"), None)
    vector = P(("seq", "dp"))
    return jax.shard_map(
        per_device,
        mesh=mesh,
        in_specs=(shards, P("dp", None)) + (copied,) * 11 + (shards,),
        out_specs=(shards, shards) + (spread,) * 6 + (vector,) * 4 + (spread,),
        check_vma=False,
    )
```

```python
import itertools
from functools import partial

import jax
import jax.numpy as jnp
from jax import lax
from jax.experimental import pallas as pl
from jax.experimental.pallas import tpu as pltpu
from jax.sharding import PartitionSpec as P

D = 768
FF = 3072
H = 12
PAIRS = H // 2
HALF = 64
PWIN = 512
QB = 128
EXTRA = 16
LANES = 128
BF16 = jnp.bfloat16
F32 = jnp.float32
MB = 1 << 20


def nn(left, right):
    return jnp.dot(left, right, preferred_element_type=F32)


def nt(left, right, precision=None):
    return lax.dot_general(
        left, right, (((1,), (1,)), ((), ())), preferred_element_type=F32, precision=precision
    )


def iota(shape, dim):
    return lax.broadcasted_iota(jnp.int32, shape, dim)


def segment_of(ends, place, row_len):
    item = jnp.zeros_like(place)
    for end in ends:
        item = item + (place >= end).astype(jnp.int32)
    return jnp.where((place >= 0) & (place < row_len), item, -2)


def head_half(block, head):
    lane = iota(block.shape, 1)
    return jnp.where((lane < 64) == (head == 0), block, jnp.zeros_like(block))


def tap_mask(ends, start, tap, shift, count, row_len):
    center = start + 4 * (iota((count, 1), 0) + shift)
    same = segment_of(ends, center + tap - 2, row_len) == segment_of(ends, center, row_len)
    return (same & (center < row_len)).astype(F32)


def folds(rows, width):
    return 2 if rows % 16 and rows % 8 == 0 and (width // 2) % LANES == 0 else 1


def folded(rows, width):
    fold = folds(rows, width)
    return (rows * fold, width // fold)


def fold_rows(block):
    rows, width = block.shape
    fold = folds(rows, width)
    part = width // fold
    return jnp.concatenate([block[:, i * part : (i + 1) * part] for i in range(fold)], axis=0)


def unfold_rows(block, rows):
    fold = block.shape[0] // rows
    return jnp.concatenate([block[i * rows : (i + 1) * rows] for i in range(fold)], axis=1)


def store_chunks(target, total):
    nz, nx = target.shape[0], target.shape[1]
    rows = total.shape[0] // (nz * nx)
    for z in range(nz):
        for x in range(nx):
            start = (z * nx + x) * rows
            target[z, x] = fold_rows(total[start : start + rows]).astype(BF16)


def store_blocks(targets, block, total):
    _, nz, nx, part, wide = targets[0].shape
    rows = total.shape[0] // (nz * nx)
    across = total.shape[1] // wide
    for z in range(nz):
        for x in range(nx):
            start = (z * nx + x) * rows
            for unit, target in enumerate(targets):
                top = start + (unit // across) * part
                left = (unit % across) * wide
                target[block, z, x] = total[top : top + part, left : left + wide].astype(BF16)


def normal_parts(v):
    bell = jnp.exp(v * v * -0.5)
    t = 1.0 / (1.0 + jnp.abs(v) * (0.3275911 * 0.7071067811865476))
    poly = t * (
        0.127414796 + t * (-0.142248368 + t * (0.7107068705 + t * (-0.7265760135 + t * 0.5307027145)))
    )
    tail = poly * bell
    return jnp.where(v < 0, tail, 1.0 - tail), v * bell * 0.3989422804014327


def normalized(values):
    shifted = values - jnp.mean(values, axis=1, keepdims=True)
    inverse = lax.rsqrt(jnp.mean(shifted * shifted, axis=1, keepdims=True) + 1e-05)
    return shifted * inverse, inverse


def dense_kernel(
    o, tok, og, vecs, w_out, w_in, w_back,
    mixed, act, slope, low_t, feed_grad, z_grad, unit_out, inv_out, att_t, sums,
    first, low, feed,
):
    step = pl.program_id(0)
    gain_one, bias_one = vecs[0:1, :], vecs[1:2, :]
    gain_two, bias_two = vecs[2:3, :], vecs[3:4, :]

    @pl.when(step == 0)
    def _():
        att = o[...].astype(BF16)
        att_t[...] = att.T
        unit, inverse = normalized(tok[...].astype(F32) + nn(att, w_out[...]))
        for c in range(PAIRS):
            unit_out[c] = unit[:, c * LANES : (c + 1) * LANES]
        inv_out[...] = jnp.broadcast_to(inverse, inv_out.shape)
        first[...] = unit * gain_one + bias_one
        low[...] = first[...].astype(BF16)
        low_t[...] = low[...].T
        feed[...] = jnp.zeros_like(feed)

    inner = nn(low[...], w_in[...])
    phi, bell = normal_parts(inner)
    act[...] = (inner * phi).astype(BF16)
    slope[...] = (phi + bell).astype(BF16)
    feed[...] += nn(act[...], w_back[...])

    @pl.when(step == CHUNKS - 1)
    def _():
        unit, inverse = normalized(first[...] + feed[...])
        mixed[...] = (unit * gain_two + bias_two).astype(BF16)
        upstream = og[...].astype(F32)
        sums[...] = jnp.zeros_like(sums)
        sums[2:3] = jnp.sum(upstream * unit, axis=0, keepdims=True)
        sums[3:4] = jnp.sum(upstream, axis=0, keepdims=True)
        e = upstream * gain_two
        centred = e - jnp.mean(e, axis=1, keepdims=True)
        total = inverse * (centred - unit * jnp.mean(e * unit, axis=1, keepdims=True))
        z_grad[...] = total
        feed_grad[...] = total.astype(BF16)


def score_delta(grad, attended):
    pick = ((iota((8, LANES), 1) // 64) == iota((8, LANES), 0)).astype(F32)
    return nt(pick, grad.astype(F32) * attended, precision=lax.Precision.HIGHEST)


def hop_pairs(axis, count, stride, hop):
    pairs = []
    for device in range(lax.axis_size(axis)):
        place = (device // stride) % count
        pairs.append((device, device + ((place + hop) % count - place) * stride))
    return pairs


MESH_ID = pl.DeviceIdType.MESH


class Summed:
    def __init__(self, order, send_of, keep, core_in, first, second, third, out_sem, in_sem):
        self.order, self.send_of = order, send_of
        self.keep, self.core_in = keep, core_in
        self.bufs = (first, second, third)
        self.out_sem, self.in_sem = out_sem, in_sem
        self.units = keep.shape[0]
        self.count = dict(zip("yzx", keep.shape[1:4]))
        self.here, self.row = lax.axis_index("seq"), lax.axis_index("dp")
        self.mine = self.here % 2
        nx = self.count["x"]
        self.own = {"y": self.here // 2, "z": self.row // nx, "x": self.row % nx}
        self.base = {"y": 1}
        self.base["x"] = self.base["y"] + self.count["y"] - 1
        self.base["z"] = self.base["x"] + nx - 1

    def copy(self, u, src, dst, slot, device):
        return pltpu.make_async_remote_copy(
            src_ref=src,
            dst_ref=dst,
            send_sem=self.out_sem.at[u, slot],
            recv_sem=self.in_sem.at[u, slot],
            device_id=device,
            device_id_type=MESH_ID,
        )

    def core_copy(self, u):
        partner = (self.own["y"] * 2 + 1 - self.mine, self.row)
        return self.copy(u, self.send_of(u), self.core_in.at[u], 0, partner)

    def hop_copy(self, u, stage, hop):
        axis = self.order[stage]
        other = (self.own[axis] + hop) % self.count[axis]
        place = dict(self.own)
        place[axis] = other
        device = (place["y"] * 2 + self.mine, place["z"] * self.count["x"] + place["x"])
        index = []
        for dim in "yzx":
            known = dim in self.order[: stage + 1]
            index.append(place[dim] if known else slice(None))
        source = self.keep.at[(u,) + tuple(index)]
        slot = self.base[axis] + hop - 1
        return self.copy(u, source, self.bufs[stage].at[u, hop - 1], slot, device)

    def hops(self, stage):
        return range(1, self.count[self.order[stage]])

    def start(self, u):
        self.core_copy(u).start()

    def core(self, u):
        self.core_copy(u).wait_recv()
        for y in range(self.count["y"]):
            for z in range(self.count["z"]):
                self.keep[u, y, z] = self.keep[u, y, z] + self.core_in[u, y, z]
        for hop in self.hops(0):
            self.hop_copy(u, 0, hop).start()

    def add(self, u, stage):
        left = [dim for dim in "yzx" if dim not in self.order[: stage + 1]]
        for hop in self.hops(stage):
            self.hop_copy(u, stage, hop).wait_recv()
            for place in itertools.product(*[range(self.count[dim]) for dim in left]):
                at = dict(self.own)
                at.update(zip(left, place))
                index = (u,) + tuple(at[dim] for dim in "yzx")
                self.keep[index] = self.keep[index] + self.bufs[stage][(u, hop - 1) + place]
        for hop in self.hops(stage + 1):
            self.hop_copy(u, stage + 1, hop).start()

    def one(self, u):
        self.add(u, 0)

    def two(self, u):
        self.add(u, 1)

    def three(self, u):
        total = self.keep[(u,) + tuple(self.own[dim] for dim in "yzx")].astype(F32)
        for hop in self.hops(2):
            self.hop_copy(u, 2, hop).wait_recv()
            total = total + self.bufs[2][u, hop - 1].astype(F32)
        return total

    def sent_core(self, u):
        self.core_copy(u).wait_send()

    def sent(self, u):
        for stage in range(3):
            for hop in self.hops(stage):
                self.hop_copy(u, stage, hop).wait_send()


def summed_scratch(units, shape, order):
    count = dict(zip("yzx", shape[:3]))
    chunk = shape[3:]
    bufs = [pltpu.VMEM((units,) + shape, BF16), pltpu.VMEM((units,) + shape, BF16)]
    for stage in range(3):
        left = tuple(count[dim] for dim in "yzx" if dim not in order[: stage + 1])
        bufs.append(pltpu.VMEM((units, max(count[order[stage]] - 1, 1)) + left + chunk, BF16))
    slots = count["y"] + count["x"] + count["z"] - 2
    bufs += [pltpu.SemaphoreType.DMA((units, slots)), pltpu.SemaphoreType.DMA((units, slots))]
    return bufs


def greet(peers):
    barrier = pltpu.get_barrier_semaphore()
    for peer in peers:
        pl.semaphore_signal(barrier, inc=1, device_id=peer, device_id_type=MESH_ID)
    pl.semaphore_wait(barrier, len(peers))


class Refs:
    pass


FORWARD_NEAR = 1
FORWARD_POOL = 1 + PAIRS
FORWARD_LAST = 2 * PAIRS


def forward_kernel(*refs, names):
    r = Refs()
    for name, ref in zip(names, refs):
        setattr(r, name, ref)
    seq, _, size, _ = r.pieces.shape
    ny = seq // 2
    count, row_len = 4 * size, 4 * size * seq
    span = count + 2 * HALF
    step = pl.program_id(0)
    here, row = lax.axis_index("seq"), lax.axis_index("dp")
    y, core = here // 2, here % 2
    start = here * count
    partner = (y * 2 + 1 - core, row)
    right, left = ((here + 1) % seq, row), ((here + seq - 1) % seq, row)
    ends = [r.lengths[0, 0]]
    for m in range(1, 4):
        ends.append(ends[-1] + r.lengths[0, m])

    def copy(src, dst, slot, device):
        return pltpu.make_async_remote_copy(
            src_ref=src, dst_ref=dst, send_sem=r.s_sem.at[slot], recv_sem=r.r_sem.at[slot],
            device_id=device, device_id_type=MESH_ID,
        )

    own = r.x.at[HALF : HALF + count]
    to_right = copy(r.tok.at[count - HALF :], r.x.at[0:HALF], 0, right)
    to_left = copy(r.tok.at[0:HALF], r.x.at[HALF + count :], 1, left)

    def to_y(hop):
        device = (((y + hop) % ny) * 2 + core, row)
        return copy(r.pieces.at[0], r.pieces.at[ny - hop], 1 + hop, device)

    def to_core(hop):
        return copy(r.pieces.at[hop], r.pieces.at[ny + hop], 1 + ny + hop, partner)

    loads = [
        pltpu.make_async_copy(r.tok, own, r.l_sem.at[0]),
        pltpu.make_async_copy(r.wk_any, r.wk, r.l_sem.at[1]),
        pltpu.make_async_copy(r.wv_any, r.wv, r.l_sem.at[2]),
        pltpu.make_async_copy(r.wq_any, r.wq, r.l_sem.at[3]),
    ]
    stores = [
        pltpu.make_async_copy(r.qs, r.q_out, r.l_sem.at[4]),
        pltpu.make_async_copy(r.ks, r.k_out, r.l_sem.at[5]),
        pltpu.make_async_copy(r.vs, r.v_out, r.l_sem.at[6]),
        pltpu.make_async_copy(r.tt, r.tt_out, r.l_sem.at[7]),
        pltpu.make_async_copy(r.mask, r.mask_out, r.l_sem.at[8]),
    ]
    store_pieces = pltpu.make_async_copy(r.pieces, r.pieces_out, r.l_sem.at[10])

    @pl.when(step == 0)
    def _():
        for load in loads:
            load.start()
        greet([partner, right, left] + [(((y + hop) % ny) * 2 + core, row) for hop in range(1, ny)])

        @pl.when(here < seq - 1)
        def _():
            to_right.start()

        @pl.when(here > 0)
        def _():
            to_left.start()

        @pl.when(here == 0)
        def _():
            r.x[0:HALF] = jnp.zeros((HALF, D), BF16)

        @pl.when(here == seq - 1)
        def _():
            r.x[HALF + count :] = jnp.zeros((HALF, D), BF16)

        for i in range(7):
            mask = tap_mask(ends, start, i % 5, i // 5, size, row_len)
            r.mask[i] = jnp.broadcast_to(mask, (size, LANES))
        loads[0].wait()
        inner = slice(HALF, HALF + count)
        for weight, load, cells in ((r.wk, loads[1], r.ks), (r.wv, loads[2], r.vs)):
            load.wait()
            cells[inner] = nn(r.x[inner], weight[...]).astype(BF16)

        @pl.when(here > 0)
        def _():
            to_right.wait_recv()

        @pl.when(here < seq - 1)
        def _():
            to_left.wait_recv()

        for weight, cells in ((r.wk, r.ks), (r.wv, r.vs)):
            for outer in (slice(0, HALF), slice(HALF + count, span)):
                cells[outer] = nn(r.x[outer], weight[...]).astype(BF16)
        for which, source in ((0, r.ks), (1, r.vs)):
            for c in range(PAIRS):
                lanes = slice(c * LANES, (c + 1) * LANES)
                r.cells[c] = source[:, lanes].astype(F32)
                total = jnp.zeros((size, LANES), F32)
                for tap in range(5):
                    taken = r.cells.at[c][pl.ds(HALF + tap - 2, size, stride=4), :]
                    total = total + taken * r.mask[tap] * r.pool_weight[tap : tap + 1, lanes]
                r.pieces[0, which, :, lanes] = total.astype(BF16)
        for hop in range(1, ny):
            to_y(hop).start()
        to_core(0).start()
        loads[3].wait()
        r.qs[...] = (nn(r.x[inner], r.wq[...]).astype(BF16).astype(F32) * 0.125).astype(BF16)
        r.tt[...] = r.x[inner].T
        for store in stores:
            store.start()
        for b in range(count // QB):
            query_place = start + b * QB + iota((1, QB), 1)
            key_place = start - HALF + b * QB + iota((2 * QB, 1), 0)
            same = segment_of(ends, key_place, row_len) == segment_of(ends, query_place, row_len)
            near = jnp.abs(key_place - query_place) <= HALF
            r.near_bias[b] = jnp.where(same & near, 0.0, -1e30)

    @pl.when((step >= FORWARD_NEAR) & (step < FORWARD_POOL))
    def _():
        p = step - FORWARD_NEAR
        lanes = pl.ds(pl.multiple_of(p * LANES, LANES), LANES)
        vt = r.vs[:, lanes].T
        ones = jnp.ones((16, span), BF16)
        for head in range(2):
            qh = head_half(r.qs[:, lanes], head)
            va = jnp.concatenate([vt[head * 64 : head * 64 + 64], ones], axis=0)
            for b in range(count // QB):
                cols = slice(b * QB, (b + 1) * QB)
                keys = slice(b * QB, (b + 2) * QB)
                s = nt(r.ks[keys, lanes], qh[cols]) + r.near_bias[b]
                top = jnp.max(s, axis=0, keepdims=True)
                e = jnp.exp(s - top).astype(BF16)
                r.near_e[head, b] = e
                oa = nn(va[:, keys], e)
                r.o_near[p, head * 64 : head * 64 + 64, cols] = oa[:64]
                r.stats[p, head : head + 1, cols] = top
                r.stats[p, 2 + head : 3 + head, cols] = oa[64:65]

    @pl.when(step == FORWARD_POOL - 2)
    def _():
        query_place = start + iota((1, count), 1)
        query_item = segment_of(ends, query_place, row_len)
        for i in range(seq):
            owner = ((y + i % ny) % ny) * 2 + (core + i // ny) % 2
            key_place = 4 * (owner * size + iota((size, 1), 0))
            same = segment_of(ends, key_place, row_len) == query_item
            near = jnp.abs(key_place - query_place) <= 2 * PWIN
            r.pool_bias[i * size : (i + 1) * size] = jnp.where(same & near, 0.0, -1e30)

    @pl.when(step == FORWARD_POOL - 1)
    def _():
        for hop in range(1, ny):
            to_y(ny - hop).wait_recv()
            to_core(hop).start()

    @pl.when(step == FORWARD_POOL)
    def _():
        for hop in range(ny):
            to_core(hop).wait_recv()
        store_pieces.start()

    @pl.when(step >= FORWARD_POOL)
    def _():
        p = step - FORWARD_POOL
        lanes = pl.ds(pl.multiple_of(p * LANES, LANES), LANES)
        kp = jnp.concatenate([r.pieces[i, 0, :, lanes] for i in range(seq)], axis=0)
        vt = jnp.concatenate([r.pieces[i, 1, :, lanes] for i in range(seq)], axis=0).T
        ones = jnp.ones((16, seq * size), BF16)
        wide = min(256, count)
        for b in range(count // wide):
            cols = slice(b * wide, (b + 1) * wide)
            outs, near_scale, pool_scale = [], [], []
            for head in range(2):
                qh = head_half(r.qs[cols, lanes], head)
                va = jnp.concatenate([vt[head * 64 : head * 64 + 64], ones], axis=0)
                s = nt(kp, qh) + r.pool_bias[:, cols]
                near_top = r.stats[p, head : head + 1, cols]
                top = jnp.maximum(jnp.max(s, axis=0, keepdims=True), near_top)
                e = jnp.exp(s - top).astype(BF16)
                r.pool_e[head, :, cols] = e
                oa = nn(va, e)
                fade = jnp.exp(near_top - top)
                inverse = 1.0 / (fade * r.stats[p, 2 + head : 3 + head, cols] + oa[64:65])
                rows = slice(head * 64, head * 64 + 64)
                outs.append((fade * r.o_near[p, rows, cols] + oa[:64]) * inverse)
                near_scale.append(jnp.broadcast_to(fade * inverse, (64, wide)))
                pool_scale.append(jnp.broadcast_to(inverse, (64, wide)))
            r.o_out[cols, :] = jnp.concatenate(outs, axis=0).T
            r.rn_out[cols, :] = jnp.concatenate(near_scale, axis=0).T
            r.rp_out[cols, :] = jnp.concatenate(pool_scale, axis=0).T

    @pl.when(step == FORWARD_LAST)
    def _():
        for store in stores + [store_pieces]:
            store.wait()
        for hop in range(1, ny):
            to_y(hop).wait_send()
        for hop in range(ny):
            to_core(hop).wait_send()

        @pl.when(here < seq - 1)
        def _():
            to_right.wait_send()

        @pl.when(here > 0)
        def _():
            to_left.wait_send()


CHUNKS = FF // D
BUFFERS = ("sum", "core", "first", "second", "third", "out", "inn")
ATTEND = CHUNKS + 1
LAG = 3
LATE = ATTEND + PAIRS
LAST = LATE + LAG - 1
SPLIT = 4 * LANES
PARTS = (("A", 0, SPLIT), ("B", SPLIT, D))
NAMES = ("in0", "in1", "in2", "in3", "b0", "b1", "b2", "b3", "out", "q", "kA", "vA", "kB", "vB", "small", "query", "tokens")
(IN0, IN1, IN2, IN3, B0, B1, B2, B3, OUT, Q, KA, VA, KB, VB, SMALL, QUERY, TOKENS) = range(17)
XYZ = "xyz"
XZY = "xzy"
YXZ = "yxz"
YZX = "yzx"
ZYX = "zyx"
ORDERS = dict(zip(NAMES, (XYZ, ZYX, YXZ, XYZ, XYZ, YZX, XYZ, XZY, ZYX, XYZ, YZX, YXZ, YXZ, XZY, YXZ)))
PLAN = {
    (2, 0): (
        (IN1, 0),
    ),
    (2, 1): (
        (IN0, 0),
    ),
    (3, 0): (
        (IN2, 0),
    ),
    (4, 1): (
        (IN3, 0), (B1, 0),
    ),
    (5, 0): (
        (B0, 0), (OUT, 0),
    ),
    (6, 0): (
        (IN0, 1),
    ),
    (6, 1): (
        (B2, 0),
    ),
    (7, 0): (
        (IN2, 1),
    ),
    (8, 0): (
        (B1, 1), (IN3, 1),
    ),
    (9, 0): (
        (B3, 0), (IN0, 2),
    ),
    (9, 1): (
        (B0, 1),
    ),
    (10, 0): (
        (IN3, 2), (IN2, 2),
    ),
    (10, 1): (
        (B2, 1),
    ),
    (11, 1): (
        (B3, 1), (IN1, 1), (B1, 2), (QUERY, 0), (B0, 2), (KA, 0), (Q, 0),
    ),
    (12, 1): (
        (IN1, 2), (IN0, 3), (VA, 0), (B2, 2),
    ),
    (13, 1): (
        (VB, 0), (KB, 0), (IN2, 3), (KA, 1), (SMALL, 0), (Q, 1), (VA, 1), (VB, 1), (VA, 2),
        (B3, 2), (IN1, 3), (KB, 1), (Q, 2), (OUT, 1), (SMALL, 1), (KB, 2), (OUT, 2), (KA, 2),
        (SMALL, 2), (IN3, 3), (VB, 2), (TOKENS, 0), (VB, 3), (OUT, 3), (B0, 3), (B1, 3), (B2, 3),
        (B3, 3), (Q, 3), (KA, 3), (VA, 3), (KB, 3), (SMALL, 3),
    ),
}


def backward_kernel(*refs, names, pieces):
    r = Refs()
    for name, ref in zip(names, refs):
        setattr(r, name, ref)
    kv = [r.piece.at[i] for i in range(pieces)]
    seq, ny = pieces, pieces // 2
    step = pl.program_id(0)
    count = r.q.shape[0]
    size = count // 4
    nz, nx = r.b_send.shape[2:4]
    here, row = lax.axis_index("seq"), lax.axis_index("dp")
    y, core = here // 2, here % 2
    partner = (y * 2 + 1 - core, row)
    right, left = ((here + 1) % seq, row), ((here + seq - 1) % seq, row)
    units_back = r.b_send.shape[0]
    senders = {"small": r.s_send}
    for f in range(CHUNKS):
        senders["in%d" % f] = r.a_send.at[f]
    for place, name in enumerate(("out", "q")):
        senders[name] = r.a_send.at[place]
    for part, _, _ in PARTS:
        for name in ("k" + part, "v" + part):
            senders[name] = getattr(r, name + "_send")
    for u in range(units_back):
        senders["b%d" % u] = r.b_send.at[u]
    sums = {}
    for name in senders:
        bufs = [getattr(r, name + "_" + part) for part in BUFFERS]
        sums[name] = Summed(ORDERS[name], lambda u, name=name: senders[name], *bufs)

    def copy(src, dst, out_sem, in_sem, device):
        return pltpu.make_async_remote_copy(
            src_ref=src, dst_ref=dst, send_sem=out_sem, recv_sem=in_sem,
            device_id=device, device_id_type=MESH_ID,
        )

    def pool_core(p):
        return copy(r.p_send.at[p], r.p_in.at[p], r.p_sem.at[0, p, 0], r.p_sem.at[1, p, 0], partner)

    def pool_y(p, hop):
        device = (((y + hop) % ny) * 2 + core, row)
        return copy(
            r.p_keep.at[p, hop], r.p_y.at[p, hop - 1], r.p_sem.at[0, p, hop], r.p_sem.at[1, p, hop], device
        )

    def halo(p, side):
        device = right if side else left
        return copy(
            r.h_out.at[p, side], r.h_in.at[p, side], r.h_sem.at[0, p, side], r.h_sem.at[1, p, side], device
        )

    def chunk_loads(f):
        slot = f % 2
        part = pl.ds(pl.multiple_of(f * D, D), D)
        return [
            pltpu.make_async_copy(r.win_any.at[:, part], r.wbuf.at[slot], r.l_sem.at[0, slot]),
            pltpu.make_async_copy(r.wback_any.at[part, :], r.wbuf.at[2 + slot], r.l_sem.at[1, slot]),
            pltpu.make_async_copy(r.act_any.at[:, part], r.tbuf.at[slot], r.l_sem.at[2, slot]),
            pltpu.make_async_copy(r.slope_any.at[:, part], r.tbuf.at[2 + slot], r.l_sem.at[3, slot]),
        ]

    load_feed = [
        pltpu.make_async_copy(r.fg_any, r.fg, r.l_sem.at[4, 0]),
        pltpu.make_async_copy(r.lowt_any, r.lt, r.l_sem.at[4, 1]),
        pltpu.make_async_copy(r.zg_any, r.sg, r.l_sem.at[5, 0]),
    ]
    load_unit = pltpu.make_async_copy(r.unit_any, r.acc.at[0], r.l_sem.at[5, 1])
    load_wout = pltpu.make_async_copy(r.wout_any, r.wbuf.at[0], r.l_sem.at[6, 0])
    load_att = pltpu.make_async_copy(r.att_any, r.att, r.l_sem.at[6, 1])
    load_wq = pltpu.make_async_copy(r.wq_any, r.wbuf.at[1], r.l_sem.at[7, 0])
    load_wk = pltpu.make_async_copy(r.wk_any, r.wbuf.at[2], r.l_sem.at[7, 1])
    load_wv = pltpu.make_async_copy(r.wv_any, r.wbuf.at[3], r.l_sem.at[8, 0])
    load_tt = pltpu.make_async_copy(r.tt_any, r.lt, r.l_sem.at[8, 1])

    def rows_of(block, mine):
        rc = D // seq
        return pl.ds(pl.multiple_of((2 * block + mine) * rc, rc), rc)

    @pl.when(step == 0)
    def _():
        for load in chunk_loads(0)[1:2] + load_feed[:1] + chunk_loads(0)[3:] + load_feed[1:2]:
            load.start()
        for load in chunk_loads(0)[:1] + chunk_loads(0)[2:3] + load_feed[2:]:
            load.start()
        z, x = row // nx, row % nx
        peers = [partner, right, left]
        peers += [(((y + hop) % ny) * 2 + core, row) for hop in range(1, ny)]
        peers += [(here, z * nx + (x + hop) % nx) for hop in range(1, nx)]
        peers += [(here, ((z + hop) % nz) * nx + x) for hop in range(1, nz)]
        greet(peers)
        for load in load_feed[:2]:
            load.wait()

    def query_gradient():
        sums["in1"].sent_core(0)
        for block in range(ny):
            store_chunks(r.a_send.at[1, block], nn(r.lt[rows_of(block, 1 - core), :], r.tbuf[0]))
        sums["q"].start(0)
        for block in range(ny):
            store_chunks(sums["q"].keep.at[0, block], nn(r.lt[rows_of(block, core), :], r.tbuf[0]))

    def tokens_gradient():
        for load in (load_wq, load_wk, load_wv):
            load.wait()
        total = r.sg[...] + nt(r.tbuf[0], r.wbuf[1])
        total = total + nt(r.tbuf[1], r.wbuf[2])
        r.tokens_grad[...] = (total + nt(r.tbuf[2], r.wbuf[3])).astype(BF16)

    results = {"out": r.t_out, "q": r.t_query, "small": r.t_small}
    for part, _, _ in PARTS:
        for name in ("k" + part, "v" + part):
            results[name] = getattr(r, "t_" + name)
    for f in range(CHUNKS):
        results["in%d" % f] = r.t_in.at[f]
    for u in range(units_back):
        results["b%d" % u] = r.t_back.at[u]

    def run(name, stage):
        if name == "query":
            query_gradient()
        elif name == "tokens":
            tokens_gradient()
        elif name in sums:
            done = getattr(sums[name], ("core", "one", "two", "three")[stage])(0)
            if stage == 3:
                results[name][...] = done

    def run_plan(half):
        for (when, part), todo in PLAN.items():
            if part == half:

                @pl.when(step == when)
                def _(todo=todo):
                    for index, stage in todo:
                        run(NAMES[index], stage)

    @pl.when(step < CHUNKS)
    def _():
        f = step
        slot = f % 2
        early, late = chunk_loads(f)[1::2], chunk_loads(f)[0::2]
        for load in early:
            load.wait()

        @pl.when(f < CHUNKS - 1)
        def _():
            for load in chunk_loads(f + 1):
                load.start()

        @pl.when(f == 1)
        def _():
            load_unit.start()
            load_att.start()

        @pl.when(f == CHUNKS - 1)
        def _():
            load_wout.start()

        slope = r.tbuf[2 + slot].astype(F32)
        inner_grad = (nt(r.fg[...], r.wbuf[2 + slot]) * slope).astype(BF16)
        for block in range(ny):
            store_chunks(r.a_send.at[f, block], nn(r.lt[rows_of(block, 1 - core), :], inner_grad))

        kept = [nn(r.lt[rows_of(block, core), :], inner_grad) for block in range(ny)]
        for i in range(CHUNKS):

            @pl.when(f == i)
            def _(i=i):
                sums["in%d" % i].start(0)
                for block in range(ny):
                    store_chunks(sums["in%d" % i].keep.at[0, block], kept[block])

        run_plan(0)
        for load in late:
            load.wait()

        @pl.when(f == 0)
        def _():
            load_feed[2].wait()

        r.sg[...] += nt(inner_grad, r.wbuf[slot])
        back = nn(r.tbuf[slot].T, r.fg[...])
        part = FF // seq
        for sub in range(D // part):
            block = f * (D // part) + sub
            piece = back[sub * part : (sub + 1) * part]

            @pl.when(block % 2 == core)
            def _(block=block, piece=piece):
                keeps = [sums["b%d" % u].keep.at[0] for u in range(units_back)]
                store_blocks(keeps, block // 2, piece)

            @pl.when(block % 2 != core)
            def _(block=block, piece=piece):
                store_blocks([r.b_send.at[u] for u in range(units_back)], block // 2, piece)

        @pl.when(f == CHUNKS - 1)
        def _():
            for u in range(units_back):
                sums["b%d" % u].start(0)

    @pl.when(step == LATE - 1)
    def _():
        load_tt.wait()

    @pl.when(step == CHUNKS)
    def _():
        load_wq.start()
        load_wk.start()
        load_wv.start()
        load_unit.wait()
        inverse = r.inv[:, 0:1]
        total = jnp.zeros((count, LANES), F32)
        total_unit = jnp.zeros((count, LANES), F32)
        r.small[...] = jnp.zeros_like(r.small)
        r.small[0:8] = r.sums[...]
        for c in range(PAIRS):
            lanes = slice(c * LANES, (c + 1) * LANES)
            grad, unit = r.sg[:, lanes], r.acc[0, c]
            r.small[0:1, lanes] = jnp.sum(grad * unit, axis=0, keepdims=True)
            r.small[1:2, lanes] = jnp.sum(grad, axis=0, keepdims=True)
            e = grad * r.vecs[0:1, lanes]
            total = total + e
            total_unit = total_unit + e * unit
        mean = jnp.sum(total, axis=1, keepdims=True) * (1.0 / D)
        mean_unit = jnp.sum(total_unit, axis=1, keepdims=True) * (1.0 / D)
        for c in range(PAIRS):
            lanes = slice(c * LANES, (c + 1) * LANES)
            e = r.sg[:, lanes] * r.vecs[0:1, lanes]
            r.sg[:, lanes] = inverse * (e - mean - r.acc[0, c] * mean_unit)
        branch_grad = r.sg[...].astype(BF16)
        load_att.wait()
        load_wout.wait()
        sums["in0"].sent_core(0)
        for block in range(ny):
            store_chunks(r.a_send.at[0, block], nn(r.att[rows_of(block, 1 - core), :], branch_grad))
        sums["out"].start(0)
        for block in range(ny):
            store_chunks(sums["out"].keep.at[0, block], nn(r.att[rows_of(block, core), :], branch_grad))
        load_tt.start()
        attended_grad = nt(branch_grad, r.wbuf[0])
        for c in range(PAIRS):
            r.acc[1, c] = attended_grad[:, c * LANES : (c + 1) * LANES]

    def pool_on(p):
        pool_core(p).wait_recv()
        for hop in range(1, ny):
            for which in range(2):
                r.p_keep[p, hop, which] = r.p_keep[p, hop, which] + r.p_in[p, hop, which]
            pool_y(p, hop).start()

    @pl.when((step >= ATTEND) & (step < LATE))
    def _():
        p = step - ATTEND
        r.gb[...] = (r.acc[1, p] * r.rp[...]).astype(BF16)
        delta = score_delta(r.gb[...], r.o[...])
        kp = jnp.concatenate([piece[0] for piece in kv], axis=0)
        kt = kp.T
        vp = jnp.concatenate([piece[1] for piece in kv], axis=0)
        wide = min(256, count)
        for head in range(2):
            for b in range(count // wide):
                cols = slice(b * wide, (b + 1) * wide)
                gh = head_half(r.gb[cols, :], head)
                qh = head_half(r.q[cols, :], head)
                low = r.pool_e[head, :, cols]
                dp = nt(vp, gh) - delta[head : head + 1, cols]
                ds = (low.astype(F32) * dp).astype(BF16)
                key_part = nn(ds, qh)
                value_part = nn(low, gh)
                if head == 0 and b == 0:
                    r.dk[0 : seq * size] = key_part
                    r.dv[0 : seq * size] = value_part
                else:
                    r.dk[0 : seq * size] += key_part
                    r.dv[0 : seq * size] += value_part
                r.dq_pool[p, head * 64 : head * 64 + 64, cols] = nn(kt[head * 64 : head * 64 + 64], ds)
        for i in range(pieces):
            target = r.p_keep if i < ny else r.p_send
            after = (((y + i % ny) % ny) * 2 + (core + i // ny) % 2 + 1) % seq
            index = ((after % 2 - core + 2) % 2) * ny + (after // 2 - y + ny) % ny
            rows = pl.ds(pl.multiple_of(index * size, size), EXTRA)
            for which, total in ((0, r.dk), (1, r.dv)):
                target[p, i % ny, which, 0:size] = total[i * size : (i + 1) * size].astype(BF16)
                target[p, i % ny, which, size:] = total[rows, :].astype(BF16)
        pool_core(p).start()

        @pl.when(p > 0)
        def _():
            pool_on(p - 1)

        run_plan(0)

        r.gb[...] = (r.acc[1, p] * r.rn[...]).astype(BF16)
        delta = score_delta(r.gb[...], r.o[...])
        kt = r.keys[...].T
        r.dk[0 : count + 2 * HALF] = jnp.zeros((count + 2 * HALF, LANES), F32)
        r.dv[0 : count + 2 * HALF] = jnp.zeros((count + 2 * HALF, LANES), F32)
        for b in range(count // QB):
            cols = slice(b * QB, (b + 1) * QB)
            keys = slice(b * QB, (b + 2) * QB)
            lows, scores, grads, queries, dqs = [], [], [], [], []
            for head in range(2):
                gh = head_half(r.gb[cols, :], head)
                low = r.near_e[head, b]
                dp = nt(r.values[keys, :], gh) - delta[head : head + 1, cols]
                ds = (low.astype(F32) * dp).astype(BF16)
                dqs.append(nn(kt[head * 64 : head * 64 + 64, keys], ds))
                lows.append(low)
                scores.append(ds)
                grads.append(gh)
                queries.append(head_half(r.q[cols, :], head))
            r.dk[keys, :] += nn(jnp.concatenate(scores, axis=1), jnp.concatenate(queries, axis=0))
            r.dv[keys, :] += nn(jnp.concatenate(lows, axis=1), jnp.concatenate(grads, axis=0))
            total = (jnp.concatenate(dqs, axis=0) + r.dq_pool[p, :, cols]) * 0.125
            lanes = pl.ds(pl.multiple_of(p * LANES, LANES), LANES)
            r.tbuf[0, cols, lanes] = total.T.astype(BF16)
        for which, total in ((0, r.dk), (1, r.dv)):
            r.h_out[p, 0, which] = total[0:HALF].astype(BF16)
            r.acc[which, p] = total[HALF : HALF + count]
            r.h_out[p, 1, which] = total[HALF + count : 2 * HALF + count].astype(BF16)

        @pl.when(here > 0)
        def _():
            halo(p, 0).start()

        @pl.when(here < seq - 1)
        def _():
            halo(p, 1).start()

        @pl.when(p == PAIRS - 1)
        def _():
            pool_on(p)

    @pl.when(step >= ATTEND + LAG)
    def _():
        p = step - ATTEND - LAG
        lanes = pl.ds(pl.multiple_of(p * LANES, LANES), LANES)
        for hop in range(1, ny):
            pool_y(p, hop).wait_recv()

        @pl.when(here < seq - 1)
        def _():
            halo(p, 0).wait_recv()
            for which in range(2):
                r.acc[which, p, count - HALF :, :] += r.h_in[p, 0, which].astype(F32)

        @pl.when(here > 0)
        def _():
            halo(p, 1).wait_recv()
            for which in range(2):
                r.acc[which, p, 0:HALF, :] += r.h_in[p, 1, which].astype(F32)

        moves = ((2, 0, 0), (3, 1, 0), (4, 2, 0), (0, 2, 1), (1, 3, 1))
        sums = [jnp.zeros((1, LANES), F32)] * 5
        for which, source in ((0, r.keys_late), (1, r.values_late)):
            grad = r.acc.at[which, p]
            r.cells[...] = source[...].astype(F32)
            total = r.p_keep[p, 0, which].astype(F32) + r.p_in[p, 0, which].astype(F32)
            for hop in range(1, ny):
                total = total + r.p_y[p, hop - 1, which].astype(F32)
            r.g[...] = total
            for tap, place, shift in moves:
                mask = r.masks[5 * shift + tap]
                spread = r.g[shift : shift + size, :] * mask * r.taps[tap : tap + 1, :]
                grad[pl.ds(place, size, stride=4), :] += spread
            for tap in range(5):
                taken = r.cells[pl.ds(HALF + tap - 2, size, stride=4), :]
                product = r.g[0:size, :] * r.masks[tap] * taken
                sums[tap] = sums[tap] + jnp.sum(product, axis=0, keepdims=True)
            r.tbuf[1 + which, :, lanes] = grad[...].astype(BF16)
        for tap in range(5):
            r.small[8 + tap : 9 + tap, lanes] = sums[tap]

    def key_gradients(part, first, last):
        for name, low in (("k" + part, 1), ("v" + part, 2)):
            for block in range(ny):
                rows = rows_of(block, 1 - core)
                store_chunks(senders[name].at[block], nn(r.lt[rows, :], r.tbuf[low, :, first:last]))
            sums[name].start(0)
            keep = sums[name].keep
            for block in range(ny):
                rows = rows_of(block, core)
                store_chunks(keep.at[0, block], nn(r.lt[rows, :], r.tbuf[low, :, first:last]))

    @pl.when(step == LATE)
    def _():
        key_gradients(*PARTS[0])

    @pl.when(step == LAST)
    def _():
        key_gradients(*PARTS[1])
        r.small_t[...] = r.small[...].T
        few = D // (seq * nz * nx)
        for block in range(ny):
            for part, mine in ((r.s_send.at[block], 1 - core), (sums["small"].keep.at[0, block], core)):
                vectors = r.small_t[rows_of(block, mine), :]
                for z in range(nz):
                    for x in range(nx):
                        start = (z * nx + x) * few
                        part[z, x] = jnp.zeros(part.shape[2:], BF16)
                        part[z, x, 0:few] = vectors[start : start + few].astype(BF16)
        sums["small"].start(0)

    run_plan(1)

    @pl.when(step == LAST)
    def _():
        reused = ["in0", "in1"]
        for name in sums:
            if name not in reused:
                sums[name].sent_core(0)
            sums[name].sent(0)
        for p in range(PAIRS):
            pool_core(p).wait_send()
            for hop in range(1, ny):
                pool_y(p, hop).wait_send()

        @pl.when(here > 0)
        def _():
            for p in range(PAIRS):
                halo(p, 0).wait_send()

        @pl.when(here < seq - 1)
        def _():
            for p in range(PAIRS):
                halo(p, 1).wait_send()


def unpack_kernel(t_in, t_back, t_query, t_ka, t_kb, t_va, t_vb, t_out, t_small, tg, *outs):
    tokens_grad, query, key, value, out, inn, back = outs[:7]
    rows = query.shape[0]
    tokens_grad[...] = tg[...]
    for source, target in ((t_query, query), (t_out, out)):
        target[...] = unfold_rows(source[...], rows)
    for one, two, target in ((t_ka, t_kb, key), (t_va, t_vb, value)):
        target[:, 0:SPLIT] = unfold_rows(one[...], rows)
        target[:, SPLIT:] = unfold_rows(two[...], rows)
    for u in range(CHUNKS):
        inn[:, u * D : (u + 1) * D] = unfold_rows(t_in[u], rows)
    units, part, wide = t_back.shape
    across = back.shape[1] // wide
    for u in range(units):
        top, start = (u // across) * part, (u % across) * wide
        back[top : top + part, start : start + wide] = t_back[u]
    small = t_small[...]
    pad = LANES - small.shape[0]
    turned = jnp.concatenate([small, jnp.zeros((pad, LANES), F32)], axis=0).T
    for i in range(4):
        outs[7 + i][...] = turned[i : i + 1, 0:rows]
    outs[11][...] = turned[8:13, 0:rows]


def call(kernel, args, in_specs, outs, out_specs, grid, scratch, flops, name):
    moved = sum(a.size * a.dtype.itemsize for a in list(args) + list(outs))
    return pl.pallas_call(
        kernel,
        grid_spec=pltpu.PrefetchScalarGridSpec(
            num_scalar_prefetch=0,
            grid=grid,
            in_specs=in_specs,
            out_specs=out_specs,
            scratch_shapes=scratch,
        ),
        out_shape=outs,
        compiler_params=pltpu.CompilerParams(
            vmem_limit_bytes=60 * MB, dimension_semantics=("arbitrary",) * len(grid)
        ),
        cost_estimate=pl.CostEstimate(flops=flops, bytes_accessed=moved, transcendentals=0),
        name=name,
    )(*args)


def whole(array):
    rank = len(array.shape)
    return pl.BlockSpec(array.shape, lambda i: (0,) * rank)


def columns(array, width=LANES):
    rank = len(array.shape)
    return pl.BlockSpec(array.shape[:-1] + (width,), lambda i: (0,) * (rank - 1) + (i,))


def leading(array, size):
    rank = len(array.shape)
    return pl.BlockSpec((size,) + array.shape[1:], lambda i: (i,) + (0,) * (rank - 1))


def per_device(
    tokens,
    item_lengths,
    w_query,
    w_key,
    w_value,
    w_out,
    w_in,
    w_back,
    norm1_gain,
    norm1_bias,
    norm2_gain,
    norm2_bias,
    pool_weight,
    out_grad,
):
    _, count, _ = tokens.shape
    seq = lax.axis_size("seq")
    ny = seq // 2
    row_len = count * seq
    span = count + 2 * HALF
    size = count // 4
    tok = tokens[0]
    og = out_grad[0]
    taps = pool_weight.T
    vecs = jnp.stack([norm1_gain, norm1_bias, norm2_gain, norm2_bias])

    def shape(dims, kind):
        return jax.ShapeDtypeStruct(dims, kind)

    blocks = count // QB
    pool_all = seq * size
    anywhere = pl.BlockSpec(memory_space=pl.ANY)

    def in_first(i):
        return jnp.clip(i - FORWARD_NEAR, 0, PAIRS - 1)

    def in_second(i):
        return jnp.clip(i - FORWARD_POOL, 0, PAIRS - 1)

    ins = [
        ("lengths", item_lengths, pl.BlockSpec(memory_space=pltpu.SMEM)),
        ("pool_weight", taps, whole(taps)),
        ("tok", tok, anywhere),
        ("wq_any", w_query, anywhere),
        ("wk_any", w_key, anywhere),
        ("wv_any", w_value, anywhere),
    ]
    near_shape = shape((H, blocks, 2 * QB, QB), BF16)
    pool_shape = shape((H, pool_all, count), BF16)
    wide_shape = shape((count, D), F32)
    outs = [
        ("q_out", shape((count, D), BF16), anywhere),
        ("k_out", shape((span, D), BF16), anywhere),
        ("v_out", shape((span, D), BF16), anywhere),
        ("tt_out", shape((D, count), BF16), anywhere),
        ("mask_out", shape((7, size, LANES), F32), anywhere),
        ("pieces_out", shape((seq, 2, size, D), BF16), anywhere),
        ("near_e", near_shape, pl.BlockSpec((2, blocks, 2 * QB, QB), lambda i: (in_first(i), 0, 0, 0))),
        ("pool_e", pool_shape, pl.BlockSpec((2, pool_all, count), lambda i: (in_second(i), 0, 0))),
        ("o_out", wide_shape, pl.BlockSpec((count, LANES), lambda i: (0, in_second(i)))),
        ("rn_out", wide_shape, pl.BlockSpec((count, LANES), lambda i: (0, in_second(i)))),
        ("rp_out", wide_shape, pl.BlockSpec((count, LANES), lambda i: (0, in_second(i)))),
    ]
    scratch = [
        ("x", pltpu.VMEM((span, D), BF16)),
        ("wq", pltpu.VMEM((D, D), BF16)),
        ("wk", pltpu.VMEM((D, D), BF16)),
        ("wv", pltpu.VMEM((D, D), BF16)),
        ("qs", pltpu.VMEM((count, D), BF16)),
        ("ks", pltpu.VMEM((span, D), BF16)),
        ("vs", pltpu.VMEM((span, D), BF16)),
        ("tt", pltpu.VMEM((D, count), BF16)),
        ("mask", pltpu.VMEM((7, size, LANES), F32)),
        ("cells", pltpu.VMEM((PAIRS, span, LANES), F32)),
        ("pieces", pltpu.VMEM((seq, 2, size, D), BF16)),
        ("o_near", pltpu.VMEM((PAIRS, LANES, count), F32)),
        ("stats", pltpu.VMEM((PAIRS, 8, count), F32)),
        ("near_bias", pltpu.VMEM((blocks, 2 * QB, QB), F32)),
        ("pool_bias", pltpu.VMEM((pool_all, count), F32)),
        ("s_sem", pltpu.SemaphoreType.DMA((2 + seq,))),
        ("r_sem", pltpu.SemaphoreType.DMA((2 + seq,))),
        ("l_sem", pltpu.SemaphoreType.DMA((11,))),
    ]
    (queries, keys, values, tok_t, tap_masks, pieces, near_e, pool_e, attention, near_scale, pool_scale) = (
        pl.pallas_call(
            partial(forward_kernel, names=[entry[0] for entry in ins + outs + scratch]),
            grid_spec=pltpu.PrefetchScalarGridSpec(
                num_scalar_prefetch=0,
                grid=(FORWARD_LAST + 1,),
                in_specs=[entry[2] for entry in ins],
                out_specs=[entry[2] for entry in outs],
                scratch_shapes=[entry[1] for entry in scratch],
            ),
            out_shape=[entry[1] for entry in outs],
            compiler_params=pltpu.CompilerParams(
                collective_id=1,
                has_side_effects=True,
                vmem_limit_bytes=60 * MB,
                dimension_semantics=("arbitrary",),
            ),
            cost_estimate=pl.CostEstimate(
                flops=4 * H * 768 * 256 * count + 6 * count * D * D, bytes_accessed=16 * MB, transcendentals=0
            ),
            name="forward",
        )(*[entry[1] for entry in ins])
    )

    dp = lax.axis_size("dp")
    nx = 2 if dp % 2 == 0 else 1
    nz = dp // nx
    rows = D // (seq * dp)
    back_rows = FF // (seq * dp)
    down = 2 if back_rows % 32 == 0 else 1
    half_one = shape((ny, nz, nx) + folded(rows, D), BF16)
    half_back = shape((2 * down, ny, nz, nx, back_rows // down, D // 2), BF16)
    args = (attention, tok, og, vecs, w_out, w_in, w_back)
    outs = (
        shape((count, D), BF16),
        shape((count, FF), BF16),
        shape((count, FF), BF16),
        shape((D, count), BF16),
        shape((count, D), BF16),
        shape((count, D), F32),
        shape((PAIRS, count, LANES), F32),
        shape((count, LANES), F32),
        shape((D, count), BF16),
        shape((8, D), F32),
    )
    mixed, act, slope, low_t, feed_grad, z_grad, unit_one, inv_one, att_t, sums = call(
        dense_kernel,
        args,
        [whole(a) for a in args[:5]]
        + [columns(w_in, D), pl.BlockSpec((D, D), lambda i: (i, 0))],
        outs,
        [whole(outs[0]), columns(outs[1], D), columns(outs[2], D)] + [whole(a) for a in outs[3:]],
        (CHUNKS,),
        [
            pltpu.VMEM((count, D), F32),
            pltpu.VMEM((count, D), BF16),
            pltpu.VMEM((count, D), F32),
        ],
        2 * count * (D * D + 2 * D * FF),
        "dense",
    )
    half_small = shape((ny, nz, nx, -(-rows // 16) * 16, LANES), BF16)
    half_pool = (PAIRS, ny, 2, size + EXTRA, LANES)
    blocks_in = []

    def block(name, array, spec):
        blocks_in.append((name, array, spec))

    def col_spec(array, index):
        lead = (0,) * (len(array.shape) - 1)
        return pl.BlockSpec(array.shape[:-1] + (LANES,), lambda i: lead + (index(i),))

    def lead_spec(array, index):
        rest = (0,) * (len(array.shape) - 1)
        return pl.BlockSpec((2,) + array.shape[1:], lambda i: (index(i),) + rest)

    def all_spec(array):
        rest = (0,) * len(array.shape)
        return pl.BlockSpec(array.shape, lambda i: rest)

    def in_pair(i):
        return jnp.clip(i - ATTEND, 0, PAIRS - 1)

    def in_late(i):
        return jnp.clip(i - ATTEND - LAG, 0, PAIRS - 1)

    block("q", queries, col_spec(queries, in_pair))
    block("o", attention, col_spec(attention, in_pair))
    block("rp", pool_scale, col_spec(pool_scale, in_pair))
    block("rn", near_scale, col_spec(near_scale, in_pair))
    block("pool_e", pool_e, lead_spec(pool_e, in_pair))
    block("near_e", near_e, lead_spec(near_e, in_pair))
    block("keys", keys, col_spec(keys, in_pair))
    block("values", values, col_spec(values, in_pair))
    block("keys_late", keys, col_spec(keys, in_late))
    block("values_late", values, col_spec(values, in_late))
    block("piece", pieces, col_spec(pieces, in_pair))
    block("masks", tap_masks, all_spec(tap_masks))
    block("taps", taps, col_spec(taps, in_late))
    block("sums", sums, all_spec(sums))
    block("vecs", vecs, all_spec(vecs))
    block("inv", inv_one, all_spec(inv_one))
    for name, array in (
        ("win_any", w_in),
        ("wback_any", w_back),
        ("act_any", act),
        ("slope_any", slope),
        ("fg_any", feed_grad),
        ("lowt_any", low_t),
        ("zg_any", z_grad),
        ("unit_any", unit_one),
        ("wout_any", w_out),
        ("att_any", att_t),
        ("tt_any", tok_t),
        ("wq_any", w_query),
        ("wk_any", w_key),
        ("wv_any", w_value),
    ):
        block(name, array, anywhere)
    outs = [
        ("t_in", shape((CHUNKS,) + half_one.shape[3:], F32)),
        ("t_back", shape((half_back.shape[0],) + half_back.shape[4:], F32)),
        ("t_query", shape(half_one.shape[3:], F32)),
        ("t_kA", shape(folded(rows, SPLIT), F32)),
        ("t_kB", shape(folded(rows, D - SPLIT), F32)),
        ("t_vA", shape(folded(rows, SPLIT), F32)),
        ("t_vB", shape(folded(rows, D - SPLIT), F32)),
        ("t_out", shape(half_one.shape[3:], F32)),
        ("t_small", shape(half_small.shape[3:], F32)),
        ("tokens_grad", shape((count, D), BF16)),
    ]
    tall = max(pool_all, span)
    scratch = [
        ("dk", pltpu.VMEM((tall, LANES), F32)),
        ("dv", pltpu.VMEM((tall, LANES), F32)),
        ("dq_pool", pltpu.VMEM((PAIRS, LANES, count), F32)),
        ("gb", pltpu.VMEM((count, LANES), BF16)),
        ("acc", pltpu.VMEM((2, PAIRS, count, LANES), F32)),
        ("tbuf", pltpu.VMEM((4, count, D), BF16)),
        ("wbuf", pltpu.VMEM((4, D, D), BF16)),
        ("fg", pltpu.VMEM((count, D), BF16)),
        ("lt", pltpu.VMEM((D, count), BF16)),
        ("att", pltpu.VMEM((D, count), BF16)),
        ("cells", pltpu.VMEM((span, LANES), F32)),
        ("g", pltpu.VMEM((size + EXTRA, LANES), F32)),
        ("small", pltpu.VMEM((LANES, D), F32)),
        ("small_t", pltpu.VMEM((D, LANES), F32)),
        ("p_keep", pltpu.VMEM(half_pool, BF16)),
        ("p_send", pltpu.VMEM(half_pool, BF16)),
        ("p_in", pltpu.VMEM(half_pool, BF16)),
        ("p_y", pltpu.VMEM((PAIRS, ny - 1) + half_pool[2:], BF16)),
        ("h_out", pltpu.VMEM((PAIRS, 2, 2, HALF, LANES), BF16)),
        ("h_in", pltpu.VMEM((PAIRS, 2, 2, HALF, LANES), BF16)),
        ("p_sem", pltpu.SemaphoreType.DMA((2, PAIRS, ny))),
        ("h_sem", pltpu.SemaphoreType.DMA((2, PAIRS, 2))),
        ("l_sem", pltpu.SemaphoreType.DMA((9, 2))),
        ("sg", pltpu.VMEM((count, D), F32)),
        ("a_send", pltpu.VMEM((CHUNKS,) + half_one.shape, BF16)),
        ("b_send", pltpu.VMEM(half_back.shape, BF16)),
        ("s_send", pltpu.VMEM(half_small.shape, BF16)),
    ]
    sizes = {name: half_one.shape for name in ORDERS}
    sizes["small"] = half_small.shape
    for part, first, after in PARTS:
        for name in ("k" + part, "v" + part):
            sizes[name] = half_one.shape[:3] + folded(rows, after - first)
            scratch.append((name + "_send", pltpu.VMEM(sizes[name], BF16)))
    for u in range(CHUNKS):
        if u < half_back.shape[0]:
            sizes["b%d" % u] = half_back.shape[1:]
        else:
            del sizes["b%d" % u]
    for name, dims in sizes.items():
        bufs = summed_scratch(1, dims, ORDERS[name])
        scratch += [(name + "_" + part, buf) for part, buf in zip(BUFFERS, bufs)]
    names = [entry[0] for entry in blocks_in] + [entry[0] for entry in outs + scratch]
    moved = sum(entry[1].size * entry[1].dtype.itemsize for entry in blocks_in)
    totals = pl.pallas_call(
        partial(backward_kernel, names=names, pieces=seq),
        grid_spec=pltpu.PrefetchScalarGridSpec(
            num_scalar_prefetch=0,
            grid=(LAST + 1,),
            in_specs=[entry[2] for entry in blocks_in],
            out_specs=[all_spec(entry[1]) for entry in outs],
            scratch_shapes=[entry[1] for entry in scratch],
        ),
        out_shape=[entry[1] for entry in outs],
        compiler_params=pltpu.CompilerParams(
            collective_id=0,
            has_side_effects=True,
            vmem_limit_bytes=63 * MB,
            dimension_semantics=("arbitrary",),
        ),
        cost_estimate=pl.CostEstimate(
            flops=8 * H * 768 * 256 * count + 12 * count * D * D + 8 * count * D * FF, bytes_accessed=moved, transcendentals=0
        ),
        name="backward",
    )(*[entry[1] for entry in blocks_in])

    outs = (
        shape((count, D), BF16),
        shape((rows, D), F32),
        shape((rows, D), F32),
        shape((rows, D), F32),
        shape((rows, D), F32),
        shape((rows, FF), F32),
        shape((back_rows, D), F32),
        shape((1, rows), F32),
        shape((1, rows), F32),
        shape((1, rows), F32),
        shape((1, rows), F32),
        shape((5, rows), F32),
    )
    done = call(
        unpack_kernel,
        tuple(totals),
        [whole(a) for a in totals],
        outs,
        [whole(a) for a in outs],
        (1,),
        [],
        0,
        "unpack",
    )
    return (
        mixed[None],
        done[0][None],
        done[1],
        done[2],
        done[3],
        done[4],
        done[5],
        done[6],
        done[7].reshape(rows),
        done[8].reshape(rows),
        done[9].reshape(rows),
        done[10].reshape(rows),
        done[11].T,
    )


def solution(mesh):
    shards, copied = P("dp", "seq", None), P()
    spread = P(("seq", "dp"), None)
    vector = P(("seq", "dp"))
    return jax.shard_map(
        per_device,
        mesh=mesh,
        in_specs=(shards, P("dp", None)) + (copied,) * 11 + (shards,),
        out_specs=(shards, shards) + (spread,) * 6 + (vector,) * 4 + (spread,),
        check_vma=False,
    )
```

```python
import itertools
from functools import partial

import jax
import jax.numpy as jnp
from jax import lax
from jax.experimental import pallas as pl
from jax.experimental.pallas import tpu as pltpu
from jax.sharding import PartitionSpec as P

D = 768
FF = 3072
H = 12
PAIRS = H // 2
HALF = 64
PWIN = 512
QB = 128
EXTRA = 16
LANES = 128
BF16 = jnp.bfloat16
F32 = jnp.float32
MB = 1 << 20


def nn(left, right):
    return jnp.dot(left, right, preferred_element_type=F32)


def nt(left, right, precision=None):
    return lax.dot_general(
        left, right, (((1,), (1,)), ((), ())), preferred_element_type=F32, precision=precision
    )


def iota(shape, dim):
    return lax.broadcasted_iota(jnp.int32, shape, dim)


def segment_of(ends, place, row_len):
    item = jnp.zeros_like(place)
    for end in ends:
        item = item + (place >= end).astype(jnp.int32)
    return jnp.where((place >= 0) & (place < row_len), item, -2)


def head_half(block, head):
    lane = iota(block.shape, 1)
    return jnp.where((lane < 64) == (head == 0), block, jnp.zeros_like(block))


def tap_mask(ends, start, tap, shift, count, row_len):
    center = start + 4 * (iota((count, 1), 0) + shift)
    same = segment_of(ends, center + tap - 2, row_len) == segment_of(ends, center, row_len)
    return (same & (center < row_len)).astype(F32)


def folds(rows, width):
    return 2 if rows % 16 and rows % 8 == 0 and (width // 2) % LANES == 0 else 1


def folded(rows, width):
    fold = folds(rows, width)
    return (rows * fold, width // fold)


def fold_rows(block):
    rows, width = block.shape
    fold = folds(rows, width)
    part = width // fold
    return jnp.concatenate([block[:, i * part : (i + 1) * part] for i in range(fold)], axis=0)


def unfold_rows(block, rows):
    fold = block.shape[0] // rows
    return jnp.concatenate([block[i * rows : (i + 1) * rows] for i in range(fold)], axis=1)


def store_chunks(target, total):
    nz, nx = target.shape[0], target.shape[1]
    rows = total.shape[0] // (nz * nx)
    for z in range(nz):
        for x in range(nx):
            start = (z * nx + x) * rows
            target[z, x] = fold_rows(total[start : start + rows]).astype(BF16)


def store_blocks(targets, block, total):
    _, nz, nx, part, wide = targets[0].shape
    rows = total.shape[0] // (nz * nx)
    across = total.shape[1] // wide
    for z in range(nz):
        for x in range(nx):
            start = (z * nx + x) * rows
            for unit, target in enumerate(targets):
                top = start + (unit // across) * part
                left = (unit % across) * wide
                target[block, z, x] = total[top : top + part, left : left + wide].astype(BF16)


def normal_parts(v):
    bell = jnp.exp(v * v * -0.5)
    t = 1.0 / (1.0 + jnp.abs(v) * (0.3275911 * 0.7071067811865476))
    poly = t * (
        0.127414796 + t * (-0.142248368 + t * (0.7107068705 + t * (-0.7265760135 + t * 0.5307027145)))
    )
    tail = poly * bell
    return jnp.where(v < 0, tail, 1.0 - tail), v * bell * 0.3989422804014327


def normalized(values):
    shifted = values - jnp.mean(values, axis=1, keepdims=True)
    inverse = lax.rsqrt(jnp.mean(shifted * shifted, axis=1, keepdims=True) + 1e-05)
    return shifted * inverse, inverse


def dense_kernel(
    o, tok, og, vecs, w_out, w_in, w_back,
    mixed, act, slope, low_t, feed_grad, z_grad, unit_out, inv_out, att_t, sums,
    first, low, feed,
):
    step = pl.program_id(0)
    gain_one, bias_one = vecs[0:1, :], vecs[1:2, :]
    gain_two, bias_two = vecs[2:3, :], vecs[3:4, :]

    @pl.when(step == 0)
    def _():
        att = o[...].astype(BF16)
        att_t[...] = att.T
        unit, inverse = normalized(tok[...].astype(F32) + nn(att, w_out[...]))
        for c in range(PAIRS):
            unit_out[c] = unit[:, c * LANES : (c + 1) * LANES]
        inv_out[...] = jnp.broadcast_to(inverse, inv_out.shape)
        first[...] = unit * gain_one + bias_one
        low[...] = first[...].astype(BF16)
        low_t[...] = low[...].T
        feed[...] = jnp.zeros_like(feed)

    inner = nn(low[...], w_in[...])
    phi, bell = normal_parts(inner)
    act[...] = (inner * phi).astype(BF16)
    slope[...] = (phi + bell).astype(BF16)
    feed[...] += nn(act[...], w_back[...])

    @pl.when(step == CHUNKS - 1)
    def _():
        unit, inverse = normalized(first[...] + feed[...])
        mixed[...] = (unit * gain_two + bias_two).astype(BF16)
        upstream = og[...].astype(F32)
        sums[...] = jnp.zeros_like(sums)
        sums[2:3] = jnp.sum(upstream * unit, axis=0, keepdims=True)
        sums[3:4] = jnp.sum(upstream, axis=0, keepdims=True)
        e = upstream * gain_two
        centred = e - jnp.mean(e, axis=1, keepdims=True)
        total = inverse * (centred - unit * jnp.mean(e * unit, axis=1, keepdims=True))
        z_grad[...] = total
        feed_grad[...] = total.astype(BF16)


def score_delta(grad, attended):
    pick = ((iota((8, LANES), 1) // 64) == iota((8, LANES), 0)).astype(F32)
    return nt(pick, grad.astype(F32) * attended, precision=lax.Precision.HIGHEST)


def hop_pairs(axis, count, stride, hop):
    pairs = []
    for device in range(lax.axis_size(axis)):
        place = (device // stride) % count
        pairs.append((device, device + ((place + hop) % count - place) * stride))
    return pairs


MESH_ID = pl.DeviceIdType.MESH


class Summed:
    def __init__(self, order, send_of, keep, core_in, first, second, third, out_sem, in_sem):
        self.order, self.send_of = order, send_of
        self.keep, self.core_in = keep, core_in
        self.bufs = (first, second, third)
        self.out_sem, self.in_sem = out_sem, in_sem
        self.units = keep.shape[0]
        self.count = dict(zip("yzx", keep.shape[1:4]))
        self.here, self.row = lax.axis_index("seq"), lax.axis_index("dp")
        self.mine = self.here % 2
        nx = self.count["x"]
        self.own = {"y": self.here // 2, "z": self.row // nx, "x": self.row % nx}
        self.base = {"y": 1}
        self.base["x"] = self.base["y"] + self.count["y"] - 1
        self.base["z"] = self.base["x"] + nx - 1

    def copy(self, u, src, dst, slot, device):
        return pltpu.make_async_remote_copy(
            src_ref=src,
            dst_ref=dst,
            send_sem=self.out_sem.at[u, slot],
            recv_sem=self.in_sem.at[u, slot],
            device_id=device,
            device_id_type=MESH_ID,
        )

    def core_copy(self, u):
        partner = (self.own["y"] * 2 + 1 - self.mine, self.row)
        return self.copy(u, self.send_of(u), self.core_in.at[u], 0, partner)

    def hop_copy(self, u, stage, hop):
        axis = self.order[stage]
        other = (self.own[axis] + hop) % self.count[axis]
        place = dict(self.own)
        place[axis] = other
        device = (place["y"] * 2 + self.mine, place["z"] * self.count["x"] + place["x"])
        index = []
        for dim in "yzx":
            known = dim in self.order[: stage + 1]
            index.append(place[dim] if known else slice(None))
        source = self.keep.at[(u,) + tuple(index)]
        slot = self.base[axis] + hop - 1
        return self.copy(u, source, self.bufs[stage].at[u, hop - 1], slot, device)

    def hops(self, stage):
        return range(1, self.count[self.order[stage]])

    def start(self, u):
        self.core_copy(u).start()

    def core(self, u):
        self.core_copy(u).wait_recv()
        for y in range(self.count["y"]):
            for z in range(self.count["z"]):
                self.keep[u, y, z] = self.keep[u, y, z] + self.core_in[u, y, z]
        for hop in self.hops(0):
            self.hop_copy(u, 0, hop).start()

    def add(self, u, stage):
        left = [dim for dim in "yzx" if dim not in self.order[: stage + 1]]
        for hop in self.hops(stage):
            self.hop_copy(u, stage, hop).wait_recv()
            for place in itertools.product(*[range(self.count[dim]) for dim in left]):
                at = dict(self.own)
                at.update(zip(left, place))
                index = (u,) + tuple(at[dim] for dim in "yzx")
                self.keep[index] = self.keep[index] + self.bufs[stage][(u, hop - 1) + place]
        for hop in self.hops(stage + 1):
            self.hop_copy(u, stage + 1, hop).start()

    def one(self, u):
        self.add(u, 0)

    def two(self, u):
        self.add(u, 1)

    def three(self, u):
        total = self.keep[(u,) + tuple(self.own[dim] for dim in "yzx")].astype(F32)
        for hop in self.hops(2):
            self.hop_copy(u, 2, hop).wait_recv()
            total = total + self.bufs[2][u, hop - 1].astype(F32)
        return total

    def sent_core(self, u):
        self.core_copy(u).wait_send()

    def sent(self, u):
        for stage in range(3):
            for hop in self.hops(stage):
                self.hop_copy(u, stage, hop).wait_send()


def summed_scratch(units, shape, order):
    count = dict(zip("yzx", shape[:3]))
    chunk = shape[3:]
    bufs = [pltpu.VMEM((units,) + shape, BF16), pltpu.VMEM((units,) + shape, BF16)]
    for stage in range(3):
        left = tuple(count[dim] for dim in "yzx" if dim not in order[: stage + 1])
        bufs.append(pltpu.VMEM((units, max(count[order[stage]] - 1, 1)) + left + chunk, BF16))
    slots = count["y"] + count["x"] + count["z"] - 2
    bufs += [pltpu.SemaphoreType.DMA((units, slots)), pltpu.SemaphoreType.DMA((units, slots))]
    return bufs


def greet(peers):
    barrier = pltpu.get_barrier_semaphore()
    for peer in peers:
        pl.semaphore_signal(barrier, inc=1, device_id=peer, device_id_type=MESH_ID)
    pl.semaphore_wait(barrier, len(peers))


class Refs:
    pass


FORWARD_NEAR = 1
FORWARD_POOL = 1 + PAIRS
FORWARD_LAST = 2 * PAIRS


def forward_kernel(*refs, names):
    r = Refs()
    for name, ref in zip(names, refs):
        setattr(r, name, ref)
    seq, _, size, _ = r.pieces.shape
    ny = seq // 2
    count, row_len = 4 * size, 4 * size * seq
    span = count + 2 * HALF
    step = pl.program_id(0)
    here, row = lax.axis_index("seq"), lax.axis_index("dp")
    y, core = here // 2, here % 2
    start = here * count
    partner = (y * 2 + 1 - core, row)
    right, left = ((here + 1) % seq, row), ((here + seq - 1) % seq, row)
    ends = [r.lengths[0, 0]]
    for m in range(1, 4):
        ends.append(ends[-1] + r.lengths[0, m])

    def copy(src, dst, slot, device):
        return pltpu.make_async_remote_copy(
            src_ref=src, dst_ref=dst, send_sem=r.s_sem.at[slot], recv_sem=r.r_sem.at[slot],
            device_id=device, device_id_type=MESH_ID,
        )

    own = r.x.at[HALF : HALF + count]
    to_right = copy(r.tok.at[count - HALF :], r.x.at[0:HALF], 0, right)
    to_left = copy(r.tok.at[0:HALF], r.x.at[HALF + count :], 1, left)

    def to_y(hop):
        device = (((y + hop) % ny) * 2 + core, row)
        return copy(r.pieces.at[0], r.pieces.at[ny - hop], 1 + hop, device)

    def to_core(hop):
        return copy(r.pieces.at[hop], r.pieces.at[ny + hop], 1 + ny + hop, partner)

    loads = [
        pltpu.make_async_copy(r.tok, own, r.l_sem.at[0]),
        pltpu.make_async_copy(r.wk_any, r.wk, r.l_sem.at[1]),
        pltpu.make_async_copy(r.wv_any, r.wv, r.l_sem.at[2]),
        pltpu.make_async_copy(r.wq_any, r.wq, r.l_sem.at[3]),
    ]
    stores = [
        pltpu.make_async_copy(r.qs, r.q_out, r.l_sem.at[4]),
        pltpu.make_async_copy(r.ks, r.k_out, r.l_sem.at[5]),
        pltpu.make_async_copy(r.vs, r.v_out, r.l_sem.at[6]),
        pltpu.make_async_copy(r.tt, r.tt_out, r.l_sem.at[7]),
        pltpu.make_async_copy(r.mask, r.mask_out, r.l_sem.at[8]),
    ]
    store_pieces = pltpu.make_async_copy(r.pieces, r.pieces_out, r.l_sem.at[10])

    @pl.when(step == 0)
    def _():
        for load in loads:
            load.start()
        greet([partner, right, left] + [(((y + hop) % ny) * 2 + core, row) for hop in range(1, ny)])

        @pl.when(here < seq - 1)
        def _():
            to_right.start()

        @pl.when(here > 0)
        def _():
            to_left.start()

        @pl.when(here == 0)
        def _():
            r.x[0:HALF] = jnp.zeros((HALF, D), BF16)

        @pl.when(here == seq - 1)
        def _():
            r.x[HALF + count :] = jnp.zeros((HALF, D), BF16)

        for i in range(7):
            mask = tap_mask(ends, start, i % 5, i // 5, size, row_len)
            r.mask[i] = jnp.broadcast_to(mask, (size, LANES))
        loads[0].wait()
        inner = slice(HALF, HALF + count)
        for weight, load, cells in ((r.wk, loads[1], r.ks), (r.wv, loads[2], r.vs)):
            load.wait()
            cells[inner] = nn(r.x[inner], weight[...]).astype(BF16)

        @pl.when(here > 0)
        def _():
            to_right.wait_recv()

        @pl.when(here < seq - 1)
        def _():
            to_left.wait_recv()

        for weight, cells in ((r.wk, r.ks), (r.wv, r.vs)):
            for outer in (slice(0, HALF), slice(HALF + count, span)):
                cells[outer] = nn(r.x[outer], weight[...]).astype(BF16)
        for which, source in ((0, r.ks), (1, r.vs)):
            for c in range(PAIRS):
                lanes = slice(c * LANES, (c + 1) * LANES)
                r.cells[c] = source[:, lanes].astype(F32)
                total = jnp.zeros((size, LANES), F32)
                for tap in range(5):
                    taken = r.cells.at[c][pl.ds(HALF + tap - 2, size, stride=4), :]
                    total = total + taken * r.mask[tap] * r.pool_weight[tap : tap + 1, lanes]
                r.pieces[0, which, :, lanes] = total.astype(BF16)
        for hop in range(1, ny):
            to_y(hop).start()
        to_core(0).start()
        loads[3].wait()
        r.qs[...] = (nn(r.x[inner], r.wq[...]).astype(BF16).astype(F32) * 0.125).astype(BF16)
        r.tt[...] = r.x[inner].T
        for store in stores:
            store.start()
        for b in range(count // QB):
            query_place = start + b * QB + iota((1, QB), 1)
            key_place = start - HALF + b * QB + iota((2 * QB, 1), 0)
            same = segment_of(ends, key_place, row_len) == segment_of(ends, query_place, row_len)
            near = jnp.abs(key_place - query_place) <= HALF
            r.near_bias[b] = jnp.where(same & near, 0.0, -1e30)

    @pl.when((step >= FORWARD_NEAR) & (step < FORWARD_POOL))
    def _():
        p = step - FORWARD_NEAR
        lanes = pl.ds(pl.multiple_of(p * LANES, LANES), LANES)
        vt = r.vs[:, lanes].T
        ones = jnp.ones((16, span), BF16)
        for head in range(2):
            qh = head_half(r.qs[:, lanes], head)
            va = jnp.concatenate([vt[head * 64 : head * 64 + 64], ones], axis=0)
            for b in range(count // QB):
                cols = slice(b * QB, (b + 1) * QB)
                keys = slice(b * QB, (b + 2) * QB)
                s = nt(r.ks[keys, lanes], qh[cols]) + r.near_bias[b]
                top = jnp.max(s, axis=0, keepdims=True)
                e = jnp.exp(s - top).astype(BF16)
                r.near_e[head, b] = e
                oa = nn(va[:, keys], e)
                r.o_near[p, head * 64 : head * 64 + 64, cols] = oa[:64]
                r.stats[p, head : head + 1, cols] = top
                r.stats[p, 2 + head : 3 + head, cols] = oa[64:65]

    @pl.when(step == FORWARD_POOL - 2)
    def _():
        query_place = start + iota((1, count), 1)
        query_item = segment_of(ends, query_place, row_len)
        for i in range(seq):
            owner = ((y + i % ny) % ny) * 2 + (core + i // ny) % 2
            key_place = 4 * (owner * size + iota((size, 1), 0))
            same = segment_of(ends, key_place, row_len) == query_item
            near = jnp.abs(key_place - query_place) <= 2 * PWIN
            r.pool_bias[i * size : (i + 1) * size] = jnp.where(same & near, 0.0, -1e30)

    @pl.when(step == FORWARD_POOL - 1)
    def _():
        for hop in range(1, ny):
            to_y(ny - hop).wait_recv()
            to_core(hop).start()

    @pl.when(step == FORWARD_POOL)
    def _():
        for hop in range(ny):
            to_core(hop).wait_recv()
        store_pieces.start()

    @pl.when(step >= FORWARD_POOL)
    def _():
        p = step - FORWARD_POOL
        lanes = pl.ds(pl.multiple_of(p * LANES, LANES), LANES)
        kp = jnp.concatenate([r.pieces[i, 0, :, lanes] for i in range(seq)], axis=0)
        vt = jnp.concatenate([r.pieces[i, 1, :, lanes] for i in range(seq)], axis=0).T
        ones = jnp.ones((16, seq * size), BF16)
        wide = min(256, count)
        for b in range(count // wide):
            cols = slice(b * wide, (b + 1) * wide)
            outs, near_scale, pool_scale = [], [], []
            for head in range(2):
                qh = head_half(r.qs[cols, lanes], head)
                va = jnp.concatenate([vt[head * 64 : head * 64 + 64], ones], axis=0)
                s = nt(kp, qh) + r.pool_bias[:, cols]
                near_top = r.stats[p, head : head + 1, cols]
                top = jnp.maximum(jnp.max(s, axis=0, keepdims=True), near_top)
                e = jnp.exp(s - top).astype(BF16)
                r.pool_e[head, :, cols] = e
                oa = nn(va, e)
                fade = jnp.exp(near_top - top)
                inverse = 1.0 / (fade * r.stats[p, 2 + head : 3 + head, cols] + oa[64:65])
                rows = slice(head * 64, head * 64 + 64)
                outs.append((fade * r.o_near[p, rows, cols] + oa[:64]) * inverse)
                near_scale.append(jnp.broadcast_to(fade * inverse, (64, wide)))
                pool_scale.append(jnp.broadcast_to(inverse, (64, wide)))
            r.o_out[cols, :] = jnp.concatenate(outs, axis=0).T
            r.rn_out[cols, :] = jnp.concatenate(near_scale, axis=0).T
            r.rp_out[cols, :] = jnp.concatenate(pool_scale, axis=0).T

    @pl.when(step == FORWARD_LAST)
    def _():
        for store in stores + [store_pieces]:
            store.wait()
        for hop in range(1, ny):
            to_y(hop).wait_send()
        for hop in range(ny):
            to_core(hop).wait_send()

        @pl.when(here < seq - 1)
        def _():
            to_right.wait_send()

        @pl.when(here > 0)
        def _():
            to_left.wait_send()


CHUNKS = FF // D
BUFFERS = ("sum", "core", "first", "second", "third", "out", "inn")
ATTEND = CHUNKS + 1
LAG = 3
LATE = ATTEND + PAIRS
LAST = LATE + LAG - 1
SPLIT = 4 * LANES
PARTS = (("A", 0, SPLIT), ("B", SPLIT, D))
NAMES = ("in0", "in1", "in2", "in3", "b0", "b1", "b2", "b3", "out", "q", "kA", "vA", "kB", "vB", "small", "query", "tokens")
(IN0, IN1, IN2, IN3, B0, B1, B2, B3, OUT, Q, KA, VA, KB, VB, SMALL, QUERY, TOKENS) = range(17)
XYZ = "xyz"
XZY = "xzy"
YXZ = "yxz"
YZX = "yzx"
ZXY = "zxy"
ZYX = "zyx"
ORDERS = dict(zip(NAMES, (ZYX, XZY, XZY, YXZ, ZXY, XZY, YXZ, XYZ, XYZ, XYZ, XYZ, YXZ, ZXY, XZY, YZX)))
PLAN = {
    (1, 0): (
        (IN0, 0),
    ),
    (2, 0): (
        (IN1, 0),
    ),
    (3, 0): (
        (IN2, 0),
    ),
    (4, 1): (
        (B3, 0), (B2, 0), (B1, 0), (B0, 0), (IN3, 0),
    ),
    (5, 1): (
        (OUT, 0), (IN1, 1), (IN0, 1),
    ),
    (8, 0): (
        (IN0, 2),
    ),
    (8, 1): (
        (IN2, 1),
    ),
    (9, 1): (
        (IN1, 2), (B2, 1),
    ),
    (10, 0): (
        (B3, 1), (B1, 1), (IN3, 1),
    ),
    (10, 1): (
        (QUERY, 0), (OUT, 1), (B2, 2), (B0, 1),
    ),
    (11, 1): (
        (Q, 0), (IN3, 2), (IN2, 2),
    ),
    (13, 1): (
        (KA, 0), (VA, 0), (B3, 2), (B0, 2), (B1, 2), (TOKENS, 0), (KB, 0), (VB, 0), (SMALL, 0),
        (OUT, 2), (Q, 1), (SMALL, 1), (VA, 1), (VB, 1), (KA, 1), (Q, 2), (VA, 2), (SMALL, 2),
        (KA, 2), (KB, 1), (VB, 2), (KB, 2), (IN0, 3), (IN1, 3), (IN2, 3), (IN3, 3), (B0, 3),
        (B1, 3), (B2, 3), (B3, 3), (OUT, 3), (SMALL, 3), (VB, 3), (KB, 3), (Q, 3), (VA, 3),
        (KA, 3),
    ),
}


def backward_kernel(*refs, names, pieces):
    r = Refs()
    for name, ref in zip(names, refs):
        setattr(r, name, ref)
    kv = [r.piece.at[i] for i in range(pieces)]
    seq, ny = pieces, pieces // 2
    step = pl.program_id(0)
    count = r.q.shape[0]
    size = count // 4
    nz, nx = r.b_send.shape[2:4]
    here, row = lax.axis_index("seq"), lax.axis_index("dp")
    y, core = here // 2, here % 2
    partner = (y * 2 + 1 - core, row)
    right, left = ((here + 1) % seq, row), ((here + seq - 1) % seq, row)
    units_back = r.b_send.shape[0]
    senders = {"small": r.s_send}
    for f in range(CHUNKS):
        senders["in%d" % f] = r.a_send.at[f]
    for place, name in enumerate(("out", "q")):
        senders[name] = r.a_send.at[place]
    for part, _, _ in PARTS:
        for name in ("k" + part, "v" + part):
            senders[name] = getattr(r, name + "_send")
    for u in range(units_back):
        senders["b%d" % u] = r.b_send.at[u]
    sums = {}
    for name in senders:
        bufs = [getattr(r, name + "_" + part) for part in BUFFERS]
        sums[name] = Summed(ORDERS[name], lambda u, name=name: senders[name], *bufs)

    def copy(src, dst, out_sem, in_sem, device):
        return pltpu.make_async_remote_copy(
            src_ref=src, dst_ref=dst, send_sem=out_sem, recv_sem=in_sem,
            device_id=device, device_id_type=MESH_ID,
        )

    def pool_core(p):
        return copy(r.p_send.at[p], r.p_in.at[p], r.p_sem.at[0, p, 0], r.p_sem.at[1, p, 0], partner)

    def pool_y(p, hop):
        device = (((y + hop) % ny) * 2 + core, row)
        return copy(
            r.p_keep.at[p, hop], r.p_y.at[p, hop - 1], r.p_sem.at[0, p, hop], r.p_sem.at[1, p, hop], device
        )

    def halo(p, side):
        device = right if side else left
        return copy(
            r.h_out.at[p, side], r.h_in.at[p, side], r.h_sem.at[0, p, side], r.h_sem.at[1, p, side], device
        )

    def chunk_loads(f):
        slot = f % 2
        part = pl.ds(pl.multiple_of(f * D, D), D)
        return [
            pltpu.make_async_copy(r.win_any.at[:, part], r.wbuf.at[slot], r.l_sem.at[0, slot]),
            pltpu.make_async_copy(r.wback_any.at[part, :], r.wbuf.at[2 + slot], r.l_sem.at[1, slot]),
            pltpu.make_async_copy(r.act_any.at[:, part], r.tbuf.at[slot], r.l_sem.at[2, slot]),
            pltpu.make_async_copy(r.slope_any.at[:, part], r.tbuf.at[2 + slot], r.l_sem.at[3, slot]),
        ]

    load_feed = [
        pltpu.make_async_copy(r.fg_any, r.fg, r.l_sem.at[4, 0]),
        pltpu.make_async_copy(r.lowt_any, r.lt, r.l_sem.at[4, 1]),
        pltpu.make_async_copy(r.zg_any, r.sg, r.l_sem.at[5, 0]),
    ]
    load_unit = pltpu.make_async_copy(r.unit_any, r.acc.at[0], r.l_sem.at[5, 1])
    load_wout = pltpu.make_async_copy(r.wout_any, r.wbuf.at[0], r.l_sem.at[6, 0])
    load_att = pltpu.make_async_copy(r.att_any, r.att, r.l_sem.at[6, 1])
    load_wq = pltpu.make_async_copy(r.wq_any, r.wbuf.at[1], r.l_sem.at[7, 0])
    load_wk = pltpu.make_async_copy(r.wk_any, r.wbuf.at[2], r.l_sem.at[7, 1])
    load_wv = pltpu.make_async_copy(r.wv_any, r.wbuf.at[3], r.l_sem.at[8, 0])
    load_tt = pltpu.make_async_copy(r.tt_any, r.lt, r.l_sem.at[8, 1])

    def rows_of(block, mine):
        rc = D // seq
        return pl.ds(pl.multiple_of((2 * block + mine) * rc, rc), rc)

    @pl.when(step == 0)
    def _():
        for load in chunk_loads(0)[1:2] + load_feed[:1] + chunk_loads(0)[3:] + load_feed[1:2]:
            load.start()
        for load in chunk_loads(0)[:1] + chunk_loads(0)[2:3] + load_feed[2:]:
            load.start()
        z, x = row // nx, row % nx
        peers = [partner, right, left]
        peers += [(((y + hop) % ny) * 2 + core, row) for hop in range(1, ny)]
        peers += [(here, z * nx + (x + hop) % nx) for hop in range(1, nx)]
        peers += [(here, ((z + hop) % nz) * nx + x) for hop in range(1, nz)]
        greet(peers)
        for load in load_feed[:2]:
            load.wait()

    def query_gradient():
        sums["in1"].sent_core(0)
        for block in range(ny):
            store_chunks(r.a_send.at[1, block], nn(r.lt[rows_of(block, 1 - core), :], r.tbuf[0]))
        sums["q"].start(0)
        for block in range(ny):
            store_chunks(sums["q"].keep.at[0, block], nn(r.lt[rows_of(block, core), :], r.tbuf[0]))

    def tokens_gradient():
        for load in (load_wq, load_wk, load_wv):
            load.wait()
        total = r.sg[...] + nt(r.tbuf[0], r.wbuf[1])
        total = total + nt(r.tbuf[1], r.wbuf[2])
        r.tokens_grad[...] = (total + nt(r.tbuf[2], r.wbuf[3])).astype(BF16)

    results = {"out": r.t_out, "q": r.t_query, "small": r.t_small}
    for part, _, _ in PARTS:
        for name in ("k" + part, "v" + part):
            results[name] = getattr(r, "t_" + name)
    for f in range(CHUNKS):
        results["in%d" % f] = r.t_in.at[f]
    for u in range(units_back):
        results["b%d" % u] = r.t_back.at[u]

    def run(name, stage):
        if name == "query":
            query_gradient()
        elif name == "tokens":
            tokens_gradient()
        elif name in sums:
            done = getattr(sums[name], ("core", "one", "two", "three")[stage])(0)
            if stage == 3:
                results[name][...] = done

    def run_plan(half):
        for (when, part), todo in PLAN.items():
            if part == half:

                @pl.when(step == when)
                def _(todo=todo):
                    for index, stage in todo:
                        run(NAMES[index], stage)

    @pl.when(step < CHUNKS)
    def _():
        f = step
        slot = f % 2
        early, late = chunk_loads(f)[1::2], chunk_loads(f)[0::2]
        for load in early:
            load.wait()

        @pl.when(f < CHUNKS - 1)
        def _():
            for load in chunk_loads(f + 1):
                load.start()

        @pl.when(f == 1)
        def _():
            load_unit.start()
            load_att.start()

        @pl.when(f == CHUNKS - 1)
        def _():
            load_wout.start()

        slope = r.tbuf[2 + slot].astype(F32)
        inner_grad = (nt(r.fg[...], r.wbuf[2 + slot]) * slope).astype(BF16)
        for block in range(ny):
            store_chunks(r.a_send.at[f, block], nn(r.lt[rows_of(block, 1 - core), :], inner_grad))

        kept = [nn(r.lt[rows_of(block, core), :], inner_grad) for block in range(ny)]
        for i in range(CHUNKS):

            @pl.when(f == i)
            def _(i=i):
                sums["in%d" % i].start(0)
                for block in range(ny):
                    store_chunks(sums["in%d" % i].keep.at[0, block], kept[block])

        run_plan(0)
        for load in late:
            load.wait()

        @pl.when(f == 0)
        def _():
            load_feed[2].wait()

        r.sg[...] += nt(inner_grad, r.wbuf[slot])
        back = nn(r.tbuf[slot].T, r.fg[...])
        part = FF // seq
        for sub in range(D // part):
            block = f * (D // part) + sub
            piece = back[sub * part : (sub + 1) * part]

            @pl.when(block % 2 == core)
            def _(block=block, piece=piece):
                keeps = [sums["b%d" % u].keep.at[0] for u in range(units_back)]
                store_blocks(keeps, block // 2, piece)

            @pl.when(block % 2 != core)
            def _(block=block, piece=piece):
                store_blocks([r.b_send.at[u] for u in range(units_back)], block // 2, piece)

        @pl.when(f == CHUNKS - 1)
        def _():
            for u in range(units_back):
                sums["b%d" % u].start(0)

    @pl.when(step == LATE - 1)
    def _():
        load_tt.wait()

    @pl.when(step == CHUNKS)
    def _():
        load_wq.start()
        load_wk.start()
        load_wv.start()
        load_unit.wait()
        inverse = r.inv[:, 0:1]
        total = jnp.zeros((count, LANES), F32)
        total_unit = jnp.zeros((count, LANES), F32)
        r.small[...] = jnp.zeros_like(r.small)
        r.small[0:8] = r.sums[...]
        for c in range(PAIRS):
            lanes = slice(c * LANES, (c + 1) * LANES)
            grad, unit = r.sg[:, lanes], r.acc[0, c]
            r.small[0:1, lanes] = jnp.sum(grad * unit, axis=0, keepdims=True)
            r.small[1:2, lanes] = jnp.sum(grad, axis=0, keepdims=True)
            e = grad * r.vecs[0:1, lanes]
            total = total + e
            total_unit = total_unit + e * unit
        mean = jnp.sum(total, axis=1, keepdims=True) * (1.0 / D)
        mean_unit = jnp.sum(total_unit, axis=1, keepdims=True) * (1.0 / D)
        for c in range(PAIRS):
            lanes = slice(c * LANES, (c + 1) * LANES)
            e = r.sg[:, lanes] * r.vecs[0:1, lanes]
            r.sg[:, lanes] = inverse * (e - mean - r.acc[0, c] * mean_unit)
        branch_grad = r.sg[...].astype(BF16)
        load_att.wait()
        load_wout.wait()
        sums["in0"].sent_core(0)
        for block in range(ny):
            store_chunks(r.a_send.at[0, block], nn(r.att[rows_of(block, 1 - core), :], branch_grad))
        sums["out"].start(0)
        for block in range(ny):
            store_chunks(sums["out"].keep.at[0, block], nn(r.att[rows_of(block, core), :], branch_grad))
        load_tt.start()
        attended_grad = nt(branch_grad, r.wbuf[0])
        for c in range(PAIRS):
            r.acc[1, c] = attended_grad[:, c * LANES : (c + 1) * LANES]

    def pool_on(p):
        pool_core(p).wait_recv()
        for hop in range(1, ny):
            for which in range(2):
                r.p_keep[p, hop, which] = r.p_keep[p, hop, which] + r.p_in[p, hop, which]
            pool_y(p, hop).start()

    @pl.when((step >= ATTEND) & (step < LATE))
    def _():
        p = step - ATTEND
        r.gb[...] = (r.acc[1, p] * r.rp[...]).astype(BF16)
        delta = score_delta(r.gb[...], r.o[...])
        kp = jnp.concatenate([piece[0] for piece in kv], axis=0)
        kt = kp.T
        vp = jnp.concatenate([piece[1] for piece in kv], axis=0)
        wide = min(256, count)
        for head in range(2):
            for b in range(count // wide):
                cols = slice(b * wide, (b + 1) * wide)
                gh = head_half(r.gb[cols, :], head)
                qh = head_half(r.q[cols, :], head)
                low = r.pool_e[head, :, cols]
                dp = nt(vp, gh) - delta[head : head + 1, cols]
                ds = (low.astype(F32) * dp).astype(BF16)
                key_part = nn(ds, qh)
                value_part = nn(low, gh)
                if head == 0 and b == 0:
                    r.dk[0 : seq * size] = key_part
                    r.dv[0 : seq * size] = value_part
                else:
                    r.dk[0 : seq * size] += key_part
                    r.dv[0 : seq * size] += value_part
                r.dq_pool[p, head * 64 : head * 64 + 64, cols] = nn(kt[head * 64 : head * 64 + 64], ds)
        for i in range(pieces):
            target = r.p_keep if i < ny else r.p_send
            after = (((y + i % ny) % ny) * 2 + (core + i // ny) % 2 + 1) % seq
            index = ((after % 2 - core + 2) % 2) * ny + (after // 2 - y + ny) % ny
            rows = pl.ds(pl.multiple_of(index * size, size), EXTRA)
            for which, total in ((0, r.dk), (1, r.dv)):
                target[p, i % ny, which, 0:size] = total[i * size : (i + 1) * size].astype(BF16)
                target[p, i % ny, which, size:] = total[rows, :].astype(BF16)
        pool_core(p).start()

        @pl.when(p > 0)
        def _():
            pool_on(p - 1)

        run_plan(0)

        r.gb[...] = (r.acc[1, p] * r.rn[...]).astype(BF16)
        delta = score_delta(r.gb[...], r.o[...])
        kt = r.keys[...].T
        r.dk[0 : count + 2 * HALF] = jnp.zeros((count + 2 * HALF, LANES), F32)
        r.dv[0 : count + 2 * HALF] = jnp.zeros((count + 2 * HALF, LANES), F32)
        for b in range(count // QB):
            cols = slice(b * QB, (b + 1) * QB)
            keys = slice(b * QB, (b + 2) * QB)
            lows, scores, grads, queries, dqs = [], [], [], [], []
            for head in range(2):
                gh = head_half(r.gb[cols, :], head)
                low = r.near_e[head, b]
                dp = nt(r.values[keys, :], gh) - delta[head : head + 1, cols]
                ds = (low.astype(F32) * dp).astype(BF16)
                dqs.append(nn(kt[head * 64 : head * 64 + 64, keys], ds))
                lows.append(low)
                scores.append(ds)
                grads.append(gh)
                queries.append(head_half(r.q[cols, :], head))
            r.dk[keys, :] += nn(jnp.concatenate(scores, axis=1), jnp.concatenate(queries, axis=0))
            r.dv[keys, :] += nn(jnp.concatenate(lows, axis=1), jnp.concatenate(grads, axis=0))
            total = (jnp.concatenate(dqs, axis=0) + r.dq_pool[p, :, cols]) * 0.125
            lanes = pl.ds(pl.multiple_of(p * LANES, LANES), LANES)
            r.tbuf[0, cols, lanes] = total.T.astype(BF16)
        for which, total in ((0, r.dk), (1, r.dv)):
            r.h_out[p, 0, which] = total[0:HALF].astype(BF16)
            r.acc[which, p] = total[HALF : HALF + count]
            r.h_out[p, 1, which] = total[HALF + count : 2 * HALF + count].astype(BF16)

        @pl.when(here > 0)
        def _():
            halo(p, 0).start()

        @pl.when(here < seq - 1)
        def _():
            halo(p, 1).start()

        @pl.when(p == PAIRS - 1)
        def _():
            pool_on(p)

    @pl.when(step >= ATTEND + LAG)
    def _():
        p = step - ATTEND - LAG
        lanes = pl.ds(pl.multiple_of(p * LANES, LANES), LANES)
        for hop in range(1, ny):
            pool_y(p, hop).wait_recv()

        @pl.when(here < seq - 1)
        def _():
            halo(p, 0).wait_recv()
            for which in range(2):
                r.acc[which, p, count - HALF :, :] += r.h_in[p, 0, which].astype(F32)

        @pl.when(here > 0)
        def _():
            halo(p, 1).wait_recv()
            for which in range(2):
                r.acc[which, p, 0:HALF, :] += r.h_in[p, 1, which].astype(F32)

        moves = ((2, 0, 0), (3, 1, 0), (4, 2, 0), (0, 2, 1), (1, 3, 1))
        sums = [jnp.zeros((1, LANES), F32)] * 5
        for which, source in ((0, r.keys_late), (1, r.values_late)):
            grad = r.acc.at[which, p]
            r.cells[...] = source[...].astype(F32)
            total = r.p_keep[p, 0, which].astype(F32) + r.p_in[p, 0, which].astype(F32)
            for hop in range(1, ny):
                total = total + r.p_y[p, hop - 1, which].astype(F32)
            r.g[...] = total
            for tap, place, shift in moves:
                mask = r.masks[5 * shift + tap]
                spread = r.g[shift : shift + size, :] * mask * r.taps[tap : tap + 1, :]
                grad[pl.ds(place, size, stride=4), :] += spread
            for tap in range(5):
                taken = r.cells[pl.ds(HALF + tap - 2, size, stride=4), :]
                product = r.g[0:size, :] * r.masks[tap] * taken
                sums[tap] = sums[tap] + jnp.sum(product, axis=0, keepdims=True)
            r.tbuf[1 + which, :, lanes] = grad[...].astype(BF16)
        for tap in range(5):
            r.small[8 + tap : 9 + tap, lanes] = sums[tap]

    def key_gradients(part, first, last):
        for name, low in (("k" + part, 1), ("v" + part, 2)):
            for block in range(ny):
                rows = rows_of(block, 1 - core)
                store_chunks(senders[name].at[block], nn(r.lt[rows, :], r.tbuf[low, :, first:last]))
            sums[name].start(0)
            keep = sums[name].keep
            for block in range(ny):
                rows = rows_of(block, core)
                store_chunks(keep.at[0, block], nn(r.lt[rows, :], r.tbuf[low, :, first:last]))

    @pl.when(step == LATE)
    def _():
        key_gradients(*PARTS[0])

    @pl.when(step == LAST)
    def _():
        key_gradients(*PARTS[1])
        r.small_t[...] = r.small[...].T
        few = D // (seq * nz * nx)
        for block in range(ny):
            for part, mine in ((r.s_send.at[block], 1 - core), (sums["small"].keep.at[0, block], core)):
                vectors = r.small_t[rows_of(block, mine), :]
                for z in range(nz):
                    for x in range(nx):
                        start = (z * nx + x) * few
                        part[z, x] = jnp.zeros(part.shape[2:], BF16)
                        part[z, x, 0:few] = vectors[start : start + few].astype(BF16)
        sums["small"].start(0)

    run_plan(1)

    @pl.when(step == LAST)
    def _():
        reused = ["in0", "in1"]
        for name in sums:
            if name not in reused:
                sums[name].sent_core(0)
            sums[name].sent(0)
        for p in range(PAIRS):
            pool_core(p).wait_send()
            for hop in range(1, ny):
                pool_y(p, hop).wait_send()

        @pl.when(here > 0)
        def _():
            for p in range(PAIRS):
                halo(p, 0).wait_send()

        @pl.when(here < seq - 1)
        def _():
            for p in range(PAIRS):
                halo(p, 1).wait_send()


def unpack_kernel(t_in, t_back, t_query, t_ka, t_kb, t_va, t_vb, t_out, t_small, tg, *outs):
    tokens_grad, query, key, value, out, inn, back = outs[:7]
    rows = query.shape[0]
    tokens_grad[...] = tg[...]
    for source, target in ((t_query, query), (t_out, out)):
        target[...] = unfold_rows(source[...], rows)
    for one, two, target in ((t_ka, t_kb, key), (t_va, t_vb, value)):
        target[:, 0:SPLIT] = unfold_rows(one[...], rows)
        target[:, SPLIT:] = unfold_rows(two[...], rows)
    for u in range(CHUNKS):
        inn[:, u * D : (u + 1) * D] = unfold_rows(t_in[u], rows)
    units, part, wide = t_back.shape
    across = back.shape[1] // wide
    for u in range(units):
        top, start = (u // across) * part, (u % across) * wide
        back[top : top + part, start : start + wide] = t_back[u]
    small = t_small[...]
    pad = LANES - small.shape[0]
    turned = jnp.concatenate([small, jnp.zeros((pad, LANES), F32)], axis=0).T
    for i in range(4):
        outs[7 + i][...] = turned[i : i + 1, 0:rows]
    outs[11][...] = turned[8:13, 0:rows]


def call(kernel, args, in_specs, outs, out_specs, grid, scratch, flops, name):
    moved = sum(a.size * a.dtype.itemsize for a in list(args) + list(outs))
    return pl.pallas_call(
        kernel,
        grid_spec=pltpu.PrefetchScalarGridSpec(
            num_scalar_prefetch=0,
            grid=grid,
            in_specs=in_specs,
            out_specs=out_specs,
            scratch_shapes=scratch,
        ),
        out_shape=outs,
        compiler_params=pltpu.CompilerParams(
            vmem_limit_bytes=60 * MB, dimension_semantics=("arbitrary",) * len(grid)
        ),
        cost_estimate=pl.CostEstimate(flops=flops, bytes_accessed=moved, transcendentals=0),
        name=name,
    )(*args)


def whole(array):
    rank = len(array.shape)
    return pl.BlockSpec(array.shape, lambda i: (0,) * rank)


def columns(array, width=LANES):
    rank = len(array.shape)
    return pl.BlockSpec(array.shape[:-1] + (width,), lambda i: (0,) * (rank - 1) + (i,))


def leading(array, size):
    rank = len(array.shape)
    return pl.BlockSpec((size,) + array.shape[1:], lambda i: (i,) + (0,) * (rank - 1))


def per_device(
    tokens,
    item_lengths,
    w_query,
    w_key,
    w_value,
    w_out,
    w_in,
    w_back,
    norm1_gain,
    norm1_bias,
    norm2_gain,
    norm2_bias,
    pool_weight,
    out_grad,
):
    _, count, _ = tokens.shape
    seq = lax.axis_size("seq")
    ny = seq // 2
    row_len = count * seq
    span = count + 2 * HALF
    size = count // 4
    tok = tokens[0]
    og = out_grad[0]
    taps = pool_weight.T
    vecs = jnp.stack([norm1_gain, norm1_bias, norm2_gain, norm2_bias])

    def shape(dims, kind):
        return jax.ShapeDtypeStruct(dims, kind)

    blocks = count // QB
    pool_all = seq * size
    anywhere = pl.BlockSpec(memory_space=pl.ANY)

    def in_first(i):
        return jnp.clip(i - FORWARD_NEAR, 0, PAIRS - 1)

    def in_second(i):
        return jnp.clip(i - FORWARD_POOL, 0, PAIRS - 1)

    ins = [
        ("lengths", item_lengths, pl.BlockSpec(memory_space=pltpu.SMEM)),
        ("pool_weight", taps, whole(taps)),
        ("tok", tok, anywhere),
        ("wq_any", w_query, anywhere),
        ("wk_any", w_key, anywhere),
        ("wv_any", w_value, anywhere),
    ]
    near_shape = shape((H, blocks, 2 * QB, QB), BF16)
    pool_shape = shape((H, pool_all, count), BF16)
    wide_shape = shape((count, D), F32)
    outs = [
        ("q_out", shape((count, D), BF16), anywhere),
        ("k_out", shape((span, D), BF16), anywhere),
        ("v_out", shape((span, D), BF16), anywhere),
        ("tt_out", shape((D, count), BF16), anywhere),
        ("mask_out", shape((7, size, LANES), F32), anywhere),
        ("pieces_out", shape((seq, 2, size, D), BF16), anywhere),
        ("near_e", near_shape, pl.BlockSpec((2, blocks, 2 * QB, QB), lambda i: (in_first(i), 0, 0, 0))),
        ("pool_e", pool_shape, pl.BlockSpec((2, pool_all, count), lambda i: (in_second(i), 0, 0))),
        ("o_out", wide_shape, pl.BlockSpec((count, LANES), lambda i: (0, in_second(i)))),
        ("rn_out", wide_shape, pl.BlockSpec((count, LANES), lambda i: (0, in_second(i)))),
        ("rp_out", wide_shape, pl.BlockSpec((count, LANES), lambda i: (0, in_second(i)))),
    ]
    scratch = [
        ("x", pltpu.VMEM((span, D), BF16)),
        ("wq", pltpu.VMEM((D, D), BF16)),
        ("wk", pltpu.VMEM((D, D), BF16)),
        ("wv", pltpu.VMEM((D, D), BF16)),
        ("qs", pltpu.VMEM((count, D), BF16)),
        ("ks", pltpu.VMEM((span, D), BF16)),
        ("vs", pltpu.VMEM((span, D), BF16)),
        ("tt", pltpu.VMEM((D, count), BF16)),
        ("mask", pltpu.VMEM((7, size, LANES), F32)),
        ("cells", pltpu.VMEM((PAIRS, span, LANES), F32)),
        ("pieces", pltpu.VMEM((seq, 2, size, D), BF16)),
        ("o_near", pltpu.VMEM((PAIRS, LANES, count), F32)),
        ("stats", pltpu.VMEM((PAIRS, 8, count), F32)),
        ("near_bias", pltpu.VMEM((blocks, 2 * QB, QB), F32)),
        ("pool_bias", pltpu.VMEM((pool_all, count), F32)),
        ("s_sem", pltpu.SemaphoreType.DMA((2 + seq,))),
        ("r_sem", pltpu.SemaphoreType.DMA((2 + seq,))),
        ("l_sem", pltpu.SemaphoreType.DMA((11,))),
    ]
    (queries, keys, values, tok_t, tap_masks, pieces, near_e, pool_e, attention, near_scale, pool_scale) = (
        pl.pallas_call(
            partial(forward_kernel, names=[entry[0] for entry in ins + outs + scratch]),
            grid_spec=pltpu.PrefetchScalarGridSpec(
                num_scalar_prefetch=0,
                grid=(FORWARD_LAST + 1,),
                in_specs=[entry[2] for entry in ins],
                out_specs=[entry[2] for entry in outs],
                scratch_shapes=[entry[1] for entry in scratch],
            ),
            out_shape=[entry[1] for entry in outs],
            compiler_params=pltpu.CompilerParams(
                collective_id=1,
                has_side_effects=True,
                vmem_limit_bytes=60 * MB,
                dimension_semantics=("arbitrary",),
            ),
            cost_estimate=pl.CostEstimate(
                flops=4 * H * 768 * 256 * count + 6 * count * D * D, bytes_accessed=16 * MB, transcendentals=0
            ),
            name="forward",
        )(*[entry[1] for entry in ins])
    )

    dp = lax.axis_size("dp")
    nx = 2 if dp % 2 == 0 else 1
    nz = dp // nx
    rows = D // (seq * dp)
    back_rows = FF // (seq * dp)
    down = 2 if back_rows % 32 == 0 else 1
    half_one = shape((ny, nz, nx) + folded(rows, D), BF16)
    half_back = shape((2 * down, ny, nz, nx, back_rows // down, D // 2), BF16)
    args = (attention, tok, og, vecs, w_out, w_in, w_back)
    outs = (
        shape((count, D), BF16),
        shape((count, FF), BF16),
        shape((count, FF), BF16),
        shape((D, count), BF16),
        shape((count, D), BF16),
        shape((count, D), F32),
        shape((PAIRS, count, LANES), F32),
        shape((count, LANES), F32),
        shape((D, count), BF16),
        shape((8, D), F32),
    )
    mixed, act, slope, low_t, feed_grad, z_grad, unit_one, inv_one, att_t, sums = call(
        dense_kernel,
        args,
        [whole(a) for a in args[:5]]
        + [columns(w_in, D), pl.BlockSpec((D, D), lambda i: (i, 0))],
        outs,
        [whole(outs[0]), columns(outs[1], D), columns(outs[2], D)] + [whole(a) for a in outs[3:]],
        (CHUNKS,),
        [
            pltpu.VMEM((count, D), F32),
            pltpu.VMEM((count, D), BF16),
            pltpu.VMEM((count, D), F32),
        ],
        2 * count * (D * D + 2 * D * FF),
        "dense",
    )
    half_small = shape((ny, nz, nx, -(-rows // 16) * 16, LANES), BF16)
    half_pool = (PAIRS, ny, 2, size + EXTRA, LANES)
    blocks_in = []

    def block(name, array, spec):
        blocks_in.append((name, array, spec))

    def col_spec(array, index):
        lead = (0,) * (len(array.shape) - 1)
        return pl.BlockSpec(array.shape[:-1] + (LANES,), lambda i: lead + (index(i),))

    def lead_spec(array, index):
        rest = (0,) * (len(array.shape) - 1)
        return pl.BlockSpec((2,) + array.shape[1:], lambda i: (index(i),) + rest)

    def all_spec(array):
        rest = (0,) * len(array.shape)
        return pl.BlockSpec(array.shape, lambda i: rest)

    def in_pair(i):
        return jnp.clip(i - ATTEND, 0, PAIRS - 1)

    def in_late(i):
        return jnp.clip(i - ATTEND - LAG, 0, PAIRS - 1)

    block("q", queries, col_spec(queries, in_pair))
    block("o", attention, col_spec(attention, in_pair))
    block("rp", pool_scale, col_spec(pool_scale, in_pair))
    block("rn", near_scale, col_spec(near_scale, in_pair))
    block("pool_e", pool_e, lead_spec(pool_e, in_pair))
    block("near_e", near_e, lead_spec(near_e, in_pair))
    block("keys", keys, col_spec(keys, in_pair))
    block("values", values, col_spec(values, in_pair))
    block("keys_late", keys, col_spec(keys, in_late))
    block("values_late", values, col_spec(values, in_late))
    block("piece", pieces, col_spec(pieces, in_pair))
    block("masks", tap_masks, all_spec(tap_masks))
    block("taps", taps, col_spec(taps, in_late))
    block("sums", sums, all_spec(sums))
    block("vecs", vecs, all_spec(vecs))
    block("inv", inv_one, all_spec(inv_one))
    for name, array in (
        ("win_any", w_in),
        ("wback_any", w_back),
        ("act_any", act),
        ("slope_any", slope),
        ("fg_any", feed_grad),
        ("lowt_any", low_t),
        ("zg_any", z_grad),
        ("unit_any", unit_one),
        ("wout_any", w_out),
        ("att_any", att_t),
        ("tt_any", tok_t),
        ("wq_any", w_query),
        ("wk_any", w_key),
        ("wv_any", w_value),
    ):
        block(name, array, anywhere)
    outs = [
        ("t_in", shape((CHUNKS,) + half_one.shape[3:], F32)),
        ("t_back", shape((half_back.shape[0],) + half_back.shape[4:], F32)),
        ("t_query", shape(half_one.shape[3:], F32)),
        ("t_kA", shape(folded(rows, SPLIT), F32)),
        ("t_kB", shape(folded(rows, D - SPLIT), F32)),
        ("t_vA", shape(folded(rows, SPLIT), F32)),
        ("t_vB", shape(folded(rows, D - SPLIT), F32)),
        ("t_out", shape(half_one.shape[3:], F32)),
        ("t_small", shape(half_small.shape[3:], F32)),
        ("tokens_grad", shape((count, D), BF16)),
    ]
    tall = max(pool_all, span)
    scratch = [
        ("dk", pltpu.VMEM((tall, LANES), F32)),
        ("dv", pltpu.VMEM((tall, LANES), F32)),
        ("dq_pool", pltpu.VMEM((PAIRS, LANES, count), F32)),
        ("gb", pltpu.VMEM((count, LANES), BF16)),
        ("acc", pltpu.VMEM((2, PAIRS, count, LANES), F32)),
        ("tbuf", pltpu.VMEM((4, count, D), BF16)),
        ("wbuf", pltpu.VMEM((4, D, D), BF16)),
        ("fg", pltpu.VMEM((count, D), BF16)),
        ("lt", pltpu.VMEM((D, count), BF16)),
        ("att", pltpu.VMEM((D, count), BF16)),
        ("cells", pltpu.VMEM((span, LANES), F32)),
        ("g", pltpu.VMEM((size + EXTRA, LANES), F32)),
        ("small", pltpu.VMEM((LANES, D), F32)),
        ("small_t", pltpu.VMEM((D, LANES), F32)),
        ("p_keep", pltpu.VMEM(half_pool, BF16)),
        ("p_send", pltpu.VMEM(half_pool, BF16)),
        ("p_in", pltpu.VMEM(half_pool, BF16)),
        ("p_y", pltpu.VMEM((PAIRS, ny - 1) + half_pool[2:], BF16)),
        ("h_out", pltpu.VMEM((PAIRS, 2, 2, HALF, LANES), BF16)),
        ("h_in", pltpu.VMEM((PAIRS, 2, 2, HALF, LANES), BF16)),
        ("p_sem", pltpu.SemaphoreType.DMA((2, PAIRS, ny))),
        ("h_sem", pltpu.SemaphoreType.DMA((2, PAIRS, 2))),
        ("l_sem", pltpu.SemaphoreType.DMA((9, 2))),
        ("sg", pltpu.VMEM((count, D), F32)),
        ("a_send", pltpu.VMEM((CHUNKS,) + half_one.shape, BF16)),
        ("b_send", pltpu.VMEM(half_back.shape, BF16)),
        ("s_send", pltpu.VMEM(half_small.shape, BF16)),
    ]
    sizes = {name: half_one.shape for name in ORDERS}
    sizes["small"] = half_small.shape
    for part, first, after in PARTS:
        for name in ("k" + part, "v" + part):
            sizes[name] = half_one.shape[:3] + folded(rows, after - first)
            scratch.append((name + "_send", pltpu.VMEM(sizes[name], BF16)))
    for u in range(CHUNKS):
        if u < half_back.shape[0]:
            sizes["b%d" % u] = half_back.shape[1:]
        else:
            del sizes["b%d" % u]
    for name, dims in sizes.items():
        bufs = summed_scratch(1, dims, ORDERS[name])
        scratch += [(name + "_" + part, buf) for part, buf in zip(BUFFERS, bufs)]
    names = [entry[0] for entry in blocks_in] + [entry[0] for entry in outs + scratch]
    moved = sum(entry[1].size * entry[1].dtype.itemsize for entry in blocks_in)
    totals = pl.pallas_call(
        partial(backward_kernel, names=names, pieces=seq),
        grid_spec=pltpu.PrefetchScalarGridSpec(
            num_scalar_prefetch=0,
            grid=(LAST + 1,),
            in_specs=[entry[2] for entry in blocks_in],
            out_specs=[all_spec(entry[1]) for entry in outs],
            scratch_shapes=[entry[1] for entry in scratch],
        ),
        out_shape=[entry[1] for entry in outs],
        compiler_params=pltpu.CompilerParams(
            collective_id=0,
            has_side_effects=True,
            vmem_limit_bytes=63 * MB,
            dimension_semantics=("arbitrary",),
        ),
        cost_estimate=pl.CostEstimate(
            flops=8 * H * 768 * 256 * count + 12 * count * D * D + 8 * count * D * FF, bytes_accessed=moved, transcendentals=0
        ),
        name="backward",
    )(*[entry[1] for entry in blocks_in])

    outs = (
        shape((count, D), BF16),
        shape((rows, D), F32),
        shape((rows, D), F32),
        shape((rows, D), F32),
        shape((rows, D), F32),
        shape((rows, FF), F32),
        shape((back_rows, D), F32),
        shape((1, rows), F32),
        shape((1, rows), F32),
        shape((1, rows), F32),
        shape((1, rows), F32),
        shape((5, rows), F32),
    )
    done = call(
        unpack_kernel,
        tuple(totals),
        [whole(a) for a in totals],
        outs,
        [whole(a) for a in outs],
        (1,),
        [],
        0,
        "unpack",
    )
    return (
        mixed[None],
        done[0][None],
        done[1],
        done[2],
        done[3],
        done[4],
        done[5],
        done[6],
        done[7].reshape(rows),
        done[8].reshape(rows),
        done[9].reshape(rows),
        done[10].reshape(rows),
        done[11].T,
    )


def solution(mesh):
    shards, copied = P("dp", "seq", None), P()
    spread = P(("seq", "dp"), None)
    vector = P(("seq", "dp"))
    return jax.shard_map(
        per_device,
        mesh=mesh,
        in_specs=(shards, P("dp", None)) + (copied,) * 11 + (shards,),
        out_specs=(shards, shards) + (spread,) * 6 + (vector,) * 4 + (spread,),
        check_vma=False,
    )
```

```python
import itertools
from functools import partial

import jax
import jax.numpy as jnp
from jax import lax
from jax.experimental import pallas as pl
from jax.experimental.pallas import tpu as pltpu
from jax.sharding import PartitionSpec as P

D = 768
FF = 3072
H = 12
PAIRS = H // 2
HALF = 64
PWIN = 512
QB = 128
EXTRA = 16
LANES = 128
BF16 = jnp.bfloat16
F32 = jnp.float32
MB = 1 << 20


def nn(left, right):
    return jnp.dot(left, right, preferred_element_type=F32)


def nt(left, right, precision=None):
    return lax.dot_general(
        left, right, (((1,), (1,)), ((), ())), preferred_element_type=F32, precision=precision
    )


def iota(shape, dim):
    return lax.broadcasted_iota(jnp.int32, shape, dim)


def segment_of(ends, place, row_len):
    item = jnp.zeros_like(place)
    for end in ends:
        item = item + (place >= end).astype(jnp.int32)
    return jnp.where((place >= 0) & (place < row_len), item, -2)


def head_half(block, head):
    lane = iota(block.shape, 1)
    return jnp.where((lane < 64) == (head == 0), block, jnp.zeros_like(block))


def tap_mask(ends, start, tap, shift, count, row_len):
    center = start + 4 * (iota((count, 1), 0) + shift)
    same = segment_of(ends, center + tap - 2, row_len) == segment_of(ends, center, row_len)
    return (same & (center < row_len)).astype(F32)


def folds(rows, width):
    return 2 if rows % 16 and rows % 8 == 0 and (width // 2) % LANES == 0 else 1


def folded(rows, width):
    fold = folds(rows, width)
    return (rows * fold, width // fold)


def fold_rows(block):
    rows, width = block.shape
    fold = folds(rows, width)
    part = width // fold
    return jnp.concatenate([block[:, i * part : (i + 1) * part] for i in range(fold)], axis=0)


def unfold_rows(block, rows):
    fold = block.shape[0] // rows
    return jnp.concatenate([block[i * rows : (i + 1) * rows] for i in range(fold)], axis=1)


def store_chunks(target, total):
    nz, nx = target.shape[0], target.shape[1]
    rows = total.shape[0] // (nz * nx)
    for z in range(nz):
        for x in range(nx):
            start = (z * nx + x) * rows
            target[z, x] = fold_rows(total[start : start + rows]).astype(BF16)


def store_blocks(targets, block, total):
    _, nz, nx, part, wide = targets[0].shape
    rows = total.shape[0] // (nz * nx)
    across = total.shape[1] // wide
    for z in range(nz):
        for x in range(nx):
            start = (z * nx + x) * rows
            for unit, target in enumerate(targets):
                top = start + (unit // across) * part
                left = (unit % across) * wide
                target[block, z, x] = total[top : top + part, left : left + wide].astype(BF16)


def normal_parts(v):
    bell = jnp.exp(v * v * -0.5)
    t = 1.0 / (1.0 + jnp.abs(v) * (0.3275911 * 0.7071067811865476))
    poly = t * (
        0.127414796 + t * (-0.142248368 + t * (0.7107068705 + t * (-0.7265760135 + t * 0.5307027145)))
    )
    tail = poly * bell
    return jnp.where(v < 0, tail, 1.0 - tail), v * bell * 0.3989422804014327


def normalized(values):
    shifted = values - jnp.mean(values, axis=1, keepdims=True)
    inverse = lax.rsqrt(jnp.mean(shifted * shifted, axis=1, keepdims=True) + 1e-05)
    return shifted * inverse, inverse


def dense_kernel(
    o, tok, og, vecs, w_out, w_in, w_back,
    mixed, act, slope, low_t, feed_grad, z_grad, unit_out, inv_out, att_t, sums,
    first, low, feed,
):
    step = pl.program_id(0)
    gain_one, bias_one = vecs[0:1, :], vecs[1:2, :]
    gain_two, bias_two = vecs[2:3, :], vecs[3:4, :]

    @pl.when(step == 0)
    def _():
        att = o[...].astype(BF16)
        att_t[...] = att.T
        unit, inverse = normalized(tok[...].astype(F32) + nn(att, w_out[...]))
        for c in range(PAIRS):
            unit_out[c] = unit[:, c * LANES : (c + 1) * LANES]
        inv_out[...] = jnp.broadcast_to(inverse, inv_out.shape)
        first[...] = unit * gain_one + bias_one
        low[...] = first[...].astype(BF16)
        low_t[...] = low[...].T
        feed[...] = jnp.zeros_like(feed)

    inner = nn(low[...], w_in[...])
    phi, bell = normal_parts(inner)
    act[...] = (inner * phi).astype(BF16)
    slope[...] = (phi + bell).astype(BF16)
    feed[...] += nn(act[...], w_back[...])

    @pl.when(step == CHUNKS - 1)
    def _():
        unit, inverse = normalized(first[...] + feed[...])
        mixed[...] = (unit * gain_two + bias_two).astype(BF16)
        upstream = og[...].astype(F32)
        sums[...] = jnp.zeros_like(sums)
        sums[2:3] = jnp.sum(upstream * unit, axis=0, keepdims=True)
        sums[3:4] = jnp.sum(upstream, axis=0, keepdims=True)
        e = upstream * gain_two
        centred = e - jnp.mean(e, axis=1, keepdims=True)
        total = inverse * (centred - unit * jnp.mean(e * unit, axis=1, keepdims=True))
        z_grad[...] = total
        feed_grad[...] = total.astype(BF16)


def score_delta(grad, attended):
    pick = ((iota((8, LANES), 1) // 64) == iota((8, LANES), 0)).astype(F32)
    return nt(pick, grad.astype(F32) * attended, precision=lax.Precision.HIGHEST)


def hop_pairs(axis, count, stride, hop):
    pairs = []
    for device in range(lax.axis_size(axis)):
        place = (device // stride) % count
        pairs.append((device, device + ((place + hop) % count - place) * stride))
    return pairs


MESH_ID = pl.DeviceIdType.MESH


class Summed:
    def __init__(self, order, send_of, keep, core_in, first, second, third, out_sem, in_sem):
        self.order, self.send_of = order, send_of
        self.keep, self.core_in = keep, core_in
        self.bufs = (first, second, third)
        self.out_sem, self.in_sem = out_sem, in_sem
        self.units = keep.shape[0]
        self.count = dict(zip("yzx", keep.shape[1:4]))
        self.here, self.row = lax.axis_index("seq"), lax.axis_index("dp")
        self.mine = self.here % 2
        nx = self.count["x"]
        self.own = {"y": self.here // 2, "z": self.row // nx, "x": self.row % nx}
        self.base = {"y": 1}
        self.base["x"] = self.base["y"] + self.count["y"] - 1
        self.base["z"] = self.base["x"] + nx - 1

    def copy(self, u, src, dst, slot, device):
        return pltpu.make_async_remote_copy(
            src_ref=src,
            dst_ref=dst,
            send_sem=self.out_sem.at[u, slot],
            recv_sem=self.in_sem.at[u, slot],
            device_id=device,
            device_id_type=MESH_ID,
        )

    def core_copy(self, u):
        partner = (self.own["y"] * 2 + 1 - self.mine, self.row)
        return self.copy(u, self.send_of(u), self.core_in.at[u], 0, partner)

    def hop_copy(self, u, stage, hop):
        axis = self.order[stage]
        other = (self.own[axis] + hop) % self.count[axis]
        place = dict(self.own)
        place[axis] = other
        device = (place["y"] * 2 + self.mine, place["z"] * self.count["x"] + place["x"])
        index = []
        for dim in "yzx":
            known = dim in self.order[: stage + 1]
            index.append(place[dim] if known else slice(None))
        source = self.keep.at[(u,) + tuple(index)]
        slot = self.base[axis] + hop - 1
        return self.copy(u, source, self.bufs[stage].at[u, hop - 1], slot, device)

    def hops(self, stage):
        return range(1, self.count[self.order[stage]])

    def start(self, u):
        self.core_copy(u).start()

    def core(self, u):
        self.core_copy(u).wait_recv()
        for y in range(self.count["y"]):
            for z in range(self.count["z"]):
                self.keep[u, y, z] = self.keep[u, y, z] + self.core_in[u, y, z]
        for hop in self.hops(0):
            self.hop_copy(u, 0, hop).start()

    def add(self, u, stage):
        left = [dim for dim in "yzx" if dim not in self.order[: stage + 1]]
        for hop in self.hops(stage):
            self.hop_copy(u, stage, hop).wait_recv()
            for place in itertools.product(*[range(self.count[dim]) for dim in left]):
                at = dict(self.own)
                at.update(zip(left, place))
                index = (u,) + tuple(at[dim] for dim in "yzx")
                self.keep[index] = self.keep[index] + self.bufs[stage][(u, hop - 1) + place]
        for hop in self.hops(stage + 1):
            self.hop_copy(u, stage + 1, hop).start()

    def one(self, u):
        self.add(u, 0)

    def two(self, u):
        self.add(u, 1)

    def three(self, u):
        total = self.keep[(u,) + tuple(self.own[dim] for dim in "yzx")].astype(F32)
        for hop in self.hops(2):
            self.hop_copy(u, 2, hop).wait_recv()
            total = total + self.bufs[2][u, hop - 1].astype(F32)
        return total

    def sent_core(self, u):
        self.core_copy(u).wait_send()

    def sent(self, u):
        for stage in range(3):
            for hop in self.hops(stage):
                self.hop_copy(u, stage, hop).wait_send()


def summed_scratch(units, shape, order):
    count = dict(zip("yzx", shape[:3]))
    chunk = shape[3:]
    bufs = [pltpu.VMEM((units,) + shape, BF16), pltpu.VMEM((units,) + shape, BF16)]
    for stage in range(3):
        left = tuple(count[dim] for dim in "yzx" if dim not in order[: stage + 1])
        bufs.append(pltpu.VMEM((units, max(count[order[stage]] - 1, 1)) + left + chunk, BF16))
    slots = count["y"] + count["x"] + count["z"] - 2
    bufs += [pltpu.SemaphoreType.DMA((units, slots)), pltpu.SemaphoreType.DMA((units, slots))]
    return bufs


def greet(peers):
    barrier = pltpu.get_barrier_semaphore()
    for peer in peers:
        pl.semaphore_signal(barrier, inc=1, device_id=peer, device_id_type=MESH_ID)
    pl.semaphore_wait(barrier, len(peers))


class Refs:
    pass


FORWARD_NEAR = 1
FORWARD_POOL = 1 + PAIRS
FORWARD_LAST = 2 * PAIRS


def forward_kernel(*refs, names):
    r = Refs()
    for name, ref in zip(names, refs):
        setattr(r, name, ref)
    seq, _, size, _ = r.pieces.shape
    ny = seq // 2
    count, row_len = 4 * size, 4 * size * seq
    span = count + 2 * HALF
    step = pl.program_id(0)
    here, row = lax.axis_index("seq"), lax.axis_index("dp")
    y, core = here // 2, here % 2
    start = here * count
    partner = (y * 2 + 1 - core, row)
    right, left = ((here + 1) % seq, row), ((here + seq - 1) % seq, row)
    ends = [r.lengths[0, 0]]
    for m in range(1, 4):
        ends.append(ends[-1] + r.lengths[0, m])

    def copy(src, dst, slot, device):
        return pltpu.make_async_remote_copy(
            src_ref=src, dst_ref=dst, send_sem=r.s_sem.at[slot], recv_sem=r.r_sem.at[slot],
            device_id=device, device_id_type=MESH_ID,
        )

    own = r.x.at[HALF : HALF + count]
    to_right = copy(r.tok.at[count - HALF :], r.x.at[0:HALF], 0, right)
    to_left = copy(r.tok.at[0:HALF], r.x.at[HALF + count :], 1, left)

    def to_y(hop):
        device = (((y + hop) % ny) * 2 + core, row)
        return copy(r.pieces.at[0], r.pieces.at[ny - hop], 1 + hop, device)

    def to_core(hop):
        return copy(r.pieces.at[hop], r.pieces.at[ny + hop], 1 + ny + hop, partner)

    loads = [
        pltpu.make_async_copy(r.tok, own, r.l_sem.at[0]),
        pltpu.make_async_copy(r.wk_any, r.wk, r.l_sem.at[1]),
        pltpu.make_async_copy(r.wv_any, r.wv, r.l_sem.at[2]),
        pltpu.make_async_copy(r.wq_any, r.wq, r.l_sem.at[3]),
    ]
    stores = [
        pltpu.make_async_copy(r.qs, r.q_out, r.l_sem.at[4]),
        pltpu.make_async_copy(r.ks, r.k_out, r.l_sem.at[5]),
        pltpu.make_async_copy(r.vs, r.v_out, r.l_sem.at[6]),
        pltpu.make_async_copy(r.tt, r.tt_out, r.l_sem.at[7]),
        pltpu.make_async_copy(r.mask, r.mask_out, r.l_sem.at[8]),
    ]
    store_pieces = pltpu.make_async_copy(r.pieces, r.pieces_out, r.l_sem.at[10])

    @pl.when(step == 0)
    def _():
        for load in loads:
            load.start()
        greet([partner, right, left] + [(((y + hop) % ny) * 2 + core, row) for hop in range(1, ny)])

        @pl.when(here < seq - 1)
        def _():
            to_right.start()

        @pl.when(here > 0)
        def _():
            to_left.start()

        @pl.when(here == 0)
        def _():
            r.x[0:HALF] = jnp.zeros((HALF, D), BF16)

        @pl.when(here == seq - 1)
        def _():
            r.x[HALF + count :] = jnp.zeros((HALF, D), BF16)

        for i in range(7):
            mask = tap_mask(ends, start, i % 5, i // 5, size, row_len)
            r.mask[i] = jnp.broadcast_to(mask, (size, LANES))
        loads[0].wait()
        inner = slice(HALF, HALF + count)
        for weight, load, cells in ((r.wk, loads[1], r.ks), (r.wv, loads[2], r.vs)):
            load.wait()
            cells[inner] = nn(r.x[inner], weight[...]).astype(BF16)

        @pl.when(here > 0)
        def _():
            to_right.wait_recv()

        @pl.when(here < seq - 1)
        def _():
            to_left.wait_recv()

        for weight, cells in ((r.wk, r.ks), (r.wv, r.vs)):
            for outer in (slice(0, HALF), slice(HALF + count, span)):
                cells[outer] = nn(r.x[outer], weight[...]).astype(BF16)
        for which, source in ((0, r.ks), (1, r.vs)):
            for c in range(PAIRS):
                lanes = slice(c * LANES, (c + 1) * LANES)
                r.cells[c] = source[:, lanes].astype(F32)
                total = jnp.zeros((size, LANES), F32)
                for tap in range(5):
                    taken = r.cells.at[c][pl.ds(HALF + tap - 2, size, stride=4), :]
                    total = total + taken * r.mask[tap] * r.pool_weight[tap : tap + 1, lanes]
                r.pieces[0, which, :, lanes] = total.astype(BF16)
        for hop in range(1, ny):
            to_y(hop).start()
        to_core(0).start()
        loads[3].wait()
        r.qs[...] = (nn(r.x[inner], r.wq[...]).astype(BF16).astype(F32) * 0.125).astype(BF16)
        r.tt[...] = r.x[inner].T
        for store in stores:
            store.start()
        for b in range(count // QB):
            query_place = start + b * QB + iota((1, QB), 1)
            key_place = start - HALF + b * QB + iota((2 * QB, 1), 0)
            same = segment_of(ends, key_place, row_len) == segment_of(ends, query_place, row_len)
            near = jnp.abs(key_place - query_place) <= HALF
            r.near_bias[b] = jnp.where(same & near, 0.0, -1e30)

    @pl.when((step >= FORWARD_NEAR) & (step < FORWARD_POOL))
    def _():
        p = step - FORWARD_NEAR
        lanes = pl.ds(pl.multiple_of(p * LANES, LANES), LANES)
        vt = r.vs[:, lanes].T
        ones = jnp.ones((16, span), BF16)
        for head in range(2):
            qh = head_half(r.qs[:, lanes], head)
            va = jnp.concatenate([vt[head * 64 : head * 64 + 64], ones], axis=0)
            for b in range(count // QB):
                cols = slice(b * QB, (b + 1) * QB)
                keys = slice(b * QB, (b + 2) * QB)
                s = nt(r.ks[keys, lanes], qh[cols]) + r.near_bias[b]
                top = jnp.max(s, axis=0, keepdims=True)
                e = jnp.exp(s - top).astype(BF16)
                r.near_e[head, b] = e
                oa = nn(va[:, keys], e)
                r.o_near[p, head * 64 : head * 64 + 64, cols] = oa[:64]
                r.stats[p, head : head + 1, cols] = top
                r.stats[p, 2 + head : 3 + head, cols] = oa[64:65]

    @pl.when(step == FORWARD_POOL - 2)
    def _():
        query_place = start + iota((1, count), 1)
        query_item = segment_of(ends, query_place, row_len)
        for i in range(seq):
            owner = ((y + i % ny) % ny) * 2 + (core + i // ny) % 2
            key_place = 4 * (owner * size + iota((size, 1), 0))
            same = segment_of(ends, key_place, row_len) == query_item
            near = jnp.abs(key_place - query_place) <= 2 * PWIN
            r.pool_bias[i * size : (i + 1) * size] = jnp.where(same & near, 0.0, -1e30)

    @pl.when(step == FORWARD_POOL - 1)
    def _():
        for hop in range(1, ny):
            to_y(ny - hop).wait_recv()
            to_core(hop).start()

    @pl.when(step == FORWARD_POOL)
    def _():
        for hop in range(ny):
            to_core(hop).wait_recv()
        store_pieces.start()

    @pl.when(step >= FORWARD_POOL)
    def _():
        p = step - FORWARD_POOL
        lanes = pl.ds(pl.multiple_of(p * LANES, LANES), LANES)
        kp = jnp.concatenate([r.pieces[i, 0, :, lanes] for i in range(seq)], axis=0)
        vt = jnp.concatenate([r.pieces[i, 1, :, lanes] for i in range(seq)], axis=0).T
        ones = jnp.ones((16, seq * size), BF16)
        wide = min(256, count)
        for b in range(count // wide):
            cols = slice(b * wide, (b + 1) * wide)
            outs, near_scale, pool_scale = [], [], []
            for head in range(2):
                qh = head_half(r.qs[cols, lanes], head)
                va = jnp.concatenate([vt[head * 64 : head * 64 + 64], ones], axis=0)
                s = nt(kp, qh) + r.pool_bias[:, cols]
                near_top = r.stats[p, head : head + 1, cols]
                top = jnp.maximum(jnp.max(s, axis=0, keepdims=True), near_top)
                e = jnp.exp(s - top).astype(BF16)
                r.pool_e[head, :, cols] = e
                oa = nn(va, e)
                fade = jnp.exp(near_top - top)
                inverse = 1.0 / (fade * r.stats[p, 2 + head : 3 + head, cols] + oa[64:65])
                rows = slice(head * 64, head * 64 + 64)
                outs.append((fade * r.o_near[p, rows, cols] + oa[:64]) * inverse)
                near_scale.append(jnp.broadcast_to(fade * inverse, (64, wide)))
                pool_scale.append(jnp.broadcast_to(inverse, (64, wide)))
            r.o_out[cols, :] = jnp.concatenate(outs, axis=0).T
            r.rn_out[cols, :] = jnp.concatenate(near_scale, axis=0).T
            r.rp_out[cols, :] = jnp.concatenate(pool_scale, axis=0).T

    @pl.when(step == FORWARD_LAST)
    def _():
        for store in stores + [store_pieces]:
            store.wait()
        for hop in range(1, ny):
            to_y(hop).wait_send()
        for hop in range(ny):
            to_core(hop).wait_send()

        @pl.when(here < seq - 1)
        def _():
            to_right.wait_send()

        @pl.when(here > 0)
        def _():
            to_left.wait_send()


CHUNKS = FF // D
BUFFERS = ("sum", "core", "first", "second", "third", "out", "inn")
ATTEND = CHUNKS + 1
LAG = 3
LATE = ATTEND + PAIRS
LAST = LATE + LAG - 1
SPLIT = 4 * LANES
PARTS = (("A", 0, SPLIT), ("B", SPLIT, D))
NAMES = ("in0", "in1", "in2", "in3", "b0", "b1", "b2", "b3", "out", "q", "kA", "vA", "kB", "vB", "small", "query", "tokens")
(IN0, IN1, IN2, IN3, B0, B1, B2, B3, OUT, Q, KA, VA, KB, VB, SMALL, QUERY, TOKENS) = range(17)
XYZ = "xyz"
XZY = "xzy"
YXZ = "yxz"
YZX = "yzx"
ZYX = "zyx"
ORDERS = dict(zip(NAMES, (XYZ, ZYX, YXZ, XYZ, XYZ, YZX, XYZ, XZY, ZYX, XYZ, YZX, YXZ, YXZ, XZY, YXZ)))
PLAN = {
    (2, 0): (
        (IN1, 0),
    ),
    (2, 1): (
        (IN0, 0),
    ),
    (3, 0): (
        (IN2, 0),
    ),
    (4, 1): (
        (IN3, 0), (B1, 0),
    ),
    (5, 0): (
        (B0, 0), (OUT, 0),
    ),
    (6, 0): (
        (IN0, 1),
    ),
    (6, 1): (
        (B2, 0),
    ),
    (7, 0): (
        (IN2, 1),
    ),
    (8, 0): (
        (B1, 1), (IN3, 1), (IN1, 1),
    ),
    (9, 0): (
        (B3, 0), (IN0, 2),
    ),
    (9, 1): (
        (B0, 1), (OUT, 1),
    ),
    (10, 0): (
        (IN3, 2), (IN2, 2), (IN1, 2),
    ),
    (10, 1): (
        (B2, 1),
    ),
    (11, 1): (
        (B3, 1), (OUT, 2), (B1, 2), (QUERY, 0), (B0, 2), (KA, 0), (Q, 0),
    ),
    (12, 1): (
        (VA, 0), (B2, 2),
    ),
    (13, 1): (
        (VB, 0), (KB, 0), (KA, 1), (SMALL, 0), (Q, 1), (VA, 1), (VB, 1), (VA, 2),
        (B3, 2), (KB, 1), (Q, 2), (SMALL, 1), (KB, 2), (KA, 2),
        (SMALL, 2), (IN3, 3), (VB, 2), (TOKENS, 0), (VB, 3), (OUT, 3), (B0, 3), (B1, 3), (B2, 3),
        (B3, 3), (IN0, 3), (IN1, 3), (IN2, 3), (Q, 3), (KA, 3), (VA, 3), (KB, 3), (SMALL, 3),
    ),
}


def backward_kernel(*refs, names, pieces):
    r = Refs()
    for name, ref in zip(names, refs):
        setattr(r, name, ref)
    kv = [r.piece.at[i] for i in range(pieces)]
    seq, ny = pieces, pieces // 2
    step = pl.program_id(0)
    count = r.q.shape[0]
    size = count // 4
    nz, nx = r.b_send.shape[2:4]
    here, row = lax.axis_index("seq"), lax.axis_index("dp")
    y, core = here // 2, here % 2
    partner = (y * 2 + 1 - core, row)
    right, left = ((here + 1) % seq, row), ((here + seq - 1) % seq, row)
    units_back = r.b_send.shape[0]
    senders = {"small": r.s_send}
    for f in range(CHUNKS):
        senders["in%d" % f] = r.a_send.at[f]
    for place, name in enumerate(("out", "q")):
        senders[name] = r.a_send.at[place]
    for part, _, _ in PARTS:
        for name in ("k" + part, "v" + part):
            senders[name] = getattr(r, name + "_send")
    for u in range(units_back):
        senders["b%d" % u] = r.b_send.at[u]
    sums = {}
    for name in senders:
        bufs = [getattr(r, name + "_" + part) for part in BUFFERS]
        sums[name] = Summed(ORDERS[name], lambda u, name=name: senders[name], *bufs)

    def copy(src, dst, out_sem, in_sem, device):
        return pltpu.make_async_remote_copy(
            src_ref=src, dst_ref=dst, send_sem=out_sem, recv_sem=in_sem,
            device_id=device, device_id_type=MESH_ID,
        )

    def pool_core(p):
        return copy(r.p_send.at[p], r.p_in.at[p], r.p_sem.at[0, p, 0], r.p_sem.at[1, p, 0], partner)

    def pool_y(p, hop):
        device = (((y + hop) % ny) * 2 + core, row)
        return copy(
            r.p_keep.at[p, hop], r.p_y.at[p, hop - 1], r.p_sem.at[0, p, hop], r.p_sem.at[1, p, hop], device
        )

    def halo(p, side):
        device = right if side else left
        return copy(
            r.h_out.at[p, side], r.h_in.at[p, side], r.h_sem.at[0, p, side], r.h_sem.at[1, p, side], device
        )

    def chunk_loads(f):
        slot = f % 2
        part = pl.ds(pl.multiple_of(f * D, D), D)
        return [
            pltpu.make_async_copy(r.win_any.at[:, part], r.wbuf.at[slot], r.l_sem.at[0, slot]),
            pltpu.make_async_copy(r.wback_any.at[part, :], r.wbuf.at[2 + slot], r.l_sem.at[1, slot]),
            pltpu.make_async_copy(r.act_any.at[:, part], r.tbuf.at[slot], r.l_sem.at[2, slot]),
            pltpu.make_async_copy(r.slope_any.at[:, part], r.tbuf.at[2 + slot], r.l_sem.at[3, slot]),
        ]

    load_feed = [
        pltpu.make_async_copy(r.fg_any, r.fg, r.l_sem.at[4, 0]),
        pltpu.make_async_copy(r.lowt_any, r.lt, r.l_sem.at[4, 1]),
        pltpu.make_async_copy(r.zg_any, r.sg, r.l_sem.at[5, 0]),
    ]
    load_unit = pltpu.make_async_copy(r.unit_any, r.acc.at[0], r.l_sem.at[5, 1])
    load_wout = pltpu.make_async_copy(r.wout_any, r.wbuf.at[0], r.l_sem.at[6, 0])
    load_att = pltpu.make_async_copy(r.att_any, r.att, r.l_sem.at[6, 1])
    load_wq = pltpu.make_async_copy(r.wq_any, r.wbuf.at[1], r.l_sem.at[7, 0])
    load_wk = pltpu.make_async_copy(r.wk_any, r.wbuf.at[2], r.l_sem.at[7, 1])
    load_wv = pltpu.make_async_copy(r.wv_any, r.wbuf.at[3], r.l_sem.at[8, 0])
    load_tt = pltpu.make_async_copy(r.tt_any, r.lt, r.l_sem.at[8, 1])

    def rows_of(block, mine):
        rc = D // seq
        return pl.ds(pl.multiple_of((2 * block + mine) * rc, rc), rc)

    @pl.when(step == 0)
    def _():
        for load in chunk_loads(0)[1:2] + load_feed[:1] + chunk_loads(0)[3:] + load_feed[1:2]:
            load.start()
        for load in chunk_loads(0)[:1] + chunk_loads(0)[2:3] + load_feed[2:]:
            load.start()
        z, x = row // nx, row % nx
        peers = [partner, right, left]
        peers += [(((y + hop) % ny) * 2 + core, row) for hop in range(1, ny)]
        peers += [(here, z * nx + (x + hop) % nx) for hop in range(1, nx)]
        peers += [(here, ((z + hop) % nz) * nx + x) for hop in range(1, nz)]
        greet(peers)
        for load in load_feed[:2]:
            load.wait()

    def query_gradient():
        sums["in1"].sent_core(0)
        for block in range(ny):
            store_chunks(r.a_send.at[1, block], nn(r.lt[rows_of(block, 1 - core), :], r.tbuf[0]))
        sums["q"].start(0)
        for block in range(ny):
            store_chunks(sums["q"].keep.at[0, block], nn(r.lt[rows_of(block, core), :], r.tbuf[0]))

    def tokens_gradient():
        for load in (load_wq, load_wk, load_wv):
            load.wait()
        total = r.sg[...] + nt(r.tbuf[0], r.wbuf[1])
        total = total + nt(r.tbuf[1], r.wbuf[2])
        r.tokens_grad[...] = (total + nt(r.tbuf[2], r.wbuf[3])).astype(BF16)

    results = {"out": r.t_out, "q": r.t_query, "small": r.t_small}
    for part, _, _ in PARTS:
        for name in ("k" + part, "v" + part):
            results[name] = getattr(r, "t_" + name)
    for f in range(CHUNKS):
        results["in%d" % f] = r.t_in.at[f]
    for u in range(units_back):
        results["b%d" % u] = r.t_back.at[u]

    def run(name, stage):
        if name == "query":
            query_gradient()
        elif name == "tokens":
            tokens_gradient()
        elif name in sums:
            done = getattr(sums[name], ("core", "one", "two", "three")[stage])(0)
            if stage == 3:
                results[name][...] = done

    def run_plan(half):
        for (when, part), todo in PLAN.items():
            if part == half:

                @pl.when(step == when)
                def _(todo=todo):
                    for index, stage in todo:
                        run(NAMES[index], stage)

    @pl.when(step < CHUNKS)
    def _():
        f = step
        slot = f % 2
        early, late = chunk_loads(f)[1::2], chunk_loads(f)[0::2]
        for load in early:
            load.wait()

        @pl.when(f < CHUNKS - 1)
        def _():
            for load in chunk_loads(f + 1):
                load.start()

        @pl.when(f == 1)
        def _():
            load_unit.start()
            load_att.start()

        @pl.when(f == CHUNKS - 1)
        def _():
            load_wout.start()

        slope = r.tbuf[2 + slot].astype(F32)
        inner_grad = (nt(r.fg[...], r.wbuf[2 + slot]) * slope).astype(BF16)
        for block in range(ny):
            store_chunks(r.a_send.at[f, block], nn(r.lt[rows_of(block, 1 - core), :], inner_grad))

        kept = [nn(r.lt[rows_of(block, core), :], inner_grad) for block in range(ny)]
        for i in range(CHUNKS):

            @pl.when(f == i)
            def _(i=i):
                sums["in%d" % i].start(0)
                for block in range(ny):
                    store_chunks(sums["in%d" % i].keep.at[0, block], kept[block])

        run_plan(0)
        for load in late:
            load.wait()

        @pl.when(f == 0)
        def _():
            load_feed[2].wait()

        r.sg[...] += nt(inner_grad, r.wbuf[slot])
        back = nn(r.tbuf[slot].T, r.fg[...])
        part = FF // seq
        for sub in range(D // part):
            block = f * (D // part) + sub
            piece = back[sub * part : (sub + 1) * part]

            @pl.when(block % 2 == core)
            def _(block=block, piece=piece):
                keeps = [sums["b%d" % u].keep.at[0] for u in range(units_back)]
                store_blocks(keeps, block // 2, piece)

            @pl.when(block % 2 != core)
            def _(block=block, piece=piece):
                store_blocks([r.b_send.at[u] for u in range(units_back)], block // 2, piece)

        @pl.when(f == CHUNKS - 1)
        def _():
            for u in range(units_back):
                sums["b%d" % u].start(0)

    @pl.when(step == LATE - 1)
    def _():
        load_tt.wait()

    @pl.when(step == CHUNKS)
    def _():
        load_wq.start()
        load_wk.start()
        load_wv.start()
        load_unit.wait()
        inverse = r.inv[:, 0:1]
        total = jnp.zeros((count, LANES), F32)
        total_unit = jnp.zeros((count, LANES), F32)
        r.small[...] = jnp.zeros_like(r.small)
        r.small[0:8] = r.sums[...]
        for c in range(PAIRS):
            lanes = slice(c * LANES, (c + 1) * LANES)
            grad, unit = r.sg[:, lanes], r.acc[0, c]
            r.small[0:1, lanes] = jnp.sum(grad * unit, axis=0, keepdims=True)
            r.small[1:2, lanes] = jnp.sum(grad, axis=0, keepdims=True)
            e = grad * r.vecs[0:1, lanes]
            total = total + e
            total_unit = total_unit + e * unit
        mean = jnp.sum(total, axis=1, keepdims=True) * (1.0 / D)
        mean_unit = jnp.sum(total_unit, axis=1, keepdims=True) * (1.0 / D)
        for c in range(PAIRS):
            lanes = slice(c * LANES, (c + 1) * LANES)
            e = r.sg[:, lanes] * r.vecs[0:1, lanes]
            r.sg[:, lanes] = inverse * (e - mean - r.acc[0, c] * mean_unit)
        branch_grad = r.sg[...].astype(BF16)
        load_att.wait()
        load_wout.wait()
        sums["in0"].sent_core(0)
        for block in range(ny):
            store_chunks(r.a_send.at[0, block], nn(r.att[rows_of(block, 1 - core), :], branch_grad))
        sums["out"].start(0)
        for block in range(ny):
            store_chunks(sums["out"].keep.at[0, block], nn(r.att[rows_of(block, core), :], branch_grad))
        load_tt.start()
        attended_grad = nt(branch_grad, r.wbuf[0])
        for c in range(PAIRS):
            r.acc[1, c] = attended_grad[:, c * LANES : (c + 1) * LANES]

    def pool_on(p):
        pool_core(p).wait_recv()
        for hop in range(1, ny):
            for which in range(2):
                r.p_keep[p, hop, which] = r.p_keep[p, hop, which] + r.p_in[p, hop, which]
            pool_y(p, hop).start()

    @pl.when((step >= ATTEND) & (step < LATE))
    def _():
        p = step - ATTEND
        r.gb[...] = (r.acc[1, p] * r.rp[...]).astype(BF16)
        delta = score_delta(r.gb[...], r.o[...])
        kp = jnp.concatenate([piece[0] for piece in kv], axis=0)
        kt = kp.T
        vp = jnp.concatenate([piece[1] for piece in kv], axis=0)
        wide = min(256, count)
        for head in range(2):
            for b in range(count // wide):
                cols = slice(b * wide, (b + 1) * wide)
                gh = head_half(r.gb[cols, :], head)
                qh = head_half(r.q[cols, :], head)
                low = r.pool_e[head, :, cols]
                dp = nt(vp, gh) - delta[head : head + 1, cols]
                ds = (low.astype(F32) * dp).astype(BF16)
                key_part = nn(ds, qh)
                value_part = nn(low, gh)
                if head == 0 and b == 0:
                    r.dk[0 : seq * size] = key_part
                    r.dv[0 : seq * size] = value_part
                else:
                    r.dk[0 : seq * size] += key_part
                    r.dv[0 : seq * size] += value_part
                r.dq_pool[p, head * 64 : head * 64 + 64, cols] = nn(kt[head * 64 : head * 64 + 64], ds)
        for i in range(pieces):
            target = r.p_keep if i < ny else r.p_send
            after = (((y + i % ny) % ny) * 2 + (core + i // ny) % 2 + 1) % seq
            index = ((after % 2 - core + 2) % 2) * ny + (after // 2 - y + ny) % ny
            rows = pl.ds(pl.multiple_of(index * size, size), EXTRA)
            for which, total in ((0, r.dk), (1, r.dv)):
                target[p, i % ny, which, 0:size] = total[i * size : (i + 1) * size].astype(BF16)
                target[p, i % ny, which, size:] = total[rows, :].astype(BF16)
        pool_core(p).start()

        @pl.when(p > 0)
        def _():
            pool_on(p - 1)

        run_plan(0)

        r.gb[...] = (r.acc[1, p] * r.rn[...]).astype(BF16)
        delta = score_delta(r.gb[...], r.o[...])
        kt = r.keys[...].T
        r.dk[0 : count + 2 * HALF] = jnp.zeros((count + 2 * HALF, LANES), F32)
        r.dv[0 : count + 2 * HALF] = jnp.zeros((count + 2 * HALF, LANES), F32)
        for b in range(count // QB):
            cols = slice(b * QB, (b + 1) * QB)
            keys = slice(b * QB, (b + 2) * QB)
            lows, scores, grads, queries, dqs = [], [], [], [], []
            for head in range(2):
                gh = head_half(r.gb[cols, :], head)
                low = r.near_e[head, b]
                dp = nt(r.values[keys, :], gh) - delta[head : head + 1, cols]
                ds = (low.astype(F32) * dp).astype(BF16)
                dqs.append(nn(kt[head * 64 : head * 64 + 64, keys], ds))
                lows.append(low)
                scores.append(ds)
                grads.append(gh)
                queries.append(head_half(r.q[cols, :], head))
            r.dk[keys, :] += nn(jnp.concatenate(scores, axis=1), jnp.concatenate(queries, axis=0))
            r.dv[keys, :] += nn(jnp.concatenate(lows, axis=1), jnp.concatenate(grads, axis=0))
            total = (jnp.concatenate(dqs, axis=0) + r.dq_pool[p, :, cols]) * 0.125
            lanes = pl.ds(pl.multiple_of(p * LANES, LANES), LANES)
            r.tbuf[0, cols, lanes] = total.T.astype(BF16)
        for which, total in ((0, r.dk), (1, r.dv)):
            r.h_out[p, 0, which] = total[0:HALF].astype(BF16)
            r.acc[which, p] = total[HALF : HALF + count]
            r.h_out[p, 1, which] = total[HALF + count : 2 * HALF + count].astype(BF16)

        @pl.when(here > 0)
        def _():
            halo(p, 0).start()

        @pl.when(here < seq - 1)
        def _():
            halo(p, 1).start()

        @pl.when(p == PAIRS - 1)
        def _():
            pool_on(p)

    @pl.when(step >= ATTEND + LAG)
    def _():
        p = step - ATTEND - LAG
        lanes = pl.ds(pl.multiple_of(p * LANES, LANES), LANES)
        for hop in range(1, ny):
            pool_y(p, hop).wait_recv()

        @pl.when(here < seq - 1)
        def _():
            halo(p, 0).wait_recv()
            for which in range(2):
                r.acc[which, p, count - HALF :, :] += r.h_in[p, 0, which].astype(F32)

        @pl.when(here > 0)
        def _():
            halo(p, 1).wait_recv()
            for which in range(2):
                r.acc[which, p, 0:HALF, :] += r.h_in[p, 1, which].astype(F32)

        moves = ((2, 0, 0), (3, 1, 0), (4, 2, 0), (0, 2, 1), (1, 3, 1))
        sums = [jnp.zeros((1, LANES), F32)] * 5
        for which, source in ((0, r.keys_late), (1, r.values_late)):
            grad = r.acc.at[which, p]
            r.cells[...] = source[...].astype(F32)
            total = r.p_keep[p, 0, which].astype(F32) + r.p_in[p, 0, which].astype(F32)
            for hop in range(1, ny):
                total = total + r.p_y[p, hop - 1, which].astype(F32)
            r.g[...] = total
            for tap, place, shift in moves:
                mask = r.masks[5 * shift + tap]
                spread = r.g[shift : shift + size, :] * mask * r.taps[tap : tap + 1, :]
                grad[pl.ds(place, size, stride=4), :] += spread
            for tap in range(5):
                taken = r.cells[pl.ds(HALF + tap - 2, size, stride=4), :]
                product = r.g[0:size, :] * r.masks[tap] * taken
                sums[tap] = sums[tap] + jnp.sum(product, axis=0, keepdims=True)
            r.tbuf[1 + which, :, lanes] = grad[...].astype(BF16)
        for tap in range(5):
            r.small[8 + tap : 9 + tap, lanes] = sums[tap]

    def key_gradients(part, first, last):
        for name, low in (("k" + part, 1), ("v" + part, 2)):
            for block in range(ny):
                rows = rows_of(block, 1 - core)
                store_chunks(senders[name].at[block], nn(r.lt[rows, :], r.tbuf[low, :, first:last]))
            sums[name].start(0)
            keep = sums[name].keep
            for block in range(ny):
                rows = rows_of(block, core)
                store_chunks(keep.at[0, block], nn(r.lt[rows, :], r.tbuf[low, :, first:last]))

    @pl.when(step == LATE)
    def _():
        key_gradients(*PARTS[0])

    @pl.when(step == LAST)
    def _():
        key_gradients(*PARTS[1])
        r.small_t[...] = r.small[...].T
        few = D // (seq * nz * nx)
        for block in range(ny):
            for part, mine in ((r.s_send.at[block], 1 - core), (sums["small"].keep.at[0, block], core)):
                vectors = r.small_t[rows_of(block, mine), :]
                for z in range(nz):
                    for x in range(nx):
                        start = (z * nx + x) * few
                        part[z, x] = jnp.zeros(part.shape[2:], BF16)
                        part[z, x, 0:few] = vectors[start : start + few].astype(BF16)
        sums["small"].start(0)

    run_plan(1)

    @pl.when(step == LAST)
    def _():
        reused = ["in0", "in1"]
        for name in sums:
            if name not in reused:
                sums[name].sent_core(0)
            sums[name].sent(0)
        for p in range(PAIRS):
            pool_core(p).wait_send()
            for hop in range(1, ny):
                pool_y(p, hop).wait_send()

        @pl.when(here > 0)
        def _():
            for p in range(PAIRS):
                halo(p, 0).wait_send()

        @pl.when(here < seq - 1)
        def _():
            for p in range(PAIRS):
                halo(p, 1).wait_send()


def unpack_kernel(t_in, t_back, t_query, t_ka, t_kb, t_va, t_vb, t_out, t_small, tg, *outs):
    tokens_grad, query, key, value, out, inn, back = outs[:7]
    rows = query.shape[0]
    tokens_grad[...] = tg[...]
    for source, target in ((t_query, query), (t_out, out)):
        target[...] = unfold_rows(source[...], rows)
    for one, two, target in ((t_ka, t_kb, key), (t_va, t_vb, value)):
        target[:, 0:SPLIT] = unfold_rows(one[...], rows)
        target[:, SPLIT:] = unfold_rows(two[...], rows)
    for u in range(CHUNKS):
        inn[:, u * D : (u + 1) * D] = unfold_rows(t_in[u], rows)
    units, part, wide = t_back.shape
    across = back.shape[1] // wide
    for u in range(units):
        top, start = (u // across) * part, (u % across) * wide
        back[top : top + part, start : start + wide] = t_back[u]
    small = t_small[...]
    pad = LANES - small.shape[0]
    turned = jnp.concatenate([small, jnp.zeros((pad, LANES), F32)], axis=0).T
    for i in range(4):
        outs[7 + i][...] = turned[i : i + 1, 0:rows]
    outs[11][...] = turned[8:13, 0:rows]


def call(kernel, args, in_specs, outs, out_specs, grid, scratch, flops, name):
    moved = sum(a.size * a.dtype.itemsize for a in list(args) + list(outs))
    return pl.pallas_call(
        kernel,
        grid_spec=pltpu.PrefetchScalarGridSpec(
            num_scalar_prefetch=0,
            grid=grid,
            in_specs=in_specs,
            out_specs=out_specs,
            scratch_shapes=scratch,
        ),
        out_shape=outs,
        compiler_params=pltpu.CompilerParams(
            vmem_limit_bytes=60 * MB, dimension_semantics=("arbitrary",) * len(grid)
        ),
        cost_estimate=pl.CostEstimate(flops=flops, bytes_accessed=moved, transcendentals=0),
        name=name,
    )(*args)


def whole(array):
    rank = len(array.shape)
    return pl.BlockSpec(array.shape, lambda i: (0,) * rank)


def columns(array, width=LANES):
    rank = len(array.shape)
    return pl.BlockSpec(array.shape[:-1] + (width,), lambda i: (0,) * (rank - 1) + (i,))


def leading(array, size):
    rank = len(array.shape)
    return pl.BlockSpec((size,) + array.shape[1:], lambda i: (i,) + (0,) * (rank - 1))


def per_device(
    tokens,
    item_lengths,
    w_query,
    w_key,
    w_value,
    w_out,
    w_in,
    w_back,
    norm1_gain,
    norm1_bias,
    norm2_gain,
    norm2_bias,
    pool_weight,
    out_grad,
):
    _, count, _ = tokens.shape
    seq = lax.axis_size("seq")
    ny = seq // 2
    row_len = count * seq
    span = count + 2 * HALF
    size = count // 4
    tok = tokens[0]
    og = out_grad[0]
    taps = pool_weight.T
    vecs = jnp.stack([norm1_gain, norm1_bias, norm2_gain, norm2_bias])

    def shape(dims, kind):
        return jax.ShapeDtypeStruct(dims, kind)

    blocks = count // QB
    pool_all = seq * size
    anywhere = pl.BlockSpec(memory_space=pl.ANY)

    def in_first(i):
        return jnp.clip(i - FORWARD_NEAR, 0, PAIRS - 1)

    def in_second(i):
        return jnp.clip(i - FORWARD_POOL, 0, PAIRS - 1)

    ins = [
        ("lengths", item_lengths, pl.BlockSpec(memory_space=pltpu.SMEM)),
        ("pool_weight", taps, whole(taps)),
        ("tok", tok, anywhere),
        ("wq_any", w_query, anywhere),
        ("wk_any", w_key, anywhere),
        ("wv_any", w_value, anywhere),
    ]
    near_shape = shape((H, blocks, 2 * QB, QB), BF16)
    pool_shape = shape((H, pool_all, count), BF16)
    wide_shape = shape((count, D), F32)
    outs = [
        ("q_out", shape((count, D), BF16), anywhere),
        ("k_out", shape((span, D), BF16), anywhere),
        ("v_out", shape((span, D), BF16), anywhere),
        ("tt_out", shape((D, count), BF16), anywhere),
        ("mask_out", shape((7, size, LANES), F32), anywhere),
        ("pieces_out", shape((seq, 2, size, D), BF16), anywhere),
        ("near_e", near_shape, pl.BlockSpec((2, blocks, 2 * QB, QB), lambda i: (in_first(i), 0, 0, 0))),
        ("pool_e", pool_shape, pl.BlockSpec((2, pool_all, count), lambda i: (in_second(i), 0, 0))),
        ("o_out", wide_shape, pl.BlockSpec((count, LANES), lambda i: (0, in_second(i)))),
        ("rn_out", wide_shape, pl.BlockSpec((count, LANES), lambda i: (0, in_second(i)))),
        ("rp_out", wide_shape, pl.BlockSpec((count, LANES), lambda i: (0, in_second(i)))),
    ]
    scratch = [
        ("x", pltpu.VMEM((span, D), BF16)),
        ("wq", pltpu.VMEM((D, D), BF16)),
        ("wk", pltpu.VMEM((D, D), BF16)),
        ("wv", pltpu.VMEM((D, D), BF16)),
        ("qs", pltpu.VMEM((count, D), BF16)),
        ("ks", pltpu.VMEM((span, D), BF16)),
        ("vs", pltpu.VMEM((span, D), BF16)),
        ("tt", pltpu.VMEM((D, count), BF16)),
        ("mask", pltpu.VMEM((7, size, LANES), F32)),
        ("cells", pltpu.VMEM((PAIRS, span, LANES), F32)),
        ("pieces", pltpu.VMEM((seq, 2, size, D), BF16)),
        ("o_near", pltpu.VMEM((PAIRS, LANES, count), F32)),
        ("stats", pltpu.VMEM((PAIRS, 8, count), F32)),
        ("near_bias", pltpu.VMEM((blocks, 2 * QB, QB), F32)),
        ("pool_bias", pltpu.VMEM((pool_all, count), F32)),
        ("s_sem", pltpu.SemaphoreType.DMA((2 + seq,))),
        ("r_sem", pltpu.SemaphoreType.DMA((2 + seq,))),
        ("l_sem", pltpu.SemaphoreType.DMA((11,))),
    ]
    (queries, keys, values, tok_t, tap_masks, pieces, near_e, pool_e, attention, near_scale, pool_scale) = (
        pl.pallas_call(
            partial(forward_kernel, names=[entry[0] for entry in ins + outs + scratch]),
            grid_spec=pltpu.PrefetchScalarGridSpec(
                num_scalar_prefetch=0,
                grid=(FORWARD_LAST + 1,),
                in_specs=[entry[2] for entry in ins],
                out_specs=[entry[2] for entry in outs],
                scratch_shapes=[entry[1] for entry in scratch],
            ),
            out_shape=[entry[1] for entry in outs],
            compiler_params=pltpu.CompilerParams(
                collective_id=1,
                has_side_effects=True,
                vmem_limit_bytes=60 * MB,
                dimension_semantics=("arbitrary",),
            ),
            cost_estimate=pl.CostEstimate(
                flops=4 * H * 768 * 256 * count + 6 * count * D * D, bytes_accessed=16 * MB, transcendentals=0
            ),
            name="forward",
        )(*[entry[1] for entry in ins])
    )

    dp = lax.axis_size("dp")
    nx = 2 if dp % 2 == 0 else 1
    nz = dp // nx
    rows = D // (seq * dp)
    back_rows = FF // (seq * dp)
    down = 2 if back_rows % 32 == 0 else 1
    half_one = shape((ny, nz, nx) + folded(rows, D), BF16)
    half_back = shape((2 * down, ny, nz, nx, back_rows // down, D // 2), BF16)
    args = (attention, tok, og, vecs, w_out, w_in, w_back)
    outs = (
        shape((count, D), BF16),
        shape((count, FF), BF16),
        shape((count, FF), BF16),
        shape((D, count), BF16),
        shape((count, D), BF16),
        shape((count, D), F32),
        shape((PAIRS, count, LANES), F32),
        shape((count, LANES), F32),
        shape((D, count), BF16),
        shape((8, D), F32),
    )
    mixed, act, slope, low_t, feed_grad, z_grad, unit_one, inv_one, att_t, sums = call(
        dense_kernel,
        args,
        [whole(a) for a in args[:5]]
        + [columns(w_in, D), pl.BlockSpec((D, D), lambda i: (i, 0))],
        outs,
        [whole(outs[0]), columns(outs[1], D), columns(outs[2], D)] + [whole(a) for a in outs[3:]],
        (CHUNKS,),
        [
            pltpu.VMEM((count, D), F32),
            pltpu.VMEM((count, D), BF16),
            pltpu.VMEM((count, D), F32),
        ],
        2 * count * (D * D + 2 * D * FF),
        "dense",
    )
    half_small = shape((ny, nz, nx, -(-rows // 16) * 16, LANES), BF16)
    half_pool = (PAIRS, ny, 2, size + EXTRA, LANES)
    blocks_in = []

    def block(name, array, spec):
        blocks_in.append((name, array, spec))

    def col_spec(array, index):
        lead = (0,) * (len(array.shape) - 1)
        return pl.BlockSpec(array.shape[:-1] + (LANES,), lambda i: lead + (index(i),))

    def lead_spec(array, index):
        rest = (0,) * (len(array.shape) - 1)
        return pl.BlockSpec((2,) + array.shape[1:], lambda i: (index(i),) + rest)

    def all_spec(array):
        rest = (0,) * len(array.shape)
        return pl.BlockSpec(array.shape, lambda i: rest)

    def in_pair(i):
        return jnp.clip(i - ATTEND, 0, PAIRS - 1)

    def in_late(i):
        return jnp.clip(i - ATTEND - LAG, 0, PAIRS - 1)

    block("q", queries, col_spec(queries, in_pair))
    block("o", attention, col_spec(attention, in_pair))
    block("rp", pool_scale, col_spec(pool_scale, in_pair))
    block("rn", near_scale, col_spec(near_scale, in_pair))
    block("pool_e", pool_e, lead_spec(pool_e, in_pair))
    block("near_e", near_e, lead_spec(near_e, in_pair))
    block("keys", keys, col_spec(keys, in_pair))
    block("values", values, col_spec(values, in_pair))
    block("keys_late", keys, col_spec(keys, in_late))
    block("values_late", values, col_spec(values, in_late))
    block("piece", pieces, col_spec(pieces, in_pair))
    block("masks", tap_masks, all_spec(tap_masks))
    block("taps", taps, col_spec(taps, in_late))
    block("sums", sums, all_spec(sums))
    block("vecs", vecs, all_spec(vecs))
    block("inv", inv_one, all_spec(inv_one))
    for name, array in (
        ("win_any", w_in),
        ("wback_any", w_back),
        ("act_any", act),
        ("slope_any", slope),
        ("fg_any", feed_grad),
        ("lowt_any", low_t),
        ("zg_any", z_grad),
        ("unit_any", unit_one),
        ("wout_any", w_out),
        ("att_any", att_t),
        ("tt_any", tok_t),
        ("wq_any", w_query),
        ("wk_any", w_key),
        ("wv_any", w_value),
    ):
        block(name, array, anywhere)
    outs = [
        ("t_in", shape((CHUNKS,) + half_one.shape[3:], F32)),
        ("t_back", shape((half_back.shape[0],) + half_back.shape[4:], F32)),
        ("t_query", shape(half_one.shape[3:], F32)),
        ("t_kA", shape(folded(rows, SPLIT), F32)),
        ("t_kB", shape(folded(rows, D - SPLIT), F32)),
        ("t_vA", shape(folded(rows, SPLIT), F32)),
        ("t_vB", shape(folded(rows, D - SPLIT), F32)),
        ("t_out", shape(half_one.shape[3:], F32)),
        ("t_small", shape(half_small.shape[3:], F32)),
        ("tokens_grad", shape((count, D), BF16)),
    ]
    tall = max(pool_all, span)
    scratch = [
        ("dk", pltpu.VMEM((tall, LANES), F32)),
        ("dv", pltpu.VMEM((tall, LANES), F32)),
        ("dq_pool", pltpu.VMEM((PAIRS, LANES, count), F32)),
        ("gb", pltpu.VMEM((count, LANES), BF16)),
        ("acc", pltpu.VMEM((2, PAIRS, count, LANES), F32)),
        ("tbuf", pltpu.VMEM((4, count, D), BF16)),
        ("wbuf", pltpu.VMEM((4, D, D), BF16)),
        ("fg", pltpu.VMEM((count, D), BF16)),
        ("lt", pltpu.VMEM((D, count), BF16)),
        ("att", pltpu.VMEM((D, count), BF16)),
        ("cells", pltpu.VMEM((span, LANES), F32)),
        ("g", pltpu.VMEM((size + EXTRA, LANES), F32)),
        ("small", pltpu.VMEM((LANES, D), F32)),
        ("small_t", pltpu.VMEM((D, LANES), F32)),
        ("p_keep", pltpu.VMEM(half_pool, BF16)),
        ("p_send", pltpu.VMEM(half_pool, BF16)),
        ("p_in", pltpu.VMEM(half_pool, BF16)),
        ("p_y", pltpu.VMEM((PAIRS, ny - 1) + half_pool[2:], BF16)),
        ("h_out", pltpu.VMEM((PAIRS, 2, 2, HALF, LANES), BF16)),
        ("h_in", pltpu.VMEM((PAIRS, 2, 2, HALF, LANES), BF16)),
        ("p_sem", pltpu.SemaphoreType.DMA((2, PAIRS, ny))),
        ("h_sem", pltpu.SemaphoreType.DMA((2, PAIRS, 2))),
        ("l_sem", pltpu.SemaphoreType.DMA((9, 2))),
        ("sg", pltpu.VMEM((count, D), F32)),
        ("a_send", pltpu.VMEM((CHUNKS,) + half_one.shape, BF16)),
        ("b_send", pltpu.VMEM(half_back.shape, BF16)),
        ("s_send", pltpu.VMEM(half_small.shape, BF16)),
    ]
    sizes = {name: half_one.shape for name in ORDERS}
    sizes["small"] = half_small.shape
    for part, first, after in PARTS:
        for name in ("k" + part, "v" + part):
            sizes[name] = half_one.shape[:3] + folded(rows, after - first)
            scratch.append((name + "_send", pltpu.VMEM(sizes[name], BF16)))
    for u in range(CHUNKS):
        if u < half_back.shape[0]:
            sizes["b%d" % u] = half_back.shape[1:]
        else:
            del sizes["b%d" % u]
    for name, dims in sizes.items():
        bufs = summed_scratch(1, dims, ORDERS[name])
        scratch += [(name + "_" + part, buf) for part, buf in zip(BUFFERS, bufs)]
    names = [entry[0] for entry in blocks_in] + [entry[0] for entry in outs + scratch]
    moved = sum(entry[1].size * entry[1].dtype.itemsize for entry in blocks_in)
    totals = pl.pallas_call(
        partial(backward_kernel, names=names, pieces=seq),
        grid_spec=pltpu.PrefetchScalarGridSpec(
            num_scalar_prefetch=0,
            grid=(LAST + 1,),
            in_specs=[entry[2] for entry in blocks_in],
            out_specs=[all_spec(entry[1]) for entry in outs],
            scratch_shapes=[entry[1] for entry in scratch],
        ),
        out_shape=[entry[1] for entry in outs],
        compiler_params=pltpu.CompilerParams(
            collective_id=0,
            has_side_effects=True,
            vmem_limit_bytes=63 * MB,
            dimension_semantics=("arbitrary",),
        ),
        cost_estimate=pl.CostEstimate(
            flops=8 * H * 768 * 256 * count + 12 * count * D * D + 8 * count * D * FF, bytes_accessed=moved, transcendentals=0
        ),
        name="backward",
    )(*[entry[1] for entry in blocks_in])

    outs = (
        shape((count, D), BF16),
        shape((rows, D), F32),
        shape((rows, D), F32),
        shape((rows, D), F32),
        shape((rows, D), F32),
        shape((rows, FF), F32),
        shape((back_rows, D), F32),
        shape((1, rows), F32),
        shape((1, rows), F32),
        shape((1, rows), F32),
        shape((1, rows), F32),
        shape((5, rows), F32),
    )
    done = call(
        unpack_kernel,
        tuple(totals),
        [whole(a) for a in totals],
        outs,
        [whole(a) for a in outs],
        (1,),
        [],
        0,
        "unpack",
    )
    return (
        mixed[None],
        done[0][None],
        done[1],
        done[2],
        done[3],
        done[4],
        done[5],
        done[6],
        done[7].reshape(rows),
        done[8].reshape(rows),
        done[9].reshape(rows),
        done[10].reshape(rows),
        done[11].T,
    )


def solution(mesh):
    shards, copied = P("dp", "seq", None), P()
    spread = P(("seq", "dp"), None)
    vector = P(("seq", "dp"))
    return jax.shard_map(
        per_device,
        mesh=mesh,
        in_specs=(shards, P("dp", None)) + (copied,) * 11 + (shards,),
        out_specs=(shards, shards) + (spread,) * 6 + (vector,) * 4 + (spread,),
        check_vma=False,
    )
```
